32 devices in a mesh: section: 2 (over core), dp: 16 (over z, y, x).
Axes of the slice: x: 2, y: 2, z: 4, core: 2. Of those that a mesh axis runs over, the one named last changes fastest.
Arguments:
- clip_input: bfloat16 [32, 16, 14, 14, 832], P('dp', 'section'), may hold values from -30 to 30
- out_grad: bfloat16 [32, 8, 7, 7, 832], P('dp', 'section'), may hold values from -6 to 6
- clip_lengths: int32 [32, 2], P('dp'), may hold values from 2 to 8, as said below
- w_one: bfloat16 [2, 832, 256], P('section'), may hold values from -0.21875 to 0.21875
- w_mid_in: bfloat16 [2, 832, 160], P('section'), may hold values from -0.21875 to 0.21875
- w_mid: bfloat16 [2, 4320, 320], P('section'), may hold values from -0.09375 to 0.09375
- w_small_in: bfloat16 [2, 832, 32], P('section'), may hold values from -0.21875 to 0.21875
- w_small: bfloat16 [2, 864, 128], P('section'), may hold values from -0.21875 to 0.21875
- w_pool: bfloat16 [2, 832, 128], P('section'), may hold values from -0.21875 to 0.21875
- bn_offset: float32 [2, 1024], P('section'), may hold values from -3 to 3
Outputs:
- block_output: bfloat16 [32, 8, 7, 7, 832], P('dp', 'section')
- input_grad: bfloat16 [32, 16, 14, 14, 832], P('dp', 'section')
- w_one_grad: float32 [2, 832, 256], P('section')
- w_mid_in_grad: float32 [2, 832, 160], P('section')
- w_mid_grad: float32 [2, 4320, 320], P('section')
- w_small_in_grad: float32 [2, 832, 32], P('section')
- w_small_grad: float32 [2, 864, 128], P('section')
- w_pool_grad: float32 [2, 832, 128], P('section')
- bn_offset_grad: float32 [2, 1024], P('section')
The draws below stay inside these ranges and needn't reach their ends.
Inputs may be any that keep to these rules, and one draw needn't show every extreme that they name: `clip_lengths`: every entry is even; the clips of a slot take at most 16 frames together, the rest of the slot is padding; in some slot the last clip has 8 frames.
All inputs are finite; a program needn't handle non-finite values.
Results may differ from the reference program's by a relative error of at most 0.019.
Values may be sent and summed in bfloat16 or wider, within the bound.
A program may use at most 512 MiB of HBM per device.

```python
import jax
import jax.numpy as jnp
from jax import lax

D = 832
C0 = 256
C1A = 160
C1B = 320
C2A = 32
C2B = 128
C3 = 128
H = 14
FRAMES = 16
CLIPS = 2
MICRO = 2
SLOT_MB = 1
SLOTS = 32
N_DP = 16


def draw_clip_input(key, part):
    key = jax.random.fold_in(key, 11)
    noise_key = jax.random.fold_in(key, 0)
    rising = jnp.arange(SLOTS, dtype=jnp.float32) / (SLOTS - 1)
    scales = (10.0 ** rising)[:, None, None, None, None]
    values = jnp.clip(jax.random.normal(noise_key, (SLOTS, FRAMES, H, H, D), jnp.float32), -3.0, 3.0)
    return (values * scales).astype(jnp.bfloat16)


def draw_clip_lengths(key, part):
    key = jax.random.fold_in(key, 23)
    pick_key, length_key = jax.random.split(key)
    halves = jax.random.randint(length_key, (SLOTS, CLIPS), 1, FRAMES // (2 * CLIPS) + 1, dtype=jnp.int32)
    chosen = jax.random.randint(pick_key, (), 0, SLOTS, dtype=jnp.int32)
    slot_ids = jnp.arange(SLOTS, dtype=jnp.int32)[:, None]
    clip_ids = jnp.arange(CLIPS, dtype=jnp.int32)[None, :]
    forced = (slot_ids == chosen) & (clip_ids == CLIPS - 1)
    halves = jnp.where(forced, FRAMES // (2 * CLIPS), halves)
    return (2 * halves).astype(jnp.int32)


def steps_of(key, dims, cuts, smallest, top_value):
    gain = 1.0
    for dim, parts in cuts:
        steps = jax.random.uniform(jax.random.fold_in(jax.random.fold_in(key, 6), dim), (parts,), jnp.float32, smallest / len(cuts), top_value / len(cuts))
        gain = gain * jnp.repeat(jnp.exp(steps), dims[dim] // parts).reshape((-1,) + (1,) * (len(dims) - 1 - dim))
    return gain


def noise(key, extent, deviation, most, pieces=(), kind=jnp.bfloat16):
    values = deviation * jax.random.normal(key, extent, jnp.float32)
    if pieces:
        values = values * steps_of(key, extent, pieces, -0.22, 0.18)
    return jnp.clip(values, -most, most).astype(kind)


def setup_inputs(seed: int = 0) -> dict:
    arg_keys = jax.random.split(jax.random.key(seed), 11)
    return {
        "clip_input": draw_clip_input(jax.random.fold_in(arg_keys[10], 71), 0),
        "out_grad": noise(arg_keys[1], (SLOTS, FRAMES // 2, H // 2, H // 2, D), 1.0, 6.0, ((0, 16), (1, 2))),
        "clip_lengths": draw_clip_lengths(jax.random.fold_in(arg_keys[10], 71), 0),
        "w_one": noise(arg_keys[3], (2, D, C0), D ** -0.5, 0.21875, ((0, 2),)),
        "w_mid_in": noise(arg_keys[4], (2, D, C1A), D ** -0.5, 0.21875, ((0, 2),)),
        "w_mid": noise(arg_keys[5], (2, 27 * C1A, C1B), (27 * C1A) ** -0.5, 0.09375, ((0, 2),)),
        "w_small_in": noise(arg_keys[6], (2, D, C2A), D ** -0.5, 0.21875, ((0, 2),)),
        "w_small": noise(arg_keys[7], (2, 27 * C2A, C2B), (27 * C2A) ** -0.5, 0.21875, ((0, 2),)),
        "w_pool": noise(arg_keys[8], (2, D, C3), D ** -0.5, 0.21875, ((0, 2),)),
        "bn_offset": noise(arg_keys[9], (2, C0 + C1A + C1B + C2A + C2B + C3), 0.7, 3.0, ((0, 2),), jnp.float32),
    }


EPS = 0.001
HIGHEST = lax.Precision.HIGHEST
TAP_LIST = [(shift_t, shift_y, shift_x) for shift_t in (-1, 0, 1) for shift_y in (-1, 0, 1) for shift_x in (-1, 0, 1)]

@jax.custom_vjp
def low(v):
    return lax.optimization_barrier(v.astype(jnp.bfloat16)).astype(jnp.float32)

@jax.custom_vjp
def low_back(v):
    return v

def low_keep(v):
    return (low(v), None)

def low_pass(kept, grad):
    return (grad,)

def back_keep(v):
    return (v, None)

def back_low(kept, grad):
    return (low(grad),)
low.defvjp(low_keep, low_pass)
low_back.defvjp(back_keep, back_low)

def shift_frames(table, shift_t):
    padded = jnp.pad(table, ((0, 0), (1, 1)))
    return lax.slice_in_dim(padded, 1 + shift_t, 1 + shift_t + table.shape[1], axis=1)

def frame_masks(lengths, frame_total, stride):
    starts = jnp.cumsum(lengths, axis=1, dtype=jnp.int32) - lengths
    places = (jnp.arange(frame_total, dtype=jnp.int32) * stride)[None, None, :]
    inside = (places >= starts[:, :, None]) & (places < (starts + lengths)[:, :, None])
    validity = jnp.any(inside, axis=1).astype(jnp.float32)
    numbers = (jnp.arange(lengths.shape[1], dtype=jnp.int32) + 1)[None, :, None]
    labels = lax.optimization_barrier(jnp.sum(inside.astype(jnp.int32) * numbers, axis=1, dtype=jnp.int32))
    masks_list = []
    for shift_t in (-1, 0, 1):
        matched = (labels == shift_frames(labels, shift_t)).astype(jnp.float32)
        masks_list.append(validity * shift_frames(validity, shift_t) * matched)
    return (validity, jnp.stack(masks_list))

def shift_grid(volume, shift_t, shift_y, shift_x):
    leading = volume.ndim - 4
    padded = jnp.pad(volume, [(0, 0)] * leading + [(1, 1), (1, 1), (1, 1), (0, 0)])
    frame_count, rows_y, rows_x = (volume.shape[-4], volume.shape[-3], volume.shape[-2])
    padded = lax.slice_in_dim(padded, 1 + shift_t, 1 + shift_t + frame_count, axis=leading)
    padded = lax.slice_in_dim(padded, 1 + shift_y, 1 + shift_y + rows_y, axis=leading + 1)
    return lax.slice_in_dim(padded, 1 + shift_x, 1 + shift_x + rows_x, axis=leading + 2)

def box_sum(volume, tap_masks):
    temporal = jnp.zeros_like(volume)
    for shift_t in (-1, 0, 1):
        temporal = temporal + shift_grid(volume, shift_t, 0, 0) * tap_masks[shift_t + 1][:, :, None, None, None]
    rows_sum = shift_grid(temporal, 0, -1, 0) + temporal + shift_grid(temporal, 0, 1, 0)
    return shift_grid(rows_sum, 0, 0, -1) + rows_sum + shift_grid(rows_sum, 0, 0, 1)

def pool_counts(tap_masks, frame_side):
    spread = lax.optimization_barrier(jnp.sum(tap_masks, axis=0))
    places = jnp.arange(frame_side, dtype=jnp.int32)
    edges = 3.0 - (places == 0).astype(jnp.float32) - (places == frame_side - 1).astype(jnp.float32)
    counts = spread[:, :, None, None, None] * edges[:, None, None] * edges[None, :, None]
    return jnp.maximum(counts, 1.0)

def pool_pairs(volume):
    slot_count, frame_count, rows_y, rows_x, channel_count = volume.shape
    blocks = volume.reshape(slot_count, frame_count // 2, 2, rows_y // 2, 2, rows_x // 2, 2, channel_count)
    return lax.optimization_barrier(jnp.mean(blocks, axis=(2, 4, 6)))

def conv_taps(volume, tap_masks, weight):
    channel_count = volume.shape[-1]

    def one_slot(inputs_pair):
        slot_grid, slot_masks = inputs_pair
        summed = jnp.zeros(slot_grid.shape[:-1] + (weight.shape[1],), jnp.float32)
        for position, (shift_t, shift_y, shift_x) in enumerate(TAP_LIST):
            shifted = shift_grid(slot_grid, shift_t, shift_y, shift_x) * slot_masks[shift_t + 1][:, None, None, None]
            block_rows = weight[position * channel_count:(position + 1) * channel_count]
            summed = summed + jnp.einsum('fyxi,io->fyxo', shifted, block_rows, precision=HIGHEST)
        return summed
    return lax.map(jax.checkpoint(one_slot), (volume, jnp.moveaxis(tap_masks, 1, 0)))

def inception_layer(source, validity, tap_masks, params):
    w_one, w_mid_in, w_mid, w_small_in, w_small, w_pool, offset = params
    mask_grid = validity[:, :, None, None, None]
    frame_side = source.shape[2]
    voxel_count = jnp.sum(validity) * frame_side * frame_side
    bounds = [0, C0, C0 + C1A, C0 + C1A + C1B, C0 + C1A + C1B + C2A, C0 + C1A + C1B + C2A + C2B, C0 + C1A + C1B + C2A + C2B + C3]

    def batch_norm(values):
        center = lax.optimization_barrier(jnp.sum(values * mask_grid, axis=(0, 1, 2, 3))) / voxel_count
        variance = lax.optimization_barrier(jnp.sum(values * values * mask_grid, axis=(0, 1, 2, 3))) / voxel_count - center * center
        return (values - center) * lax.rsqrt(variance + EPS)

    def activate(values, position):
        return jax.nn.softplus(batch_norm(values) + offset[bounds[position]:bounds[position + 1]]) * mask_grid

    def project(values, weight):
        return jnp.einsum('sfyxi,io->sfyxo', values, weight, precision=HIGHEST)
    out_one = activate(low_back(project(source, w_one)), 0)
    mid_in = low(activate(low_back(project(source, w_mid_in)), 1))
    out_mid = activate(low_back(conv_taps(mid_in, tap_masks, w_mid)), 2)
    small_in = low(activate(low_back(project(source, w_small_in)), 3))
    out_small = activate(low_back(conv_taps(small_in, tap_masks, w_small)), 4)
    pooled_in = low(box_sum(source, tap_masks) / pool_counts(tap_masks, frame_side))
    out_pool = activate(low_back(project(pooled_in, w_pool)), 5)
    return jnp.concatenate([out_one, out_mid, out_small, out_pool], axis=-1)

def reference(clip_input, out_grad, clip_lengths, w_one, w_mid_in, w_mid, w_small_in, w_small, w_pool, bn_offset):
    params = (w_one.astype(jnp.float32), w_mid_in.astype(jnp.float32), w_mid.astype(jnp.float32), w_small_in.astype(jnp.float32), w_small.astype(jnp.float32), w_pool.astype(jnp.float32), bn_offset.astype(jnp.float32))
    inputs = clip_input.astype(jnp.float32)
    lengths = clip_lengths.reshape(N_DP, MICRO, SLOT_MB, CLIPS)

    def forward(weights, volume):
        grid = volume.reshape(N_DP, MICRO, SLOT_MB, FRAMES, H, H, D)
        results = []
        for micro_index in range(MICRO):
            source = grid[:, micro_index].reshape(N_DP * SLOT_MB, FRAMES, H, H, D)
            clip_rows = lengths[:, micro_index].reshape(N_DP * SLOT_MB, CLIPS)
            validity, tap_masks = frame_masks(clip_rows, FRAMES, 1)
            first = inception_layer(source, validity, tap_masks, tuple((stacked[0] for stacked in weights)))
            handoff = low_back(low(pool_pairs(first)))
            validity, tap_masks = frame_masks(clip_rows, FRAMES // 2, 2)
            second = low(inception_layer(handoff, validity, tap_masks, tuple((stacked[1] for stacked in weights))))
            results.append(second.reshape(N_DP, SLOT_MB, FRAMES // 2, H // 2, H // 2, D))
        return jnp.stack(results, axis=1).reshape(SLOTS, FRAMES // 2, H // 2, H // 2, D)
    block_output, pullback = jax.vjp(forward, params, inputs)
    weight_grads, input_grad = pullback(out_grad.astype(jnp.float32))
    return (block_output.astype(jnp.bfloat16), input_grad.astype(jnp.bfloat16), weight_grads[0], weight_grads[1], weight_grads[2], weight_grads[3], weight_grads[4], weight_grads[5], weight_grads[6])
```

```python
import functools

import jax
import jax.numpy as jnp
from jax import lax
from jax.experimental import pallas as pl
from jax.experimental.pallas import tpu as pltpu
from jax.sharding import PartitionSpec as P

D = 832
DP = 896
C0 = 256
C1A = 160
C1B = 320
C2A = 32
C2B = 128
C3 = 128
EPS = 0.001
MESH = pl.DeviceIdType.MESH
F32 = jnp.float32
BF16 = jnp.bfloat16
VMEM_LIMIT = 60 * 2**20


def dot(a, b):
    return jnp.dot(a, b, preferred_element_type=F32)


def dot_nt(a, b):
    return lax.dot_general(a, b, (((1,), (1,)), ((), ())), preferred_element_type=F32)


def dot_tn(a, b):
    return lax.dot_general(a, b, (((0,), (0,)), ((), ())), preferred_element_type=F32)


def roll_rows(x, by):
    return pltpu.roll(x, by % x.shape[0], 0)


def roll_lanes(x, by):
    return pltpu.roll(x, by % x.shape[1], 1)


def lane_below(x, count):
    lanes = lax.broadcasted_iota(jnp.int32, x.shape, 1)
    return jnp.where(lanes < count, x, 0.0)


class Grid:
    def __init__(self, frames, side, pitch, stride, len_ref):
        self.frames, self.side, self.pitch, self.stride = frames, side, pitch, stride
        self.rows = side * pitch
        self.len_ref = len_ref
        self.sec = lax.axis_index("section")

    def label(self, frame):
        place = frame * self.stride
        label = jnp.int32(0)
        start = jnp.int32(0)
        for c in range(self.len_ref.shape[1]):
            end = start + self.len_ref[0, c]
            label = jnp.where((place >= start) & (place < end), jnp.int32(c + 1), label)
            start = end
        return label

    def place(self, j):
        return lax.rem(j + self.sec * (self.frames // 2), self.frames)

    def valid(self, j):
        return jnp.where(self.label(self.place(j)) > 0, 1.0, 0.0).astype(F32)

    def taps(self, j):
        f = self.place(j)
        here = self.label(f)
        out = []
        for dt in (-1, 0, 1):
            there = f + dt
            inside = (there >= 0) & (there < self.frames)
            same = inside & (here > 0) & (self.label(there) == here)
            out.append(jnp.where(same, 1.0, 0.0).astype(F32))
        return out

    def wrap(self, j):
        return lax.rem(j + self.frames, self.frames)

    def inv_spread(self, taps):
        return 1.0 / jnp.maximum(taps[0] + taps[1] + taps[2], 1.0)

    def places_yx(self):
        r = lax.broadcasted_iota(jnp.int32, (self.rows, 128), 0)
        y = r // self.pitch
        return y, r - y * self.pitch

    def colmask(self):
        y, x = self.places_yx()
        return jnp.where(x < self.side, 1.0, 0.0).astype(F32)

    def inv_edges(self):
        y, x = self.places_yx()
        last = self.side - 1
        ey = jnp.where((y == 0) | (y == last), 2.0, 3.0)
        ex = jnp.where((x == 0) | (x == last), 2.0, 3.0)
        return jnp.where(x < self.side, 1.0 / (ey * ex), 0.0).astype(F32)

    def box(self, load, j, taps):
        t = None
        for dt in (-1, 0, 1):
            term = load(self.wrap(j + dt)) * taps[dt + 1]
            t = term if t is None else t + term
        lanes = t.shape[-1]
        v = t.reshape(self.side, self.pitch, lanes)
        zero = jnp.zeros((1, self.pitch, lanes), F32)
        v = v + jnp.concatenate([v[1:], zero], 0) + jnp.concatenate([zero, v[:-1]], 0)
        v = v.reshape(self.rows, lanes)
        return v + roll_rows(v, 1) + roll_rows(v, -1)


def fold8(v):
    return jnp.sum(v.reshape(-1, 8, v.shape[-1]), axis=0)


def add_stats(acc, lanes, v, w=None):
    acc[0, :, lanes] += fold8(v)
    acc[1, :, lanes] += fold8(v * (v if w is None else w))


def affine(st, lanes, beta):
    total, square, count = st[0:1, lanes], st[1:2, lanes], st[2:3, lanes]
    mean = total / count
    scale = lax.rsqrt(square / count - mean * mean + EPS)
    return scale, mean


def soft(t):
    e = jnp.exp(-jnp.abs(t))
    r = 1.0 / (1.0 + e)
    return jnp.maximum(t, 0.0) + jnp.log(1.0 + e), jnp.where(t >= 0, r, e * r)


def sigm(t):
    e = jnp.exp(-jnp.abs(t))
    r = 1.0 / (1.0 + e)
    return jnp.where(t >= 0, r, e * r)


def greet():
    n = lax.axis_size("dp")
    me = lax.axis_index("dp")
    barrier = pltpu.get_barrier_semaphore()

    def go(k, _):
        pl.semaphore_signal(
            barrier, inc=1, device_id={"dp": lax.rem(me + k, n)}, device_id_type=MESH
        )
        return 0

    lax.fori_loop(1, n, go, 0)


def greeted():
    pl.semaphore_wait(pltpu.get_barrier_semaphore(), lax.axis_size("dp") - 1)


def exchange(loc, buf, ssem, rsem, out):
    n = lax.axis_size("dp")
    me = lax.axis_index("dp")

    def copy(k):
        return pltpu.make_async_remote_copy(
            src_ref=loc,
            dst_ref=buf.at[me],
            send_sem=ssem.at[k],
            recv_sem=rsem.at[me],
            device_id={"dp": lax.rem(me + k, n)},
            device_id_type=MESH,
        )

    def start(k, _):
        copy(k).start()
        return 0

    lax.fori_loop(1, n, start, 0)
    buf[me] = loc[...]

    def wait(k, _):
        copy(k).wait_send()
        j = lax.rem(me + k, n)
        pltpu.make_async_remote_copy(
            src_ref=loc,
            dst_ref=buf.at[j],
            send_sem=ssem.at[k],
            recv_sem=rsem.at[j],
            device_id={"dp": j},
            device_id_type=MESH,
        ).wait_recv()
        return 0

    lax.fori_loop(1, n, wait, 0)
    out[...] = jnp.sum(buf[...], axis=0)


def exchange_scratch(n, lanes):
    return [
        pltpu.VMEM((8, lanes), F32),
        pltpu.VMEM((n, 8, lanes), F32),
        pltpu.SemaphoreType.DMA((n,)),
        pltpu.SemaphoreType.DMA((n,)),
    ]


def pack_stats(loc, acc, count=None):
    lanes = loc.shape[1]
    loc[0:1, :] = jnp.sum(acc[0, :, 0:lanes], axis=0, keepdims=True)
    loc[1:2, :] = jnp.sum(acc[1, :, 0:lanes], axis=0, keepdims=True)
    if count is not None:
        loc[2:3, :] = jnp.full((1, loc.shape[1]), 1.0, F32) * count


def count_voxels(g):
    total = jnp.float32(0.0)
    for j in range(g.frames):
        total = total + g.valid(j)
    return total * float(g.side * g.side)


def loop(n, body):
    def step(i, _):
        body(i)
        return 0

    lax.fori_loop(0, n, step, 0)


def first_kernel(len_ref, xo, xr, wp, xp, z1, zin, st, yp, acc, loc, buf, ssem, rsem):
    greet()
    half, side = xo.shape[0], xo.shape[1]
    g = Grid(2 * half, side, 16, 1, len_ref)
    nf = 2
    acc[...] = jnp.zeros_like(acc)
    loc[...] = jnp.zeros_like(loc)
    for part, src in enumerate((xo, xr)):

        def body(i, src=src, part=part):
            f0 = part * half + i * nf
            for q in range(nf):
                vm = g.valid(f0 + q).astype(BF16)
                xp[f0 + q, :, 0:side, :] = src[i * nf + q] * vm
                xp[f0 + q, :, side:16, :] = jnp.zeros((side, 16 - side, D), BF16)
            lhs = xp[pl.ds(f0, nf)].reshape(nf * g.rows, D)
            y = dot(lhs, wp[...])
            z1[pl.ds(f0, nf), :, 0:C0] = y[:, 0:C0].reshape(nf, g.rows, C0)
            yp[pl.ds(f0, nf)] = y[:, 256:384].reshape(nf, g.rows, 128)
            zin[pl.ds(f0, nf)] = y[:, 384:640].reshape(nf, g.rows, 256)
            add_stats(acc, pl.ds(0, 256), y[:, 0:256])
            add_stats(acc, pl.ds(384, 256), y[:, 384:640])

        loop(half // nf, body)
    pool_forward(g, yp, z1, acc)
    pack_stats(loc, acc, count_voxels(g))
    greeted()
    exchange(loc, buf, ssem, rsem, st)


def pool_forward(g, yp, z1, acc):
    edges = g.inv_edges()

    def body(f):
        taps = g.taps(f)
        z = g.box(lambda j: yp[j], f, taps) * (edges * g.inv_spread(taps))
        z1[f, :, 256:384] = z
        add_stats(acc, pl.ds(256, 128), z)

    loop(g.frames, body)


def inner_tiles(g, zf, st, beta, f, mask):
    tiles = []
    for t in range(2):
        lanes = pl.ds(384 + 128 * t, 128)
        scale, mean = affine(st, lanes, None)
        b = beta[0:1, pl.ds(896 + 128 * t, 128)]
        act, _ = soft(zf[:, 128 * t : 128 * (t + 1)] * scale + (b - mean * scale))
        tiles.append(act * mask)
    return tiles


def neighbours32(v):
    return roll_rows(v, 1) + roll_lanes(v, 32) + roll_lanes(roll_rows(v, -1), 64)


def tap_tiles(a, b, mask):
    tail = lane_below(b, 32)
    small = lane_below(roll_lanes(b, -32), 32)
    ones = jnp.where(lax.broadcasted_iota(jnp.int32, b.shape, 1) == 96, mask, 0.0)
    return (
        [roll_rows(a, 1), a, roll_rows(a, -1), neighbours32(tail) + ones],
        neighbours32(small) + ones,
    )


def typical(beta):
    sp, sg = soft(jnp.broadcast_to(beta, (8, beta.shape[-1])))
    return sp + 0.5 * sg * (1.0 - sg)


def outer(c, s):
    k = lax.broadcasted_iota(jnp.int32, c.shape, 0)
    c = jnp.where(k < 2, c, 0.0).astype(BF16)
    s = jnp.broadcast_to(s, (8, s.shape[-1]))
    high = s.astype(BF16).astype(F32)
    k = lax.broadcasted_iota(jnp.int32, s.shape, 0)
    s = jnp.where(k == 0, high, jnp.where(k == 1, s - high, 0.0)).astype(BF16)
    return dot_tn(c, s)


def tap_points(beta):
    a = typical(beta[0:1, 896:1024])
    b = typical(beta[0:1, 1024:1152])

    def three(v):
        return v + roll_lanes(v, 32) + roll_lanes(v, 64)

    tail = three(lane_below(b, 32))
    small = three(lane_below(roll_lanes(b, -32), 32))
    return jnp.concatenate([a, a, a, tail], 1), small


def centre_mid(grad, beta):
    c, _ = tap_points(beta)
    row = jnp.broadcast_to(grad[992:993, :], (8, 1024))
    main = row[:, 256:512]
    tail = lane_below(roll_lanes(row[:, 768:896], 64), 64)
    s = jnp.concatenate([main, main, main, tail + roll_lanes(tail, 64), tail], 1)
    return outer(c, s)


def centre_small(grad, beta):
    _, c = tap_points(beta)
    row = jnp.broadcast_to(grad[224:225, 128:256], (8, 128))
    return outer(c, jnp.concatenate([row, row, row], 1))


def untap(parts, small):
    def back32(v):
        left = lane_below(roll_rows(v, -1), 32)
        centre = lane_below(roll_lanes(v, -32), 32)
        right = lane_below(roll_lanes(roll_rows(v, 1), -64), 32)
        return left + centre + right

    a = roll_rows(parts[0], -1) + parts[1] + roll_rows(parts[2], 1)
    return a, back32(parts[3]) + roll_lanes(back32(small), 32)


def conv_gather(taps, load_mid, load_small, g, f):
    main = small = tail = None
    for dt in (-1, 0, 1):
        p = load_mid(g.wrap(f + dt))
        s = load_small(g.wrap(f + dt))
        m = taps[dt + 1]
        k = dt + 1
        piece = p[:, 768:896] if k < 2 else p[:, 896:1024]
        if k == 1:
            piece = roll_lanes(piece, 64)
        terms = (p[:, 256 * k : 256 * k + 256] * m, s[:, 128 * k : 128 * k + 128] * m, piece * m)
        if main is None:
            main, small, tail = terms
        else:
            main, small, tail = main + terms[0], small + terms[1], tail + terms[2]
    return main, small, lane_below(tail, 64)


def conv_kernel(
    len_ref, zin, st1, beta, wf, ws, cat, scat, z2, st2, pbuf, sbuf, acc, loc, buf, ssem, rsem
):
    greet()
    frames = zin.shape[0]
    side = cat.shape[1] - 2
    g = Grid(frames, side, 16, 1, len_ref)
    acc[...] = jnp.zeros_like(acc)
    loc[...] = jnp.zeros_like(loc)
    colmask = g.colmask()

    def build(f):
        a, b = inner_tiles(g, zin[f], st1, beta, f, colmask * g.valid(f))
        parts, small = tap_tiles(a, b, colmask * g.valid(f))
        zero = jnp.zeros((1, 16, 512), BF16)
        cat[f, 0:1] = zero
        cat[f, side + 1 : side + 2] = zero
        scat[f, 0:1] = zero[:, :, 0:128]
        scat[f, side + 1 : side + 2] = zero[:, :, 0:128]
        for i, part in enumerate(parts):
            cat[f, 1 : side + 1, :, 128 * i : 128 * i + 128] = part.astype(BF16).reshape(
                side, 16, 128
            )
        scat[f, 1 : side + 1] = small.astype(BF16).reshape(side, 16, 128)

    loop(frames, build)
    nf = 4

    def products(i):
        f0 = i * nf
        lhs = jnp.concatenate(
            [
                cat[pl.ds(f0, nf), dy : dy + side].reshape(nf * g.rows, 512)
                for dy in range(3)
            ],
            axis=1,
        )
        pbuf[pl.ds(f0, nf)] = dot(lhs, wf[...]).reshape(nf, g.rows, 1024)
        lhs = jnp.concatenate(
            [
                scat[pl.ds(f0, nf), dy : dy + side].reshape(nf * g.rows, 128)
                for dy in range(3)
            ],
            axis=1,
        )
        sbuf[pl.ds(f0, nf)] = dot(lhs, ws[...]).reshape(nf, g.rows, 384)

    loop(frames // nf, products)
    gather_conv(g, colmask, pbuf, sbuf, z2, acc)
    pack_stats(loc, acc)
    greeted()
    exchange(loc, buf, ssem, rsem, st2)


def gather_conv(g, colmask, pbuf, sbuf, z2, acc):
    def body(f):
        main, small, tail = conv_gather(
            g.taps(f), lambda j: pbuf[j], lambda j: sbuf[j], g, f
        )
        wide = jnp.concatenate([colmask, colmask], 1)
        main, small, tail = main * wide, small * colmask, tail * colmask
        z2[f, :, 0:256] = main
        z2[f, :, 256:384] = small
        z2[f, :, 384:512] = tail
        add_stats(acc, pl.ds(0, 256), main)
        add_stats(acc, pl.ds(256, 128), small)
        add_stats(acc, pl.ds(384, 128), tail)

    loop(g.frames, body)


def final_tile(t, z1, z2):
    if t < 3:
        return z1, 128 * t, False
    return z2, 128 * (t - 3), True


def tile_norm(t, st1, st2, beta):
    if t < 3:
        scale, mean = affine(st1, pl.ds(128 * t, 128), None)
    else:
        lanes = pl.ds(128 * (t - 3), 128)
        total, square, count = st2[0:1, lanes], st2[1:2, lanes], st1[2:3, 0:128]
        mean = total / count
        scale = lax.rsqrt(square / count - mean * mean + EPS)
    return scale, mean, beta[0:1, pl.ds(128 * t, 128)]


def output_kernel(len_ref, z1, z2, st1, st2, beta, sig, hand, asum, bsum, scr):
    frames = z1.shape[0]
    side = z1.shape[1] // 16
    half = side // 2
    g = Grid(frames, side, 16, 1, len_ref)
    colmask = g.colmask()

    def body(k):
        mask = colmask * g.valid(2 * k)
        for t in range(7):
            ref, lane, _ = final_tile(t, z1, z2)
            scale, mean, b = tile_norm(t, st1, st2, beta)
            pooled = None
            for q in range(2):
                u = (ref[2 * k + q, :, lane : lane + 128] - mean) * scale
                sp, sg = soft(u + b)
                sp, sg = sp * mask, sg * mask
                if t == 6:
                    lanes = lax.broadcasted_iota(jnp.int32, sp.shape, 1)
                    sp = jnp.where(lanes == 127, mask, lane_below(sp, 64))
                    sg = lane_below(sg, 64)
                sig[2 * k + q, :, 128 * t : 128 * t + 128] = sg.astype(BF16)
                three = [sp, sg, sg * u]
                three = [
                    jnp.sum(v.reshape(half, 2, 16, 128), axis=1) for v in three
                ]
                pooled = three if pooled is None else [x + y for x, y in zip(pooled, three)]
            for v, dst in zip(pooled, (hand, asum, bsum)):
                scr[...] = v
                dst[k, :, :, 128 * t : 128 * t + 128] = (
                    scr[:, pl.ds(0, 8, stride=2), :] + scr[:, pl.ds(1, 8, stride=2), :]
                ) * 0.125

    loop(frames // 2, body)


def second_kernel(
    len_ref, hand, asum, bsum, grad, wp, wf, ws, beta, beta1,
    out, hg, dwp, dwf, dws, sums5, sums6, sums7,
    hbuf, z1, zin, z2, yp, cat, scat, pbuf, sbuf, dbuf, dzf, dzc, dzs, dz1, din,
    acc, st3, st4, acc7, accm, accs, accp,
    loc3, buf3, ss3, rs3, loc4, buf4, ss4, rs4, loc5, buf5, ss5, rs5,
    loc6, buf6, ss6, rs6, loc7, buf7, ss7, rs7,
):
    greet()
    frames, side = hand.shape[0], hand.shape[1]
    g = Grid(frames, side, 8, 2, len_ref)
    rows = g.rows
    colmask = g.colmask()
    for ref in (acc, acc7, loc3, loc4, loc5, loc6, loc7):
        ref[...] = jnp.zeros_like(ref)

    hbuf[...] = hand[...].reshape(frames * rows, DP).astype(BF16)
    y = dot(hbuf[...], wp[...])
    z1[:, :, 0:C0] = y[:, 0:C0].reshape(frames, rows, C0)
    yp[...] = y[:, 256:384].reshape(frames, rows, 128)
    zin[...] = y[:, 384:640].reshape(frames, rows, 256)

    def first_sums(f):
        vm = colmask * g.valid(f)
        wide = jnp.concatenate([vm, vm], 1)
        one, inner = z1[f, :, 0:256], zin[f]
        add_stats(acc, pl.ds(0, 256), one * wide)
        add_stats(acc, pl.ds(384, 256), inner * wide)

    loop(frames, first_sums)
    pool_forward(g, yp, z1, acc)
    pack_stats(loc3, acc, count_voxels(g))
    greeted()
    exchange(loc3, buf3, ss3, rs3, st3)

    def shifted(v, dy):
        v = v.reshape(2, side, 8, v.shape[-1])
        zero = jnp.zeros((2, 1, 8, v.shape[-1]), F32)
        if dy < 0:
            v = jnp.concatenate([zero, v[:, :-1]], 1)
        elif dy > 0:
            v = jnp.concatenate([v[:, 1:], zero], 1)
        return v.reshape(2 * rows, v.shape[-1])

    def build(i):
        pairs = []
        for q in range(2):
            f = 2 * i + q
            a, b = inner_tiles(g, zin[f], st3, beta, f, colmask * g.valid(f))
            parts, small = tap_tiles(a, b, colmask * g.valid(f))
            pairs.append(parts + [small])
        here = pl.ds(pl.multiple_of(i * 2 * rows, 16), 2 * rows)
        for t in range(5):
            both = jnp.concatenate([pairs[0][t], pairs[1][t]], 0)
            for dy in (-1, 0, 1):
                v = shifted(both, dy).astype(BF16)
                if t < 4:
                    lane = (dy + 1) * 512 + 128 * t
                    cat[here, lane : lane + 128] = v
                else:
                    scat[here, (dy + 1) * 128 : (dy + 1) * 128 + 128] = v

    loop(frames // 2, build)
    pbuf[...] = dot(cat[...], wf[...]).reshape(frames, rows, 1024)
    sbuf[...] = dot(scat[...], ws[...]).reshape(frames, rows, 384)
    acc[...] = jnp.zeros_like(acc)
    gather_conv(g, colmask, pbuf, sbuf, z2, acc)
    pack_stats(loc4, acc)
    exchange(loc4, buf4, ss4, rs4, st4)

    acc7[...] = jnp.zeros_like(acc7)

    def emit(i):
        here = pl.ds(pl.multiple_of(i * 2 * rows, 16), 2 * rows)
        for t in range(7):
            lanes = pl.ds(128 * t, 128)
            ref, lane, _ = final_tile(t, z1, z2)
            scale, mean, b = tile_norm(t, st3, st4, beta)
            gr = grad[here, lanes].astype(F32)
            outs = []
            for q in range(2):
                f = 2 * i + q
                mask = colmask * g.valid(f)
                u = (ref[f, :, lane : lane + 128] - mean) * scale
                sp, sg = soft(u + b)
                outs.append(sp * mask)
                d = gr[q * rows : (q + 1) * rows] * sg * mask
                dbuf[f, :, lanes] = d
                add_stats(acc7, lanes, d, u)
            out[here, lanes] = jnp.concatenate(outs, 0).astype(BF16)

    loop(frames // 2, emit)
    pack_stats(loc5, acc7)
    exchange(loc5, buf5, ss5, rs5, sums5)

    count = st3[2:3, 0:128]

    def dz_of(f, t, mask):
        ref, lane, _ = final_tile(t, z1, z2)
        lanes = pl.ds(128 * t, 128)
        scale, mean, _ = tile_norm(t, st3, st4, beta)
        u = (ref[f, :, lane : lane + 128] - mean) * scale
        m1, m2 = sums5[0:1, lanes] / count, sums5[1:2, lanes] / count
        return (dbuf[f, :, lanes] - m1 - u * m2) * (scale * mask)

    def dz_final(f):
        mask = colmask * g.valid(f)
        for t in range(2):
            dz1[f, :, 128 * t : 128 * t + 128] = dz_of(f, t, mask)
        yp[f] = dz_of(f, 2, mask) * (g.inv_edges() * g.inv_spread(g.taps(f)))
        for t in range(3, 7):
            z = dz_of(f, t, mask)
            if t == 6:
                z = lane_below(z, 64)
            dzf[f, :, 128 * (t - 3) : 128 * (t - 3) + 128] = z

    loop(frames, dz_final)

    def spread(f):
        boxed = g.box(lambda j: yp[j], f, g.taps(f)) * colmask
        dz1[f, :, 256:384] = boxed
        for dt in (-1, 0, 1):
            k = dt + 1
            j = g.wrap(f - dt)
            m = g.taps(j)[k]
            dzc[f, :, 256 * k : 256 * k + 256] = dzf[j, :, 0:256] * m
            dzs[f, :, 128 * k : 128 * k + 128] = dzf[j, :, 256:384] * m
            tail = dzf[j, :, 384:512] * m
            if k == 0:
                low_tail = tail
            elif k == 1:
                dzc[f, :, 768:896] = low_tail + roll_lanes(tail, 64)
            else:
                dzc[f, :, 896:1024] = tail

    loop(frames, spread)
    dzc_b = dzc[...].reshape(frames * rows, 1024).astype(BF16)
    dzs_b = dzs[...].reshape(frames * rows, 384).astype(BF16)
    q = dot_nt(dzc_b, wf[...])
    for dy in range(3):
        pbuf[:, :, 0:512] = q[:, 512 * dy : 512 * dy + 512].reshape(frames, rows, 512)
        back_rows(g, pbuf, 512, dy - 1, din if dy == 1 else None, dbuf, dy == 0)
    q = dot_nt(dzs_b, ws[...])
    for dy in range(3):
        sbuf[:, :, 0:128] = q[:, 128 * dy : 128 * dy + 128].reshape(frames, rows, 128)
        back_rows(g, sbuf, 128, dy - 1, None, dzf, dy == 0)
    acc[...] = jnp.zeros_like(acc)

    def inner_back(f):
        back = [dbuf[f, :, 128 * t : 128 * t + 128] for t in range(4)]
        tiles = untap(back, dzf[f, :, 0:128])
        mask = colmask * g.valid(f)
        for t in range(2):
            inner_up(g, t, zin[f, :, 128 * t : 128 * t + 128], tiles[t] * mask, st3, beta, din, f, acc)

    loop(frames, inner_back)
    pack_stats(loc6, acc)
    exchange(loc6, buf6, ss6, rs6, sums6)
    accm[...] = dot_tn(cat[...], dzc_b)
    mid = centre_mid(accm, beta)
    for k in range(3):
        dwf[512 * k : 512 * k + 512] = (accm[512 * k : 512 * k + 512] - mid).astype(BF16)
    accs[...] = dot_tn(scat[...], dzs_b)
    small = centre_small(accs, beta)
    for k in range(3):
        dws[128 * k : 128 * k + 128] = (accs[128 * k : 128 * k + 128] - small).astype(BF16)

    def dz_inner(f):
        mask = colmask * g.valid(f)
        for t in range(2):
            dz1[f, :, 384 + 128 * t : 512 + 128 * t] = inner_dz(t, zin, din, st3, sums6, count, f, mask)

    loop(frames, dz_inner)
    dz1_b = dz1[...].reshape(frames * rows, 640).astype(BF16)
    hgv = dot_nt(dz1_b, wp[...]).astype(BF16).astype(F32)
    hg[...] = hgv.reshape(frames, side, 8, DP)
    acc7[...] = jnp.zeros_like(acc7)

    def upstream(f):
        for t in range(7):
            lanes = pl.ds(128 * t, 128)
            gr = hg[f, :, :, lanes].reshape(rows, 128)
            acc7[0, :, lanes] += fold8(gr * asum[f, :, :, lanes].reshape(rows, 128))
            acc7[1, :, lanes] += fold8(gr * bsum[f, :, :, lanes].reshape(rows, 128))

    loop(frames, upstream)
    pack_stats(loc7, acc7)
    exchange(loc7, buf7, ss7, rs7, sums7)
    accp[...] = dot_tn(hbuf[...], dz1_b)
    pool = dz1[:, :, 256:384].reshape(frames * rows, 128)
    rest = (pool - dz1_b[:, 256:384].astype(F32)).astype(BF16)
    accp[:, 256:384] += dot_tn(hbuf[...], rest)
    c = jnp.concatenate([typical(beta1[0:1, 0:832]), jnp.zeros((8, 64), F32)], 1)
    dwp[...] = (accp[...] - outer(c, accp[DP - 1 : DP, :])).astype(BF16)


def back_rows(g, src, lanes, dy, _, dst, first):
    def body(f):
        v = src[f, :, 0:lanes].reshape(g.side, g.pitch, lanes)
        zero = jnp.zeros((1, g.pitch, lanes), F32)
        if dy > 0:
            v = jnp.concatenate([zero, v[:-1]], 0)
        elif dy < 0:
            v = jnp.concatenate([v[1:], zero], 0)
        v = v.reshape(g.rows, lanes)
        dst[f, :, 0:lanes] = v if first else dst[f, :, 0:lanes] + v

    loop(g.frames, body)


def inner_up(g, t, z, back, st, beta, din, f, acc):
    lanes = pl.ds(384 + 128 * t, 128)
    scale, mean = affine(st, lanes, None)
    u = (z - mean) * scale
    d = back * sigm(u + beta[0:1, pl.ds(896 + 128 * t, 128)])
    din[f, :, 128 * t : 128 * t + 128] = d
    add_stats(acc, lanes, d, u)


def inner_dz(t, zin, din, st, sums, count, f, mask):
    lanes = pl.ds(384 + 128 * t, 128)
    scale, mean = affine(st, lanes, None)
    u = (zin[f, :, 128 * t : 128 * t + 128] - mean) * scale
    m1, m2 = sums[0:1, lanes] / count, sums[1:2, lanes] / count
    dz = (din[f, :, 128 * t : 128 * t + 128] - m1 - u * m2) * (scale * mask)
    return lane_below(dz, 64) if t == 1 else dz


def dz_kernel(len_ref, z1, z2, sig, hg, st1, st2, sums7, beta, dzc, dzs, dz1, scr, yp, dzf):
    frames = z1.shape[0]
    side = z1.shape[1] // 16
    half = side // 2
    g = Grid(frames, side, 16, 1, len_ref)
    colmask = g.colmask()
    edges = g.inv_edges()
    count = st1[2:3, 0:128]

    def body(k):
        mask = colmask * g.valid(2 * k)
        for t in range(7):
            lanes = pl.ds(128 * t, 128)
            ref, lane, _ = final_tile(t, z1, z2)
            scale, mean, _ = tile_norm(t, st1, st2, beta)
            m1, m2 = sums7[0:1, lanes] / count, sums7[1:2, lanes] / count
            gr = hg[k, :, :, lanes] * 0.125
            scr[:, pl.ds(0, 8, stride=2), :] = gr
            scr[:, pl.ds(1, 8, stride=2), :] = gr
            gr = scr[...]
            gr = jnp.broadcast_to(gr[:, None], (half, 2, 16, 128)).reshape(g.rows, 128)
            for q in range(2):
                f = 2 * k + q
                u = (ref[f, :, lane : lane + 128] - mean) * scale
                d = gr * sig[f, :, lanes].astype(F32)
                dz = (d - m1 - u * m2) * (scale * mask)
                if t < 2:
                    dz1[f, :, lanes] = dz.astype(BF16)
                elif t == 2:
                    yp[f] = dz * (edges * g.inv_spread(g.taps(f)))
                else:
                    if t == 6:
                        dz = lane_below(dz, 64)
                    dzf[f, :, 128 * (t - 3) : 128 * (t - 3) + 128] = dz.astype(BF16)

    loop(frames // 2, body)

    def spread(f):
        boxed = g.box(lambda j: yp[j], f, g.taps(f)) * colmask
        dz1[f, :, 256:384] = boxed.astype(BF16)
        zero = jnp.zeros((1, 16, 1024), BF16)
        dzc[f, 0:1] = zero
        dzc[f, side + 1 : side + 2] = zero
        dzs[f, 0:1] = zero[:, :, 0:384]
        dzs[f, side + 1 : side + 2] = zero[:, :, 0:384]

        def put(ref, lane, v):
            ref[f, 1 : side + 1, :, lane : lane + v.shape[-1]] = v.reshape(side, 16, v.shape[-1])

        for dt in (-1, 0, 1):
            k = dt + 1
            j = g.wrap(f - dt)
            m = g.taps(j)[k]
            mb = m.astype(BF16)
            put(dzc, 256 * k, dzf[j, :, 0:256] * mb)
            put(dzs, 128 * k, dzf[j, :, 256:384] * mb)
            tail = dzf[j, :, 384:512].astype(F32) * m
            if k == 0:
                low_tail = tail
            elif k == 1:
                put(dzc, 768, (low_tail + roll_lanes(tail, 64)).astype(BF16))
            else:
                put(dzc, 896, tail.astype(BF16))

    loop(frames, spread)


def conv_grad_kernel(cat, scat, dzc, dzs, beta, dwf, dws, acc, accs):
    frames = cat.shape[0]
    side = cat.shape[1] - 2
    rows = side * 16
    nf = 4
    acc[...] = jnp.zeros_like(acc)
    accs[...] = jnp.zeros_like(accs)

    def body(i):
        f0 = i * nf
        here = pl.ds(f0, nf)
        a = cat[here, 1 : side + 1].reshape(nf * rows, 512)
        s = scat[here, 1 : side + 1].reshape(nf * rows, 128)
        for dy in (-1, 0, 1):
            k = dy + 1
            b = dzc[here, 1 - dy : 1 - dy + side].reshape(nf * rows, 1024)
            acc[512 * k : 512 * k + 512] += dot_tn(a, b)
            b = dzs[here, 1 - dy : 1 - dy + side].reshape(nf * rows, 384)
            accs[128 * k : 128 * k + 128] += dot_tn(s, b)

    loop(frames // nf, body)
    mid = centre_mid(acc, beta)
    small = centre_small(accs, beta)
    for k in range(3):
        dwf[512 * k : 512 * k + 512] = (acc[512 * k : 512 * k + 512] - mid).astype(BF16)
        dws[128 * k : 128 * k + 128] = (accs[128 * k : 128 * k + 128] - small).astype(BF16)


def conv_back_kernel(
    len_ref, dzc, dzs, wf, ws, zin, st1, beta, dzi, sums8, din, acc, loc, buf, ssem, rsem
):
    greet()
    frames = zin.shape[0]
    side = dzc.shape[1] - 2
    g = Grid(frames, side, 16, 1, len_ref)
    rows = g.rows
    colmask = g.colmask()
    acc[...] = jnp.zeros_like(acc)
    loc[...] = jnp.zeros_like(loc)
    nf = 4

    def body(i):
        here = pl.ds(i * nf, nf)
        q = s = None
        for dy in (-1, 0, 1):
            k = dy + 1
            v = dzc[here, 1 - dy : 1 - dy + side].reshape(nf * rows, 1024)
            t = dot_nt(v, wf[512 * k : 512 * k + 512])
            q = t if q is None else q + t
            v = dzs[here, 1 - dy : 1 - dy + side].reshape(nf * rows, 384)
            t = dot_nt(v, ws[128 * k : 128 * k + 128])
            s = t if s is None else s + t
        for j in range(nf):
            f = i * nf + j
            qs = q[j * rows : (j + 1) * rows]
            tiles = untap([qs[:, 128 * t : 128 * t + 128] for t in range(4)], s[j * rows : (j + 1) * rows])
            mask = colmask * g.valid(f)
            for t in range(2):
                inner_up(g, t, zin[f, :, 128 * t : 128 * t + 128], tiles[t] * mask, st1, beta, din, f, acc)

    loop(frames // nf, body)
    pack_stats(loc, acc)
    greeted()
    exchange(loc, buf, ssem, rsem, sums8)
    count = st1[2:3, 0:128]

    def dz(f):
        mask = colmask * g.valid(f)
        for t in range(2):
            dzi[f, :, 128 * t : 128 * t + 128] = inner_dz(
                t, zin, din, st1, sums8, count, f, mask
            ).astype(BF16)

    loop(frames, dz)


def input_kernel(xp, dz1, dzi, wp, gin, dwp, acc):
    frames, side = xp.shape[0], xp.shape[1]
    rows = side * 16
    nf = 2
    acc[...] = jnp.zeros_like(acc)

    def body(i):
        here = pl.ds(i * nf, nf)
        d = jnp.concatenate([dz1[here], dzi[here]], -1).reshape(nf * rows, 640)
        back = dot_nt(d, wp[...]).astype(BF16).reshape(nf, side, 16, D)
        gin[here] = back[:, :, 0:side]
        acc[...] += dot_tn(xp[here].reshape(nf * rows, D), d)

    loop(frames // nf, body)
    dwp[...] = acc[...].astype(BF16)


def vmem(*shape, dtype=F32):
    return pltpu.VMEM(shape, dtype)


def call(kernel, outs, args, scratch, collective=None, smem_first=True):
    specs = [pl.BlockSpec(memory_space=pltpu.VMEM)] * len(args)
    if smem_first:
        specs[0] = pl.BlockSpec(memory_space=pltpu.SMEM)
    params = {"vmem_limit_bytes": VMEM_LIMIT}
    if collective is not None:
        params.update(collective_id=collective, has_side_effects=True)
    return pl.pallas_call(
        kernel,
        out_shape=[jax.ShapeDtypeStruct(shape, dtype) for shape, dtype in outs],
        in_specs=specs,
        out_specs=[pl.BlockSpec(memory_space=pltpu.VMEM)] * len(outs),
        scratch_shapes=scratch,
        compiler_params=pltpu.CompilerParams(**params),
    )(*args)


def to_final(v):
    one, mid, small, pool = v[..., :256], v[..., 256:576], v[..., 576:704], v[..., 704:]
    zero = jnp.zeros(v.shape[:-1] + (64,), v.dtype)
    return jnp.concatenate([one, pool, mid[..., :256], small, mid[..., 256:], zero], -1)


def from_final(v):
    return jnp.concatenate(
        [v[..., 0:256], v[..., 384:640], v[..., 768:832], v[..., 640:768], v[..., 256:384]], -1
    )


def arrange_first(w_one, w_mid_in, w_small_in, w_pool):
    zero = jnp.zeros((w_one.shape[0], 64), w_one.dtype)
    return jnp.concatenate([w_one, w_pool, w_mid_in, w_small_in, zero], 1)


def arrange_mid(w):
    w = w.reshape(3, 3, 3, C1A, C1B).transpose(1, 2, 3, 0, 4)
    rows = jnp.concatenate(
        [
            w[:, :, :128].reshape(3, 384, 3, C1B),
            w[:, :, 128:].reshape(3, 96, 3, C1B),
            jnp.zeros((3, 32, 3, C1B), w.dtype),
        ],
        1,
    )
    return jnp.concatenate(
        [
            rows[..., :256].reshape(1536, 768),
            rows[..., 256:].reshape(1536, 192),
            jnp.zeros((1536, 64), w.dtype),
        ],
        1,
    )


def restore_mid(g):
    g = g.reshape(3, 512, 1024)
    cols = jnp.concatenate(
        [g[..., :768].reshape(3, 512, 3, 256), g[..., 768:960].reshape(3, 512, 3, 64)], -1
    )
    w = jnp.concatenate(
        [cols[:, :384].reshape(3, 3, 128, 3, C1B), cols[:, 384:480].reshape(3, 3, 32, 3, C1B)], 2
    )
    return w.transpose(3, 0, 1, 2, 4).reshape(27 * C1A, C1B)


def arrange_small(w):
    w = w.reshape(3, 3, 96, C2B).transpose(1, 2, 0, 3)
    w = jnp.concatenate([w, jnp.zeros((3, 32, 3, C2B), w.dtype)], 1)
    return w.reshape(384, 384)


def restore_small(g):
    g = g.reshape(3, 128, 3, C2B)[:, :96]
    return g.transpose(2, 0, 1, 3).reshape(27 * C2A, C2B)


def arrange_beta(b):
    one, mid_in, mid = b[0:256], b[256:416], b[416:736]
    small_in, small, pool = b[736:768], b[768:896], b[896:1024]
    zero = jnp.zeros((64,), b.dtype)
    return jnp.concatenate(
        [one, pool, mid[:256], small, mid[256:], zero, mid_in, small_in, zero]
    )[None]


def restore_beta(final, inner):
    return jnp.concatenate(
        [
            final[0:256],
            inner[384:544],
            final[384:640],
            final[768:832],
            inner[544:576],
            final[640:768],
            final[256:384],
        ]
    )


def swap(x):
    return lax.ppermute(x, "section", [(0, 1), (1, 0)])


def on_device(
    clip_input, out_grad, clip_lengths, w_one, w_mid_in, w_mid, w_small_in, w_small, w_pool, bn_offset
):
    n = lax.axis_size("dp")
    sec = lax.axis_index("section")
    first = sec == 0

    def mine(v, axis=0):
        return lax.dynamic_index_in_dim(v, sec, axis, keepdims=False)

    def other(v, axis=0):
        return lax.dynamic_index_in_dim(v, 1 - sec, axis, keepdims=False)

    def both(v):
        got = swap(v[0])
        return jnp.where(first, v[0], got), jnp.where(first, got, v[0])

    x_got = swap(other(clip_input))
    x_own = mine(clip_input)
    half, side = x_own.shape[0], x_own.shape[1]
    frames = 2 * half
    rows = side * 16
    frames2, side2 = frames // 2, side // 2
    rows2 = side2 * 8
    lengths = lax.dynamic_slice_in_dim(clip_lengths, sec, 1, 0)

    wp1, wp2 = both(arrange_first(w_one[0], w_mid_in[0], w_small_in[0], w_pool[0])[None])
    wp2 = to_final(wp2.T).T
    beta1, beta2 = both(arrange_beta(bn_offset[0])[None])
    wf1, wf2 = both(arrange_mid(w_mid[0])[None])
    ws1, ws2 = both(arrange_small(w_small[0])[None])

    xp, z1, zin, st1 = call(
        first_kernel,
        [
            ((frames, side, 16, D), BF16),
            ((frames, rows, 384), F32),
            ((frames, rows, 256), F32),
            ((8, 640), F32),
        ],
        (lengths, x_own, x_got, wp1),
        [vmem(frames, rows, 128), vmem(2, 8, 640)] + exchange_scratch(n, 640),
        collective=1,
    )
    cat, scat, z2, st2 = call(
        conv_kernel,
        [
            ((frames, side + 2, 16, 512), BF16),
            ((frames, side + 2, 16, 128), BF16),
            ((frames, rows, 512), F32),
            ((8, 512), F32),
        ],
        (lengths, zin, st1, beta1, wf1, ws1),
        [vmem(frames, rows, 1024), vmem(frames, rows, 384), vmem(2, 8, 512)]
        + exchange_scratch(n, 512),
        collective=2,
    )
    sig, hand, asum, bsum = call(
        output_kernel,
        [((frames, rows, DP), BF16)] + [((frames2, side2, 8, DP), F32)] * 3,
        (lengths, z1, z2, st1, st2, beta1),
        [vmem(side2, 16, 128)],
    )
    grad_got = swap(other(out_grad))
    grad = jnp.concatenate([mine(out_grad), grad_got], 0)
    grad = jnp.pad(to_final(grad), ((0, 0), (0, 0), (0, 1), (0, 0))).reshape(frames2 * rows2, DP)
    total2 = frames2 * rows2
    out, hg, dwp2, dwf2, dws2, sums5, sums6, sums7 = call(
        second_kernel,
        [
            ((total2, DP), BF16),
            ((frames2, side2, 8, DP), F32),
            ((DP, 640), BF16),
            ((1536, 1024), BF16),
            ((384, 384), BF16),
            ((8, DP), F32),
            ((8, 640), F32),
            ((8, DP), F32),
        ],
        (lengths, hand, asum, bsum, grad, wp2, wf2, ws2, beta2, beta1),
        [
            vmem(total2, DP, dtype=BF16),
            vmem(frames2, rows2, 384),
            vmem(frames2, rows2, 256),
            vmem(frames2, rows2, 512),
            vmem(frames2, rows2, 128),
            vmem(total2, 1536, dtype=BF16),
            vmem(total2, 384, dtype=BF16),
            vmem(frames2, rows2, 1024),
            vmem(frames2, rows2, 384),
            vmem(frames2, rows2, DP),
            vmem(frames2, rows2, 512),
            vmem(frames2, rows2, 1024),
            vmem(frames2, rows2, 384),
            vmem(frames2, rows2, 640),
            vmem(frames2, rows2, 256),
            vmem(2, 8, 640),
            vmem(8, 640),
            vmem(8, 512),
            vmem(2, 8, DP),
            vmem(1536, 1024),
            vmem(384, 384),
            vmem(DP, 640),
        ]
        + exchange_scratch(n, 640)
        + exchange_scratch(n, 512)
        + exchange_scratch(n, DP)
        + exchange_scratch(n, 640)
        + exchange_scratch(n, DP),
        collective=3,
    )
    dzc, dzs, dz1 = call(
        dz_kernel,
        [
            ((frames, side + 2, 16, 1024), BF16),
            ((frames, side + 2, 16, 384), BF16),
            ((frames, rows, 384), BF16),
        ],
        (lengths, z1, z2, sig, hg, st1, st2, sums7, beta1),
        [vmem(side2, 16, 128), vmem(frames, rows, 128), vmem(frames, rows, 512, dtype=BF16)],
    )
    dwf1, dws1 = call(
        conv_grad_kernel,
        [((1536, 1024), BF16), ((384, 384), BF16)],
        (cat, scat, dzc, dzs, beta1),
        [vmem(1536, 1024), vmem(384, 384)],
        smem_first=False,
    )
    dzi, sums8 = call(
        conv_back_kernel,
        [((frames, rows, 256), BF16), ((8, 640), F32)],
        (lengths, dzc, dzs, wf1, ws1, zin, st1, beta1),
        [vmem(frames, rows, 256), vmem(2, 8, 640)] + exchange_scratch(n, 640),
        collective=4,
    )
    gin, dwp1 = call(
        input_kernel,
        [((frames, side, side, D), BF16), ((D, 640), BF16)],
        (xp, dz1, dzi, wp1),
        [vmem(D, 640)],
        smem_first=False,
    )

    dwp2 = from_final(dwp2.T).T
    beta_grad1 = restore_beta(sums7[0], sums8[0])
    beta_grad2 = restore_beta(sums5[0], sums6[0])

    def to_section(one, two):
        keep = jnp.where(first, one, two)
        send = jnp.where(first, two, one)
        return keep + swap(send)

    offset_grad = to_section(beta_grad1, beta_grad2)
    dwp = lax.psum(to_section(dwp1, dwp2), "dp").astype(F32)
    dwf = lax.psum(to_section(dwf1, dwf2), "dp").astype(F32)
    dws = lax.psum(to_section(dws1, dws2), "dp").astype(F32)

    out = from_final(out.reshape(frames2, side2, 8, DP)[:, :, :side2])
    out_got = swap(out[frames2 // 2 :])
    out_own = out[: frames2 // 2]
    block_output = jnp.stack([jnp.where(first, out_own, out_got), jnp.where(first, out_got, out_own)])
    gin_got = swap(gin[half:])
    gin_own = gin[:half]
    input_grad = jnp.stack([jnp.where(first, gin_own, gin_got), jnp.where(first, gin_got, gin_own)])
    return (
        block_output,
        input_grad,
        dwp[None, :, 0:256],
        dwp[None, :, 384:544],
        restore_mid(dwf)[None],
        dwp[None, :, 544:576],
        restore_small(dws)[None],
        dwp[None, :, 256:384],
        offset_grad[None],
    )


def solution(mesh):
    placed = (
        P("dp", "section", None, None, None),
        P("dp", "section", None, None, None),
        P("dp", None),
        P("section", None, None),
        P("section", None, None),
        P("section", None, None),
        P("section", None, None),
        P("section", None, None),
        P("section", None, None),
        P("section", None),
    )
    return jax.shard_map(
        on_device,
        mesh=mesh,
        in_specs=placed,
        out_specs=(
            P("dp", "section", None, None, None),
            P("dp", "section", None, None, None),
            P("section", None, None),
            P("section", None, None),
            P("section", None, None),
            P("section", None, None),
            P("section", None, None),
            P("section", None, None),
            P("section", None),
        ),
        check_vma=False,
    )
```

```python
import functools

import jax
import jax.numpy as jnp
from jax import lax
from jax.experimental import pallas as pl
from jax.experimental.pallas import tpu as pltpu
from jax.sharding import PartitionSpec as P

D = 832
DP = 896
C0 = 256
C1A = 160
C1B = 320
C2A = 32
C2B = 128
C3 = 128
EPS = 0.001
MESH = pl.DeviceIdType.MESH
F32 = jnp.float32
BF16 = jnp.bfloat16
VMEM_LIMIT = 60 * 2**20


def dot(a, b):
    return jnp.dot(a, b, preferred_element_type=F32)


def dot_nt(a, b):
    return lax.dot_general(a, b, (((1,), (1,)), ((), ())), preferred_element_type=F32)


def dot_tn(a, b):
    return lax.dot_general(a, b, (((0,), (0,)), ((), ())), preferred_element_type=F32)


def roll_rows(x, by):
    return pltpu.roll(x, by % x.shape[0], 0)


def roll_lanes(x, by):
    return pltpu.roll(x, by % x.shape[1], 1)


def lane_below(x, count):
    lanes = lax.broadcasted_iota(jnp.int32, x.shape, 1)
    return jnp.where(lanes < count, x, 0.0)


class Clips:
    def __init__(self, len_ref, frames, stride):
        sec = lax.axis_index("section")
        f = lax.broadcasted_iota(jnp.int32, (frames, 128), 0)

        def label(v):
            place = v * stride
            out = jnp.zeros_like(v)
            start = jnp.int32(0)
            for c in range(len_ref.shape[1]):
                end = start + len_ref[sec, c]
                out = jnp.where((place >= start) & (place < end), c + 1, out)
                start = end
            return out

        here = label(f)
        inside = here > 0

        def mask(m):
            return jnp.where(m, 1.0, 0.0).astype(F32)

        self.frames = frames
        self.valid = mask(inside)
        self.before = mask(inside & (f > 0) & (label(f - 1) == here))
        self.after = mask(inside & (f < frames - 1) & (label(f + 1) == here))
        self.inv = 1.0 / jnp.maximum(self.valid + self.before + self.after, 1.0)

    def times(self, v, pattern):
        return (v.reshape(-1, self.frames, 128) * pattern).reshape(v.shape)

    def fold(self, v):
        return jnp.sum(v.reshape(-1, self.frames, v.shape[-1]), axis=0)


def shift_places(v, frames, by):
    lanes = v.shape[-1]
    v3 = v.reshape(-1, frames, lanes)
    zero = jnp.zeros((1, frames, lanes), v.dtype)
    if by > 0:
        v3 = jnp.concatenate([v3[1:], zero], 0)
    else:
        v3 = jnp.concatenate([zero, v3[:-1]], 0)
    return v3.reshape(v.shape)


def add_stats(clips, acc, lanes, v, w=None):
    acc[0, :, lanes] += clips.fold(v)
    acc[1, :, lanes] += clips.fold(v * (v if w is None else w))


def affine(st, lanes):
    total, square, count = st[0:1, lanes], st[1:2, lanes], st[2:3, lanes]
    mean = total / count
    scale = lax.rsqrt(square / count - mean * mean + EPS)
    return scale, mean


def soft(t):
    e = jnp.exp(-jnp.abs(t))
    r = 1.0 / (1.0 + e)
    return jnp.maximum(t, 0.0) + jnp.log(1.0 + e), jnp.where(t >= 0, r, e * r)


def sigm(t):
    e = jnp.exp(-jnp.abs(t))
    r = 1.0 / (1.0 + e)
    return jnp.where(t >= 0, r, e * r)


def greet(partner=False):
    n = lax.axis_size("dp")
    me = lax.axis_index("dp")
    barrier = pltpu.get_barrier_semaphore()

    def go(k, _):
        pl.semaphore_signal(
            barrier, inc=1, device_id={"dp": lax.rem(me + k, n)}, device_id_type=MESH
        )
        return 0

    if partner:
        other = 1 - lax.axis_index("section")
        pl.semaphore_signal(barrier, inc=1, device_id={"section": other}, device_id_type=MESH)
    lax.fori_loop(1, n, go, 0)


def greeted(partner=False):
    pl.semaphore_wait(pltpu.get_barrier_semaphore(), lax.axis_size("dp") - 1 + int(partner))


def exchange_start(loc, buf, ssem, rsem):
    n = lax.axis_size("dp")
    me = lax.axis_index("dp")

    def start(k, _):
        pltpu.make_async_remote_copy(
            src_ref=loc,
            dst_ref=buf.at[me],
            send_sem=ssem.at[k],
            recv_sem=rsem.at[me],
            device_id={"dp": lax.rem(me + k, n)},
            device_id_type=MESH,
        ).start()
        return 0

    lax.fori_loop(1, n, start, 0)
    buf[me] = loc[...]


def exchange_finish(loc, buf, ssem, rsem, out):
    n = lax.axis_size("dp")
    me = lax.axis_index("dp")

    def wait(k, _):
        j = lax.rem(me + k, n)
        copy = pltpu.make_async_remote_copy(
            src_ref=loc,
            dst_ref=buf.at[j],
            send_sem=ssem.at[k],
            recv_sem=rsem.at[j],
            device_id={"dp": j},
            device_id_type=MESH,
        )
        copy.wait_send()
        copy.wait_recv()
        return 0

    lax.fori_loop(1, n, wait, 0)
    out[...] = jnp.sum(buf[...], axis=0)


def exchange(loc, buf, ssem, rsem, out):
    exchange_start(loc, buf, ssem, rsem)
    exchange_finish(loc, buf, ssem, rsem, out)


def swap_copy(src, dst, ssem, rsem):
    return pltpu.make_async_remote_copy(
        src_ref=src,
        dst_ref=dst,
        send_sem=ssem,
        recv_sem=rsem,
        device_id={"section": 1 - lax.axis_index("section")},
        device_id_type=MESH,
    )


def exchange_scratch(n, lanes):
    return [
        pltpu.VMEM((8, lanes), F32),
        pltpu.VMEM((n, 8, lanes), F32),
        pltpu.SemaphoreType.DMA((n,)),
        pltpu.SemaphoreType.DMA((n,)),
    ]


def pack_stats(clips, loc, acc, count=None):
    for t in range(loc.shape[1] // 128):
        lanes = pl.ds(128 * t, 128)
        loc[0:1, lanes] = jnp.sum(acc[0, :, lanes] * clips.valid, axis=0, keepdims=True)
        loc[1:2, lanes] = jnp.sum(acc[1, :, lanes] * clips.valid, axis=0, keepdims=True)
    if count is not None:
        total = jnp.sum(clips.valid, axis=0, keepdims=True) * float(count)
        for t in range(loc.shape[1] // 128):
            loc[2:3, 128 * t : 128 * t + 128] = total


def loop(n, body):
    def step(i, _):
        body(i)
        return 0

    lax.fori_loop(0, n, step, 0)


def inv_edges(side, frames, y):
    x = lax.broadcasted_iota(jnp.int32, (side, frames, 128), 0)
    ex = jnp.where((x == 0) | (x == side - 1), 0.5, 1.0 / 3.0).astype(F32)
    ey = jnp.where((y == 0) | (y == side - 1), 0.5, 1.0 / 3.0).astype(F32)
    return (ex * ey).reshape(side * frames, 128)


def box(clips, side, load, tx, store):
    frames = clips.frames
    tx[0] = jnp.zeros(tx.shape[1:], F32)
    tx[side + 1] = jnp.zeros(tx.shape[1:], F32)

    def across(y):
        v = load(y)
        t = clips.times(v, clips.valid)
        t = t + clips.times(roll_rows(v, 1), clips.before)
        t = t + clips.times(roll_rows(v, -1), clips.after)
        tx[y + 1] = t + shift_places(t, frames, 1) + shift_places(t, frames, -1)

    def down(y):
        store(y, tx[y] + tx[y + 1] + tx[y + 2])

    loop(side, across)
    loop(side, down)


def pool_forward(clips, side, load, tx, zp, acc):
    def store(y, v):
        z = clips.times(v * inv_edges(side, clips.frames, y), clips.inv)
        zp[y] = z
        add_stats(clips, acc, pl.ds(256, 128), z)

    box(clips, side, load, tx, store)


def upright(src, dst):
    rows = src.shape[1]
    width = src.shape[0]

    def body(i):
        at = pl.ds(pl.multiple_of(i * 128, 128), 128)
        dst[at, 0:width] = src[:, at].astype(F32).T.astype(BF16)

    loop(rows // 128, body)
    if rows % 128:
        at = slice(rows - rows % 128, rows)
        dst[at, 0:width] = src[:, at].astype(F32).T.astype(BF16)


def arrange_first(src, wp, b, flip):
    one, mid_in, small_in, pool = src
    wp[b, :, 0:256] = one[...]
    wp[b, :, 256:384] = pool[...]
    upright(mid_in, flip)
    wp[b, :, 384:544] = flip[0:D, 0:C1A]
    upright(small_in, flip)
    wp[b, :, 544:576] = flip[0:D, 0:C2A]
    wp[b, :, 576:640] = jnp.zeros((D, 64), BF16)


def arrange_beta(src, dst):
    v = jnp.concatenate([jnp.broadcast_to(src[...], (8, 1024)), jnp.zeros((8, 128), F32)], 1)
    lane = lax.broadcasted_iota(jnp.int32, v.shape, 1)
    out = jnp.zeros_like(v)
    for lo, hi, by in (
        (0, 256, 0),
        (256, 576, -160),
        (576, 832, -192),
        (896, 1056, 640),
        (1056, 1088, 320),
    ):
        out = jnp.where((lane >= lo) & (lane < hi), roll_lanes(v, by), out)
    dst[...] = out[0:1]


def arrange_conv(mid_flat, small, wf, ws, b, mid):
    upright(mid_flat, mid)
    for dy in range(3):
        wf[b, 512 * dy + 480 : 512 * dy + 512, :] = jnp.zeros((32, 1024), BF16)
        ws[b, 128 * dy + 96 : 128 * dy + 128, :] = jnp.zeros((32, 384), BF16)
        wf[b, 512 * dy : 512 * dy + 512, 960:1024] = jnp.zeros((512, 64), BF16)
        for dt in range(3):
            for dx in range(3):
                r = 96 * (3 * dt + dy) + 32 * dx
                to = 128 * dy + 32 * dt
                ws[b, to : to + 32, 128 * dx : 128 * dx + 128] = small[r : r + 32, :]
            for dx in range(3):
                r = 480 * (3 * dt + dy) + 160 * dx
                for rows, to in ((128, 128 * dt), (32, 384 + 32 * dt)):
                    to = to + 512 * dy
                    wf[b, to : to + rows, 256 * dx : 256 * dx + 256] = mid[r : r + rows, 0:256]
                    wf[b, to : to + rows, 768 + 64 * dx : 832 + 64 * dx] = mid[
                        r : r + rows, 256:320
                    ]
                    r = r + rows


def start_kernel(
    len_ref, x, og, w_one, w_mid_in, w_small_in, w_pool, w_mid, w_small, bn,
    xgot_out, zone_out, zin_out, zp_out, st, wp1, wp2, wf1, wf2, ws1, ws2, beta1, beta2, og_got,
    x_own, x_got, zone, zin, zp, yp, tx,
    own_one, own_mid_in, own_small_in, own_pool, own_mid, own_small,
    got_one, got_mid_in, got_small_in, got_pool, got_mid, got_small, beta, got_beta, flip,
    wp, wf, ws, hacc, acc, loc, buf, ssem, rsem, lsem, osem, psem, qsem,
):
    greet(partner=True)
    sec = lax.axis_index("section")
    side = zone.shape[0]
    clips = Clips(len_ref, 16, 1)
    raw = (w_one, w_mid_in, w_small_in, w_pool, w_mid, w_small)
    own = (own_one, own_mid_in, own_small_in, own_pool, own_mid, own_small)
    got = (got_one, got_mid_in, got_small_in, got_pool, got_mid, got_small)
    local = [pltpu.make_async_copy(x.at[sec], x_own, lsem.at[0])]
    local += [
        pltpu.make_async_copy(a.at[0], b, lsem.at[i + 1]) for i, (a, b) in enumerate(zip(raw, own))
    ]
    for c in local:
        c.start()
    hacc[...] = jnp.zeros_like(hacc)
    acc[...] = jnp.zeros_like(acc)
    loc[...] = jnp.zeros_like(loc)
    arrange_beta(bn, beta)
    greeted(partner=True)
    pairs = [(a.at[0], b) for a, b in zip(raw[:4], got[:4])]
    pairs += [(beta, got_beta), (x.at[1 - sec], x_got)]
    pairs += [(a.at[0], b) for a, b in zip(raw[4:], got[4:])]
    pairs += [(og.at[1 - sec], og_got)]
    remote = [swap_copy(a, b, psem.at[i], qsem.at[i]) for i, (a, b) in enumerate(pairs)]
    for c in remote:
        c.start()
    for c in local[1:]:
        c.wait()
    arrange_first(own[:4], wp, sec, flip)
    arrange_conv(own_mid, own_small, wf, ws, sec, flip)
    for c in remote[:5]:
        c.wait()
    arrange_first(got[:4], wp, 1 - sec, flip)
    beta1[...] = jnp.where(sec == 0, beta[...], got_beta[...])
    beta2[...] = jnp.where(sec == 0, got_beta[...], beta[...])
    ny = side // 2
    rows = ny * side * 8
    outs = []

    def put(src, dst):
        c = pltpu.make_async_copy(src, dst, osem.at[len(outs)])
        c.start()
        outs.append(c)

    for part, src in enumerate((x_own, x_got)):
        (local[0] if part == 0 else remote[5]).wait()
        half = sec if part == 0 else 1 - sec

        def body(i, src=src, half=half):
            here = pl.ds(i * ny, ny)
            y = dot(src[pl.ds(pl.multiple_of(i * rows, 16), rows)], wp[0])

            def place(lo, hi):
                return y[:, lo:hi].reshape(ny, side, 8, hi - lo)

            zone[here, :, half] = place(0, 256)
            yp[here, :, half] = place(256, 384)
            zin[here, :, half] = place(384, 640)
            for lo, hi in ((0, 256), (384, 640)):
                v = y[:, lo:hi].reshape(-1, 8, 256)
                hacc[0, half, :, lo:hi] += jnp.sum(v, axis=0)
                hacc[1, half, :, lo:hi] += jnp.sum(v * v, axis=0)

        loop(2, body)
    put(x_got, xgot_out)
    put(zin, zin_out)
    put(zone, zone_out)
    acc[...] = hacc[...].reshape(acc.shape)
    pool_forward(clips, side, lambda y: yp[y].reshape(side * 16, 128), tx, zp, acc)
    put(zp, zp_out)
    pack_stats(clips, loc, acc, side * side)
    exchange_start(loc, buf, ssem, rsem)
    for c in remote[6:]:
        c.wait()
    arrange_conv(got_mid, got_small, wf, ws, 1 - sec, flip)
    for a, b in ((wf, (wf1, wf2)), (ws, (ws1, ws2)), (wp, (wp1, wp2))):
        for i in range(2):
            put(a.at[i], b[i])
    exchange_finish(loc, buf, ssem, rsem, st)
    for c in outs:
        c.wait()


def inner_tiles(clips, z, st, beta):
    tiles = []
    for t in range(2):
        scale, mean = affine(st, pl.ds(384 + 128 * t, 128))
        b = beta[0:1, pl.ds(896 + 128 * t, 128)]
        act, _ = soft(z[:, 128 * t : 128 * (t + 1)] * scale + (b - mean * scale))
        tiles.append(clips.times(act, clips.valid))
    return tiles


def tap_tiles(clips, a, b):
    def before(v):
        return clips.times(roll_rows(v, 1), clips.before)

    def after(v):
        return clips.times(roll_rows(v, -1), clips.after)

    lane = lax.broadcasted_iota(jnp.int32, b.shape, 1)
    ones = clips.times(jnp.where(lane == 96, 1.0, 0.0).astype(F32), clips.valid)

    def three32(v):
        return before(v) + roll_lanes(v, 32) + roll_lanes(after(v), 64) + ones

    tail = lane_below(b, 32)
    small = lane_below(roll_lanes(b, -32), 32)
    return [before(a), a, after(a), three32(tail)], three32(small)


def untap(clips, parts, small):
    def before(v):
        return roll_rows(clips.times(v, clips.before), -1)

    def after(v):
        return roll_rows(clips.times(v, clips.after), 1)

    def back32(v):
        return (
            lane_below(before(v), 32)
            + lane_below(roll_lanes(v, -32), 32)
            + lane_below(roll_lanes(after(v), -64), 32)
        )

    a = before(parts[0]) + parts[1] + after(parts[2])
    return a, back32(parts[3]) + roll_lanes(back32(small), 32)


def typical(beta):
    sp, sg = soft(jnp.broadcast_to(beta, (8, beta.shape[-1])))
    return sp + 0.5 * sg * (1.0 - sg)


def outer(c, s):
    k = lax.broadcasted_iota(jnp.int32, c.shape, 0)
    c = jnp.where(k < 2, c, 0.0).astype(BF16)
    s = jnp.broadcast_to(s, (8, s.shape[-1]))
    high = s.astype(BF16).astype(F32)
    k = lax.broadcasted_iota(jnp.int32, s.shape, 0)
    s = jnp.where(k == 0, high, jnp.where(k == 1, s - high, 0.0)).astype(BF16)
    return dot_tn(c, s)


def tap_points(beta):
    a = typical(beta[0:1, 896:1024])
    b = typical(beta[0:1, 1024:1152])

    def three(v):
        return v + roll_lanes(v, 32) + roll_lanes(v, 64)

    tail = three(lane_below(b, 32))
    small = three(lane_below(roll_lanes(b, -32), 32))
    return jnp.concatenate([a, a, a, tail], 1), small


def centre_mid(grad, beta):
    c, _ = tap_points(beta)
    row = jnp.broadcast_to(grad[992:993, :], (8, 1024))
    main = row[:, 256:512]
    tail = lane_below(roll_lanes(row[:, 768:896], 64), 64)
    s = jnp.concatenate([main, main, main, tail + roll_lanes(tail, 64), tail], 1)
    return outer(c, s)


def centre_small(grad, beta):
    _, c = tap_points(beta)
    row = jnp.broadcast_to(grad[224:225, 128:256], (8, 128))
    return outer(c, jnp.concatenate([row, row, row], 1))


def conv_gather(frames, p, s):
    def three(at):
        return (
            shift_places(at(0), frames, -1) + at(1) + shift_places(at(2), frames, 1)
        )

    main = three(lambda k: p[:, 256 * k : 256 * k + 256])
    small = three(lambda k: s[:, 128 * k : 128 * k + 128])
    ends = p[:, 768:896]
    tail = three(lambda k: (ends, roll_lanes(ends, 64), p[:, 896:1024])[k])
    return main, small, lane_below(tail, 64)


def spread_x(frames, v, by):
    return v if by == 0 else shift_places(v, frames, -by)


def put_spread(frames, main, small, tail, put_mid, put_small):
    for k in range(3):
        put_mid(256 * k, spread_x(frames, main, k - 1))
        put_small(128 * k, spread_x(frames, small, k - 1))
    put_mid(768, spread_x(frames, tail, -1) + roll_lanes(tail, 64))
    put_mid(896, spread_x(frames, tail, 1))


def join_final(small, tail, pool):
    s, p = roll_lanes(small, 64), roll_lanes(pool, 64)
    low = lax.broadcasted_iota(jnp.int32, small.shape, 1) < 64
    return jnp.where(low, tail, s), jnp.where(low, s, p), jnp.where(low, p, 0.0)


def split_final(t4, t5, t6):
    a, b, c = roll_lanes(t4, 64), roll_lanes(t5, 64), roll_lanes(t6, 64)
    low = lax.broadcasted_iota(jnp.int32, t4.shape, 1) < 64
    return jnp.where(low, a, b), jnp.where(low, t4, 0.0), jnp.where(low, b, c)


def final_stats(st1, st2, stf):
    stf[:, 0:256] = st1[:, 0:256]
    stf[:, 256:512] = st2[:, 0:256]
    for t, v in enumerate(join_final(st2[:, 256:384], st2[:, 384:512], st1[:, 256:384])):
        stf[:, 512 + 128 * t : 640 + 128 * t] = v
    stf[2:3, :] = jnp.broadcast_to(st1[2:3, 0:1], (1, DP))


def store_conv(clips, y, p, s, zp, zf, acc):
    main, small, tail = conv_gather(clips.frames, p, s)
    zf[y, :, 256:512] = main
    for t, v in enumerate(join_final(small, tail, zp[y])):
        zf[y, :, 512 + 128 * t : 640 + 128 * t] = v
    add_stats(clips, acc, pl.ds(0, 256), main)
    add_stats(clips, acc, pl.ds(256, 128), small)
    add_stats(clips, acc, pl.ds(384, 128), tail)


def conv_kernel(
    len_ref, zin, zone, zp, st1, beta, wf, ws, cat, scat, zf, stf, st2, acc, loc, buf, ssem, rsem
):
    greet()
    side, rows = zin.shape[0], zin.shape[1]
    clips = Clips(len_ref, 16, 1)
    acc[...] = jnp.zeros_like(acc)
    loc[...] = jnp.zeros_like(loc)
    for y in (0, side + 1):
        cat[y] = jnp.zeros(cat.shape[1:], BF16)
        scat[y] = jnp.zeros(scat.shape[1:], BF16)

    def build(y):
        a, b = inner_tiles(clips, zin[y], st1, beta)
        parts, small = tap_tiles(clips, a, b)
        for i, part in enumerate(parts):
            cat[y + 1, :, 128 * i : 128 * i + 128] = part.astype(BF16)
        scat[y + 1] = small.astype(BF16)

    loop(side, build)
    ny = 2

    def products(i):
        y0 = i * ny

        def taps(ref):
            return jnp.concatenate(
                [ref[pl.ds(y0 + dy, ny)].reshape(ny * rows, ref.shape[-1]) for dy in range(3)], axis=1
            )

        p = dot(taps(cat), wf[...])
        s = dot(taps(scat), ws[...])
        for q in range(ny):
            here = slice(q * rows, (q + 1) * rows)
            store_conv(clips, y0 + q, p[here], s[here], zp, zf, acc)

    loop(side // ny, products)
    pack_stats(clips, loc, acc)
    greeted()
    exchange_start(loc, buf, ssem, rsem)

    def move(y):
        zf[y, :, 0:256] = zone[y]

    loop(side, move)
    exchange_finish(loc, buf, ssem, rsem, st2)
    final_stats(st1, st2, stf)


def output_kernel(len_ref, zf, stf, beta, sig, hand, asum, bsum, scr):
    side = zf.shape[0]
    half = side // 2
    clips = Clips(len_ref, 16, 1)

    def body(k):
        for t in range(7):
            lanes = pl.ds(128 * t, 128)
            scale, mean = affine(stf, lanes)
            b = beta[0:1, lanes]
            pooled = None
            for q in range(2):
                u = (zf[2 * k + q, :, lanes] - mean) * scale
                sp, sg = soft(u + b)
                sp, sg = clips.times(sp, clips.valid), clips.times(sg, clips.valid)
                if t == 6:
                    lane = lax.broadcasted_iota(jnp.int32, sp.shape, 1)
                    one = clips.times(jnp.ones_like(sp), clips.valid)
                    sp = jnp.where(lane == 127, one, lane_below(sp, 64))
                    sg = lane_below(sg, 64)
                sig[2 * k + q, :, lanes] = sg.astype(BF16)
                three = [
                    jnp.sum(v.reshape(half, 2, 16, 128), axis=1) for v in (sp, sg, sg * u)
                ]
                pooled = three if pooled is None else [x + y for x, y in zip(pooled, three)]
            for v, dst in zip(pooled, (hand, asum, bsum)):
                scr[...] = v
                dst[k, :, :, lanes] = (
                    scr[:, pl.ds(0, 8, stride=2), :] + scr[:, pl.ds(1, 8, stride=2), :]
                ) * 0.125

    loop(half, body)


def second_kernel(
    len_ref, hand, asum, bsum, og, og_got, wp, wf, ws, beta, beta1,
    block_out, hg, packed, sums5, sums6, sums7,
    gown, grad, out, lsem, psem, qsem,
    hbuf, zin, zp, zf, stf, yp, tx, catf, cat, scat, pbuf, sbuf, dbuf, dzc, dzs, dz1, din,
    acc, st3, st4, acc7, accm, accs, accp,
    loc3, buf3, ss3, rs3, loc4, buf4, ss4, rs4, loc5, buf5, ss5, rs5,
    loc6, buf6, ss6, rs6, loc7, buf7, ss7, rs7,
):
    greet(partner=True)
    sec = lax.axis_index("section")
    own = pltpu.make_async_copy(og.at[sec], gown, lsem.at[0])
    own.start()
    side = hand.shape[0]
    rows = side * 8
    total = side * rows
    clips = Clips(len_ref, 8, 2)
    for ref in (acc, acc7, loc3, loc4, loc5, loc6, loc7):
        ref[...] = jnp.zeros_like(ref)

    hbuf[...] = hand[...].reshape(total, DP).astype(BF16)
    y = dot(hbuf[:, 0:D], wp[...])
    zf[:, :, 0:C0] = y[:, 0:C0].reshape(side, rows, C0)
    yp[...] = y[:, 256:384].reshape(side, rows, 128)
    zin[...] = y[:, 384:640].reshape(side, rows, 256)

    def first_sums(y):
        add_stats(clips, acc, pl.ds(0, 256), zf[y, :, 0:256])
        add_stats(clips, acc, pl.ds(384, 256), zin[y])

    loop(side, first_sums)
    pool_forward(clips, side, lambda y: yp[y], tx, zp, acc)
    pack_stats(clips, loc3, acc, side * side)
    greeted(partner=True)
    exchange_start(loc3, buf3, ss3, rs3)
    own.wait()
    mine, theirs = gown[...].astype(F32), og_got[...].astype(F32)
    low = jnp.where(sec == 0, mine, theirs)
    high = jnp.where(sec == 0, theirs, mine)
    grad[...] = jnp.concatenate([low, high], 2)
    exchange_finish(loc3, buf3, ss3, rs3, st3)

    catf[0] = jnp.zeros(catf.shape[1:], F32)
    catf[side + 1] = jnp.zeros(catf.shape[1:], F32)

    def build(y):
        a, b = inner_tiles(clips, zin[y], st3, beta)
        parts, small = tap_tiles(clips, a, b)
        for t, v in enumerate(parts + [small]):
            catf[y + 1, :, 128 * t : 128 * t + 128] = v

    loop(side, build)
    for dy in range(3):
        v = catf[dy : dy + side].reshape(total, 640).astype(BF16)
        cat[:, 512 * dy : 512 * dy + 512] = v[:, 0:512]
        scat[:, 128 * dy : 128 * dy + 128] = v[:, 512:640]
    pbuf[...] = dot(cat[...], wf[...]).reshape(side, rows, 1024)
    sbuf[...] = dot(scat[...], ws[...]).reshape(side, rows, 384)
    acc[...] = jnp.zeros_like(acc)
    loop(side, lambda y: store_conv(clips, y, pbuf[y], sbuf[y], zp, zf, acc))
    pack_stats(clips, loc4, acc)
    exchange(loc4, buf4, ss4, rs4, st4)
    final_stats(st3, st4, stf)

    def emit(y):
        for t in range(7):
            lanes = pl.ds(128 * t, 128)
            scale, mean = affine(stf, lanes)
            u = (zf[y, :, lanes] - mean) * scale
            sp, sg = soft(u + beta[0:1, lanes])
            width = 128 if t < 6 else 64
            gr = grad[y, :, :, 128 * t : 128 * t + width].reshape(rows, width)
            if t == 6:
                gr = jnp.concatenate([gr, jnp.zeros((rows, 64), F32)], 1)
            d = gr * clips.times(sg, clips.valid)
            dbuf[y, :, lanes] = d
            add_stats(clips, acc7, lanes, d, u)
            sp = clips.times(sp, clips.valid).reshape(side, 8, 128)[:, :, 0:width]
            for h in range(2):
                out[h, y, :, :, 128 * t : 128 * t + width] = sp[:, 4 * h : 4 * h + 4].astype(BF16)

    loop(side, emit)
    mine = pltpu.make_async_copy(out.at[sec], block_out.at[sec], lsem.at[1])
    mine.start()
    theirs = swap_copy(out.at[1 - sec], block_out.at[sec], psem, qsem)
    theirs.start()
    pack_stats(clips, loc5, acc7)
    exchange(loc5, buf5, ss5, rs5, sums5)
    count = st3[2:3, 0:128]

    def dz_of(y, t):
        lanes = pl.ds(128 * t, 128)
        scale, mean = affine(stf, lanes)
        u = (zf[y, :, lanes] - mean) * scale
        m1, m2 = sums5[0:1, lanes] / count, sums5[1:2, lanes] / count
        return clips.times((dbuf[y, :, lanes] - m1 - u * m2) * scale, clips.valid)

    def dz_final(y):
        for t in range(2):
            dz1[y, :, 128 * t : 128 * t + 128] = dz_of(y, t)
        main = jnp.concatenate([dz_of(y, 2), dz_of(y, 3)], 1)
        small, tail, pool = split_final(*(dz_of(y, t) for t in (4, 5, 6)))
        yp[y] = clips.times(pool * inv_edges(side, 8, y), clips.inv)

        def put(ref):
            def go(lane, v):
                ref[y, :, lane : lane + v.shape[-1]] = v

            return go

        put_spread(8, main, small, tail, put(dzc), put(dzs))

    loop(side, dz_final)

    def boxed(y, v):
        dz1[y, :, 256:384] = clips.times(v, clips.valid)

    box(clips, side, lambda y: yp[y], tx, boxed)
    dzc_b = dzc[...].reshape(total, 1024).astype(BF16)
    dzs_b = dzs[...].reshape(total, 384).astype(BF16)
    for dy in (-1, 0, 1):
        k = dy + 1
        q = dot_nt(dzc_b, wf[512 * k : 512 * k + 512]).reshape(side, rows, 512)
        r = dot_nt(dzs_b, ws[128 * k : 128 * k + 128]).reshape(side, rows, 128)
        if k == 0:
            catf[1 : side + 1] = jnp.zeros((side, rows, 640), F32)
        catf[1 + dy : 1 + dy + side, :, 0:512] += q
        catf[1 + dy : 1 + dy + side, :, 512:640] += r
    acc[...] = jnp.zeros_like(acc)

    def inner_back(y):
        parts = [catf[y + 1, :, 128 * t : 128 * t + 128] for t in range(5)]
        inner_up(clips, zin[y], untap(clips, parts[:4], parts[4]), st3, beta, acc, din, y)

    loop(side, inner_back)
    pack_stats(clips, loc6, acc)
    exchange_start(loc6, buf6, ss6, rs6)
    accm[...] = dot_tn(cat[...], dzc_b)
    exchange_finish(loc6, buf6, ss6, rs6, sums6)

    def dz_inner(y):
        for t in range(2):
            dz1[y, :, 384 + 128 * t : 512 + 128 * t] = inner_dz(
                clips, t, zin[y], din[y], st3, sums6, count
            )

    loop(side, dz_inner)
    dz1_b = dz1[...].reshape(total, 640).astype(BF16)
    hgv = dot_nt(dz1_b, wp[...]).astype(BF16).astype(F32)
    hg[:, :, :, 0:D] = hgv.reshape(side, side, 8, D)
    hg[:, :, :, D:DP] = jnp.zeros((side, side, 8, DP - D), F32)
    acc7[...] = jnp.zeros_like(acc7)

    def upstream(y):
        for t in range(7):
            lanes = pl.ds(128 * t, 128)
            gr = hg[y, :, :, lanes]
            acc7[0, :, lanes] += jnp.sum(gr * asum[y, :, :, lanes], axis=0)
            acc7[1, :, lanes] += jnp.sum(gr * bsum[y, :, :, lanes], axis=0)

    loop(side, upstream)
    pack_stats(clips, loc7, acc7)
    exchange_start(loc7, buf7, ss7, rs7)
    accs[...] = dot_tn(scat[...], dzs_b)
    accp[...] = dot_tn(hbuf[...], dz1_b)
    pool = dz1[:, :, 256:384].reshape(total, 128)
    rest = (pool - dz1_b[:, 256:384].astype(F32)).astype(BF16)
    accp[:, 256:384] += dot_tn(hbuf[...], rest)
    c = jnp.concatenate([typical(beta1[0:1, 0:D]), jnp.zeros((8, DP - D), F32)], 1)
    full = accp[...] - outer(c, accp[DP - 1 : DP, :])
    pack_grads(packed, accm, accs, beta, lambda t: full[0:D, 128 * t : 128 * t + 128])
    exchange_finish(loc7, buf7, ss7, rs7, sums7)
    mine.wait()
    theirs.wait()


def pack_grads(packed, accm, accs, beta, first):
    mid = centre_mid(accm, beta)
    small = centre_small(accs, beta)
    end = packed.shape[1]
    for t in range(8):
        lanes = slice(128 * t, 128 * t + 128)
        for k in range(3):
            packed[t, 480 * k : 480 * k + 480] = (
                accm[512 * k : 512 * k + 480, lanes] - mid[0:480, lanes]
            ).astype(BF16)
        if t < 5:
            if first is not None:
                packed[t, 1440 : 1440 + D] = first(t).astype(BF16)
        else:
            lanes = slice(128 * (t - 5), 128 * (t - 5) + 128)
            for k in range(3):
                packed[t, 1440 + 128 * k : 1568 + 128 * k] = (
                    accs[128 * k : 128 * k + 128, lanes] - small[:, lanes]
                ).astype(BF16)
            packed[t, 1824 : 1440 + D] = jnp.zeros((D - 384, 128), BF16)
        packed[t, 1440 + D : end] = jnp.zeros((end - 1440 - D, 128), BF16)


def inner_up(clips, z, backs, st, beta, acc, din, y):
    for t in range(2):
        lanes = pl.ds(384 + 128 * t, 128)
        scale, mean = affine(st, lanes)
        u = (z[:, 128 * t : 128 * t + 128] - mean) * scale
        d = backs[t] * clips.times(sigm(u + beta[0:1, pl.ds(896 + 128 * t, 128)]), clips.valid)
        din[y, :, 128 * t : 128 * t + 128] = d
        add_stats(clips, acc, lanes, d, u)


def inner_dz(clips, t, z, d, st, sums, count):
    lanes = pl.ds(384 + 128 * t, 128)
    here = slice(128 * t, 128 * t + 128)
    scale, mean = affine(st, lanes)
    u = (z[:, here] - mean) * scale
    m1, m2 = sums[0:1, lanes] / count, sums[1:2, lanes] / count
    dz = clips.times((d[:, here] - m1 - u * m2) * scale, clips.valid)
    return lane_below(dz, 64) if t == 1 else dz


def put_halves(ref, y, lane, v):
    side, lanes = v.shape[0] // 16, v.shape[1]
    v = v.reshape(side, 2, 8, lanes)
    for h in range(2):
        ref[h, y, :, lane : lane + lanes] = v[:, h].reshape(side * 8, lanes).astype(BF16)


def dz_kernel(len_ref, zf, sig, hg, stf, sums7, dzc, dzs, dz1, scr, yp, tx):
    side = zf.shape[0]
    half = side // 2
    rows = side * 16
    clips = Clips(len_ref, 16, 1)
    count = stf[2:3, 0:128]
    for y in (0, side + 1):
        dzc[y] = jnp.zeros(dzc.shape[1:], BF16)
        dzs[y] = jnp.zeros(dzs.shape[1:], BF16)

    def body(k):
        tiles = ([], [])
        for t in range(7):
            lanes = pl.ds(128 * t, 128)
            scale, mean = affine(stf, lanes)
            m1, m2 = sums7[0:1, lanes] / count, sums7[1:2, lanes] / count
            gr = hg[k, :, :, lanes] * 0.125
            scr[:, pl.ds(0, 8, stride=2), :] = gr
            scr[:, pl.ds(1, 8, stride=2), :] = gr
            gr = scr[...]
            gr = jnp.broadcast_to(gr[:, None], (half, 2, 16, 128)).reshape(rows, 128)
            for q in range(2):
                y = 2 * k + q
                u = (zf[y, :, lanes] - mean) * scale
                d = gr * sig[y, :, lanes].astype(F32)
                dz = clips.times((d - m1 - u * m2) * scale, clips.valid)
                if t < 2:
                    put_halves(dz1, y, 128 * t, dz)
                else:
                    tiles[q].append(dz)
        for q in range(2):
            y = 2 * k + q
            small, tail, pool = split_final(*tiles[q][2:])
            yp[y] = clips.times(pool * inv_edges(side, 16, y), clips.inv)

            def put(ref, y=y):
                def go(lane, v):
                    ref[y + 1, :, lane : lane + v.shape[-1]] = v.astype(BF16)

                return go

            put_spread(
                16, jnp.concatenate(tiles[q][:2], 1), small, tail, put(dzc), put(dzs)
            )

    loop(half, body)

    def boxed(y, v):
        put_halves(dz1, y, 256, clips.times(v, clips.valid))

    box(clips, side, lambda y: yp[y], tx, boxed)


def conv_grad_kernel(cat, scat, dzc, dzs, beta, packed, acc, accs):
    side = cat.shape[0] - 2
    rows = cat.shape[1]
    ny = 7
    acc[...] = jnp.zeros_like(acc)
    accs[...] = jnp.zeros_like(accs)

    def body(i):
        y0 = i * ny + 1

        def take(ref, y):
            return ref[pl.ds(y, ny)].reshape(ny * rows, ref.shape[-1])

        a, s = take(cat, y0), take(scat, y0)
        for dy in (-1, 0, 1):
            k = dy + 1
            acc[512 * k : 512 * k + 512] += dot_tn(a, take(dzc, y0 - dy))
            accs[128 * k : 128 * k + 128] += dot_tn(s, take(dzs, y0 - dy))

    loop(side // ny, body)
    pack_grads(packed, acc, accs, beta, None)


def conv_back_kernel(
    len_ref, dzc, dzs, wf, ws, zin, st1, beta, dzi, sums8, din, acc, loc, buf, ssem, rsem
):
    greet()
    side, rows = zin.shape[0], zin.shape[1]
    clips = Clips(len_ref, 16, 1)
    acc[...] = jnp.zeros_like(acc)
    loc[...] = jnp.zeros_like(loc)
    ny = 2

    def body(i):
        y0 = i * ny + 1
        q = s = None
        for dy in (-1, 0, 1):
            k = dy + 1
            here = pl.ds(y0 - dy, ny)
            t = dot_nt(dzc[here].reshape(ny * rows, 1024), wf[512 * k : 512 * k + 512])
            q = t if q is None else q + t
            t = dot_nt(dzs[here].reshape(ny * rows, 384), ws[128 * k : 128 * k + 128])
            s = t if s is None else s + t
        for j in range(ny):
            y = i * ny + j
            here = slice(j * rows, (j + 1) * rows)
            parts = [q[here, 128 * t : 128 * t + 128] for t in range(4)]
            inner_up(clips, zin[y], untap(clips, parts, s[here]), st1, beta, acc, din, y)

    loop(side // ny, body)
    pack_stats(clips, loc, acc)
    greeted()
    exchange(loc, buf, ssem, rsem, sums8)
    count = st1[2:3, 0:128]

    def dz(y):
        for t in range(2):
            put_halves(dzi, y, 128 * t, inner_dz(clips, t, zin[y], din[y], st1, sums8, count))

    loop(side, dz)


def input_kernel(
    x, x_got, dz1, dzi, wp, packed_in, gin, packed,
    x_own, near, far, acc, lsem, psem, qsem,
):
    greet_core()
    sec = lax.axis_index("section")
    own = pltpu.make_async_copy(x.at[sec], x_own, lsem.at[0])
    own.start()
    keep = pltpu.make_async_copy(packed_in, packed, lsem.at[1])
    keep.start()
    side = dz1.shape[1]
    rows = dz1.shape[2]
    ny = 7
    acc[...] = jnp.zeros_like(acc)
    for src, dst, half in ((x_got, far, 1 - sec), (x_own, near, sec)):

        def body(i, src=src, dst=dst, half=half):
            here = pl.ds(i * ny, ny)
            d = jnp.concatenate([dz1[half, here], dzi[half, here]], -1).reshape(ny * rows, 640)
            at = pl.ds(pl.multiple_of(i * ny * rows, 16), ny * rows)
            dst[at] = dot_nt(d, wp[...]).astype(BF16)
            acc[...] += dot_tn(src[at], d)

        if src is x_own:
            own.wait()
        loop(side // ny, body)
        if src is x_got:
            greeted_core()
            send = swap_copy(far, gin.at[sec], psem, qsem)
            send.start()
    mine = pltpu.make_async_copy(near, gin.at[sec], lsem.at[0])
    mine.start()
    keep.wait()
    for t in range(5):
        packed[t, 1440 : 1440 + D] = acc[:, 128 * t : 128 * t + 128].astype(BF16)
    mine.wait()
    send.wait()


def greet_core():
    pl.semaphore_signal(
        pltpu.get_barrier_semaphore(),
        inc=1,
        device_id={"section": 1 - lax.axis_index("section")},
        device_id_type=MESH,
    )


def greeted_core():
    pl.semaphore_wait(pltpu.get_barrier_semaphore(), 1)


def bit_of(me, k):
    return lax.rem(me // (1 << k), 2)


class Reducer:
    def __init__(self, q, land, ssem, rsem, ready, order, base):
        self.q, self.land, self.ssem, self.rsem, self.ready = q, land, ssem, rsem, ready
        self.order, self.base = order, base
        me = lax.axis_index("dp")
        self.steps = []
        tiles, rows = q.shape[0], q.shape[1]
        t0, r0 = 0, 0
        for i, k in enumerate(order):
            bit = bit_of(me, k)
            partner = me + (1 - 2 * bit) * (1 << k)
            if tiles > 1:
                tiles //= 2
                keep, send = (t0 + bit * tiles, r0), (t0 + (1 - bit) * tiles, r0)
            else:
                rows //= 2
                keep, send = (t0, r0 + bit * rows), (t0, r0 + (1 - bit) * rows)
            t0, r0 = keep
            self.steps.append((partner, keep, send, tiles, rows))

    def region(self, at, tiles, rows):
        t, r = at
        if not isinstance(r, int):
            r = pl.multiple_of(r, 16)
        return self.q.at[pl.ds(t, tiles), pl.ds(r, rows)]

    def copy(self, src, dst, sem, partner):
        return pltpu.make_async_remote_copy(
            src_ref=src,
            dst_ref=dst,
            send_sem=self.ssem.at[self.base + sem],
            recv_sem=self.rsem.at[self.base + sem],
            device_id={"dp": partner},
            device_id_type=MESH,
        )

    def halve(self, i):
        partner, keep, send, tiles, rows = self.steps[i]
        return self.copy(self.region(send, tiles, rows), self.land[i], i, partner)

    def add(self, i):
        partner, keep, send, tiles, rows = self.steps[i]
        q, land = self.region(keep, tiles, rows), self.land[i]
        chunk = 96 if rows % 96 == 0 else 16
        parts = rows // chunk

        def body(j):
            t, r = j // parts, pl.multiple_of(lax.rem(j, parts) * chunk, 16)
            at = pl.ds(r, chunk)
            q[t, at] = (q[t, at].astype(F32) + land[t, at].astype(F32)).astype(BF16)

        loop(tiles * parts, body)

    def free(self, i):
        pl.semaphore_signal(
            self.ready.at[self.base // 2 + i],
            inc=1,
            device_id={"dp": self.steps[i][0]},
            device_id_type=MESH,
        )

    def await_free(self, i):
        pl.semaphore_wait(self.ready.at[self.base // 2 + i], 1)

    def double(self, i):
        partner, keep, send, tiles, rows = self.steps[i]
        q = self.region(keep, tiles, rows)
        return self.copy(q, q, len(self.steps) + i, partner)


def land_shapes(tiles, rows, bits):
    out = []
    for _ in range(bits):
        if tiles > 1:
            tiles //= 2
        else:
            rows //= 2
        out.append((tiles, rows, 128))
    return out


def orders(bits):
    plain = list(range(bits))
    swapped = plain[:]
    if bits > 1:
        swapped[0], swapped[1] = 1, 0
    return plain, swapped


def reduce_kernel(bits, packed1, packed2, s5, s6, s7, s8, full, offs, *scratch):
    n = bits
    q = scratch[0:2]
    core_land = scratch[2:4]
    land = (scratch[4 : 4 + n], scratch[4 + n : 4 + 2 * n])
    sums, sums_got, csend, crecv, ssem, rsem, lsem, ready = scratch[4 + 2 * n :]
    sec = lax.axis_index("section")
    me = lax.axis_index("dp")
    barrier = pltpu.get_barrier_semaphore()
    greet_core()
    for k in range(n):
        partner = me + (1 - 2 * bit_of(me, k)) * (1 << k)
        pl.semaphore_signal(barrier, inc=1, device_id={"dp": partner}, device_id_type=MESH)
    half = q[0].shape[1]
    packed = (packed1, packed2)
    mine = []
    for b in range(2):
        src = packed[b].at[:, pl.ds(pl.multiple_of(sec * half, 16), half)]
        mine.append(pltpu.make_async_copy(src, q[b], lsem.at[b]))
        mine[b].start()
    sums[:, 0:DP] = jnp.where(sec == 0, s5[...], s7[...])
    sums[:, DP : DP + 640] = jnp.where(sec == 0, s6[...], s8[...])
    pl.semaphore_wait(barrier, n + 1)
    swaps = []
    for b in range(2):
        src = packed[b].at[:, pl.ds(pl.multiple_of((1 - sec) * half, 16), half)]
        swaps.append(swap_copy(src, core_land[b], csend.at[b], crecv.at[b]))
        swaps[b].start()
    small = swap_copy(sums, sums_got, csend.at[2], crecv.at[2])
    small.start()

    def core_sum(b):
        swaps[b].wait()
        mine[b].wait()
        chunk = 96 if half % 96 == 0 else 16
        parts = half // chunk

        def body(j):
            t, r = j // parts, pl.multiple_of(lax.rem(j, parts) * chunk, 16)
            at = pl.ds(r, chunk)
            q[b][t, at] = (q[b][t, at].astype(F32) + core_land[b][t, at].astype(F32)).astype(BF16)

        loop(8 * parts, body)

    plain, swapped = orders(n)

    def run(order1, order2):
        red = [
            Reducer(q[0], land[0], ssem, rsem, ready, order1, 0),
            Reducer(q[1], land[1], ssem, rsem, ready, order2, 2 * n),
        ]
        lag = 2
        flight = [None, None]
        for step in range(2 * n + lag + 1):
            for b in range(2):
                i = step - lag * b
                if i < 0 or i > 2 * n:
                    continue
                if i == 0:
                    core_sum(b)
                elif i <= n:
                    flight[b].wait()
                    red[b].free(i - 1)
                    red[b].add(i - 1)
                else:
                    flight[b].wait()
                if i < n:
                    flight[b] = red[b].halve(i)
                elif i < 2 * n:
                    red[b].await_free(2 * n - 1 - i)
                    flight[b] = red[b].double(2 * n - 1 - i)
                if i < 2 * n:
                    flight[b].start()

    pl.when(sec == 0)(lambda: run(plain, swapped))
    pl.when(sec == 1)(lambda: run(swapped, plain))

    def finish(b):
        keep = pltpu.make_async_copy(q[b], full.at[sec], lsem.at[2])
        keep.start()
        last = swap_copy(q[1 - b], full.at[sec], csend.at[3], crecv.at[3])
        last.start()
        keep.wait()
        last.wait()

    pl.when(sec == 0)(lambda: finish(0))
    pl.when(sec == 1)(lambda: finish(1))
    small.wait()
    for lanes, a, b in ((slice(0, DP), s7, s5), (slice(DP, DP + 640), s8, s6)):
        offs[:, lanes] = jnp.where(sec == 0, a[...], b[...]) + sums_got[:, lanes]


def unpack_kernel(full, offs, one, mid_in, mid, small_in, small, pool, offset, buf, nat, sem):
    half = full.shape[2]
    copies = [
        pltpu.make_async_copy(full.at[h], buf.at[:, h * half : (h + 1) * half], sem.at[h])
        for h in range(2)
    ]
    for c in copies:
        c.start()
    v = offs[...]
    lane = lax.broadcasted_iota(jnp.int32, v.shape, 1)
    out = jnp.where(lane < 256, v, 0.0)
    for lo, hi, by in ((256, 416, -1024), (416, 736, 160), (736, 768, -704), (768, 1024, 192)):
        out = jnp.where((lane >= lo) & (lane < hi), roll_lanes(v, by), out)
    offset[...] = out[0:1, 0:1024]
    for c in copies:
        c.wait()

    def take(t, r, rows):
        return buf[t, r : r + rows].astype(F32)

    for dt in range(3):
        for dy in range(3):
            for dx in range(3):
                to = 160 * (9 * dt + 3 * dy + dx)
                for rows, r in ((128, 480 * dy + 128 * dt), (32, 480 * dy + 384 + 32 * dt)):
                    nat[to : to + rows, 0:128] = take(2 * dx, r, rows)
                    nat[to : to + rows, 128:256] = take(2 * dx + 1, r, rows)
                    tail = take(6 + dx // 2, r, rows)
                    nat[to : to + rows, 256:384] = roll_lanes(tail, 64) if dx == 1 else tail
                    to = to + rows
                r = 1440 + 128 * dy + 32 * dt
                to = 32 * (9 * dt + 3 * dy + dx)
                small[to : to + 32, :] = take(5 + dx, r, 32)

    def turn(i):
        at = pl.ds(pl.multiple_of(i * 128, 128), 128)
        mid[0:256, at] = nat[at, 0:256].T
        mid[256:320, at] = nat[at, 256:384].T[0:64]

    total = mid.shape[1]
    loop(total // 128, turn)
    at = slice(total - total % 128, total)
    mid[0:256, at] = nat[at, 0:256].T
    mid[256:320, at] = nat[at, 256:384].T[0:64]
    for r in range(0, D, 128):
        rows = min(128, D - r)
        at = slice(r, r + rows)
        mid_in[0:128, at] = take(3, 1440 + r, rows).T
        last = take(4, 1440 + r, rows).T
        mid_in[128:160, at] = last[0:32]
        small_in[:, at] = last[32:64]
    one[:, 0:128] = take(0, 1440, D)
    one[:, 128:256] = take(1, 1440, D)
    pool[...] = take(2, 1440, D)


def vmem(*shape, dtype=F32):
    return pltpu.VMEM(shape, dtype)


def call(kernel, outs, args, scratch, collective=None, smem_first=True, any_in=(), any_out=()):
    def specs(count, anywhere):
        return [
            pl.BlockSpec(memory_space=pl.ANY if i in anywhere else pltpu.VMEM)
            for i in range(count)
        ]

    in_specs = specs(len(args), any_in)
    if smem_first:
        in_specs[0] = pl.BlockSpec(memory_space=pltpu.SMEM)
    params = {"vmem_limit_bytes": VMEM_LIMIT}
    if collective is not None:
        params.update(collective_id=collective, has_side_effects=True)
    return pl.pallas_call(
        kernel,
        out_shape=[jax.ShapeDtypeStruct(shape, dtype) for shape, dtype in outs],
        in_specs=in_specs,
        out_specs=specs(len(outs), any_out),
        scratch_shapes=scratch,
        compiler_params=pltpu.CompilerParams(**params),
    )(*args)


def on_device(
    clip_input, out_grad, clip_lengths, w_one, w_mid_in, w_mid, w_small_in, w_small, w_pool, bn_offset
):
    n = lax.axis_size("dp")
    bits = n.bit_length() - 1
    half, side = clip_input.shape[1], clip_input.shape[2]
    rows = side * 16
    side2 = side // 2
    rows2 = side2 * 8
    total2 = side2 * rows2
    unit = 32 << max(bits - 3, 0)
    packed_rows = -(-(1440 + D) // unit) * unit
    x = clip_input.transpose(0, 2, 3, 1, 4).reshape(2, side * side * half, D)
    og = out_grad.transpose(0, 2, 3, 1, 4)

    def like(a, dtype=BF16):
        return pltpu.VMEM(a.shape[1:], dtype)

    def turned(w):
        return w.transpose(0, 2, 1)

    weights = (w_one, turned(w_mid_in), turned(w_small_in), w_pool, turned(w_mid), w_small)
    dma = pltpu.SemaphoreType.DMA
    grid = (side, side, 2, 8)
    xgot, zone, zin, zp, st1, wp1, wp2, wf1, wf2, ws1, ws2, beta1, beta2, og_got = call(
        start_kernel,
        [
            (x.shape[1:], BF16),
            (grid + (256,), F32),
            (grid + (256,), F32),
            ((side, rows, 128), F32),
            ((8, 640), F32),
            ((D, 640), BF16),
            ((D, 640), BF16),
            ((1536, 1024), BF16),
            ((1536, 1024), BF16),
            ((384, 384), BF16),
            ((384, 384), BF16),
            ((1, 1152), F32),
            ((1, 1152), F32),
            (og.shape[1:], BF16),
        ],
        (clip_lengths, x, og) + weights + (bn_offset,),
        [
            like(x),
            like(x),
            vmem(*grid, 256),
            vmem(*grid, 256),
            vmem(side, rows, 128),
            vmem(*grid, 128),
            vmem(side + 2, rows, 128),
        ]
        + [like(w) for w in weights] * 2
        + [
            vmem(1, 1152),
            vmem(1, 1152),
            vmem(27 * C1A, 384, dtype=BF16),
            vmem(2, D, 640, dtype=BF16),
            vmem(2, 1536, 1024, dtype=BF16),
            vmem(2, 384, 384, dtype=BF16),
            vmem(2, 2, 8, 640),
            vmem(2, 16, 640),
        ]
        + exchange_scratch(n, 640)
        + [dma((7,)), dma((10,)), dma((9,)), dma((9,))],
        collective=1,
        any_in=range(1, 9),
        any_out=(0, 1, 2, 3, 5, 6, 7, 8, 9, 10, 13),
    )
    zone = zone.reshape(side, rows, 256)
    zin = zin.reshape(side, rows, 256)
    cat, scat, zf, stf = call(
        conv_kernel,
        [
            ((side + 2, rows, 512), BF16),
            ((side + 2, rows, 128), BF16),
            ((side, rows, DP), F32),
            ((8, DP), F32),
        ],
        (clip_lengths, zin, zone, zp, st1, beta1, wf1, ws1),
        [vmem(8, 512), vmem(2, 16, 512)] + exchange_scratch(n, 512),
        collective=2,
    )
    sig, hand, asum, bsum = call(
        output_kernel,
        [((side, rows, DP), BF16)] + [((side2, side2, 8, DP), F32)] * 3,
        (clip_lengths, zf, stf, beta1),
        [vmem(side2, 16, 128)],
    )
    block_output, hg, packed2, sums5, sums6, sums7 = call(
        second_kernel,
        [
            (og.shape, BF16),
            ((side2, side2, 8, DP), F32),
            ((8, packed_rows, 128), BF16),
            ((8, DP), F32),
            ((8, 640), F32),
            ((8, DP), F32),
        ],
        (clip_lengths, hand, asum, bsum, og, og_got, wp2, wf2, ws2, beta2, beta1),
        [
            like(og),
            vmem(side2, side2, 8, D),
            vmem(2, *og.shape[1:], dtype=BF16),
            dma((2,)),
            dma(()),
            dma(()),
            vmem(total2, DP, dtype=BF16),
            vmem(side2, rows2, 256),
            vmem(side2, rows2, 128),
            vmem(side2, rows2, DP),
            vmem(8, DP),
            vmem(side2, rows2, 128),
            vmem(side2 + 2, rows2, 128),
            vmem(side2 + 2, rows2, 640),
            vmem(total2, 1536, dtype=BF16),
            vmem(total2, 384, dtype=BF16),
            vmem(side2, rows2, 1024),
            vmem(side2, rows2, 384),
            vmem(side2, rows2, DP),
            vmem(side2, rows2, 1024),
            vmem(side2, rows2, 384),
            vmem(side2, rows2, 640),
            vmem(side2, rows2, 256),
            vmem(2, 8, 640),
            vmem(8, 640),
            vmem(8, 512),
            vmem(2, 8, DP),
            vmem(1536, 1024),
            vmem(384, 384),
            vmem(DP, 640),
        ]
        + exchange_scratch(n, 640)
        + exchange_scratch(n, 512)
        + exchange_scratch(n, DP)
        + exchange_scratch(n, 640)
        + exchange_scratch(n, DP),
        collective=3,
        any_in=(4,),
        any_out=(0,),
    )
    dzc, dzs, dz1 = call(
        dz_kernel,
        [
            ((side + 2, rows, 1024), BF16),
            ((side + 2, rows, 384), BF16),
            ((2, side, rows // 2, 384), BF16),
        ],
        (clip_lengths, zf, sig, hg, stf, sums7),
        [vmem(side2, 16, 128), vmem(side, rows, 128), vmem(side + 2, rows, 128)],
    )
    packed1 = call(
        conv_grad_kernel,
        [((8, packed_rows, 128), BF16)],
        (cat, scat, dzc, dzs, beta1),
        [vmem(1536, 1024), vmem(384, 384)],
        smem_first=False,
    )[0]
    dzi, sums8 = call(
        conv_back_kernel,
        [((2, side, rows // 2, 256), BF16), ((8, 640), F32)],
        (clip_lengths, dzc, dzs, wf1, ws1, zin, st1, beta1),
        [vmem(side, rows, 256), vmem(2, 16, 640)] + exchange_scratch(n, 640),
        collective=4,
    )
    gin, packed1 = call(
        input_kernel,
        [(x.shape, BF16), ((8, packed_rows, 128), BF16)],
        (x, xgot, dz1, dzi, wp1, packed1),
        [like(x), like(x), like(x), vmem(D, 640), dma((2,)), dma(()), dma(())],
        smem_first=False,
        collective=5,
        any_in=(0, 5),
        any_out=(0,),
    )
    half_rows = packed_rows // 2
    lands = [vmem(*shape, dtype=BF16) for shape in land_shapes(8, half_rows, bits)]
    full, offs = call(
        functools.partial(reduce_kernel, bits),
        [((2, 8, half_rows, 128), BF16), ((8, DP + 640), F32)],
        (packed1, packed2, sums5, sums6, sums7, sums8),
        [vmem(8, half_rows, 128, dtype=BF16)] * 4
        + lands * 2
        + [vmem(8, DP + 640)] * 2
        + [dma((4,)), dma((4,)), dma((4 * bits,)), dma((4 * bits,)), dma((3,))]
        + [pltpu.SemaphoreType.REGULAR((2 * bits,))],
        smem_first=False,
        collective=6,
        any_in=(0, 1),
        any_out=(0,),
    )
    one, mid_in, mid, small_in, small, pool, offset = call(
        unpack_kernel,
        [
            ((D, C0), F32),
            ((C1A, D), F32),
            ((C1B, 27 * C1A), F32),
            ((C2A, D), F32),
            ((27 * C2A, C2B), F32),
            ((D, C3), F32),
            ((1, 1024), F32),
        ],
        (full, offs),
        [vmem(8, packed_rows, 128, dtype=BF16), vmem(27 * C1A, 384), dma((2,))],
        smem_first=False,
        any_in=(0,),
    )
    input_grad = gin.reshape(2, side, side, half, D).transpose(0, 3, 1, 2, 4)
    return (
        block_output.transpose(0, 3, 1, 2, 4),
        input_grad,
        one[None],
        mid_in.T[None],
        mid.T[None],
        small_in.T[None],
        small[None],
        pool[None],
        offset,
    )


def solution(mesh):
    placed = (
        P("dp", "section", None, None, None),
        P("dp", "section", None, None, None),
        P("dp", None),
        P("section", None, None),
        P("section", None, None),
        P("section", None, None),
        P("section", None, None),
        P("section", None, None),
        P("section", None, None),
        P("section", None),
    )
    return jax.shard_map(
        on_device,
        mesh=mesh,
        in_specs=placed,
        out_specs=(
            P("dp", "section", None, None, None),
            P("dp", "section", None, None, None),
            P("section", None, None),
            P("section", None, None),
            P("section", None, None),
            P("section", None, None),
            P("section", None, None),
            P("section", None, None),
            P("section", None),
        ),
        check_vma=False,
    )
```

```python
import functools

import jax
import jax.numpy as jnp
from jax import lax
from jax.experimental import pallas as pl
from jax.experimental.pallas import tpu as pltpu
from jax.sharding import PartitionSpec as P

D = 832
DP = 896
C0 = 256
C1A = 160
C1B = 320
C2A = 32
C2B = 128
C3 = 128
EPS = 0.001
MESH = pl.DeviceIdType.MESH
F32 = jnp.float32
BF16 = jnp.bfloat16
VMEM_LIMIT = 60 * 2**20


def dot(a, b):
    return jnp.dot(a, b, preferred_element_type=F32)


def dot_nt(a, b):
    return lax.dot_general(a, b, (((1,), (1,)), ((), ())), preferred_element_type=F32)


def dot_tn(a, b):
    return lax.dot_general(a, b, (((0,), (0,)), ((), ())), preferred_element_type=F32)


def roll_rows(x, by):
    return pltpu.roll(x, by % x.shape[0], 0)


def roll_lanes(x, by):
    return pltpu.roll(x, by % x.shape[1], 1)


def lane_below(x, count):
    lanes = lax.broadcasted_iota(jnp.int32, x.shape, 1)
    return jnp.where(lanes < count, x, 0.0)


class Clips:
    def __init__(self, len_ref, frames, stride):
        sec = lax.axis_index("section")
        f = lax.broadcasted_iota(jnp.int32, (frames, 128), 0)

        def label(v):
            place = v * stride
            out = jnp.zeros_like(v)
            start = jnp.int32(0)
            for c in range(len_ref.shape[1]):
                end = start + len_ref[sec, c]
                out = jnp.where((place >= start) & (place < end), c + 1, out)
                start = end
            return out

        here = label(f)
        inside = here > 0

        def mask(m):
            return jnp.where(m, 1.0, 0.0).astype(F32)

        self.frames = frames
        self.valid = mask(inside)
        self.before = mask(inside & (f > 0) & (label(f - 1) == here))
        self.after = mask(inside & (f < frames - 1) & (label(f + 1) == here))
        self.inv = 1.0 / jnp.maximum(self.valid + self.before + self.after, 1.0)

    def times(self, v, pattern):
        return (v.reshape(-1, self.frames, 128) * pattern).reshape(v.shape)

    def fold(self, v):
        return jnp.sum(v.reshape(-1, self.frames, v.shape[-1]), axis=0)


def shift_places(v, frames, by):
    lanes = v.shape[-1]
    v3 = v.reshape(-1, frames, lanes)
    zero = jnp.zeros((1, frames, lanes), v.dtype)
    if by > 0:
        v3 = jnp.concatenate([v3[1:], zero], 0)
    else:
        v3 = jnp.concatenate([zero, v3[:-1]], 0)
    return v3.reshape(v.shape)


def add_stats(clips, acc, lanes, v, w=None):
    acc[0, :, lanes] += clips.fold(v)
    acc[1, :, lanes] += clips.fold(v * (v if w is None else w))


def affine(st, lanes):
    total, square, count = st[0:1, lanes], st[1:2, lanes], st[2:3, lanes]
    mean = total / count
    scale = lax.rsqrt(square / count - mean * mean + EPS)
    return scale, mean


def soft(t):
    e = jnp.exp(-jnp.abs(t))
    r = 1.0 / (1.0 + e)
    return jnp.maximum(t, 0.0) + jnp.log(1.0 + e), jnp.where(t >= 0, r, e * r)


def sigm(t):
    e = jnp.exp(-jnp.abs(t))
    r = 1.0 / (1.0 + e)
    return jnp.where(t >= 0, r, e * r)


def greet(partner=False):
    n = lax.axis_size("dp")
    me = lax.axis_index("dp")
    barrier = pltpu.get_barrier_semaphore()

    def go(k, _):
        pl.semaphore_signal(
            barrier, inc=1, device_id={"dp": lax.rem(me + k, n)}, device_id_type=MESH
        )
        return 0

    if partner:
        other = 1 - lax.axis_index("section")
        pl.semaphore_signal(barrier, inc=1, device_id={"section": other}, device_id_type=MESH)
    lax.fori_loop(1, n, go, 0)


def greeted(partner=False):
    pl.semaphore_wait(pltpu.get_barrier_semaphore(), lax.axis_size("dp") - 1 + int(partner))


def exchange_start(loc, buf, ssem, rsem):
    n = lax.axis_size("dp")
    me = lax.axis_index("dp")

    def start(k, _):
        pltpu.make_async_remote_copy(
            src_ref=loc,
            dst_ref=buf.at[me],
            send_sem=ssem.at[k],
            recv_sem=rsem.at[me],
            device_id={"dp": lax.rem(me + k, n)},
            device_id_type=MESH,
        ).start()
        return 0

    lax.fori_loop(1, n, start, 0)
    buf[me] = loc[...]


def exchange_finish(loc, buf, ssem, rsem, out, tiles):
    n = lax.axis_size("dp")
    me = lax.axis_index("dp")

    def wait(k, _):
        j = lax.rem(me + k, n)
        copy = pltpu.make_async_remote_copy(
            src_ref=loc,
            dst_ref=buf.at[j],
            send_sem=ssem.at[k],
            recv_sem=rsem.at[j],
            device_id={"dp": j},
            device_id_type=MESH,
        )
        copy.wait_send()
        copy.wait_recv()
        return 0

    lax.fori_loop(1, n, wait, 0)
    total = jnp.sum(buf[...], axis=0)
    at = 2 * len(tiles)
    for i, t in enumerate(tiles):
        lanes = slice(128 * t, 128 * t + 128)
        out[0:1, lanes] = total[2 * i : 2 * i + 1]
        out[1:2, lanes] = total[2 * i + 1 : 2 * i + 2]
        if at < loc.shape[0]:
            out[2:3, lanes] = total[at : at + 1]


def exchange(loc, buf, ssem, rsem, out, tiles):
    exchange_start(loc, buf, ssem, rsem)
    exchange_finish(loc, buf, ssem, rsem, out, tiles)


def swap_copy(src, dst, ssem, rsem):
    return pltpu.make_async_remote_copy(
        src_ref=src,
        dst_ref=dst,
        send_sem=ssem,
        recv_sem=rsem,
        device_id={"section": 1 - lax.axis_index("section")},
        device_id_type=MESH,
    )


def exchange_scratch(n, rows):
    return [
        pltpu.VMEM((rows, 128), F32),
        pltpu.VMEM((n, rows, 128), F32),
        pltpu.SemaphoreType.DMA((n,)),
        pltpu.SemaphoreType.DMA((n,)),
    ]


FIRST, CONV, FINAL, INNER = range(5), range(4), range(7), (3, 4)


def pack_stats(clips, loc, acc, tiles, count=None):
    for i, t in enumerate(tiles):
        lanes = pl.ds(128 * t, 128)
        for k in range(2):
            loc[2 * i + k : 2 * i + k + 1, :] = jnp.sum(
                acc[k, :, lanes] * clips.valid, axis=0, keepdims=True
            )
    if count is not None:
        at = 2 * len(tiles)
        loc[at : at + 1, :] = jnp.sum(clips.valid, axis=0, keepdims=True) * float(count)


def loop(n, body):
    def step(i, _):
        body(i)
        return 0

    lax.fori_loop(0, n, step, 0)


def inv_edges(side, frames, y):
    x = lax.broadcasted_iota(jnp.int32, (side, frames, 128), 0)
    ex = jnp.where((x == 0) | (x == side - 1), 0.5, 1.0 / 3.0).astype(F32)
    ey = jnp.where((y == 0) | (y == side - 1), 0.5, 1.0 / 3.0).astype(F32)
    return (ex * ey).reshape(side * frames, 128)


def box(clips, side, load, tx, store):
    frames = clips.frames
    tx[0] = jnp.zeros(tx.shape[1:], F32)
    tx[side + 1] = jnp.zeros(tx.shape[1:], F32)

    def across(y):
        v = load(y)
        t = clips.times(v, clips.valid)
        t = t + clips.times(roll_rows(v, 1), clips.before)
        t = t + clips.times(roll_rows(v, -1), clips.after)
        tx[y + 1] = t + shift_places(t, frames, 1) + shift_places(t, frames, -1)

    def down(y):
        store(y, tx[y] + tx[y + 1] + tx[y + 2])

    loop(side, across)
    loop(side, down)


def pool_forward(clips, side, load, tx, zp, acc):
    def store(y, v):
        z = clips.times(v * inv_edges(side, clips.frames, y), clips.inv)
        zp[y] = z
        add_stats(clips, acc, pl.ds(256, 128), z)

    box(clips, side, load, tx, store)


def upright(src, dst):
    rows = src.shape[1]
    width = src.shape[0]

    def body(i):
        at = pl.ds(pl.multiple_of(i * 128, 128), 128)
        dst[at, 0:width] = src[:, at].astype(F32).T.astype(BF16)

    loop(rows // 128, body)
    if rows % 128:
        at = slice(rows - rows % 128, rows)
        dst[at, 0:width] = src[:, at].astype(F32).T.astype(BF16)


def arrange_first(src, wp, b, flip):
    one, mid_in, small_in, pool = src
    wp[b, :, 0:256] = one[...]
    wp[b, :, 256:384] = pool[...]
    upright(mid_in, flip)
    wp[b, :, 384:544] = flip[0:D, 0:C1A]
    upright(small_in, flip)
    wp[b, :, 544:576] = flip[0:D, 0:C2A]
    wp[b, :, 576:640] = jnp.zeros((D, 64), BF16)


def arrange_beta(src, dst):
    v = jnp.concatenate([jnp.broadcast_to(src[...], (8, 1024)), jnp.zeros((8, 128), F32)], 1)
    lane = lax.broadcasted_iota(jnp.int32, v.shape, 1)
    out = jnp.zeros_like(v)
    for lo, hi, by in (
        (0, 256, 0),
        (256, 576, -160),
        (576, 832, -192),
        (896, 1056, 640),
        (1056, 1088, 320),
    ):
        out = jnp.where((lane >= lo) & (lane < hi), roll_lanes(v, by), out)
    dst[...] = out[0:1]


def arrange_conv(mid_flat, small, wf, ws, b, mid):
    upright(mid_flat, mid)
    for dy in range(3):
        wf[b, 512 * dy + 480 : 512 * dy + 512, :] = jnp.zeros((32, 1024), BF16)
        ws[b, 128 * dy + 96 : 128 * dy + 128, :] = jnp.zeros((32, 384), BF16)
        wf[b, 512 * dy : 512 * dy + 512, 960:1024] = jnp.zeros((512, 64), BF16)
        for dt in range(3):
            for dx in range(3):
                r = 96 * (3 * dt + dy) + 32 * dx
                to = 128 * dy + 32 * dt
                ws[b, to : to + 32, 128 * dx : 128 * dx + 128] = small[r : r + 32, :]
            for dx in range(3):
                r = 480 * (3 * dt + dy) + 160 * dx
                for rows, to in ((128, 128 * dt), (32, 384 + 32 * dt)):
                    to = to + 512 * dy
                    wf[b, to : to + rows, 256 * dx : 256 * dx + 256] = mid[r : r + rows, 0:256]
                    wf[b, to : to + rows, 768 + 64 * dx : 832 + 64 * dx] = mid[
                        r : r + rows, 256:320
                    ]
                    r = r + rows


def start_kernel(
    len_ref, x, og, w_one, w_mid_in, w_small_in, w_pool, w_mid, w_small, bn,
    xgot_out, zone_out, zin_out, zp_out, st, wp1, wp2, wf1, wf2, ws1, ws2, beta1, beta2, og_got,
    x_own, x_got, zone, zin, zp, yp, tx,
    own_one, own_mid_in, own_small_in, own_pool, own_mid, own_small,
    beta, got_beta, flip,
    wp, wf, ws, hacc, acc, loc, buf, ssem, rsem, lsem, osem, psem, qsem,
):
    greet(partner=True)
    sec = lax.axis_index("section")
    side = zone.shape[0]
    clips = Clips(len_ref, 16, 1)
    raw = (w_one, w_mid_in, w_small_in, w_pool, w_mid, w_small)
    own = (own_one, own_mid_in, own_small_in, own_pool, own_mid, own_small)
    local = [pltpu.make_async_copy(x.at[sec], x_own, lsem.at[0])]
    local += [
        pltpu.make_async_copy(a.at[0], b, lsem.at[i + 1]) for i, (a, b) in enumerate(zip(raw, own))
    ]
    for c in local:
        c.start()
    hacc[...] = jnp.zeros_like(hacc)
    acc[...] = jnp.zeros_like(acc)
    loc[...] = jnp.zeros_like(loc)
    arrange_beta(bn, beta)
    for c in local[1:5]:
        c.wait()
    arrange_first(own[:4], wp, sec, flip)
    greeted(partner=True)
    pairs = ((wp.at[sec], wp.at[sec]), (beta, got_beta), (x.at[1 - sec], x_got))
    pairs += ((og.at[1 - sec], og_got), (wf.at[sec], wf.at[sec]), (ws.at[sec], ws.at[sec]))
    remote = [swap_copy(a, b, psem.at[i], qsem.at[i]) for i, (a, b) in enumerate(pairs)]
    for c in remote[:4]:
        c.start()
    for c in local[5:]:
        c.wait()
    arrange_conv(own_mid, own_small, wf, ws, sec, flip)
    for c in remote[4:]:
        c.start()
    for c in remote[:2]:
        c.wait()
    beta1[...] = jnp.where(sec == 0, beta[...], got_beta[...])
    beta2[...] = jnp.where(sec == 0, got_beta[...], beta[...])
    ny = side // 2
    rows = ny * side * 8
    outs = []

    def put(src, dst):
        c = pltpu.make_async_copy(src, dst, osem.at[len(outs)])
        c.start()
        outs.append(c)

    for part, src in enumerate((x_own, x_got)):
        (local[0] if part == 0 else remote[2]).wait()
        half = sec if part == 0 else 1 - sec

        def body(i, src=src, half=half):
            here = pl.ds(i * ny, ny)
            y = dot(src[pl.ds(pl.multiple_of(i * rows, 16), rows)], wp[0])

            def place(lo, hi):
                return y[:, lo:hi].reshape(ny, side, 8, hi - lo)

            zone[here, :, half] = place(0, 256)
            yp[here, :, half] = place(256, 384)
            zin[here, :, half] = place(384, 640)
            for lo, hi in ((0, 256), (384, 640)):
                v = y[:, lo:hi].reshape(-1, 8, 256)
                hacc[0, half, :, lo:hi] += jnp.sum(v, axis=0)
                hacc[1, half, :, lo:hi] += jnp.sum(v * v, axis=0)

        loop(2, body)
    put(x_got, xgot_out)
    put(zin, zin_out)
    put(zone, zone_out)
    acc[...] = hacc[...].reshape(acc.shape)
    pool_forward(clips, side, lambda y: yp[y].reshape(side * 16, 128), tx, zp, acc)
    put(zp, zp_out)
    pack_stats(clips, loc, acc, FIRST, side * side)
    exchange_start(loc, buf, ssem, rsem)
    for c in remote[3:]:
        c.wait()
    for a, b in ((wf, (wf1, wf2)), (ws, (ws1, ws2)), (wp, (wp1, wp2))):
        for i in range(2):
            put(a.at[i], b[i])
    exchange_finish(loc, buf, ssem, rsem, st, FIRST)
    for c in outs:
        c.wait()


def inner_tiles(clips, z, st, beta):
    tiles = []
    for t in range(2):
        scale, mean = affine(st, pl.ds(384 + 128 * t, 128))
        b = beta[0:1, pl.ds(896 + 128 * t, 128)]
        act, _ = soft(z[:, 128 * t : 128 * (t + 1)] * scale + (b - mean * scale))
        tiles.append(clips.times(act, clips.valid))
    return tiles


def tap_tiles(clips, a, b):
    def before(v):
        return clips.times(roll_rows(v, 1), clips.before)

    def after(v):
        return clips.times(roll_rows(v, -1), clips.after)

    lane = lax.broadcasted_iota(jnp.int32, b.shape, 1)
    ones = clips.times(jnp.where(lane == 96, 1.0, 0.0).astype(F32), clips.valid)

    def three32(v):
        return before(v) + roll_lanes(v, 32) + roll_lanes(after(v), 64) + ones

    tail = lane_below(b, 32)
    small = lane_below(roll_lanes(b, -32), 32)
    return [before(a), a, after(a), three32(tail)], three32(small)


def untap(clips, parts, small):
    def before(v):
        return roll_rows(clips.times(v, clips.before), -1)

    def after(v):
        return roll_rows(clips.times(v, clips.after), 1)

    def back32(v):
        return (
            lane_below(before(v), 32)
            + lane_below(roll_lanes(v, -32), 32)
            + lane_below(roll_lanes(after(v), -64), 32)
        )

    a = before(parts[0]) + parts[1] + after(parts[2])
    return a, back32(parts[3]) + roll_lanes(back32(small), 32)


def typical(beta):
    sp, sg = soft(jnp.broadcast_to(beta, (8, beta.shape[-1])))
    return sp + 0.5 * sg * (1.0 - sg)


def outer(c, s):
    k = lax.broadcasted_iota(jnp.int32, c.shape, 0)
    c = jnp.where(k < 2, c, 0.0).astype(BF16)
    s = jnp.broadcast_to(s, (8, s.shape[-1]))
    high = s.astype(BF16).astype(F32)
    k = lax.broadcasted_iota(jnp.int32, s.shape, 0)
    s = jnp.where(k == 0, high, jnp.where(k == 1, s - high, 0.0)).astype(BF16)
    return dot_tn(c, s)


def tap_points(beta):
    a = typical(beta[0:1, 896:1024])
    b = typical(beta[0:1, 1024:1152])

    def three(v):
        return v + roll_lanes(v, 32) + roll_lanes(v, 64)

    tail = three(lane_below(b, 32))
    small = three(lane_below(roll_lanes(b, -32), 32))
    return jnp.concatenate([a, a, a, tail], 1), small


def centre_mid(grad, beta):
    c, _ = tap_points(beta)
    row = jnp.broadcast_to(grad[992:993, :], (8, 1024))
    main = row[:, 256:512]
    tail = lane_below(roll_lanes(row[:, 768:896], 64), 64)
    s = jnp.concatenate([main, main, main, tail + roll_lanes(tail, 64), tail], 1)
    return outer(c, s)


def centre_small(grad, beta):
    _, c = tap_points(beta)
    row = jnp.broadcast_to(grad[224:225, 128:256], (8, 128))
    return outer(c, jnp.concatenate([row, row, row], 1))


def conv_gather(frames, p, s):
    def three(at):
        return (
            shift_places(at(0), frames, -1) + at(1) + shift_places(at(2), frames, 1)
        )

    main = three(lambda k: p[:, 256 * k : 256 * k + 256])
    small = three(lambda k: s[:, 128 * k : 128 * k + 128])
    ends = p[:, 768:896]
    tail = three(lambda k: (ends, roll_lanes(ends, 64), p[:, 896:1024])[k])
    return main, small, lane_below(tail, 64)


def spread_x(frames, v, by):
    return v if by == 0 else shift_places(v, frames, -by)


def put_spread(frames, main, small, tail, put_mid, put_small):
    for k in range(3):
        put_mid(256 * k, spread_x(frames, main, k - 1))
        put_small(128 * k, spread_x(frames, small, k - 1))
    put_mid(768, spread_x(frames, tail, -1) + roll_lanes(tail, 64))
    put_mid(896, spread_x(frames, tail, 1))


def join_final(small, tail, pool):
    s, p = roll_lanes(small, 64), roll_lanes(pool, 64)
    low = lax.broadcasted_iota(jnp.int32, small.shape, 1) < 64
    return jnp.where(low, tail, s), jnp.where(low, s, p), jnp.where(low, p, 0.0)


def split_final(t4, t5, t6):
    a, b, c = roll_lanes(t4, 64), roll_lanes(t5, 64), roll_lanes(t6, 64)
    low = lax.broadcasted_iota(jnp.int32, t4.shape, 1) < 64
    return jnp.where(low, a, b), jnp.where(low, t4, 0.0), jnp.where(low, b, c)


def final_stats(st1, st2, stf):
    stf[:, 0:256] = st1[:, 0:256]
    stf[:, 256:512] = st2[:, 0:256]
    for t, v in enumerate(join_final(st2[:, 256:384], st2[:, 384:512], st1[:, 256:384])):
        stf[:, 512 + 128 * t : 640 + 128 * t] = v
    stf[2:3, :] = jnp.broadcast_to(st1[2:3, 0:1], (1, DP))


def store_conv(clips, y, p, s, zp, zf, acc):
    main, small, tail = conv_gather(clips.frames, p, s)
    zf[y, :, 256:512] = main
    for t, v in enumerate(join_final(small, tail, zp[y])):
        zf[y, :, 512 + 128 * t : 640 + 128 * t] = v
    add_stats(clips, acc, pl.ds(0, 256), main)
    add_stats(clips, acc, pl.ds(256, 128), small)
    add_stats(clips, acc, pl.ds(384, 128), tail)


def conv_kernel(
    len_ref, zin, zone, zp, st1, beta, wf, ws, cat, scat, zf, stf, st2, acc, loc, buf, ssem, rsem
):
    greet()
    side, rows = zin.shape[0], zin.shape[1]
    clips = Clips(len_ref, 16, 1)
    acc[...] = jnp.zeros_like(acc)
    loc[...] = jnp.zeros_like(loc)
    for y in (0, side + 1):
        cat[y] = jnp.zeros(cat.shape[1:], BF16)
        scat[y] = jnp.zeros(scat.shape[1:], BF16)

    def build(y):
        a, b = inner_tiles(clips, zin[y], st1, beta)
        parts, small = tap_tiles(clips, a, b)
        for i, part in enumerate(parts):
            cat[y + 1, :, 128 * i : 128 * i + 128] = part.astype(BF16)
        scat[y + 1] = small.astype(BF16)

    loop(side, build)
    ny = 2

    def products(i):
        y0 = i * ny

        def taps(ref):
            return jnp.concatenate(
                [ref[pl.ds(y0 + dy, ny)].reshape(ny * rows, ref.shape[-1]) for dy in range(3)], axis=1
            )

        p = dot(taps(cat), wf[...])
        s = dot(taps(scat), ws[...])
        for q in range(ny):
            here = slice(q * rows, (q + 1) * rows)
            store_conv(clips, y0 + q, p[here], s[here], zp, zf, acc)

    loop(side // ny, products)
    pack_stats(clips, loc, acc, CONV)
    greeted()
    exchange_start(loc, buf, ssem, rsem)

    def move(y):
        zf[y, :, 0:256] = zone[y]

    loop(side, move)
    exchange_finish(loc, buf, ssem, rsem, st2, CONV)
    final_stats(st1, st2, stf)


def output_kernel(len_ref, zf, stf, beta, sig, hand, asum, bsum, scr):
    side = zf.shape[0]
    half = side // 2
    clips = Clips(len_ref, 16, 1)

    def body(k):
        for t in range(7):
            lanes = pl.ds(128 * t, 128)
            scale, mean = affine(stf, lanes)
            b = beta[0:1, lanes]
            pooled = None
            for q in range(2):
                u = (zf[2 * k + q, :, lanes] - mean) * scale
                sp, sg = soft(u + b)
                sp, sg = clips.times(sp, clips.valid), clips.times(sg, clips.valid)
                if t == 6:
                    lane = lax.broadcasted_iota(jnp.int32, sp.shape, 1)
                    one = clips.times(jnp.ones_like(sp), clips.valid)
                    sp = jnp.where(lane == 127, one, lane_below(sp, 64))
                    sg = lane_below(sg, 64)
                sig[2 * k + q, :, lanes] = sg.astype(BF16)
                three = [
                    jnp.sum(v.reshape(half, 2, 16, 128), axis=1) for v in (sp, sg, sg * u)
                ]
                pooled = three if pooled is None else [x + y for x, y in zip(pooled, three)]
            for v, dst in zip(pooled, (hand, asum, bsum)):
                scr[...] = v
                dst[k, :, :, lanes] = (
                    scr[:, pl.ds(0, 8, stride=2), :] + scr[:, pl.ds(1, 8, stride=2), :]
                ) * 0.125

    loop(half, body)


def second_kernel(
    len_ref, hand, asum, bsum, og, og_got, wp, wf, ws, beta, beta1,
    block_out, hg, packed_a, packed_b, sums5, sums6, sums7,
    gown, grad, out, lsem, psem, qsem,
    hbuf, zin, zp, zf, stf, yp, tx, catf, cat, scat, pbuf, sbuf, dbuf, dzc, dzs, dz1, din,
    acc, st3, st4, acc7, accm, accs, accp,
    loc3, buf3, ss3, rs3, loc4, buf4, ss4, rs4, loc5, buf5, ss5, rs5,
    loc6, buf6, ss6, rs6, loc7, buf7, ss7, rs7,
):
    greet(partner=True)
    sec = lax.axis_index("section")
    own = pltpu.make_async_copy(og.at[sec], gown, lsem.at[0])
    own.start()
    side = hand.shape[0]
    rows = side * 8
    total = side * rows
    clips = Clips(len_ref, 8, 2)
    for ref in (acc, acc7, loc3, loc4, loc5, loc6, loc7):
        ref[...] = jnp.zeros_like(ref)

    hbuf[...] = hand[...].reshape(total, DP).astype(BF16)
    y = dot(hbuf[:, 0:D], wp[...])
    zf[:, :, 0:C0] = y[:, 0:C0].reshape(side, rows, C0)
    yp[...] = y[:, 256:384].reshape(side, rows, 128)
    zin[...] = y[:, 384:640].reshape(side, rows, 256)

    def first_sums(y):
        add_stats(clips, acc, pl.ds(0, 256), zf[y, :, 0:256])
        add_stats(clips, acc, pl.ds(384, 256), zin[y])

    loop(side, first_sums)
    pool_forward(clips, side, lambda y: yp[y], tx, zp, acc)
    pack_stats(clips, loc3, acc, FIRST, side * side)
    greeted(partner=True)
    exchange_start(loc3, buf3, ss3, rs3)
    own.wait()
    mine, theirs = gown[...].astype(F32), og_got[...].astype(F32)
    low = jnp.where(sec == 0, mine, theirs)
    high = jnp.where(sec == 0, theirs, mine)
    grad[...] = jnp.concatenate([low, high], 2)
    exchange_finish(loc3, buf3, ss3, rs3, st3, FIRST)

    catf[0] = jnp.zeros(catf.shape[1:], F32)
    catf[side + 1] = jnp.zeros(catf.shape[1:], F32)

    def build(y):
        a, b = inner_tiles(clips, zin[y], st3, beta)
        parts, small = tap_tiles(clips, a, b)
        for t, v in enumerate(parts + [small]):
            catf[y + 1, :, 128 * t : 128 * t + 128] = v

    loop(side, build)
    for dy in range(3):
        v = catf[dy : dy + side].reshape(total, 640).astype(BF16)
        cat[:, 512 * dy : 512 * dy + 512] = v[:, 0:512]
        scat[:, 128 * dy : 128 * dy + 128] = v[:, 512:640]
    pbuf[...] = dot(cat[...], wf[...]).reshape(side, rows, 1024)
    sbuf[...] = dot(scat[...], ws[...]).reshape(side, rows, 384)
    acc[...] = jnp.zeros_like(acc)
    loop(side, lambda y: store_conv(clips, y, pbuf[y], sbuf[y], zp, zf, acc))
    pack_stats(clips, loc4, acc, CONV)
    exchange(loc4, buf4, ss4, rs4, st4, CONV)
    final_stats(st3, st4, stf)

    def emit(y):
        for t in range(7):
            lanes = pl.ds(128 * t, 128)
            scale, mean = affine(stf, lanes)
            u = (zf[y, :, lanes] - mean) * scale
            sp, sg = soft(u + beta[0:1, lanes])
            width = 128 if t < 6 else 64
            gr = grad[y, :, :, 128 * t : 128 * t + width].reshape(rows, width)
            if t == 6:
                gr = jnp.concatenate([gr, jnp.zeros((rows, 64), F32)], 1)
            d = gr * clips.times(sg, clips.valid)
            dbuf[y, :, lanes] = d
            add_stats(clips, acc7, lanes, d, u)
            sp = clips.times(sp, clips.valid).reshape(side, 8, 128)[:, :, 0:width]
            for h in range(2):
                out[h, y, :, :, 128 * t : 128 * t + width] = sp[:, 4 * h : 4 * h + 4].astype(BF16)

    loop(side, emit)
    mine = pltpu.make_async_copy(out.at[sec], block_out.at[sec], lsem.at[1])
    mine.start()
    theirs = swap_copy(out.at[1 - sec], block_out.at[sec], psem, qsem)
    theirs.start()
    pack_stats(clips, loc5, acc7, FINAL)
    exchange(loc5, buf5, ss5, rs5, sums5, FINAL)
    count = st3[2:3, 0:128]

    def dz_of(y, t):
        lanes = pl.ds(128 * t, 128)
        scale, mean = affine(stf, lanes)
        u = (zf[y, :, lanes] - mean) * scale
        m1, m2 = sums5[0:1, lanes] / count, sums5[1:2, lanes] / count
        return clips.times((dbuf[y, :, lanes] - m1 - u * m2) * scale, clips.valid)

    def dz_final(y):
        for t in range(2):
            dz1[y, :, 128 * t : 128 * t + 128] = dz_of(y, t)
        main = jnp.concatenate([dz_of(y, 2), dz_of(y, 3)], 1)
        small, tail, pool = split_final(*(dz_of(y, t) for t in (4, 5, 6)))
        yp[y] = clips.times(pool * inv_edges(side, 8, y), clips.inv)

        def put(ref):
            def go(lane, v):
                ref[y, :, lane : lane + v.shape[-1]] = v

            return go

        put_spread(8, main, small, tail, put(dzc), put(dzs))

    loop(side, dz_final)

    def boxed(y, v):
        dz1[y, :, 256:384] = clips.times(v, clips.valid)

    box(clips, side, lambda y: yp[y], tx, boxed)
    dzc_b = dzc[...].reshape(total, 1024).astype(BF16)
    dzs_b = dzs[...].reshape(total, 384).astype(BF16)
    for dy in (-1, 0, 1):
        k = dy + 1
        q = dot_nt(dzc_b, wf[512 * k : 512 * k + 512]).reshape(side, rows, 512)
        r = dot_nt(dzs_b, ws[128 * k : 128 * k + 128]).reshape(side, rows, 128)
        if k == 0:
            catf[1 : side + 1] = jnp.zeros((side, rows, 640), F32)
        catf[1 + dy : 1 + dy + side, :, 0:512] += q
        catf[1 + dy : 1 + dy + side, :, 512:640] += r
    acc[...] = jnp.zeros_like(acc)

    def inner_back(y):
        parts = [catf[y + 1, :, 128 * t : 128 * t + 128] for t in range(5)]
        inner_up(clips, zin[y], untap(clips, parts[:4], parts[4]), st3, beta, acc, din, y)

    loop(side, inner_back)
    pack_stats(clips, loc6, acc, INNER)
    exchange_start(loc6, buf6, ss6, rs6)
    accm[...] = dot_tn(cat[...], dzc_b)
    exchange_finish(loc6, buf6, ss6, rs6, sums6, INNER)

    def dz_inner(y):
        for t in range(2):
            dz1[y, :, 384 + 128 * t : 512 + 128 * t] = inner_dz(
                clips, t, zin[y], din[y], st3, sums6, count
            )

    loop(side, dz_inner)
    dz1_b = dz1[...].reshape(total, 640).astype(BF16)
    hgv = dot_nt(dz1_b, wp[...]).astype(BF16).astype(F32)
    hg[:, :, :, 0:D] = hgv.reshape(side, side, 8, D)
    hg[:, :, :, D:DP] = jnp.zeros((side, side, 8, DP - D), F32)
    acc7[...] = jnp.zeros_like(acc7)

    def upstream(y):
        for t in range(7):
            lanes = pl.ds(128 * t, 128)
            gr = hg[y, :, :, lanes]
            acc7[0, :, lanes] += jnp.sum(gr * asum[y, :, :, lanes], axis=0)
            acc7[1, :, lanes] += jnp.sum(gr * bsum[y, :, :, lanes], axis=0)

    loop(side, upstream)
    pack_stats(clips, loc7, acc7, FINAL)
    exchange_start(loc7, buf7, ss7, rs7)
    accs[...] = dot_tn(scat[...], dzs_b)
    accp[...] = dot_tn(hbuf[...], dz1_b)
    pool = dz1[:, :, 256:384].reshape(total, 128)
    rest = (pool - dz1_b[:, 256:384].astype(F32)).astype(BF16)
    accp[:, 256:384] += dot_tn(hbuf[...], rest)
    c = jnp.concatenate([typical(beta1[0:1, 0:D]), jnp.zeros((8, DP - D), F32)], 1)
    full = accp[...] - outer(c, accp[DP - 1 : DP, :])
    pack_mid(packed_a, accm, beta)
    pack_first(packed_b, lambda t: full[0:D, 128 * t : 128 * t + 128], accs, beta)
    exchange_finish(loc7, buf7, ss7, rs7, sums7, FINAL)
    mine.wait()
    theirs.wait()


def pack_mid(packed, acc, beta):
    mid = centre_mid(acc, beta)
    end = packed.shape[1]
    for t in range(8):
        lanes = slice(128 * t, 128 * t + 128)
        for k in range(3):
            packed[t, 480 * k : 480 * k + 480] = (
                acc[512 * k : 512 * k + 480, lanes] - mid[0:480, lanes]
            ).astype(BF16)
        if end > 1440:
            packed[t, 1440:end] = jnp.zeros((end - 1440, 128), BF16)


def pack_first(packed, first, acc, beta):
    small = centre_small(acc, beta)
    end = packed.shape[1]
    for t in range(8):
        if t < 5:
            packed[t, 0:D] = first(t).astype(BF16)
        else:
            lanes = slice(128 * (t - 5), 128 * (t - 5) + 128)
            for k in range(3):
                packed[t, 128 * k : 128 * k + 128] = (
                    acc[128 * k : 128 * k + 128, lanes] - small[:, lanes]
                ).astype(BF16)
            packed[t, 384:D] = jnp.zeros((D - 384, 128), BF16)
        if end > D:
            packed[t, D:end] = jnp.zeros((end - D, 128), BF16)


def inner_up(clips, z, backs, st, beta, acc, din, y):
    for t in range(2):
        lanes = pl.ds(384 + 128 * t, 128)
        scale, mean = affine(st, lanes)
        u = (z[:, 128 * t : 128 * t + 128] - mean) * scale
        d = backs[t] * clips.times(sigm(u + beta[0:1, pl.ds(896 + 128 * t, 128)]), clips.valid)
        din[y, :, 128 * t : 128 * t + 128] = d
        add_stats(clips, acc, lanes, d, u)


def inner_dz(clips, t, z, d, st, sums, count):
    lanes = pl.ds(384 + 128 * t, 128)
    here = slice(128 * t, 128 * t + 128)
    scale, mean = affine(st, lanes)
    u = (z[:, here] - mean) * scale
    m1, m2 = sums[0:1, lanes] / count, sums[1:2, lanes] / count
    dz = clips.times((d[:, here] - m1 - u * m2) * scale, clips.valid)
    return lane_below(dz, 64) if t == 1 else dz


def put_halves(ref, y, lane, v):
    side, lanes = v.shape[0] // 16, v.shape[1]
    v = v.reshape(side, 2, 8, lanes)
    for h in range(2):
        ref[h, y, :, lane : lane + lanes] = v[:, h].reshape(side * 8, lanes).astype(BF16)


def backward_kernel(
    bits, len_ref, hg, stf, sums7, st1, beta, sums5, sums6,
    zf, sig, zin_in, wf_in, ws_in, wp_in, cat_in, scat_in, x, x_got, packed2a, packed2b,
    gin, full_a, full_b, offs,
    zin, wf, ws, wp, dzc, dzs, dz1, dzi, sums8, snd, got,
    p1a, p1b, q2a, q2b, core_a1, core_b1, core_a2, core_b2,
    acc, loc, buf, ss8, rs8, lsem, csend, crecv, ssem, rsem, gsend, grecv, ready, *lands,
):
    greet(partner=True)
    sec = lax.axis_index("section")
    side = dz1.shape[1]
    half = side // 2
    rows = side * 16
    clips = Clips(len_ref, 16, 1)
    count = stf[2:3, 0:128]
    loads = [
        pltpu.make_async_copy(a, b, lsem.at[i])
        for i, (a, b) in enumerate(((zin_in, zin), (wf_in, wf), (ws_in, ws), (wp_in, wp)))
    ]
    for i, (a, b) in enumerate(((packed2a, q2a), (packed2b, q2b))):
        h = b.shape[1]
        src = a.at[:, pl.ds(pl.multiple_of(sec * h, 16), h)]
        loads.append(pltpu.make_async_copy(src, b, lsem.at[4 + i]))
    for c in loads:
        c.start()

    def reducer(i, q, base_row, half_rows, swap_src, core_land, flip, load):
        return Reducer(
            bits, i, q, base_row, half_rows, swap_src, core_land, lands[bits * i : bits * i + bits],
            csend, crecv, ssem, rsem, ready, flip, load,
        )

    def part(ref, half_rows, which):
        return ref.at[:, pl.ds(pl.multiple_of(which * half_rows, 16), half_rows)]

    ha, hb = q2a.shape[1], q2b.shape[1]
    a2 = reducer(0, q2a, 0, ha, part(packed2a, ha, 1 - sec), core_a2, 1 - sec, loads[4])
    b2 = reducer(1, q2b, 0, hb, part(packed2b, hb, 1 - sec), core_b2, 1 - sec, loads[5])
    a1 = reducer(2, p1a, sec * ha, ha, part(p1a, ha, 1 - sec), core_a1, sec, None)
    b1 = reducer(3, p1b, sec * hb, hb, part(p1b, hb, 1 - sec), core_b1, sec, None)

    acc[...] = jnp.zeros_like(acc)
    loc[...] = jnp.zeros_like(loc)
    for y in (0, side + 1):
        dzc[y] = jnp.zeros(dzc.shape[1:], BF16)
        dzs[y] = jnp.zeros(dzs.shape[1:], BF16)

    def dz_phase(zb, sb, scr, yp, tx, zsem):
        def fetch(k, slot):
            here = pl.ds(2 * k, 2)
            return (
                pltpu.make_async_copy(zf.at[here], zb.at[slot], zsem.at[0, slot]),
                pltpu.make_async_copy(sig.at[here], sb.at[slot], zsem.at[1, slot]),
            )

        for c in fetch(0, 0):
            c.start()

        def body(k):
            slot = lax.rem(k, 2)

            @pl.when(k < half - 1)
            def _():
                for c in fetch(k + 1, 1 - slot):
                    c.start()

            @pl.when(k == 1)
            def _():
                greeted(partner=True)
                a2.point(0)
                b2.point(0)

            pl.when(k == 4)(lambda: a2.point(1))
            pl.when(k == 5)(lambda: b2.point(1))
            for c in fetch(k, slot):
                c.wait()
            tiles = ([], [])
            for t in range(7):
                lanes = pl.ds(128 * t, 128)
                scale, mean = affine(stf, lanes)
                m1, m2 = sums7[0:1, lanes] / count, sums7[1:2, lanes] / count
                gr = hg[k, :, :, lanes] * 0.125
                scr[:, pl.ds(0, 8, stride=2), :] = gr
                scr[:, pl.ds(1, 8, stride=2), :] = gr
                gr = scr[...]
                gr = jnp.broadcast_to(gr[:, None], (half, 2, 16, 128)).reshape(rows, 128)
                for q in range(2):
                    u = (zb[slot, q, :, lanes] - mean) * scale
                    d = gr * sb[slot, q, :, lanes].astype(F32)
                    dz = clips.times((d - m1 - u * m2) * scale, clips.valid)
                    if t < 2:
                        put_halves(dz1, 2 * k + q, 128 * t, dz)
                    else:
                        tiles[q].append(dz)
            for q in range(2):
                y = 2 * k + q
                small, tail, pool = split_final(*tiles[q][2:])
                yp[y] = clips.times(pool * inv_edges(side, 16, y), clips.inv)

                def put(ref, y=y):
                    def go(lane, v):
                        ref[y + 1, :, lane : lane + v.shape[-1]] = v.astype(BF16)

                    return go

                put_spread(
                    16, jnp.concatenate(tiles[q][:2], 1), small, tail, put(dzc), put(dzs)
                )

        loop(half, body)

        def boxed(y, v):
            put_halves(dz1, y, 256, clips.times(v, clips.valid))

        box(clips, side, lambda y: yp[y], tx, boxed)

    pl.run_scoped(
        dz_phase,
        vmem(2, 2, rows, DP),
        vmem(2, 2, rows, DP, dtype=BF16),
        vmem(half, 16, 128),
        vmem(side, rows, 128),
        vmem(side + 2, rows, 128),
        pltpu.SemaphoreType.DMA((2, 2)),
    )

    def grad_phase(cat, scat, accm, accs, sems):
        copies = [
            pltpu.make_async_copy(cat_in, cat, sems.at[0]),
            pltpu.make_async_copy(scat_in, scat, sems.at[1]),
        ]
        for c in copies:
            c.start()
        a2.point(2)
        accm[...] = jnp.zeros_like(accm)
        accs[...] = jnp.zeros_like(accs)
        for c in copies:
            c.wait()
        ny = 2

        def body(i):
            y0 = i * ny + 1

            def take(ref, y):
                return ref[pl.ds(y, ny)].reshape(ny * rows, ref.shape[-1])

            pl.when(i == 1)(lambda: b2.point(2))
            pl.when(i == 2)(lambda: a2.point(3))
            pl.when(i == 3)(lambda: b2.point(3))
            pl.when(i == 5)(lambda: a2.point(4))
            pl.when(i == 6)(lambda: b2.point(4))
            a, s = take(cat, y0), take(scat, y0)
            for dy in (-1, 0, 1):
                k = dy + 1
                accm[512 * k : 512 * k + 512] += dot_tn(a, take(dzc, y0 - dy))
                accs[128 * k : 128 * k + 128] += dot_tn(s, take(dzs, y0 - dy))

        loop(side // ny, body)
        pack_mid(p1a, accm, beta)
        a1.point(0)
        pack_first(p1b, lambda t: jnp.zeros((D, 128), F32), accs, beta)

    pl.run_scoped(
        grad_phase,
        vmem(side + 2, rows, 512, dtype=BF16),
        vmem(side + 2, rows, 128, dtype=BF16),
        vmem(1536, 1024),
        vmem(384, 384),
        pltpu.SemaphoreType.DMA((2,)),
    )

    def last_phase(din, x0, x1, ring, accp, sems):
        own = pltpu.make_async_copy(x.at[sec], x0, sems.at[0])
        other = pltpu.make_async_copy(x_got, x1, sems.at[1])
        own.start()
        other.start()
        for c in loads[:4]:
            c.wait()
        a2.point(5)
        ny = 2

        def body(i):
            y0 = i * ny + 1
            pl.when(i == 1)(lambda: b2.point(5))
            pl.when(i == 2)(lambda: a1.point(1))
            pl.when(i == 3)(lambda: a2.point(6))
            pl.when(i == 4)(lambda: b2.point(6))
            pl.when(i == 6)(lambda: a2.point(7))
            q = s = None
            for dy in (-1, 0, 1):
                k = dy + 1
                here = pl.ds(y0 - dy, ny)
                t = dot_nt(dzc[here].reshape(ny * rows, 1024), wf[512 * k : 512 * k + 512])
                q = t if q is None else q + t
                t = dot_nt(dzs[here].reshape(ny * rows, 384), ws[128 * k : 128 * k + 128])
                s = t if s is None else s + t
            for j in range(ny):
                y = i * ny + j
                here = slice(j * rows, (j + 1) * rows)
                parts = [q[here, 128 * t : 128 * t + 128] for t in range(4)]
                inner_up(clips, zin[y], untap(clips, parts, s[here]), st1, beta, acc, din, y)

        loop(side // ny, body)
        pack_stats(clips, loc, acc, INNER)
        exchange_start(loc, buf, ss8, rs8)
        a1.point(2)
        b2.point(7)
        other.wait()
        own.wait()
        sides = ((x1, 1 - sec), (x0, sec))
        step = 7
        size = step * side * 8

        def outer_first(d_ref, lanes):
            accp[:, lanes] = jnp.zeros((D, lanes.stop - lanes.start), F32)
            for src, which in sides:

                def body(i, src=src, which=which):
                    at = pl.ds(pl.multiple_of(i * size, 16), size)
                    d = d_ref[which, pl.ds(i * step, step)].reshape(size, d_ref.shape[-1])
                    accp[:, lanes] += dot_tn(src[at], d)

                loop(side // step, body)

        outer_first(dz1, slice(0, 384))
        a2.point(8)
        exchange_finish(loc, buf, ss8, rs8, sums8, INNER)

        def dz(y):
            for t in range(2):
                put_halves(dzi, y, 128 * t, inner_dz(clips, t, zin[y], din[y], st1, sums8, count))

        loop(side, dz)
        a1.point(3)
        outer_first(dzi, slice(384, 640))
        for t in range(5):
            p1b[t, 0:D] = accp[:, 128 * t : 128 * t + 128].astype(BF16)
        b1.point(0)
        b2.point(8)
        sent = []
        ticks = (
            lambda: (a1.point(4), b1.point(1)),
            lambda: (a1.point(5), b1.point(2)),
            lambda: (b1.point(3),),
            lambda: (a1.point(6), b1.point(4)),
        )
        for p in range(4):
            src, which = sides[p // 2]
            i = p % 2
            slot = p % 2
            here = pl.ds(i * step, step)
            if p >= 2:
                sent[p - 2].wait()
            d = jnp.concatenate([dz1[which, here], dzi[which, here]], -1).reshape(size, 640)
            ring[slot] = dot_nt(d, wp[...]).astype(BF16)
            to = gin.at[sec, i * size : (i + 1) * size]
            if p < 2:
                c = swap_copy(ring.at[slot], to, gsend.at[i], grecv.at[i])
            else:
                c = pltpu.make_async_copy(ring.at[slot], to, sems.at[2 + i])
            c.start()
            sent.append(c)
            ticks[p]()
        sent[2].wait()
        sent[3].wait()

    dma = pltpu.SemaphoreType.DMA
    pl.run_scoped(
        last_phase,
        vmem(side, rows, 256),
        vmem(side * side * 8, D, dtype=BF16),
        vmem(side * side * 8, D, dtype=BF16),
        vmem(2, 7 * side * 8, D, dtype=BF16),
        vmem(D, 640),
        dma((4,)),
    )
    snd[:, 0:DP] = jnp.where(sec == 0, sums5[...], sums7[...])
    snd[:, DP : DP + 640] = jnp.where(sec == 0, sums6[...], sums8[...])
    small = swap_copy(snd, got, csend.at[6], crecv.at[6])
    small.start()
    b1.point(5)
    a1.point(7)
    b1.point(6)
    a2.flush()
    b2.flush()
    a1.point(8)
    b1.point(7)
    b1.point(8)
    a1.flush()
    b1.flush()

    def finish(mine, theirs):
        copies = []
        for i, (full, m, t) in enumerate(((full_a, mine[0], theirs[0]), (full_b, mine[1], theirs[1]))):
            copies.append(pltpu.make_async_copy(m, full.at[sec], lsem.at[6 + i]))
            copies.append(swap_copy(t, full.at[sec], csend.at[4 + i], crecv.at[4 + i]))
        for c in copies:
            c.start()
        for c in copies:
            c.wait()

    ones = (part(p1a, ha, sec), part(p1b, hb, sec))
    twos = (q2a, q2b)
    pl.when(sec == 0)(lambda: finish(ones, twos))
    pl.when(sec == 1)(lambda: finish(twos, ones))
    small.wait()
    for lanes, a, b in ((slice(0, DP), sums7, sums5), (slice(DP, DP + 640), sums8, sums6)):
        offs[:, lanes] = jnp.where(sec == 0, a[...], b[...]) + got[:, lanes]


def put_halves(ref, y, lane, v):
    side, lanes = v.shape[0] // 16, v.shape[1]
    v = v.reshape(side, 2, 8, lanes)
    for h in range(2):
        ref[h, y, :, lane : lane + lanes] = v[:, h].reshape(side * 8, lanes).astype(BF16)


class Reducer:
    POINTS = 9

    def __init__(
        self, bits, index, q, base, rows, swap_src, core_land, land, csend, crecv, ssem, rsem, ready, flip, load
    ):
        self.bits, self.index, self.q, self.base, self.rows = bits, index, q, base, rows
        self.core_land, self.land, self.load = core_land, land, load
        self.ssem, self.rsem, self.ready = ssem, rsem, ready
        self.swap = swap_copy(swap_src, core_land, csend.at[index], crecv.at[index])
        me = lax.axis_index("dp")
        plain, swapped = orders(bits)
        self.steps = []
        tiles, t0, r0 = 8, 0, base
        for k, j in zip(plain, swapped):
            power = (1 << k) + flip * ((1 << j) - (1 << k))
            bit = lax.rem(me // power, 2)
            partner = me + (1 - 2 * bit) * power
            if tiles > 1:
                tiles //= 2
                keep, send = (t0 + bit * tiles, r0), (t0 + (1 - bit) * tiles, r0)
            else:
                rows //= 2
                keep, send = (t0, r0 + bit * rows), (t0, r0 + (1 - bit) * rows)
            t0, r0 = keep
            self.steps.append((partner, keep, send, tiles, rows))
        self.last = 2 * bits

    def region(self, at, tiles, rows):
        t, r = at
        if not isinstance(r, int):
            r = pl.multiple_of(r, 16)
        return self.q.at[pl.ds(t, tiles), pl.ds(r, rows)]

    def copy(self, i):
        if i == 0:
            return self.swap
        halving = i <= self.bits
        partner, keep, send, tiles, rows = self.steps[i - 1 if halving else self.last - i]
        src = self.region(send if halving else keep, tiles, rows)
        sem = self.index * (self.last + 1) + i
        return pltpu.make_async_remote_copy(
            src_ref=src,
            dst_ref=self.land[i - 1] if halving else src,
            send_sem=self.ssem.at[sem],
            recv_sem=self.rsem.at[sem],
            device_id={"dp": partner},
            device_id_type=MESH,
        )

    def free(self, i):
        return self.ready.at[self.index * self.bits + i]

    def add(self, q, land, tiles, rows):
        chunk = next(c for c in range(min(rows, 416), 0, -16) if rows % c == 0 and c % 16 == 0)
        parts = rows // chunk

        def body(j):
            t, r = j // parts, pl.multiple_of(lax.rem(j, parts) * chunk, 16)
            at = pl.ds(r, chunk)
            q[t, at] = (q[t, at].astype(F32) + land[t, at].astype(F32)).astype(BF16)

        loop(tiles * parts, body)

    def start(self, i):
        if i > self.bits:
            pl.semaphore_wait(self.free(self.last - i), 1)
        self.copy(i).start()

    def finish(self, i):
        self.copy(i).wait()
        if i == 0:
            if self.load is not None:
                self.load.wait()
            self.add(self.region((0, self.base), 8, self.rows), self.core_land, 8, self.rows)
        elif i <= self.bits:
            partner, keep, send, tiles, rows = self.steps[i - 1]
            pl.semaphore_signal(
                self.free(i - 1), inc=1, device_id={"dp": partner}, device_id_type=MESH
            )
            self.add(self.region(keep, tiles, rows), self.land[i - 1], tiles, rows)

    def point(self, p):
        count = self.last + 1
        for i in range(p * count // self.POINTS, (p + 1) * count // self.POINTS):
            if i > 0:
                self.finish(i - 1)
            self.start(i)

    def flush(self):
        self.finish(self.last)


def land_shapes(tiles, rows, bits):
    out = []
    for _ in range(bits):
        if tiles > 1:
            tiles //= 2
        else:
            rows //= 2
        out.append((tiles, rows, 128))
    return out


def orders(bits):
    plain = list(range(bits))
    swapped = plain[:]
    if bits > 1:
        swapped[0], swapped[1] = 1, 0
    return plain, swapped


def unpack_kernel(
    full_a, full_b, offs, one, mid_in, mid, small_in, small, pool, offset, buf_a, buf_b, nat, sem
):
    copies = []
    for i, (full, buf) in enumerate(((full_a, buf_a), (full_b, buf_b))):
        half = full.shape[2]
        for h in range(2):
            copies.append(
                pltpu.make_async_copy(full.at[h], buf.at[:, h * half : (h + 1) * half], sem.at[2 * i + h])
            )
    for c in copies:
        c.start()
    v = offs[...]
    lane = lax.broadcasted_iota(jnp.int32, v.shape, 1)
    out = jnp.where(lane < 256, v, 0.0)
    for lo, hi, by in ((256, 416, -1024), (416, 736, 160), (736, 768, -704), (768, 1024, 192)):
        out = jnp.where((lane >= lo) & (lane < hi), roll_lanes(v, by), out)
    offset[...] = out[0:1, 0:1024]
    for c in copies:
        c.wait()

    def take(t, r, rows):
        if r < 1440:
            return buf_a[t, r : r + rows].astype(F32)
        return buf_b[t, r - 1440 : r - 1440 + rows].astype(F32)

    for dt in range(3):
        for dy in range(3):
            for dx in range(3):
                to = 160 * (9 * dt + 3 * dy + dx)
                for rows, r in ((128, 480 * dy + 128 * dt), (32, 480 * dy + 384 + 32 * dt)):
                    nat[to : to + rows, 0:128] = take(2 * dx, r, rows)
                    nat[to : to + rows, 128:256] = take(2 * dx + 1, r, rows)
                    tail = take(6 + dx // 2, r, rows)
                    nat[to : to + rows, 256:384] = roll_lanes(tail, 64) if dx == 1 else tail
                    to = to + rows
                r = 1440 + 128 * dy + 32 * dt
                to = 32 * (9 * dt + 3 * dy + dx)
                small[to : to + 32, :] = take(5 + dx, r, 32)

    def turn(i):
        at = pl.ds(pl.multiple_of(i * 128, 128), 128)
        mid[0:256, at] = nat[at, 0:256].T
        mid[256:320, at] = nat[at, 256:384].T[0:64]

    total = mid.shape[1]
    loop(total // 128, turn)
    at = slice(total - total % 128, total)
    mid[0:256, at] = nat[at, 0:256].T
    mid[256:320, at] = nat[at, 256:384].T[0:64]
    for r in range(0, D, 128):
        rows = min(128, D - r)
        at = slice(r, r + rows)
        mid_in[0:128, at] = take(3, 1440 + r, rows).T
        last = take(4, 1440 + r, rows).T
        mid_in[128:160, at] = last[0:32]
        small_in[:, at] = last[32:64]
    one[:, 0:128] = take(0, 1440, D)
    one[:, 128:256] = take(1, 1440, D)
    pool[...] = take(2, 1440, D)


def vmem(*shape, dtype=F32):
    return pltpu.VMEM(shape, dtype)


def call(kernel, outs, args, scratch, collective=None, smem_first=True, any_in=(), any_out=()):
    def specs(count, anywhere):
        return [
            pl.BlockSpec(memory_space=pl.ANY if i in anywhere else pltpu.VMEM)
            for i in range(count)
        ]

    in_specs = specs(len(args), any_in)
    if smem_first:
        in_specs[0] = pl.BlockSpec(memory_space=pltpu.SMEM)
    params = {"vmem_limit_bytes": VMEM_LIMIT}
    if collective is not None:
        params.update(collective_id=collective, has_side_effects=True)
    return pl.pallas_call(
        kernel,
        out_shape=[jax.ShapeDtypeStruct(shape, dtype) for shape, dtype in outs],
        in_specs=in_specs,
        out_specs=specs(len(outs), any_out),
        scratch_shapes=scratch,
        compiler_params=pltpu.CompilerParams(**params),
    )(*args)


def on_device(
    clip_input, out_grad, clip_lengths, w_one, w_mid_in, w_mid, w_small_in, w_small, w_pool, bn_offset
):
    n = lax.axis_size("dp")
    bits = n.bit_length() - 1
    half, side = clip_input.shape[1], clip_input.shape[2]
    rows = side * 16
    side2 = side // 2
    rows2 = side2 * 8
    total2 = side2 * rows2
    unit = 32 << max(bits - 3, 0)
    rows_a, rows_b = -(-1440 // unit) * unit, -(-D // unit) * unit
    x = clip_input.transpose(0, 2, 3, 1, 4).reshape(2, side * side * half, D)
    og = out_grad.transpose(0, 2, 3, 1, 4)

    def like(a, dtype=BF16):
        return pltpu.VMEM(a.shape[1:], dtype)

    def turned(w):
        return w.transpose(0, 2, 1)

    weights = (w_one, turned(w_mid_in), turned(w_small_in), w_pool, turned(w_mid), w_small)
    dma = pltpu.SemaphoreType.DMA
    grid = (side, side, 2, 8)
    xgot, zone, zin, zp, st1, wp1, wp2, wf1, wf2, ws1, ws2, beta1, beta2, og_got = call(
        start_kernel,
        [
            (x.shape[1:], BF16),
            (grid + (256,), F32),
            (grid + (256,), F32),
            ((side, rows, 128), F32),
            ((8, 640), F32),
            ((D, 640), BF16),
            ((D, 640), BF16),
            ((1536, 1024), BF16),
            ((1536, 1024), BF16),
            ((384, 384), BF16),
            ((384, 384), BF16),
            ((1, 1152), F32),
            ((1, 1152), F32),
            (og.shape[1:], BF16),
        ],
        (clip_lengths, x, og) + weights + (bn_offset,),
        [
            like(x),
            like(x),
            vmem(*grid, 256),
            vmem(*grid, 256),
            vmem(side, rows, 128),
            vmem(*grid, 128),
            vmem(side + 2, rows, 128),
        ]
        + [like(w) for w in weights]
        + [
            vmem(1, 1152),
            vmem(1, 1152),
            vmem(27 * C1A, 384, dtype=BF16),
            vmem(2, D, 640, dtype=BF16),
            vmem(2, 1536, 1024, dtype=BF16),
            vmem(2, 384, 384, dtype=BF16),
            vmem(2, 2, 8, 640),
            vmem(2, 16, 640),
        ]
        + exchange_scratch(n, 16)
        + [dma((7,)), dma((10,)), dma((6,)), dma((6,))],
        collective=1,
        any_in=range(1, 9),
        any_out=(0, 1, 2, 3, 5, 6, 7, 8, 9, 10, 13),
    )
    zone = zone.reshape(side, rows, 256)
    zin = zin.reshape(side, rows, 256)
    cat, scat, zf, stf = call(
        conv_kernel,
        [
            ((side + 2, rows, 512), BF16),
            ((side + 2, rows, 128), BF16),
            ((side, rows, DP), F32),
            ((8, DP), F32),
        ],
        (clip_lengths, zin, zone, zp, st1, beta1, wf1, ws1),
        [vmem(8, 512), vmem(2, 16, 512)] + exchange_scratch(n, 8),
        collective=2,
    )
    sig, hand, asum, bsum = call(
        output_kernel,
        [((side, rows, DP), BF16)] + [((side2, side2, 8, DP), F32)] * 3,
        (clip_lengths, zf, stf, beta1),
        [vmem(side2, 16, 128)],
    )
    block_output, hg, packed2a, packed2b, sums5, sums6, sums7 = call(
        second_kernel,
        [
            (og.shape, BF16),
            ((side2, side2, 8, DP), F32),
            ((8, rows_a, 128), BF16),
            ((8, rows_b, 128), BF16),
            ((8, DP), F32),
            ((8, 640), F32),
            ((8, DP), F32),
        ],
        (clip_lengths, hand, asum, bsum, og, og_got, wp2, wf2, ws2, beta2, beta1),
        [
            like(og),
            vmem(side2, side2, 8, D),
            vmem(2, *og.shape[1:], dtype=BF16),
            dma((2,)),
            dma(()),
            dma(()),
            vmem(total2, DP, dtype=BF16),
            vmem(side2, rows2, 256),
            vmem(side2, rows2, 128),
            vmem(side2, rows2, DP),
            vmem(8, DP),
            vmem(side2, rows2, 128),
            vmem(side2 + 2, rows2, 128),
            vmem(side2 + 2, rows2, 640),
            vmem(total2, 1536, dtype=BF16),
            vmem(total2, 384, dtype=BF16),
            vmem(side2, rows2, 1024),
            vmem(side2, rows2, 384),
            vmem(side2, rows2, DP),
            vmem(side2, rows2, 1024),
            vmem(side2, rows2, 384),
            vmem(side2, rows2, 640),
            vmem(side2, rows2, 256),
            vmem(2, 8, 640),
            vmem(8, 640),
            vmem(8, 512),
            vmem(2, 8, DP),
            vmem(1536, 1024),
            vmem(384, 384),
            vmem(DP, 640),
        ]
        + exchange_scratch(n, 16)
        + exchange_scratch(n, 8)
        + exchange_scratch(n, 16)
        + exchange_scratch(n, 8)
        + exchange_scratch(n, 16),
        collective=3,
        any_in=(4,),
        any_out=(0,),
    )
    ha, hb = rows_a // 2, rows_b // 2

    def bf(*shape):
        return vmem(*shape, dtype=BF16)

    lands = []
    for h in (ha, hb, ha, hb):
        lands += [bf(*shape) for shape in land_shapes(8, h, bits)]
    steps = 4 * (2 * bits + 1)
    gin, full_a, full_b, offs = call(
        functools.partial(backward_kernel, bits),
        [
            (x.shape, BF16),
            ((2, 8, ha, 128), BF16),
            ((2, 8, hb, 128), BF16),
            ((8, DP + 640), F32),
        ],
        (clip_lengths, hg, stf, sums7, st1, beta1, sums5, sums6)
        + (zf, sig, zin, wf1, ws1, wp1, cat, scat, x, xgot, packed2a, packed2b),
        [
            vmem(side, rows, 256),
            bf(1536, 1024),
            bf(384, 384),
            bf(D, 640),
            bf(side + 2, rows, 1024),
            bf(side + 2, rows, 384),
            bf(2, side, rows // 2, 384),
            bf(2, side, rows // 2, 256),
            vmem(8, 640),
            vmem(8, DP + 640),
            vmem(8, DP + 640),
            bf(8, rows_a, 128),
            bf(8, rows_b, 128),
        ]
        + [bf(8, h, 128) for h in (ha, hb) * 3]
        + [vmem(2, 16, 640)]
        + exchange_scratch(n, 8)
        + [dma((8,)), dma((7,)), dma((7,)), dma((steps,)), dma((steps,)), dma((2,)), dma((2,))]
        + [pltpu.SemaphoreType.REGULAR((4 * bits,))]
        + lands,
        collective=4,
        any_in=range(8, 20),
        any_out=(0, 1, 2),
    )
    one, mid_in, mid, small_in, small, pool, offset = call(
        unpack_kernel,
        [
            ((D, C0), F32),
            ((C1A, D), F32),
            ((C1B, 27 * C1A), F32),
            ((C2A, D), F32),
            ((27 * C2A, C2B), F32),
            ((D, C3), F32),
            ((1, 1024), F32),
        ],
        (full_a, full_b, offs),
        [bf(8, rows_a, 128), bf(8, rows_b, 128), vmem(27 * C1A, 384), dma((4,))],
        smem_first=False,
        any_in=(0, 1),
    )
    input_grad = gin.reshape(2, side, side, half, D).transpose(0, 3, 1, 2, 4)
    return (
        block_output.transpose(0, 3, 1, 2, 4),
        input_grad,
        one[None],
        mid_in.T[None],
        mid.T[None],
        small_in.T[None],
        small[None],
        pool[None],
        offset,
    )


def solution(mesh):
    placed = (
        P("dp", "section", None, None, None),
        P("dp", "section", None, None, None),
        P("dp", None),
        P("section", None, None),
        P("section", None, None),
        P("section", None, None),
        P("section", None, None),
        P("section", None, None),
        P("section", None, None),
        P("section", None),
    )
    return jax.shard_map(
        on_device,
        mesh=mesh,
        in_specs=placed,
        out_specs=(
            P("dp", "section", None, None, None),
            P("dp", "section", None, None, None),
            P("section", None, None),
            P("section", None, None),
            P("section", None, None),
            P("section", None, None),
            P("section", None, None),
            P("section", None, None),
            P("section", None),
        ),
        check_vma=False,
    )
```

```python
import functools

import jax
import jax.numpy as jnp
from jax import lax
from jax.experimental import pallas as pl
from jax.experimental.pallas import tpu as pltpu
from jax.sharding import PartitionSpec as P

D = 832
DP = 896
C0 = 256
C1A = 160
C1B = 320
C2A = 32
C2B = 128
C3 = 128
EPS = 0.001
MESH = pl.DeviceIdType.MESH
F32 = jnp.float32
BF16 = jnp.bfloat16
VMEM_LIMIT = 60 * 2**20


def dot(a, b):
    return jnp.dot(a, b, preferred_element_type=F32)


def dot_nt(a, b):
    return lax.dot_general(a, b, (((1,), (1,)), ((), ())), preferred_element_type=F32)


def dot_tn(a, b):
    return lax.dot_general(a, b, (((0,), (0,)), ((), ())), preferred_element_type=F32)


def roll_rows(x, by):
    return pltpu.roll(x, by % x.shape[0], 0)


def roll_lanes(x, by):
    return pltpu.roll(x, by % x.shape[1], 1)


def lane_below(x, count):
    lanes = lax.broadcasted_iota(jnp.int32, x.shape, 1)
    return jnp.where(lanes < count, x, 0.0)


class Clips:
    def __init__(self, len_ref, frames, stride):
        sec = lax.axis_index("section")
        f = lax.broadcasted_iota(jnp.int32, (frames, 128), 0)

        def label(v):
            place = v * stride
            out = jnp.zeros_like(v)
            start = jnp.int32(0)
            for c in range(len_ref.shape[1]):
                end = start + len_ref[sec, c]
                out = jnp.where((place >= start) & (place < end), c + 1, out)
                start = end
            return out

        here = label(f)
        inside = here > 0

        def mask(m):
            return jnp.where(m, 1.0, 0.0).astype(F32)

        self.frames = frames
        self.valid = mask(inside)
        self.before = mask(inside & (f > 0) & (label(f - 1) == here))
        self.after = mask(inside & (f < frames - 1) & (label(f + 1) == here))
        self.inv = 1.0 / jnp.maximum(self.valid + self.before + self.after, 1.0)

    def times(self, v, pattern):
        return (v.reshape(-1, self.frames, 128) * pattern).reshape(v.shape)

    def fold(self, v):
        return jnp.sum(v.reshape(-1, self.frames, v.shape[-1]), axis=0)


def shift_places(v, frames, by):
    lanes = v.shape[-1]
    v3 = v.reshape(-1, frames, lanes)
    zero = jnp.zeros((1, frames, lanes), v.dtype)
    if by > 0:
        v3 = jnp.concatenate([v3[1:], zero], 0)
    else:
        v3 = jnp.concatenate([zero, v3[:-1]], 0)
    return v3.reshape(v.shape)


def add_stats(clips, acc, lanes, v, w=None):
    acc[0, :, lanes] += clips.fold(v)
    acc[1, :, lanes] += clips.fold(v * (v if w is None else w))


def affine(st, lanes):
    total, square, count = st[0:1, lanes], st[1:2, lanes], st[2:3, lanes]
    mean = total / count
    scale = lax.rsqrt(square / count - mean * mean + EPS)
    return scale, mean


def soft(t):
    e = jnp.exp(-jnp.abs(t))
    r = 1.0 / (1.0 + e)
    return jnp.maximum(t, 0.0) + jnp.log(1.0 + e), jnp.where(t >= 0, r, e * r)


def sigm(t):
    e = jnp.exp(-jnp.abs(t))
    r = 1.0 / (1.0 + e)
    return jnp.where(t >= 0, r, e * r)


def greet(partner=False):
    n = lax.axis_size("dp")
    me = lax.axis_index("dp")
    barrier = pltpu.get_barrier_semaphore()

    def go(k, _):
        pl.semaphore_signal(
            barrier, inc=1, device_id={"dp": lax.rem(me + k, n)}, device_id_type=MESH
        )
        return 0

    if partner:
        other = 1 - lax.axis_index("section")
        pl.semaphore_signal(barrier, inc=1, device_id={"section": other}, device_id_type=MESH)
    lax.fori_loop(1, n, go, 0)


def greeted(partner=False):
    pl.semaphore_wait(pltpu.get_barrier_semaphore(), lax.axis_size("dp") - 1 + int(partner))


def exchange_start(loc, buf, ssem, rsem):
    n = lax.axis_size("dp")
    me = lax.axis_index("dp")

    def start(k, _):
        pltpu.make_async_remote_copy(
            src_ref=loc,
            dst_ref=buf.at[me],
            send_sem=ssem.at[k],
            recv_sem=rsem.at[me],
            device_id={"dp": lax.rem(me + k, n)},
            device_id_type=MESH,
        ).start()
        return 0

    lax.fori_loop(1, n, start, 0)
    buf[me] = loc[...]


def exchange_finish(loc, buf, ssem, rsem, out, tiles):
    n = lax.axis_size("dp")
    me = lax.axis_index("dp")

    def wait(k, _):
        j = lax.rem(me + k, n)
        copy = pltpu.make_async_remote_copy(
            src_ref=loc,
            dst_ref=buf.at[j],
            send_sem=ssem.at[k],
            recv_sem=rsem.at[j],
            device_id={"dp": j},
            device_id_type=MESH,
        )
        copy.wait_send()
        copy.wait_recv()
        return 0

    lax.fori_loop(1, n, wait, 0)
    total = jnp.sum(buf[...], axis=0)
    at = 2 * len(tiles)
    for i, t in enumerate(tiles):
        lanes = slice(128 * t, 128 * t + 128)
        out[0:1, lanes] = total[2 * i : 2 * i + 1]
        out[1:2, lanes] = total[2 * i + 1 : 2 * i + 2]
        if at < loc.shape[0]:
            out[2:3, lanes] = total[at : at + 1]


def exchange(loc, buf, ssem, rsem, out, tiles):
    exchange_start(loc, buf, ssem, rsem)
    exchange_finish(loc, buf, ssem, rsem, out, tiles)


def swap_copy(src, dst, ssem, rsem):
    return pltpu.make_async_remote_copy(
        src_ref=src,
        dst_ref=dst,
        send_sem=ssem,
        recv_sem=rsem,
        device_id={"section": 1 - lax.axis_index("section")},
        device_id_type=MESH,
    )


def exchange_scratch(n, rows):
    return [
        pltpu.VMEM((rows, 128), F32),
        pltpu.VMEM((n, rows, 128), F32),
        pltpu.SemaphoreType.DMA((n,)),
        pltpu.SemaphoreType.DMA((n,)),
    ]


FIRST, CONV, FINAL, INNER = range(5), range(4), range(7), (3, 4)


def pack_stats(clips, loc, acc, tiles, count=None):
    for i, t in enumerate(tiles):
        lanes = pl.ds(128 * t, 128)
        for k in range(2):
            loc[2 * i + k : 2 * i + k + 1, :] = jnp.sum(
                acc[k, :, lanes] * clips.valid, axis=0, keepdims=True
            )
    if count is not None:
        at = 2 * len(tiles)
        loc[at : at + 1, :] = jnp.sum(clips.valid, axis=0, keepdims=True) * float(count)


def loop(n, body):
    def step(i, _):
        body(i)
        return 0

    lax.fori_loop(0, n, step, 0)


def inv_edges(side, frames, y):
    x = lax.broadcasted_iota(jnp.int32, (side, frames, 128), 0)
    ex = jnp.where((x == 0) | (x == side - 1), 0.5, 1.0 / 3.0).astype(F32)
    ey = jnp.where((y == 0) | (y == side - 1), 0.5, 1.0 / 3.0).astype(F32)
    return (ex * ey).reshape(side * frames, 128)


def box(clips, side, load, tx, store):
    frames = clips.frames
    tx[0] = jnp.zeros(tx.shape[1:], F32)
    tx[side + 1] = jnp.zeros(tx.shape[1:], F32)

    def across(y):
        v = load(y)
        t = clips.times(v, clips.valid)
        t = t + clips.times(roll_rows(v, 1), clips.before)
        t = t + clips.times(roll_rows(v, -1), clips.after)
        tx[y + 1] = t + shift_places(t, frames, 1) + shift_places(t, frames, -1)

    def down(y):
        store(y, tx[y] + tx[y + 1] + tx[y + 2])

    loop(side, across)
    loop(side, down)


def pool_forward(clips, side, load, tx, zp, acc):
    def store(y, v):
        z = clips.times(v * inv_edges(side, clips.frames, y), clips.inv)
        zp[y] = z
        add_stats(clips, acc, pl.ds(256, 128), z)

    box(clips, side, load, tx, store)


def upright(src, dst):
    rows = src.shape[1]
    width = src.shape[0]

    def body(i):
        at = pl.ds(pl.multiple_of(i * 128, 128), 128)
        dst[at, 0:width] = src[:, at].astype(F32).T.astype(BF16)

    loop(rows // 128, body)
    if rows % 128:
        at = slice(rows - rows % 128, rows)
        dst[at, 0:width] = src[:, at].astype(F32).T.astype(BF16)


def arrange_first(src, wp, b, flip):
    one, mid_in, small_in, pool = src
    wp[b, :, 0:256] = one[...]
    wp[b, :, 256:384] = pool[...]
    upright(mid_in, flip)
    wp[b, :, 384:544] = flip[0:D, 0:C1A]
    upright(small_in, flip)
    wp[b, :, 544:576] = flip[0:D, 0:C2A]
    wp[b, :, 576:640] = jnp.zeros((D, 64), BF16)


def arrange_beta(src, dst):
    v = jnp.concatenate([jnp.broadcast_to(src[...], (8, 1024)), jnp.zeros((8, 128), F32)], 1)
    lane = lax.broadcasted_iota(jnp.int32, v.shape, 1)
    out = jnp.zeros_like(v)
    for lo, hi, by in (
        (0, 256, 0),
        (256, 576, -160),
        (576, 832, -192),
        (896, 1056, 640),
        (1056, 1088, 320),
    ):
        out = jnp.where((lane >= lo) & (lane < hi), roll_lanes(v, by), out)
    dst[...] = out[0:1]


def arrange_conv(mid_flat, small, wf, ws, b, mid):
    upright(mid_flat, mid)
    for dy in range(3):
        wf[b, 512 * dy + 480 : 512 * dy + 512, :] = jnp.zeros((32, 1024), BF16)
        ws[b, 128 * dy + 96 : 128 * dy + 128, :] = jnp.zeros((32, 384), BF16)
        wf[b, 512 * dy : 512 * dy + 512, 960:1024] = jnp.zeros((512, 64), BF16)
        for dt in range(3):
            for dx in range(3):
                r = 96 * (3 * dt + dy) + 32 * dx
                to = 128 * dy + 32 * dt
                ws[b, to : to + 32, 128 * dx : 128 * dx + 128] = small[r : r + 32, :]
            for dx in range(3):
                r = 480 * (3 * dt + dy) + 160 * dx
                for rows, to in ((128, 128 * dt), (32, 384 + 32 * dt)):
                    to = to + 512 * dy
                    wf[b, to : to + rows, 256 * dx : 256 * dx + 256] = mid[r : r + rows, 0:256]
                    wf[b, to : to + rows, 768 + 64 * dx : 832 + 64 * dx] = mid[
                        r : r + rows, 256:320
                    ]
                    r = r + rows


def inner_tiles(clips, z, st, beta):
    tiles = []
    for t in range(2):
        scale, mean = affine(st, pl.ds(384 + 128 * t, 128))
        b = beta[0:1, pl.ds(896 + 128 * t, 128)]
        act, _ = soft(z[:, 128 * t : 128 * (t + 1)] * scale + (b - mean * scale))
        tiles.append(clips.times(act, clips.valid))
    return tiles


def tap_tiles(clips, a, b):
    def before(v):
        return clips.times(roll_rows(v, 1), clips.before)

    def after(v):
        return clips.times(roll_rows(v, -1), clips.after)

    lane = lax.broadcasted_iota(jnp.int32, b.shape, 1)
    ones = clips.times(jnp.where(lane == 96, 1.0, 0.0).astype(F32), clips.valid)

    def three32(v):
        return before(v) + roll_lanes(v, 32) + roll_lanes(after(v), 64) + ones

    tail = lane_below(b, 32)
    small = lane_below(roll_lanes(b, -32), 32)
    return [before(a), a, after(a), three32(tail)], three32(small)


def untap(clips, parts, small):
    def before(v):
        return roll_rows(clips.times(v, clips.before), -1)

    def after(v):
        return roll_rows(clips.times(v, clips.after), 1)

    def back32(v):
        return (
            lane_below(before(v), 32)
            + lane_below(roll_lanes(v, -32), 32)
            + lane_below(roll_lanes(after(v), -64), 32)
        )

    a = before(parts[0]) + parts[1] + after(parts[2])
    return a, back32(parts[3]) + roll_lanes(back32(small), 32)


def typical(beta):
    sp, sg = soft(jnp.broadcast_to(beta, (8, beta.shape[-1])))
    return sp + 0.5 * sg * (1.0 - sg)


def outer(c, s):
    k = lax.broadcasted_iota(jnp.int32, c.shape, 0)
    c = jnp.where(k < 2, c, 0.0).astype(BF16)
    s = jnp.broadcast_to(s, (8, s.shape[-1]))
    high = s.astype(BF16).astype(F32)
    k = lax.broadcasted_iota(jnp.int32, s.shape, 0)
    s = jnp.where(k == 0, high, jnp.where(k == 1, s - high, 0.0)).astype(BF16)
    return dot_tn(c, s)


def tap_points(beta):
    a = typical(beta[0:1, 896:1024])
    b = typical(beta[0:1, 1024:1152])

    def three(v):
        return v + roll_lanes(v, 32) + roll_lanes(v, 64)

    tail = three(lane_below(b, 32))
    small = three(lane_below(roll_lanes(b, -32), 32))
    return jnp.concatenate([a, a, a, tail], 1), small


def centre_mid(row, beta):
    c, _ = tap_points(beta)
    row = jnp.broadcast_to(row, (8, 1024))
    main = row[:, 256:512]
    tail = lane_below(roll_lanes(row[:, 768:896], 64), 64)
    s = jnp.concatenate([main, main, main, tail + roll_lanes(tail, 64), tail], 1)
    return outer(c, s)


def centre_small(grad, beta):
    _, c = tap_points(beta)
    row = jnp.broadcast_to(grad[224:225, 128:256], (8, 128))
    return outer(c, jnp.concatenate([row, row, row], 1))


def conv_gather(frames, p, s):
    def three(at):
        return (
            shift_places(at(0), frames, -1) + at(1) + shift_places(at(2), frames, 1)
        )

    main = three(lambda k: p[:, 256 * k : 256 * k + 256])
    small = three(lambda k: s[:, 128 * k : 128 * k + 128])
    ends = p[:, 768:896]
    tail = three(lambda k: (ends, roll_lanes(ends, 64), p[:, 896:1024])[k])
    return main, small, lane_below(tail, 64)


def spread_x(frames, v, by):
    return v if by == 0 else shift_places(v, frames, -by)


def put_spread(frames, main, small, tail, put_mid, put_small):
    for k in range(3):
        put_mid(256 * k, spread_x(frames, main, k - 1))
        put_small(128 * k, spread_x(frames, small, k - 1))
    put_mid(768, spread_x(frames, tail, -1) + roll_lanes(tail, 64))
    put_mid(896, spread_x(frames, tail, 1))


def join_final(small, tail, pool):
    s, p = roll_lanes(small, 64), roll_lanes(pool, 64)
    low = lax.broadcasted_iota(jnp.int32, small.shape, 1) < 64
    return jnp.where(low, tail, s), jnp.where(low, s, p), jnp.where(low, p, 0.0)


def split_final(t4, t5, t6):
    a, b, c = roll_lanes(t4, 64), roll_lanes(t5, 64), roll_lanes(t6, 64)
    low = lax.broadcasted_iota(jnp.int32, t4.shape, 1) < 64
    return jnp.where(low, a, b), jnp.where(low, t4, 0.0), jnp.where(low, b, c)


def final_stats(st1, st2, stf):
    stf[:, 0:256] = st1[:, 0:256]
    stf[:, 256:512] = st2[:, 0:256]
    for t, v in enumerate(join_final(st2[:, 256:384], st2[:, 384:512], st1[:, 256:384])):
        stf[:, 512 + 128 * t : 640 + 128 * t] = v
    stf[2:3, :] = jnp.broadcast_to(st1[2:3, 0:1], (1, DP))


def store_conv(clips, y, p, s, zp, put, acc):
    main, small, tail = conv_gather(clips.frames, p, s)
    put(y, 256, main)
    for t, v in enumerate(join_final(small, tail, zp[y])):
        put(y, 512 + 128 * t, v)
    add_stats(clips, acc, pl.ds(0, 256), main)
    add_stats(clips, acc, pl.ds(256, 128), small)
    add_stats(clips, acc, pl.ds(384, 128), tail)


def forward_kernel(
    len_ref, bn, x, og, w_one, w_mid_in, w_small_in, w_pool, w_mid, w_small,
    st1, stf, beta1, beta2,
    xgot_out, zin_out, zf_out, sig_out, hand_out, asum_out, bsum_out, cat_out, scat_out,
    wp1, wp2, wf1, wf2, ws1, ws2, og_got,
    x_got, zf, zin, zp, cat, scat, sig, hand, asum, bsum, scr, beta, got_beta, wp, wf, ws, st2,
    hacc, acc, acc2, loc, buf, ssem, rsem, loc2, buf2, ssem2, rsem2, osem, psem, qsem,
):
    greet(partner=True)
    sec = lax.axis_index("section")
    side = zp.shape[0]
    rows = side * 16
    clips = Clips(len_ref, 16, 1)
    hacc[...] = jnp.zeros_like(hacc)
    acc[...] = jnp.zeros_like(acc)
    acc2[...] = jnp.zeros_like(acc2)
    loc[...] = jnp.zeros_like(loc)
    loc2[...] = jnp.zeros_like(loc2)
    outs = []

    def put(src, dst):
        c = pltpu.make_async_copy(src, dst, osem.at[len(outs)])
        c.start()
        outs.append(c)

    pairs = ((wp.at[sec], wp.at[sec]), (beta, got_beta), (x.at[1 - sec], x_got))
    pairs += ((og.at[1 - sec], og_got), (wf.at[sec], wf.at[sec]), (ws.at[sec], ws.at[sec]))
    remote = [swap_copy(a, b, psem.at[i], qsem.at[i]) for i, (a, b) in enumerate(pairs)]

    def first_phase(x_own, yp, tx, one, mid_in, small_in, pool, mid, small, flip, lsem):
        local = [
            pltpu.make_async_copy(a, b, lsem.at[i])
            for i, (a, b) in enumerate(
                (
                    (x.at[sec], x_own),
                    (w_one.at[0], one),
                    (w_mid_in.at[0], mid_in),
                    (w_small_in.at[0], small_in),
                    (w_pool.at[0], pool),
                    (w_mid.at[0], mid),
                    (w_small.at[0], small),
                )
            )
        ]
        for c in local[1:] + local[:1]:
            c.start()
        arrange_beta(bn, beta)
        for c in local[1:5]:
            c.wait()
        arrange_first((one, mid_in, small_in, pool), wp, sec, flip)
        greeted(partner=True)
        for c in remote[:4]:
            c.start()
        for c in local[5:]:
            c.wait()
        arrange_conv(mid, small, wf, ws, sec, flip)
        for c in remote[4:]:
            c.start()
        for c in remote[:2]:
            c.wait()
        beta1[...] = jnp.where(sec == 0, beta[...], got_beta[...])
        beta2[...] = jnp.where(sec == 0, got_beta[...], beta[...])
        ny = side // 2
        size = ny * side * 8
        for k, src in enumerate((x_own, x_got)):
            (local[0] if k == 0 else remote[2]).wait()
            half = sec if k == 0 else 1 - sec

            def body(i, src=src, half=half):
                here = pl.ds(i * ny, ny)
                y = dot(src[pl.ds(pl.multiple_of(i * size, 16), size)], wp[0])

                def place(lo, hi):
                    return y[:, lo:hi].reshape(ny, side, 8, hi - lo)

                zf[here, :, half, :, 0:256] = place(0, 256)
                yp[here, :, half] = place(256, 384)
                zin[here, :, half] = place(384, 640)
                for lo, hi in ((0, 256), (384, 640)):
                    v = y[:, lo:hi].reshape(-1, 8, 256)
                    hacc[0, half, :, lo:hi] += jnp.sum(v, axis=0)
                    hacc[1, half, :, lo:hi] += jnp.sum(v * v, axis=0)

            loop(2, body)
        acc[...] = hacc[...].reshape(acc.shape)
        pool_forward(clips, side, lambda y: yp[y].reshape(rows, 128), tx, zp, acc)

    like = [pltpu.VMEM(a.shape[1:], BF16) for a in (w_one, w_mid_in, w_small_in, w_pool, w_mid, w_small)]
    pl.run_scoped(
        first_phase,
        pltpu.VMEM(x.shape[1:], BF16),
        vmem(side, side, 2, 8, 128),
        vmem(side + 2, rows, 128),
        *like,
        vmem(27 * C1A, 384, dtype=BF16),
        pltpu.SemaphoreType.DMA((7,)),
    )
    pack_stats(clips, loc, acc, FIRST, side * side)
    exchange_start(loc, buf, ssem, rsem)
    put(x_got, xgot_out)
    put(zin, zin_out)
    for y in (0, side + 1):
        cat[y] = jnp.zeros(cat.shape[1:], BF16)
        scat[y] = jnp.zeros(scat.shape[1:], BF16)
    exchange_finish(loc, buf, ssem, rsem, st1, FIRST)

    def build(y):
        a, b = inner_tiles(clips, zin[y].reshape(rows, 256), st1, beta1)
        parts, small = tap_tiles(clips, a, b)
        for i, part in enumerate(parts):
            cat[y + 1, :, 128 * i : 128 * i + 128] = part.astype(BF16)
        scat[y + 1] = small.astype(BF16)

    loop(side, build)
    for c in remote[3:]:
        c.wait()
    put(cat, cat_out)
    put(scat, scat_out)
    for a, b in ((wf, (wf1, wf2)), (ws, (ws1, ws2)), (wp, (wp1, wp2))):
        for i in range(2):
            put(a.at[i], b[i])
    ny = 2

    def put_row(y, lane, v):
        zf[y, :, :, :, lane : lane + v.shape[-1]] = v.reshape(side, 2, 8, v.shape[-1])

    def products(i):
        y0 = i * ny

        def taps(ref):
            return jnp.concatenate(
                [ref[pl.ds(y0 + dy, ny)].reshape(ny * rows, ref.shape[-1]) for dy in range(3)], axis=1
            )

        p = dot(taps(cat), wf[0])
        s = dot(taps(scat), ws[0])
        for q in range(ny):
            here = slice(q * rows, (q + 1) * rows)
            store_conv(clips, y0 + q, p[here], s[here], zp, put_row, acc2)

    loop(side // ny, products)
    pack_stats(clips, loc2, acc2, CONV)
    exchange_start(loc2, buf2, ssem2, rsem2)
    put(zf, zf_out)
    half = side // 2

    def emit(k, tiles, st):
        for t in tiles:
            lanes = pl.ds(128 * t, 128)
            scale, mean = affine(st, lanes)
            b = beta1[0:1, lanes]
            pooled = None
            for q in range(2):
                z = zf[2 * k + q, :, :, :, lanes].reshape(rows, 128)
                u = (z - mean) * scale
                sp, sg = soft(u + b)
                sp, sg = clips.times(sp, clips.valid), clips.times(sg, clips.valid)
                if t == 6:
                    lane = lax.broadcasted_iota(jnp.int32, sp.shape, 1)
                    one = clips.times(jnp.ones_like(sp), clips.valid)
                    sp = jnp.where(lane == 127, one, lane_below(sp, 64))
                    sg = lane_below(sg, 64)
                sig[2 * k + q, :, lanes] = sg.astype(BF16)
                three = [
                    jnp.sum(v.reshape(half, 2, 16, 128), axis=1) for v in (sp, sg, sg * u)
                ]
                pooled = three if pooled is None else [x + y for x, y in zip(pooled, three)]
            for v, dst in zip(pooled, (hand, asum, bsum)):
                scr[...] = v
                dst[k, :, :, lanes] = (
                    scr[:, pl.ds(0, 8, stride=2), :] + scr[:, pl.ds(1, 8, stride=2), :]
                ) * 0.125

    loop(half, lambda k: emit(k, (0, 1), st1))
    exchange_finish(loc2, buf2, ssem2, rsem2, st2, CONV)
    final_stats(st1, st2, stf)
    last = ((sig, sig_out, 2), (hand, hand_out, 1), (asum, asum_out, 1), (bsum, bsum_out, 1))
    base = len(outs)

    def rest(k):
        emit(k, range(2, 7), stf)
        for i, (src, dst, n) in enumerate(last):
            here = pl.ds(n * k, n)
            pltpu.make_async_copy(src.at[here], dst.at[here], osem.at[base + i]).start()

    loop(half, rest)
    for c in outs:
        c.wait()
    for i, (src, dst, n) in enumerate(last):
        pltpu.make_async_copy(src, dst, osem.at[base + i]).wait()


def second_kernel(
    len_ref, hand, asum, bsum, og, og_got, wp, wf, ws, beta, beta1,
    block_out, hg, packed0, packed1, packed2, packed3, packed4, sums5, sums6, sums7,
    gown, grad, out, lsem, psem, qsem,
    hbuf, zin, zp, zf, stf, yp, tx, catf, cat, scat, pbuf, sbuf, dbuf, dzc, dzs, dz1, din,
    acc, st3, st4, acc7, accm, accs, accp,
    loc3, buf3, ss3, rs3, loc4, buf4, ss4, rs4, loc5, buf5, ss5, rs5,
    loc6, buf6, ss6, rs6, loc7, buf7, ss7, rs7,
):
    greet(partner=True)
    sec = lax.axis_index("section")
    own = pltpu.make_async_copy(og.at[sec], gown, lsem.at[0])
    own.start()
    side = hand.shape[0]
    rows = side * 8
    total = side * rows
    clips = Clips(len_ref, 8, 2)
    for ref in (acc, acc7, loc3, loc4, loc5, loc6, loc7):
        ref[...] = jnp.zeros_like(ref)

    hbuf[...] = hand[...].reshape(total, DP).astype(BF16)
    y = dot(hbuf[:, 0:D], wp[...])
    zf[:, :, 0:C0] = y[:, 0:C0].reshape(side, rows, C0)
    yp[...] = y[:, 256:384].reshape(side, rows, 128)
    zin[...] = y[:, 384:640].reshape(side, rows, 256)

    def first_sums(y):
        add_stats(clips, acc, pl.ds(0, 256), zf[y, :, 0:256])
        add_stats(clips, acc, pl.ds(384, 256), zin[y])

    loop(side, first_sums)
    pool_forward(clips, side, lambda y: yp[y], tx, zp, acc)
    pack_stats(clips, loc3, acc, FIRST, side * side)
    greeted(partner=True)
    exchange_start(loc3, buf3, ss3, rs3)
    own.wait()
    mine, theirs = gown[...].astype(F32), og_got[...].astype(F32)
    low = jnp.where(sec == 0, mine, theirs)
    high = jnp.where(sec == 0, theirs, mine)
    grad[...] = jnp.concatenate([low, high], 2)
    exchange_finish(loc3, buf3, ss3, rs3, st3, FIRST)

    catf[0] = jnp.zeros(catf.shape[1:], F32)
    catf[side + 1] = jnp.zeros(catf.shape[1:], F32)

    def build(y):
        a, b = inner_tiles(clips, zin[y], st3, beta)
        parts, small = tap_tiles(clips, a, b)
        for t, v in enumerate(parts + [small]):
            catf[y + 1, :, 128 * t : 128 * t + 128] = v

    loop(side, build)
    for dy in range(3):
        v = catf[dy : dy + side].reshape(total, 640).astype(BF16)
        cat[:, 512 * dy : 512 * dy + 512] = v[:, 0:512]
        scat[:, 128 * dy : 128 * dy + 128] = v[:, 512:640]
    pbuf[...] = dot(cat[...], wf[...]).reshape(side, rows, 1024)
    sbuf[...] = dot(scat[...], ws[...]).reshape(side, rows, 384)
    acc[...] = jnp.zeros_like(acc)

    def put_row(y, lane, v):
        zf[y, :, lane : lane + v.shape[-1]] = v

    loop(side, lambda y: store_conv(clips, y, pbuf[y], sbuf[y], zp, put_row, acc))
    pack_stats(clips, loc4, acc, CONV)
    exchange(loc4, buf4, ss4, rs4, st4, CONV)
    final_stats(st3, st4, stf)

    def emit(y):
        for t in range(7):
            lanes = pl.ds(128 * t, 128)
            scale, mean = affine(stf, lanes)
            u = (zf[y, :, lanes] - mean) * scale
            sp, sg = soft(u + beta[0:1, lanes])
            width = 128 if t < 6 else 64
            gr = grad[y, :, :, 128 * t : 128 * t + width].reshape(rows, width)
            if t == 6:
                gr = jnp.concatenate([gr, jnp.zeros((rows, 64), F32)], 1)
            d = gr * clips.times(sg, clips.valid)
            dbuf[y, :, lanes] = d
            add_stats(clips, acc7, lanes, d, u)
            sp = clips.times(sp, clips.valid).reshape(side, 8, 128)[:, :, 0:width]
            for h in range(2):
                out[h, y, :, :, 128 * t : 128 * t + width] = sp[:, 4 * h : 4 * h + 4].astype(BF16)

    loop(side, emit)
    mine = pltpu.make_async_copy(out.at[sec], block_out.at[sec], lsem.at[1])
    mine.start()
    theirs = swap_copy(out.at[1 - sec], block_out.at[sec], psem, qsem)
    theirs.start()
    pack_stats(clips, loc5, acc7, FINAL)
    exchange(loc5, buf5, ss5, rs5, sums5, FINAL)
    count = st3[2:3, 0:128]

    def dz_of(y, t):
        lanes = pl.ds(128 * t, 128)
        scale, mean = affine(stf, lanes)
        u = (zf[y, :, lanes] - mean) * scale
        m1, m2 = sums5[0:1, lanes] / count, sums5[1:2, lanes] / count
        return clips.times((dbuf[y, :, lanes] - m1 - u * m2) * scale, clips.valid)

    def dz_final(y):
        for t in range(2):
            dz1[y, :, 128 * t : 128 * t + 128] = dz_of(y, t)
        main = jnp.concatenate([dz_of(y, 2), dz_of(y, 3)], 1)
        small, tail, pool = split_final(*(dz_of(y, t) for t in (4, 5, 6)))
        yp[y] = clips.times(pool * inv_edges(side, 8, y), clips.inv)

        def put(ref):
            def go(lane, v):
                ref[y, :, lane : lane + v.shape[-1]] = v

            return go

        put_spread(8, main, small, tail, put(dzc), put(dzs))

    loop(side, dz_final)

    def boxed(y, v):
        dz1[y, :, 256:384] = clips.times(v, clips.valid)

    box(clips, side, lambda y: yp[y], tx, boxed)
    dzc_b = dzc[...].reshape(total, 1024).astype(BF16)
    dzs_b = dzs[...].reshape(total, 384).astype(BF16)
    for dy in (-1, 0, 1):
        k = dy + 1
        q = dot_nt(dzc_b, wf[512 * k : 512 * k + 512]).reshape(side, rows, 512)
        r = dot_nt(dzs_b, ws[128 * k : 128 * k + 128]).reshape(side, rows, 128)
        if k == 0:
            catf[1 : side + 1] = jnp.zeros((side, rows, 640), F32)
        catf[1 + dy : 1 + dy + side, :, 0:512] += q
        catf[1 + dy : 1 + dy + side, :, 512:640] += r
    acc[...] = jnp.zeros_like(acc)

    def inner_back(y):
        parts = [catf[y + 1, :, 128 * t : 128 * t + 128] for t in range(5)]
        inner_up(clips, zin[y], untap(clips, parts[:4], parts[4]), st3, beta, acc, din, y)

    loop(side, inner_back)
    pack_stats(clips, loc6, acc, INNER)
    exchange_start(loc6, buf6, ss6, rs6)
    accm[...] = dot_tn(cat[...], dzc_b)
    exchange_finish(loc6, buf6, ss6, rs6, sums6, INNER)

    def dz_inner(y):
        for t in range(2):
            dz1[y, :, 384 + 128 * t : 512 + 128 * t] = inner_dz(
                clips, t, zin[y], din[y], st3, sums6, count
            )

    loop(side, dz_inner)
    dz1_b = dz1[...].reshape(total, 640).astype(BF16)
    hgv = dot_nt(dz1_b, wp[...]).astype(BF16).astype(F32)
    hg[:, :, :, 0:D] = hgv.reshape(side, side, 8, D)
    hg[:, :, :, D:DP] = jnp.zeros((side, side, 8, DP - D), F32)
    acc7[...] = jnp.zeros_like(acc7)

    def upstream(y):
        for t in range(7):
            lanes = pl.ds(128 * t, 128)
            gr = hg[y, :, :, lanes]
            acc7[0, :, lanes] += jnp.sum(gr * asum[y, :, :, lanes], axis=0)
            acc7[1, :, lanes] += jnp.sum(gr * bsum[y, :, :, lanes], axis=0)

    loop(side, upstream)
    pack_stats(clips, loc7, acc7, FINAL)
    exchange_start(loc7, buf7, ss7, rs7)
    accs[...] = dot_tn(scat[...], dzs_b)
    accp[...] = dot_tn(hbuf[...], dz1_b)
    pool = dz1[:, :, 256:384].reshape(total, 128)
    rest = (pool - dz1_b[:, 256:384].astype(F32)).astype(BF16)
    accp[:, 256:384] += dot_tn(hbuf[...], rest)
    c = jnp.concatenate([typical(beta1[0:1, 0:D]), jnp.zeros((8, DP - D), F32)], 1)
    full = accp[...] - outer(c, accp[DP - 1 : DP, :])
    mid = centre_mid(accm[992:993, :], beta)
    small = centre_small(accs, beta)
    for k, packed in enumerate((packed0, packed1, packed2)):
        pack_mid(packed, accm.at[512 * k : 512 * k + 512], mid, accs, small, k)

    def column(t, r, rows):
        return full[r : r + rows, 128 * t : 128 * t + 128]

    pack_one(packed3, column)
    pack_inner(packed4, column, accs, small)
    exchange_finish(loc7, buf7, ss7, rs7, sums7, FINAL)
    mine.wait()
    theirs.wait()


def pack_mid(packed, acc, mid, accs, small, k):
    for t in range(8):
        lanes = slice(128 * t, 128 * t + 128)
        packed[t, 0:480] = (acc[0:480, lanes] - mid[0:480, lanes]).astype(BF16)
        packed[t, 480:512] = small_piece(accs, small, 8 * k + t)
        if packed.shape[1] > 512:
            packed[t, 512:] = jnp.zeros((packed.shape[1] - 512, 128), BF16)


def small_piece(accs, small, b):
    dy, dt, dx = b // 9, b // 3 % 3, b % 3
    lanes = slice(128 * dx, 128 * dx + 128)
    r = 128 * dy + 32 * dt
    return (accs[r : r + 32, lanes] - small[32 * dt : 32 * dt + 32, lanes]).astype(BF16)


def pack_one(packed, column):
    end = packed.shape[1]
    for j in range(8):
        packed[j, 0:208] = column(j // 4, 208 * (j % 4), 208).astype(BF16)
        rows = min(112, D - 112 * j)
        packed[j, 208 : 208 + rows] = column(2, 112 * j, rows).astype(BF16)
        if 208 + rows < end:
            packed[j, 208 + rows : end] = jnp.zeros((end - 208 - rows, 128), BF16)


def pack_inner(packed, column, accs, small):
    end = packed.shape[1]
    for j in range(8):
        packed[j, 0:208] = column(3 + j // 4, 208 * (j % 4), 208).astype(BF16)
        packed[j, 208:end] = jnp.zeros((end - 208, 128), BF16)
        if j < 3:
            packed[j, 208:240] = small_piece(accs, small, 24 + j)


def inner_up(clips, z, backs, st, beta, acc, din, y):
    for t in range(2):
        lanes = pl.ds(384 + 128 * t, 128)
        scale, mean = affine(st, lanes)
        u = (z[:, 128 * t : 128 * t + 128] - mean) * scale
        d = backs[t] * clips.times(sigm(u + beta[0:1, pl.ds(896 + 128 * t, 128)]), clips.valid)
        din[y, :, 128 * t : 128 * t + 128] = d
        add_stats(clips, acc, lanes, d, u)


def inner_dz(clips, t, z, d, st, sums, count):
    lanes = pl.ds(384 + 128 * t, 128)
    here = slice(128 * t, 128 * t + 128)
    scale, mean = affine(st, lanes)
    u = (z[:, here] - mean) * scale
    m1, m2 = sums[0:1, lanes] / count, sums[1:2, lanes] / count
    dz = clips.times((d[:, here] - m1 - u * m2) * scale, clips.valid)
    return lane_below(dz, 64) if t == 1 else dz


def put_halves(ref, y, lane, v):
    side, lanes = v.shape[0] // 16, v.shape[1]
    v = v.reshape(side, 2, 8, lanes)
    for h in range(2):
        ref[h, y, :, lane : lane + lanes] = v[:, h].reshape(side * 8, lanes).astype(BF16)


SCHEDULE = {
    "start": ((1, 0), (0, 0), (2, 0), (3, 0), (4, 0),),
    "dz3": ((1, 1), (0, 1),),
    "dz4": ((2, 1), (3, 1), (4, 1),),
    "dz5": ((1, 2),),
    "dzend": ((0, 2),),
    "box": ((2, 2),),
    "scat": ((3, 2), (4, 2),),
    "m1": ((1, 3),),
    "d1": ((6, 0), (0, 3), (2, 3), (3, 3), (4, 3),),
    "m0": ((1, 4),),
    "d0": ((6, 1), (5, 0), (0, 4),),
    "m2": ((2, 4),),
    "d2": ((6, 2), (5, 1), (7, 0), (3, 4), (4, 4),),
    "e": ((6, 3), (7, 1), (8, 0), (1, 5),),
    "cb0": ((0, 5),),
    "cb1": ((5, 2), (8, 1),),
    "cb2": ((7, 2), (2, 5), (3, 5),),
    "cb3": ((1, 6), (4, 5),),
    "cb4": ((5, 3), (0, 6),),
    "cb5": ((6, 4), (8, 2),),
    "cb6": ((7, 3), (2, 6),),
    "s8a": ((5, 4), (3, 6),),
    "s8b": ((6, 5), (7, 4), (1, 7), (0, 7), (4, 6),),
    "dzi": ((5, 5), (8, 3),),
    "l": ((9, 0), (2, 7),),
    "in0": ((7, 5), (3, 7),),
    "in1": ((6, 6),),
    "in2": ((9, 1), (8, 4), (4, 7),),
    "in4": ((5, 6),),
    "in5": ((7, 6),),
    "in6": ((8, 5),),
    "in9": ((6, 7),),
    "in10": ((9, 2),),
    "in13": ((5, 7),),
    "end": ((7, 7), (8, 6), (9, 3), (8, 7), (9, 4), (9, 5), (9, 6), (9, 7),),
}


def backward_kernel(
    bits, len_ref, hg, stf, sums7, st1, beta, sums5, sums6,
    zf, sig, zin_in, wf_in, ws_in, wp_in, cat_in, scat_in, x, x_got, two0, two1, two2, two3, two4,
    gin, full0, full1, full2, full3, full4, offs,
    zin, wf, ws, wp, dzc, dzs, dz1, dzi, sums8, snd, got,
    acc, loc, buf, ss8, rs8, lsem, csend, crecv, ssem, rsem, gsend, grecv, *arrays,
):
    greet(partner=True)
    sec = lax.axis_index("section")
    side = dz1.shape[1]
    half = side // 2
    rows = side * 16
    clips = Clips(len_ref, 16, 1)
    count = stf[2:3, 0:128]
    loads = [
        pltpu.make_async_copy(a, b, lsem.at[i])
        for i, (a, b) in enumerate(((zin_in, zin), (wf_in, wf), (ws_in, ws), (wp_in, wp)))
    ]
    two = (two0, two1, two2, two3, two4)
    full = (full0, full1, full2, full3, full4)
    own_two, ones = arrays[0:5], arrays[5:10]
    core_land = arrays[10:20]
    pieces = 2 ** len(groups(bits)[-1]) - 1 + len(groups(bits)) - 1
    lands = arrays[20:]

    def part(ref, which):
        h = ref.shape[1] // 2
        return ref.at[:, pl.ds(pl.multiple_of(which * h, 16), h)]

    def reducer(i, q, base, rows, swap_src, flip, load):
        return Reducer(
            bits, i, q, base, rows, swap_src, core_land[i], lands[pieces * i : pieces * i + pieces],
            csend, crecv, ssem, rsem, flip, load,
        )

    g, h = [], []
    for i, (a, b) in enumerate(zip(two, own_two)):
        load = pltpu.make_async_copy(part(a, sec), b, lsem.at[4 + i])
        loads.append(load)
        g.append(reducer(i, b, 0, b.shape[1], part(a, 1 - sec), 1 - sec, load))
    for i, a in enumerate(ones):
        rows_half = a.shape[1] // 2
        h.append(
            reducer(5 + i, a, sec * rows_half, rows_half, part(a, 1 - sec), sec, None)
        )
    for c in loads:
        c.start()

    def at(name):
        for r, e in SCHEDULE.get(name, ()):
            (g + h)[r].event(e)

    acc[...] = jnp.zeros_like(acc)
    loc[...] = jnp.zeros_like(loc)
    for y in (0, side + 1):
        dzc[y] = jnp.zeros(dzc.shape[1:], BF16)
        dzs[y] = jnp.zeros(dzs.shape[1:], BF16)

    def dz_phase(zb, sb, scr, yp, tx, zsem):
        def fetch(k, slot):
            here = pl.ds(2 * k, 2)
            return (
                pltpu.make_async_copy(zf.at[here], zb.at[slot], zsem.at[0, slot]),
                pltpu.make_async_copy(sig.at[here], sb.at[slot], zsem.at[1, slot]),
            )

        for c in fetch(0, 0):
            c.start()

        def body(k):
            slot = lax.rem(k, 2)

            @pl.when(k < half - 1)
            def _():
                for c in fetch(k + 1, 1 - slot):
                    c.start()

            @pl.when(k == 1)
            def _():
                greeted(partner=True)
                at("start")

            for j in range(2, half):
                pl.when(k == j)(lambda j=j: at(f"dz{j}"))
            for c in fetch(k, slot):
                c.wait()
            tiles = ([], [])
            for t in range(7):
                lanes = pl.ds(128 * t, 128)
                scale, mean = affine(stf, lanes)
                m1, m2 = sums7[0:1, lanes] / count, sums7[1:2, lanes] / count
                gr = hg[k, :, :, lanes] * 0.125
                scr[:, pl.ds(0, 8, stride=2), :] = gr
                scr[:, pl.ds(1, 8, stride=2), :] = gr
                gr = scr[...]
                gr = jnp.broadcast_to(gr[:, None], (half, 2, 16, 128)).reshape(rows, 128)
                for q in range(2):
                    u = (zb[slot, q, :, lanes] - mean) * scale
                    d = gr * sb[slot, q, :, lanes].astype(F32)
                    dz = clips.times((d - m1 - u * m2) * scale, clips.valid)
                    if t < 2:
                        put_halves(dz1, 2 * k + q, 128 * t, dz)
                    else:
                        tiles[q].append(dz)
            for q in range(2):
                y = 2 * k + q
                small, tail, pool = split_final(*tiles[q][2:])
                yp[y] = clips.times(pool * inv_edges(side, 16, y), clips.inv)

                def put(ref, y=y):
                    def go(lane, v):
                        ref[y + 1, :, lane : lane + v.shape[-1]] = v.astype(BF16)

                    return go

                put_spread(
                    16, jnp.concatenate(tiles[q][:2], 1), small, tail, put(dzc), put(dzs)
                )

        loop(half, body)
        at("dzend")

        def boxed(y, v):
            put_halves(dz1, y, 256, clips.times(v, clips.valid))

        box(clips, side, lambda y: yp[y], tx, boxed)
        at("box")

    pl.run_scoped(
        dz_phase,
        vmem(2, 2, rows, DP),
        vmem(2, 2, rows, DP, dtype=BF16),
        vmem(half, 16, 128),
        vmem(side, rows, 128),
        vmem(side + 2, rows, 128),
        pltpu.SemaphoreType.DMA((2, 2)),
    )

    def grad_phase(cat, scat, accm, mid, accs, x0, x1, accp, sems):
        copies = [
            pltpu.make_async_copy(a, b, sems.at[i])
            for i, (a, b) in enumerate(
                ((cat_in, cat), (scat_in, scat), (x.at[sec], x0), (x_got, x1))
            )
        ]
        for c in copies:
            c.start()
        for c in copies[:2]:
            c.wait()
        ny = side // 2

        def take(ref, y):
            return ref[pl.ds(y, ny)].reshape(ny * rows, ref.shape[-1])

        def sums(k, between):
            accm[...] = dot_tn(take(cat, 1), take(dzc, 2 - k))
            between()
            accm[...] += dot_tn(take(cat, 1 + ny), take(dzc, 2 - k + ny))

        for k in range(3):
            here = slice(128 * k, 128 * k + 128)
            accs[here] = dot_tn(take(scat, 1), take(dzs, 2 - k))
            accs[here] += dot_tn(take(scat, 1 + ny), take(dzs, 2 - k + ny))
        small = centre_small(accs, beta)
        at("scat")
        for k in (1, 0, 2):
            sums(k, lambda: at(f"m{k}"))
            if k == 1:
                mid[...] = centre_mid(accm[480:481, :], beta)
            pack_mid(ones[k], accm, mid, accs, small, k)
            at(f"d{k}")
        for c in copies[2:]:
            c.wait()
        accp[...] = jnp.zeros_like(accp)
        add_outer(accp, dz1, ((x1, 1 - sec), (x0, sec)))
        pack_one(ones[3], lambda t, r, n: accp[r : r + n, 128 * t : 128 * t + 128])
        pack_inner(ones[4], lambda t, r, n: jnp.zeros((n, 128), F32), accs, small)
        at("e")

    def add_outer(accp, d_ref, sides):
        step = side // 2
        size = step * side * 8
        for src, which in sides:

            def body(i, src=src, which=which):
                at = pl.ds(pl.multiple_of(i * size, 16), size)
                d = d_ref[which, pl.ds(i * step, step)].reshape(size, d_ref.shape[-1])
                accp[...] += dot_tn(src[at], d)

            loop(side // step, body)

    pl.run_scoped(
        grad_phase,
        vmem(side + 2, rows, 512, dtype=BF16),
        vmem(side + 2, rows, 128, dtype=BF16),
        vmem(512, 1024),
        vmem(512, 1024),
        vmem(384, 384),
        vmem(side * side * 8, D, dtype=BF16),
        vmem(side * side * 8, D, dtype=BF16),
        vmem(D, 384),
        pltpu.SemaphoreType.DMA((4,)),
    )

    def last_phase(din, x0, x1, ring, accp, sems):
        own = pltpu.make_async_copy(x.at[sec], x0, sems.at[0])
        other = pltpu.make_async_copy(x_got, x1, sems.at[1])
        own.start()
        other.start()
        for c in loads[:4]:
            c.wait()
        ny = 2

        def body(i):
            y0 = i * ny + 1
            for j in range(side // ny):
                pl.when(i == j)(lambda j=j: at(f"cb{j}"))
            q = s = None
            for dy in (-1, 0, 1):
                k = dy + 1
                here = pl.ds(y0 - dy, ny)
                t = dot_nt(dzc[here].reshape(ny * rows, 1024), wf[512 * k : 512 * k + 512])
                q = t if q is None else q + t
                t = dot_nt(dzs[here].reshape(ny * rows, 384), ws[128 * k : 128 * k + 128])
                s = t if s is None else s + t
            for j in range(ny):
                y = i * ny + j
                here = slice(j * rows, (j + 1) * rows)
                parts = [q[here, 128 * t : 128 * t + 128] for t in range(4)]
                inner_up(clips, zin[y], untap(clips, parts, s[here]), st1, beta, acc, din, y)

        loop(side // ny, body)
        pack_stats(clips, loc, acc, INNER)
        exchange_start(loc, buf, ss8, rs8)
        at("s8a")
        other.wait()
        own.wait()
        sides = ((x1, 1 - sec), (x0, sec))
        step = side // 2
        size = step * side * 8
        exchange_finish(loc, buf, ss8, rs8, sums8, INNER)
        at("s8b")

        def dz(y):
            for t in range(2):
                put_halves(dzi, y, 128 * t, inner_dz(clips, t, zin[y], din[y], st1, sums8, count))

        loop(side, dz)
        at("dzi")
        accp[...] = jnp.zeros_like(accp)
        add_outer(accp, dzi, sides)
        for j in range(8):
            ones[4][j, 0:208] = accp[
                208 * (j % 4) : 208 * (j % 4) + 208, 128 * (j // 4) : 128 * (j // 4) + 128
            ].astype(BF16)
        at("l")
        sent = []
        step = 2
        size = step * side * 8
        chunks = side // step
        for p in range(2 * chunks):
            which = sides[p // chunks][1]
            i = p % chunks
            slot = p % 2
            if p >= 2:
                sent[p - 2].wait()
            here = pl.ds(i * step, step)
            d = jnp.concatenate([dz1[which, here], dzi[which, here]], -1).reshape(size, 640)
            ring[slot] = dot_nt(d, wp[...]).astype(BF16)
            to = gin.at[sec, i * size : (i + 1) * size]
            if p < chunks:
                c = swap_copy(ring.at[slot], to, gsend.at[i], grecv.at[i])
            else:
                c = pltpu.make_async_copy(ring.at[slot], to, sems.at[2 + slot])
            c.start()
            sent.append(c)
            at(f"in{p}")
        sent[-2].wait()
        sent[-1].wait()

    dma = pltpu.SemaphoreType.DMA
    pl.run_scoped(
        last_phase,
        vmem(side, rows, 256),
        vmem(side * side * 8, D, dtype=BF16),
        vmem(side * side * 8, D, dtype=BF16),
        vmem(2, 2 * side * 8, D, dtype=BF16),
        vmem(D, 256),
        dma((4,)),
    )
    snd[:, 0:DP] = jnp.where(sec == 0, sums5[...], sums7[...])
    snd[:, DP : DP + 640] = jnp.where(sec == 0, sums6[...], sums8[...])
    small = swap_copy(snd, got, csend.at[15], crecv.at[15])
    small.start()
    at("end")

    def finish(mine, theirs):
        copies = []
        for i, (dst, m, t) in enumerate(zip(full, mine, theirs)):
            copies.append(pltpu.make_async_copy(m, dst.at[sec], lsem.at[9 + i]))
            copies.append(swap_copy(t, dst.at[sec], csend.at[10 + i], crecv.at[10 + i]))
        for c in copies:
            c.start()
        for c in copies:
            c.wait()

    pl.when(sec == 0)(lambda: finish(core_land[5:10], core_land[0:5]))
    pl.when(sec == 1)(lambda: finish(core_land[0:5], core_land[5:10]))
    small.wait()
    for lanes, a, b in ((slice(0, DP), sums7, sums5), (slice(DP, DP + 640), sums8, sums6)):
        offs[:, lanes] = jnp.where(sec == 0, a[...], b[...]) + got[:, lanes]


def put_halves(ref, y, lane, v):
    side, lanes = v.shape[0] // 16, v.shape[1]
    v = v.reshape(side, 2, 8, lanes)
    for h in range(2):
        ref[h, y, :, lane : lane + lanes] = v[:, h].reshape(side * 8, lanes).astype(BF16)


def groups(bits):
    if bits < 3:
        return [(k,) for k in range(bits)]
    return [(k,) for k in range(bits - 2)] + [(bits - 2, bits - 1)]


class Reducer:
    EVENTS = 8

    def __init__(
        self, bits, index, q, base, rows, swap_src, core_land, land, csend, crecv, ssem, rsem, flip, load
    ):
        self.index, self.q, self.base, self.rows = index, q, base, rows
        self.core_land, self.land, self.load = core_land, land, load
        self.ssem, self.rsem = ssem, rsem
        self.swap = swap_copy(swap_src, core_land, csend.at[index], crecv.at[index])
        me = lax.axis_index("dp")
        plan = groups(bits)
        self.count = len(plan)
        self.last = 2 * self.count
        self.steps = []
        tiles, t0, r0 = 8, 0, 0
        at = 0
        for step, ks in enumerate(plan):
            powers = []
            for k in ks:
                power = 1 << k
                if bits > 1 and k < 2:
                    power = power + flip * ((1 << (1 - k)) - power)
                powers.append((power, lax.rem(me // power, 2)))
            cuts = []
            for power, bit in powers:
                if tiles > 1:
                    tiles //= 2
                    cuts.append((bit, tiles, 0))
                else:
                    rows //= 2
                    cuts.append((bit, 0, rows))
            sends = []
            for c in range(1, 1 << len(ks)):
                partner, t, r = me, t0, r0
                for i, ((power, bit), (_, dt, dr)) in enumerate(zip(powers, cuts)):
                    turned = (c >> i) & 1
                    partner = partner + turned * (1 - 2 * bit) * power
                    here = bit + turned * (1 - 2 * bit)
                    t, r = t + here * dt, r + here * dr
                sends.append((partner, (t, r), at))
                at += 1
            for bit, dt, dr in cuts:
                t0, r0 = t0 + bit * dt, r0 + bit * dr
            self.steps.append((sends, (t0, r0), tiles, rows))
        self.pieces = at

    def region(self, ref, base, at, tiles, rows):
        t, r = at
        r = base + r
        if not isinstance(r, int):
            r = pl.multiple_of(r, 16)
        return ref.at[pl.ds(t, tiles), pl.ds(r, rows)]

    def mine(self, at, tiles, rows):
        return self.region(self.q, self.base, at, tiles, rows)

    def total(self, at, tiles, rows):
        return self.region(self.core_land, 0, at, tiles, rows)

    def copies(self, i):
        if i == 0:
            return [self.swap]
        halving = i <= self.count
        sends, keep, tiles, rows = self.steps[i - 1 if halving else self.last - i]
        out = []
        for partner, send, piece in sends:
            src = self.mine(send, tiles, rows) if halving else self.total(keep, tiles, rows)
            sem = 2 * (self.index * self.pieces + piece) + int(halving)
            out.append(
                pltpu.make_async_remote_copy(
                    src_ref=src,
                    dst_ref=self.land[piece] if halving else src,
                    send_sem=self.ssem.at[sem],
                    recv_sem=self.rsem.at[sem],
                    device_id={"dp": partner},
                    device_id_type=MESH,
                )
            )
        return out

    def received(self, i):
        sends, keep, tiles, rows = self.steps[self.last - i]
        out = []
        for partner, send, piece in sends:
            sem = 2 * (self.index * self.pieces + piece)
            dst = self.total(send, tiles, rows)
            out.append(
                pltpu.make_async_remote_copy(
                    src_ref=dst,
                    dst_ref=dst,
                    send_sem=self.ssem.at[sem],
                    recv_sem=self.rsem.at[sem],
                    device_id={"dp": partner},
                    device_id_type=MESH,
                )
            )
        return out

    def add(self, dst, q, lands, tiles, rows):
        chunk = next(c for c in range(min(rows, 256), 0, -16) if rows % c == 0 and c % 16 == 0)
        parts = rows // chunk

        def body(j):
            t, r = j // parts, pl.multiple_of(lax.rem(j, parts) * chunk, 16)
            at = pl.ds(r, chunk)
            total = q[t, at].astype(F32)
            for land in lands:
                total = total + land[t, at].astype(F32)
            dst[t, at] = total.astype(BF16)

        loop(tiles * parts, body)

    def finish(self, i):
        if i > self.count:
            for c in self.copies(i):
                c.wait_send()
            for c in self.received(i):
                c.wait_recv()
            return
        for c in self.copies(i):
            c.wait()
        if i == 0:
            if self.load is not None:
                self.load.wait()
            q = self.mine((0, 0), 8, self.rows)
            self.add(q, q, [self.core_land], 8, self.rows)
        else:
            sends, keep, tiles, rows = self.steps[i - 1]
            lands = [self.land[piece] for _, _, piece in sends]
            q = self.mine(keep, tiles, rows)
            dst = self.total(keep, tiles, rows) if i == self.count else q
            self.add(dst, q, lands, tiles, rows)

    def event(self, e):
        count = self.last + 2
        for i in range(e * count // self.EVENTS, (e + 1) * count // self.EVENTS):
            if i > 0:
                self.finish(i - 1)
            if i <= self.last:
                for c in self.copies(i):
                    c.start()


def land_shapes(tiles, rows, bits):
    out = []
    for ks in groups(bits):
        for _ in ks:
            if tiles > 1:
                tiles //= 2
            else:
                rows //= 2
        out += [(tiles, rows, 128)] * (2 ** len(ks) - 1)
    return out


def unpack_kernel(
    full0, full1, full2, full3, full4, gin_in, out_in, offs,
    one, mid_in, mid, small_in, small, pool, offset, gin, out,
    buf0, buf1, buf2, buf3, buf4, nat, inner, gin_buf, out_buf, sem,
):
    copies = []
    bufs = (buf0, buf1, buf2, buf3, buf4)
    for i, (full, buf) in enumerate(zip((full0, full1, full2, full3, full4), bufs)):
        half = full.shape[2]
        for h in range(2):
            copies.append(
                pltpu.make_async_copy(full.at[h], buf.at[:, h * half : (h + 1) * half], sem.at[2 * i + h])
            )
    for c in copies:
        c.start()
    through = ((gin_in, gin_buf, gin), (out_in, out_buf, out))
    for i, (src, buf, dst) in enumerate(through):
        pltpu.make_async_copy(src, buf, sem.at[10 + i]).start()
    v = offs[...]
    lane = lax.broadcasted_iota(jnp.int32, v.shape, 1)
    out = jnp.where(lane < 256, v, 0.0)
    for lo, hi, by in ((256, 416, -1024), (416, 736, 160), (736, 768, -704), (768, 1024, 192)):
        out = jnp.where((lane >= lo) & (lane < hi), roll_lanes(v, by), out)
    offset[...] = out[0:1, 0:1024]
    for c in copies:
        c.wait()

    def take(b, t, r, rows):
        return bufs[b][t, r : r + rows].astype(F32)

    for dt in range(3):
        for dy in range(3):
            for dx in range(3):
                to = 160 * (9 * dt + 3 * dy + dx)
                for rows, r in ((128, 128 * dt), (32, 384 + 32 * dt)):
                    nat[to : to + rows, 0:128] = take(dy, 2 * dx, r, rows)
                    nat[to : to + rows, 128:256] = take(dy, 2 * dx + 1, r, rows)
                    tail = take(dy, 6 + dx // 2, r, rows)
                    nat[to : to + rows, 256:384] = roll_lanes(tail, 64) if dx == 1 else tail
                    to = to + rows
                b = 9 * dy + 3 * dt + dx
                to = 32 * (9 * dt + 3 * dy + dx)
                small[to : to + 32, :] = (
                    take(b // 8, b % 8, 480, 32) if b < 24 else take(4, b - 24, 208, 32)
                )

    def turn(i):
        at = pl.ds(pl.multiple_of(i * 128, 128), 128)
        mid[0:256, at] = nat[at, 0:256].T
        mid[256:320, at] = nat[at, 256:384].T[0:64]

    total = mid.shape[1]
    passed = []
    for i, (src, buf, dst) in enumerate(through):
        pltpu.make_async_copy(src, buf, sem.at[10 + i]).wait()
        passed.append(pltpu.make_async_copy(buf, dst, sem.at[10 + i]))
        passed[i].start()
    loop(total // 128, turn)
    at = slice(total - total % 128, total)
    mid[0:256, at] = nat[at, 0:256].T
    mid[256:320, at] = nat[at, 256:384].T[0:64]
    for j in range(8):
        at = slice(208 * (j % 4), 208 * (j % 4) + 208)
        one[at, 128 * (j // 4) : 128 * (j // 4) + 128] = take(3, j, 0, 208)
        inner[j // 4, at] = take(4, j, 0, 208)
        rows = min(112, D - 112 * j)
        pool[112 * j : 112 * j + rows, :] = take(3, j, 208, rows)
    for r in range(0, D, 128):
        at = slice(r, min(r + 128, D))
        mid_in[0:128, at] = inner[0, at].T
        last = inner[1, at].T
        mid_in[128:160, at] = last[0:32]
        small_in[:, at] = last[32:64]
    for c in passed:
        c.wait()


def vmem(*shape, dtype=F32):
    return pltpu.VMEM(shape, dtype)


def call(kernel, outs, args, scratch, collective=None, smem_first=True, any_in=(), any_out=()):
    def specs(count, anywhere):
        return [
            pl.BlockSpec(memory_space=pl.ANY if i in anywhere else pltpu.VMEM)
            for i in range(count)
        ]

    in_specs = specs(len(args), any_in)
    if smem_first:
        in_specs[0] = pl.BlockSpec(memory_space=pltpu.SMEM)
    params = {"vmem_limit_bytes": VMEM_LIMIT}
    if collective is not None:
        params.update(collective_id=collective, has_side_effects=True)
    return pl.pallas_call(
        kernel,
        out_shape=[jax.ShapeDtypeStruct(shape, dtype) for shape, dtype in outs],
        in_specs=in_specs,
        out_specs=specs(len(outs), any_out),
        scratch_shapes=scratch,
        compiler_params=pltpu.CompilerParams(**params),
    )(*args)


def on_device(
    clip_input, out_grad, clip_lengths, w_one, w_mid_in, w_mid, w_small_in, w_small, w_pool, bn_offset
):
    n = lax.axis_size("dp")
    bits = n.bit_length() - 1
    half, side = clip_input.shape[1], clip_input.shape[2]
    rows = side * 16
    side2 = side // 2
    rows2 = side2 * 8
    total2 = side2 * rows2
    unit = 32 << max(bits - 3, 0)
    packed_rows = [-(-r // unit) * unit for r in (512, 512, 512, 320, 256)]
    x = clip_input.transpose(0, 2, 3, 1, 4).reshape(2, side * side * half, D)
    og = out_grad.transpose(0, 2, 3, 1, 4)

    def like(a, dtype=BF16):
        return pltpu.VMEM(a.shape[1:], dtype)

    def turned(w):
        return w.transpose(0, 2, 1)

    weights = (w_one, turned(w_mid_in), turned(w_small_in), w_pool, turned(w_mid), w_small)
    dma = pltpu.SemaphoreType.DMA
    grid = (side, side, 2, 8)

    def bf(*shape):
        return vmem(*shape, dtype=BF16)

    pooled = (side2, side2, 8, DP)
    st1, stf, beta1, beta2, xgot, zin, zf, sig, hand, asum, bsum, cat, scat, *arranged, og_got = call(
        forward_kernel,
        [
            ((8, 640), F32),
            ((8, DP), F32),
            ((1, 1152), F32),
            ((1, 1152), F32),
            (x.shape[1:], BF16),
            (grid + (256,), F32),
            (grid + (DP,), F32),
            ((side, rows, DP), BF16),
            (pooled, F32),
            (pooled, F32),
            (pooled, F32),
            ((side + 2, rows, 512), BF16),
            ((side + 2, rows, 128), BF16),
            ((D, 640), BF16),
            ((D, 640), BF16),
            ((1536, 1024), BF16),
            ((1536, 1024), BF16),
            ((384, 384), BF16),
            ((384, 384), BF16),
            (og.shape[1:], BF16),
        ],
        (clip_lengths, bn_offset, x, og) + weights,
        [
            like(x),
            vmem(*grid, DP),
            vmem(*grid, 256),
            vmem(side, rows, 128),
            bf(side + 2, rows, 512),
            bf(side + 2, rows, 128),
            bf(side, rows, DP),
            vmem(*pooled),
            vmem(*pooled),
            vmem(*pooled),
            vmem(side2, 16, 128),
            vmem(1, 1152),
            vmem(1, 1152),
            bf(2, D, 640),
            bf(2, 1536, 1024),
            bf(2, 384, 384),
            vmem(8, 512),
            vmem(2, 2, 8, 640),
            vmem(2, 16, 640),
            vmem(2, 16, 512),
        ]
        + exchange_scratch(n, 16)
        + exchange_scratch(n, 8)
        + [dma((15,)), dma((6,)), dma((6,))],
        collective=1,
        any_in=range(2, 10),
        any_out=range(4, 20),
    )
    wp1, wp2, wf1, wf2, ws1, ws2 = arranged
    zin = zin.reshape(side, rows, 256)
    zf = zf.reshape(side, rows, DP)
    block_output, hg, *two, sums5, sums6, sums7 = call(
        second_kernel,
        [
            (og.shape, BF16),
            ((side2, side2, 8, DP), F32),
        ]
        + [((8, r, 128), BF16) for r in packed_rows]
        + [
            ((8, DP), F32),
            ((8, 640), F32),
            ((8, DP), F32),
        ],
        (clip_lengths, hand, asum, bsum, og, og_got, wp2, wf2, ws2, beta2, beta1),
        [
            like(og),
            vmem(side2, side2, 8, D),
            vmem(2, *og.shape[1:], dtype=BF16),
            dma((2,)),
            dma(()),
            dma(()),
            vmem(total2, DP, dtype=BF16),
            vmem(side2, rows2, 256),
            vmem(side2, rows2, 128),
            vmem(side2, rows2, DP),
            vmem(8, DP),
            vmem(side2, rows2, 128),
            vmem(side2 + 2, rows2, 128),
            vmem(side2 + 2, rows2, 640),
            vmem(total2, 1536, dtype=BF16),
            vmem(total2, 384, dtype=BF16),
            vmem(side2, rows2, 1024),
            vmem(side2, rows2, 384),
            vmem(side2, rows2, DP),
            vmem(side2, rows2, 1024),
            vmem(side2, rows2, 384),
            vmem(side2, rows2, 640),
            vmem(side2, rows2, 256),
            vmem(2, 8, 640),
            vmem(8, 640),
            vmem(8, 512),
            vmem(2, 8, DP),
            vmem(1536, 1024),
            vmem(384, 384),
            vmem(DP, 640),
        ]
        + exchange_scratch(n, 16)
        + exchange_scratch(n, 8)
        + exchange_scratch(n, 16)
        + exchange_scratch(n, 8)
        + exchange_scratch(n, 16),
        collective=2,
        any_in=(4,),
        any_out=(0,),
    )
    halves = [r // 2 for r in packed_rows]
    lands = []
    for h in halves * 2:
        lands += [bf(*shape) for shape in land_shapes(8, h, bits)]
    gin, *full, offs = call(
        functools.partial(backward_kernel, bits),
        [(x.shape, BF16)]
        + [((2, 8, h, 128), BF16) for h in halves]
        + [((8, DP + 640), F32)],
        (clip_lengths, hg, stf, sums7, st1, beta1, sums5, sums6)
        + (zf, sig, zin, wf1, ws1, wp1, cat, scat, x, xgot, *two),
        [
            vmem(side, rows, 256),
            bf(1536, 1024),
            bf(384, 384),
            bf(D, 640),
            bf(side + 2, rows, 1024),
            bf(side + 2, rows, 384),
            bf(2, side, rows // 2, 384),
            bf(2, side, rows // 2, 256),
            vmem(8, 640),
            vmem(8, DP + 640),
            vmem(8, DP + 640),
            vmem(2, 16, 640),
        ]
        + exchange_scratch(n, 8)
        + [dma((14,)), dma((16,)), dma((16,)), dma((2 * len(lands),)), dma((2 * len(lands),))]
        + [dma((side,)), dma((side,))]
        + [bf(8, h, 128) for h in halves]
        + [bf(8, r, 128) for r in packed_rows]
        + [bf(8, h, 128) for h in halves * 2]
        + lands,
        collective=3,
        any_in=range(8, 23),
        any_out=range(6),
    )
    one, mid_in, mid, small_in, small, pool, offset, gin, block_output = call(
        unpack_kernel,
        [
            ((D, C0), F32),
            ((C1A, D), F32),
            ((C1B, 27 * C1A), F32),
            ((C2A, D), F32),
            ((27 * C2A, C2B), F32),
            ((D, C3), F32),
            ((1, 1024), F32),
            (x.shape, BF16),
            (og.shape, BF16),
        ],
        (*full, gin, block_output, offs),
        [bf(8, r, 128) for r in packed_rows]
        + [vmem(27 * C1A, 384), vmem(2, D, 128), bf(*x.shape), bf(*og.shape), dma((12,))],
        smem_first=False,
        any_in=range(7),
        any_out=(7, 8),
    )
    input_grad = gin.reshape(2, side, side, half, D).transpose(0, 3, 1, 2, 4)
    return (
        block_output.transpose(0, 3, 1, 2, 4),
        input_grad,
        one[None],
        mid_in.T[None],
        mid.T[None],
        small_in.T[None],
        small[None],
        pool[None],
        offset,
    )


def solution(mesh):
    placed = (
        P("dp", "section", None, None, None),
        P("dp", "section", None, None, None),
        P("dp", None),
        P("section", None, None),
        P("section", None, None),
        P("section", None, None),
        P("section", None, None),
        P("section", None, None),
        P("section", None, None),
        P("section", None),
    )
    return jax.shard_map(
        on_device,
        mesh=mesh,
        in_specs=placed,
        out_specs=(
            P("dp", "section", None, None, None),
            P("dp", "section", None, None, None),
            P("section", None, None),
            P("section", None, None),
            P("section", None, None),
            P("section", None, None),
            P("section", None, None),
            P("section", None, None),
            P("section", None),
        ),
        check_vma=False,
    )
```

```python
import functools

import jax
import jax.numpy as jnp
from jax import lax
from jax.experimental import pallas as pl
from jax.experimental.pallas import tpu as pltpu
from jax.sharding import PartitionSpec as P

D = 832
DP = 896
C0 = 256
C1A = 160
C1B = 320
C2A = 32
C2B = 128
C3 = 128
EPS = 0.001
MESH = pl.DeviceIdType.MESH
F32 = jnp.float32
BF16 = jnp.bfloat16
VMEM_LIMIT = 60 * 2**20


def dot(a, b):
    return jnp.dot(a, b, preferred_element_type=F32)


def dot_nt(a, b):
    return lax.dot_general(a, b, (((1,), (1,)), ((), ())), preferred_element_type=F32)


def dot_tn(a, b):
    return lax.dot_general(a, b, (((0,), (0,)), ((), ())), preferred_element_type=F32)


def roll_rows(x, by):
    return pltpu.roll(x, by % x.shape[0], 0)


def roll_lanes(x, by):
    return pltpu.roll(x, by % x.shape[1], 1)


def lane_below(x, count):
    lanes = lax.broadcasted_iota(jnp.int32, x.shape, 1)
    return jnp.where(lanes < count, x, 0.0)


class Clips:
    def __init__(self, len_ref, frames, stride):
        sec = lax.axis_index("section")
        f = lax.broadcasted_iota(jnp.int32, (frames, 128), 0)

        def label(v):
            place = v * stride
            out = jnp.zeros_like(v)
            start = jnp.int32(0)
            for c in range(len_ref.shape[1]):
                end = start + len_ref[sec, c]
                out = jnp.where((place >= start) & (place < end), c + 1, out)
                start = end
            return out

        here = label(f)
        inside = here > 0

        def mask(m):
            return jnp.where(m, 1.0, 0.0).astype(F32)

        self.frames = frames
        self.valid = mask(inside)
        self.before = mask(inside & (f > 0) & (label(f - 1) == here))
        self.after = mask(inside & (f < frames - 1) & (label(f + 1) == here))
        self.inv = 1.0 / jnp.maximum(self.valid + self.before + self.after, 1.0)

    def times(self, v, pattern):
        return (v.reshape(-1, self.frames, 128) * pattern).reshape(v.shape)

    def fold(self, v):
        return jnp.sum(v.reshape(-1, self.frames, v.shape[-1]), axis=0)


def shift_places(v, frames, by):
    lanes = v.shape[-1]
    v3 = v.reshape(-1, frames, lanes)
    zero = jnp.zeros((1, frames, lanes), v.dtype)
    if by > 0:
        v3 = jnp.concatenate([v3[1:], zero], 0)
    else:
        v3 = jnp.concatenate([zero, v3[:-1]], 0)
    return v3.reshape(v.shape)


def add_stats(clips, acc, lanes, v, w=None):
    acc[0, :, lanes] += clips.fold(v)
    acc[1, :, lanes] += clips.fold(v * (v if w is None else w))


def affine(st, lanes):
    total, square, count = st[0:1, lanes], st[1:2, lanes], st[2:3, lanes]
    mean = total / count
    scale = lax.rsqrt(square / count - mean * mean + EPS)
    return scale, mean


def fill_norm(coef, to, st, lanes, beta):
    scale, mean = affine(st, lanes)
    coef[0:1, to] = scale
    coef[1:2, to] = mean * scale
    coef[2:3, to] = beta - mean * scale
    coef[3:4, to] = beta


def fill_back(coef, to, sums, lanes, count):
    m1, m2 = sums[0:1, lanes] / count, sums[1:2, lanes] / count
    scale = coef[0:1, to]
    coef[4:5, to] = -scale * scale * m2
    coef[5:6, to] = scale * (coef[1:2, to] * m2 - m1)


def soft(t):
    s = 0.5 + 0.5 * jnp.tanh(0.5 * jnp.abs(t))
    return jnp.maximum(t, 0.0) - jnp.log(s), jnp.where(t >= 0, s, 1.0 - s)


def sigm(t):
    return 0.5 + 0.5 * jnp.tanh(0.5 * t)


def greet(partner=False):
    n = lax.axis_size("dp")
    me = lax.axis_index("dp")
    barrier = pltpu.get_barrier_semaphore()

    def go(k, _):
        pl.semaphore_signal(
            barrier, inc=1, device_id={"dp": lax.rem(me + k, n)}, device_id_type=MESH
        )
        return 0

    if partner:
        other = 1 - lax.axis_index("section")
        pl.semaphore_signal(barrier, inc=1, device_id={"section": other}, device_id_type=MESH)
    lax.fori_loop(1, n, go, 0)


def greeted(partner=False):
    pl.semaphore_wait(pltpu.get_barrier_semaphore(), lax.axis_size("dp") - 1 + int(partner))


def exchange_start(loc, buf, ssem, rsem):
    n = lax.axis_size("dp")
    me = lax.axis_index("dp")

    def start(k, _):
        pltpu.make_async_remote_copy(
            src_ref=loc,
            dst_ref=buf.at[me],
            send_sem=ssem.at[k],
            recv_sem=rsem.at[me],
            device_id={"dp": lax.rem(me + k, n)},
            device_id_type=MESH,
        ).start()
        return 0

    lax.fori_loop(1, n, start, 0)
    buf[me] = loc[...]


def exchange_finish(loc, buf, ssem, rsem, out, tiles):
    n = lax.axis_size("dp")
    me = lax.axis_index("dp")

    def wait(k, _):
        j = lax.rem(me + k, n)
        copy = pltpu.make_async_remote_copy(
            src_ref=loc,
            dst_ref=buf.at[j],
            send_sem=ssem.at[k],
            recv_sem=rsem.at[j],
            device_id={"dp": j},
            device_id_type=MESH,
        )
        copy.wait_send()
        copy.wait_recv()
        return 0

    lax.fori_loop(1, n, wait, 0)
    total = jnp.sum(buf[...], axis=0)
    at = 2 * len(tiles)
    for i, t in enumerate(tiles):
        lanes = slice(128 * t, 128 * t + 128)
        out[0:1, lanes] = total[2 * i : 2 * i + 1]
        out[1:2, lanes] = total[2 * i + 1 : 2 * i + 2]
        if at < loc.shape[0]:
            out[2:3, lanes] = total[at : at + 1]


def exchange(loc, buf, ssem, rsem, out, tiles):
    exchange_start(loc, buf, ssem, rsem)
    exchange_finish(loc, buf, ssem, rsem, out, tiles)


def swap_copy(src, dst, ssem, rsem):
    return pltpu.make_async_remote_copy(
        src_ref=src,
        dst_ref=dst,
        send_sem=ssem,
        recv_sem=rsem,
        device_id={"section": 1 - lax.axis_index("section")},
        device_id_type=MESH,
    )


def exchange_scratch(n, rows):
    return [
        pltpu.VMEM((rows, 128), F32),
        pltpu.VMEM((n, rows, 128), F32),
        pltpu.SemaphoreType.DMA((n,)),
        pltpu.SemaphoreType.DMA((n,)),
    ]


FIRST, CONV, FINAL, INNER = range(5), range(4), range(7), (3, 4)


def pack_stats(clips, loc, acc, tiles, count=None):
    for i, t in enumerate(tiles):
        lanes = pl.ds(128 * t, 128)
        for k in range(2):
            loc[2 * i + k : 2 * i + k + 1, :] = jnp.sum(
                acc[k, :, lanes] * clips.valid, axis=0, keepdims=True
            )
    if count is not None:
        at = 2 * len(tiles)
        loc[at : at + 1, :] = jnp.sum(clips.valid, axis=0, keepdims=True) * float(count)


def loop(n, body):
    def step(i, _):
        body(i)
        return 0

    lax.fori_loop(0, n, step, 0)


def inv_edges(side, frames, y):
    x = lax.broadcasted_iota(jnp.int32, (side, frames, 128), 0)
    ex = jnp.where((x == 0) | (x == side - 1), 0.5, 1.0 / 3.0).astype(F32)
    ey = jnp.where((y == 0) | (y == side - 1), 0.5, 1.0 / 3.0).astype(F32)
    return (ex * ey).reshape(side * frames, 128)


def box(clips, side, load, tx, store):
    frames = clips.frames
    tx[0] = jnp.zeros(tx.shape[1:], F32)
    tx[side + 1] = jnp.zeros(tx.shape[1:], F32)

    def across(y):
        v = load(y)
        t = clips.times(v, clips.valid)
        t = t + clips.times(roll_rows(v, 1), clips.before)
        t = t + clips.times(roll_rows(v, -1), clips.after)
        tx[y + 1] = t + shift_places(t, frames, 1) + shift_places(t, frames, -1)

    def down(y):
        store(y, tx[y] + tx[y + 1] + tx[y + 2])

    loop(side, across)
    loop(side, down)


def pool_forward(clips, side, load, tx, zp, acc):
    def store(y, v):
        z = clips.times(v * inv_edges(side, clips.frames, y), clips.inv)
        zp[y] = z
        add_stats(clips, acc, pl.ds(256, 128), z)

    box(clips, side, load, tx, store)


def upright(src, dst):
    rows = src.shape[1]
    width = src.shape[0]

    def body(i):
        at = pl.ds(pl.multiple_of(i * 128, 128), 128)
        dst[at, 0:width] = src[:, at].astype(F32).T.astype(BF16)

    loop(rows // 128, body)
    if rows % 128:
        at = slice(rows - rows % 128, rows)
        dst[at, 0:width] = src[:, at].astype(F32).T.astype(BF16)


def arrange_first(src, wp, b, flip):
    one, mid_in, small_in, pool = src
    wp[b, :, 0:256] = one[...]
    wp[b, :, 256:384] = pool[...]
    upright(mid_in, flip)
    wp[b, :, 384:544] = flip[0:D, 0:C1A]
    upright(small_in, flip)
    wp[b, :, 544:576] = flip[0:D, 0:C2A]
    wp[b, :, 576:640] = jnp.zeros((D, 64), BF16)


def arrange_beta(src, dst):
    v = jnp.concatenate([jnp.broadcast_to(src[...], (8, 1024)), jnp.zeros((8, 128), F32)], 1)
    lane = lax.broadcasted_iota(jnp.int32, v.shape, 1)
    out = jnp.zeros_like(v)
    for lo, hi, by in (
        (0, 256, 0),
        (256, 576, -160),
        (576, 832, -192),
        (896, 1056, 640),
        (1056, 1088, 320),
    ):
        out = jnp.where((lane >= lo) & (lane < hi), roll_lanes(v, by), out)
    dst[...] = out[0:1]


def arrange_conv(mid_flat, small, wf, ws, b, mid):
    upright(mid_flat, mid)
    for dy in range(3):
        wf[b, 512 * dy + 480 : 512 * dy + 512, :] = jnp.zeros((32, 1024), BF16)
        ws[b, 128 * dy + 96 : 128 * dy + 128, :] = jnp.zeros((32, 384), BF16)
        wf[b, 512 * dy : 512 * dy + 512, 960:1024] = jnp.zeros((512, 64), BF16)
        for dt in range(3):
            for dx in range(3):
                r = 96 * (3 * dt + dy) + 32 * dx
                to = 128 * dy + 32 * dt
                ws[b, to : to + 32, 128 * dx : 128 * dx + 128] = small[r : r + 32, :]
            for dx in range(3):
                r = 480 * (3 * dt + dy) + 160 * dx
                for rows, to in ((128, 128 * dt), (32, 384 + 32 * dt)):
                    to = to + 512 * dy
                    wf[b, to : to + rows, 256 * dx : 256 * dx + 256] = mid[r : r + rows, 0:256]
                    wf[b, to : to + rows, 768 + 64 * dx : 832 + 64 * dx] = mid[
                        r : r + rows, 256:320
                    ]
                    r = r + rows


def inner_tiles(clips, z, coef):
    tiles = []
    for t in range(2):
        lanes = slice(128 * t, 128 * t + 128)
        act, _ = soft(z[:, lanes] * coef[0:1, lanes] + coef[2:3, lanes])
        tiles.append(clips.times(act, clips.valid))
    return tiles


def fill_inner(coef, st, beta):
    for t in range(2):
        lanes = pl.ds(128 * t, 128)
        fill_norm(coef, lanes, st, pl.ds(384 + 128 * t, 128), beta[0:1, 896 + 128 * t : 1024 + 128 * t])


def tap_tiles(clips, a, b):
    def before(v):
        return clips.times(roll_rows(v, 1), clips.before)

    def after(v):
        return clips.times(roll_rows(v, -1), clips.after)

    lane = lax.broadcasted_iota(jnp.int32, b.shape, 1)
    ones = clips.times(jnp.where(lane == 96, 1.0, 0.0).astype(F32), clips.valid)

    def three32(v):
        return before(v) + roll_lanes(v, 32) + roll_lanes(after(v), 64) + ones

    tail = lane_below(b, 32)
    small = lane_below(roll_lanes(b, -32), 32)
    return [before(a), a, after(a), three32(tail)], three32(small)


def untap(clips, parts, small):
    def before(v):
        return roll_rows(clips.times(v, clips.before), -1)

    def after(v):
        return roll_rows(clips.times(v, clips.after), 1)

    def back32(v):
        return (
            lane_below(before(v), 32)
            + lane_below(roll_lanes(v, -32), 32)
            + lane_below(roll_lanes(after(v), -64), 32)
        )

    a = before(parts[0]) + parts[1] + after(parts[2])
    return a, back32(parts[3]) + roll_lanes(back32(small), 32)


def typical(beta):
    sp, sg = soft(jnp.broadcast_to(beta, (8, beta.shape[-1])))
    return sp + 0.5 * sg * (1.0 - sg)


def outer(c, s):
    k = lax.broadcasted_iota(jnp.int32, c.shape, 0)
    c = jnp.where(k < 2, c, 0.0).astype(BF16)
    s = jnp.broadcast_to(s, (8, s.shape[-1]))
    high = s.astype(BF16).astype(F32)
    k = lax.broadcasted_iota(jnp.int32, s.shape, 0)
    s = jnp.where(k == 0, high, jnp.where(k == 1, s - high, 0.0)).astype(BF16)
    return dot_tn(c, s)


def tap_points(beta):
    a = typical(beta[0:1, 896:1024])
    b = typical(beta[0:1, 1024:1152])

    def three(v):
        return v + roll_lanes(v, 32) + roll_lanes(v, 64)

    tail = three(lane_below(b, 32))
    small = three(lane_below(roll_lanes(b, -32), 32))
    return jnp.concatenate([a, a, a, tail], 1), small


def centre_mid(row, beta):
    c, _ = tap_points(beta)
    row = jnp.broadcast_to(row, (8, 1024))
    main = row[:, 256:512]
    tail = lane_below(roll_lanes(row[:, 768:896], 64), 64)
    s = jnp.concatenate([main, main, main, tail + roll_lanes(tail, 64), tail], 1)
    return outer(c, s)


def centre_small(grad, beta):
    _, c = tap_points(beta)
    row = jnp.broadcast_to(grad[224:225, 128:256], (8, 128))
    return outer(c, jnp.concatenate([row, row, row], 1))


def conv_gather(frames, p, s):
    def three(at):
        return (
            shift_places(at(0), frames, -1) + at(1) + shift_places(at(2), frames, 1)
        )

    main = three(lambda k: p[:, 256 * k : 256 * k + 256])
    small = three(lambda k: s[:, 128 * k : 128 * k + 128])
    ends = p[:, 768:896]
    tail = three(lambda k: (ends, roll_lanes(ends, 64), p[:, 896:1024])[k])
    return main, small, lane_below(tail, 64)


def spread_x(frames, v, by):
    return v if by == 0 else shift_places(v, frames, -by)


def put_spread(frames, main, small, tail, put_mid, put_small):
    for k in range(3):
        put_mid(256 * k, spread_x(frames, main, k - 1))
        put_small(128 * k, spread_x(frames, small, k - 1))
    put_mid(768, spread_x(frames, tail, -1) + roll_lanes(tail, 64))
    put_mid(896, spread_x(frames, tail, 1))


def join_final(small, tail, pool):
    s, p = roll_lanes(small, 64), roll_lanes(pool, 64)
    low = lax.broadcasted_iota(jnp.int32, small.shape, 1) < 64
    return jnp.where(low, tail, s), jnp.where(low, s, p), jnp.where(low, p, 0.0)


def split_final(t4, t5, t6):
    a, b, c = roll_lanes(t4, 64), roll_lanes(t5, 64), roll_lanes(t6, 64)
    low = lax.broadcasted_iota(jnp.int32, t4.shape, 1) < 64
    return jnp.where(low, a, b), jnp.where(low, t4, 0.0), jnp.where(low, b, c)


def final_stats(st1, st2, stf):
    stf[:, 0:256] = st1[:, 0:256]
    stf[:, 256:512] = st2[:, 0:256]
    for t, v in enumerate(join_final(st2[:, 256:384], st2[:, 384:512], st1[:, 256:384])):
        stf[:, 512 + 128 * t : 640 + 128 * t] = v
    stf[2:3, :] = jnp.broadcast_to(st1[2:3, 0:1], (1, DP))


def store_conv(clips, y, p, s, zp, put, acc):
    main, small, tail = conv_gather(clips.frames, p, s)
    put(y, 256, main)
    for t, v in enumerate(join_final(small, tail, zp[y])):
        put(y, 512 + 128 * t, v)
    add_stats(clips, acc, pl.ds(0, 256), main)
    add_stats(clips, acc, pl.ds(256, 128), small)
    add_stats(clips, acc, pl.ds(384, 128), tail)


def forward_kernel(
    len_ref, bn, x, og, w_one, w_mid_in, w_small_in, w_pool, w_mid, w_small,
    st1, stf, beta1, beta2,
    xgot_out, zin_out, zf_out, sig_out, hand_out, asum_out, bsum_out, cat_out, scat_out,
    wp1, wp2, wf1, wf2, ws1, ws2, og_got,
    x_got, zf, zin, zp, cat, scat, sig, hand, asum, bsum, scr, beta, got_beta, wp, wf, ws, st2, coef, coef_in,
    hacc, acc, acc2, loc, buf, ssem, rsem, loc2, buf2, ssem2, rsem2, osem, psem, qsem,
):
    greet(partner=True)
    sec = lax.axis_index("section")
    side = zp.shape[0]
    rows = side * 16
    clips = Clips(len_ref, 16, 1)
    hacc[...] = jnp.zeros_like(hacc)
    acc[...] = jnp.zeros_like(acc)
    acc2[...] = jnp.zeros_like(acc2)
    loc[...] = jnp.zeros_like(loc)
    loc2[...] = jnp.zeros_like(loc2)
    outs = []

    def put(src, dst):
        c = pltpu.make_async_copy(src, dst, osem.at[len(outs)])
        c.start()
        outs.append(c)

    pairs = ((wp.at[sec], wp.at[sec]), (beta, got_beta), (x.at[1 - sec], x_got))
    pairs += ((og.at[1 - sec], og_got), (wf.at[sec], wf.at[sec]), (ws.at[sec], ws.at[sec]))
    remote = [swap_copy(a, b, psem.at[i], qsem.at[i]) for i, (a, b) in enumerate(pairs)]

    def first_phase(x_own, yp, tx, one, mid_in, small_in, pool, mid, small, flip, lsem):
        local = [
            pltpu.make_async_copy(a, b, lsem.at[i])
            for i, (a, b) in enumerate(
                (
                    (x.at[sec], x_own),
                    (w_one.at[0], one),
                    (w_mid_in.at[0], mid_in),
                    (w_small_in.at[0], small_in),
                    (w_pool.at[0], pool),
                    (w_mid.at[0], mid),
                    (w_small.at[0], small),
                )
            )
        ]
        for c in local[1:] + local[:1]:
            c.start()
        arrange_beta(bn, beta)
        for c in local[1:5]:
            c.wait()
        arrange_first((one, mid_in, small_in, pool), wp, sec, flip)
        greeted(partner=True)
        for c in remote[:4]:
            c.start()
        for c in local[5:]:
            c.wait()
        arrange_conv(mid, small, wf, ws, sec, flip)
        for c in remote[4:]:
            c.start()
        for c in remote[:2]:
            c.wait()
        beta1[...] = jnp.where(sec == 0, beta[...], got_beta[...])
        beta2[...] = jnp.where(sec == 0, got_beta[...], beta[...])
        ny = side // 2
        size = ny * side * 8
        for k, src in enumerate((x_own, x_got)):
            (local[0] if k == 0 else remote[2]).wait()
            half = sec if k == 0 else 1 - sec

            def body(i, src=src, half=half):
                here = pl.ds(i * ny, ny)
                y = dot(src[pl.ds(pl.multiple_of(i * size, 16), size)], wp[0])

                def place(lo, hi):
                    return y[:, lo:hi].reshape(ny, side, 8, hi - lo)

                zf[here, :, half, :, 0:256] = place(0, 256)
                yp[here, :, half] = place(256, 384)
                zin[here, :, half] = place(384, 640)
                for lo, hi in ((0, 256), (384, 640)):
                    v = y[:, lo:hi].reshape(-1, 8, 256)
                    hacc[0, half, :, lo:hi] += jnp.sum(v, axis=0)
                    hacc[1, half, :, lo:hi] += jnp.sum(v * v, axis=0)

            loop(2, body)
        acc[...] = hacc[...].reshape(acc.shape)
        pool_forward(clips, side, lambda y: yp[y].reshape(rows, 128), tx, zp, acc)

    like = [pltpu.VMEM(a.shape[1:], BF16) for a in (w_one, w_mid_in, w_small_in, w_pool, w_mid, w_small)]
    pl.run_scoped(
        first_phase,
        pltpu.VMEM(x.shape[1:], BF16),
        vmem(side, side, 2, 8, 128),
        vmem(side + 2, rows, 128),
        *like,
        vmem(27 * C1A, 384, dtype=BF16),
        pltpu.SemaphoreType.DMA((7,)),
    )
    pack_stats(clips, loc, acc, FIRST, side * side)
    exchange_start(loc, buf, ssem, rsem)
    put(x_got, xgot_out)
    put(zin, zin_out)
    for y in (0, side + 1):
        cat[y] = jnp.zeros(cat.shape[1:], BF16)
        scat[y] = jnp.zeros(scat.shape[1:], BF16)
    exchange_finish(loc, buf, ssem, rsem, st1, FIRST)
    fill_inner(coef_in, st1, beta1)

    def build(y):
        a, b = inner_tiles(clips, zin[y].reshape(rows, 256), coef_in)
        parts, small = tap_tiles(clips, a, b)
        for i, part in enumerate(parts):
            cat[y + 1, :, 128 * i : 128 * i + 128] = part.astype(BF16)
        scat[y + 1] = small.astype(BF16)

    loop(side, build)
    for c in remote[3:]:
        c.wait()
    put(cat, cat_out)
    put(scat, scat_out)
    for a, b in ((wf, (wf1, wf2)), (ws, (ws1, ws2)), (wp, (wp1, wp2))):
        for i in range(2):
            put(a.at[i], b[i])
    ny = 2

    def put_row(y, lane, v):
        zf[y, :, :, :, lane : lane + v.shape[-1]] = v.reshape(side, 2, 8, v.shape[-1])

    def products(i):
        y0 = i * ny

        def taps(ref):
            return jnp.concatenate(
                [ref[pl.ds(y0 + dy, ny)].reshape(ny * rows, ref.shape[-1]) for dy in range(3)], axis=1
            )

        p = dot(taps(cat), wf[0])
        s = dot(taps(scat), ws[0])
        for q in range(ny):
            here = slice(q * rows, (q + 1) * rows)
            store_conv(clips, y0 + q, p[here], s[here], zp, put_row, acc2)

    loop(side // ny, products)
    pack_stats(clips, loc2, acc2, CONV)
    exchange_start(loc2, buf2, ssem2, rsem2)
    put(zf, zf_out)
    half = side // 2

    pair_valid = clips.valid.reshape(8, 2, 128)[:, 0] * 0.125

    def emit(k, tiles):
        for t in tiles:
            lanes = pl.ds(128 * t, 128)
            scale, shift, b = coef[0:1, lanes], coef[2:3, lanes], coef[3:4, lanes]
            pooled = None
            for q in range(2):
                t_in = zf[2 * k + q, :, :, :, lanes].reshape(rows, 128) * scale + shift
                sp, sg = soft(t_in)
                if t == 6:
                    lane = lax.broadcasted_iota(jnp.int32, sp.shape, 1)
                    sp = jnp.where(lane == 127, 1.0, lane_below(sp, 64))
                    sg = lane_below(sg, 64)
                sig[2 * k + q, :, lanes] = sg.astype(BF16)
                three = [
                    jnp.sum(v.reshape(half, 2, 16, 128), axis=1) for v in (sp, sg, sg * (t_in - b))
                ]
                pooled = three if pooled is None else [x + y for x, y in zip(pooled, three)]
            for v, dst in zip(pooled, (hand, asum, bsum)):
                scr[...] = v
                dst[k, :, :, lanes] = (
                    scr[:, pl.ds(0, 8, stride=2), :] + scr[:, pl.ds(1, 8, stride=2), :]
                ) * pair_valid

    for t in range(2):
        lanes = pl.ds(128 * t, 128)
        fill_norm(coef, lanes, st1, lanes, beta1[0:1, lanes])
    loop(half, lambda k: emit(k, (0, 1)))
    exchange_finish(loc2, buf2, ssem2, rsem2, st2, CONV)
    final_stats(st1, st2, stf)
    for t in range(2, 7):
        lanes = pl.ds(128 * t, 128)
        fill_norm(coef, lanes, stf, lanes, beta1[0:1, lanes])
    last = ((sig, sig_out, 2), (hand, hand_out, 1), (asum, asum_out, 1), (bsum, bsum_out, 1))
    base = len(outs)

    def rest(k):
        emit(k, range(2, 7))
        for i, (src, dst, n) in enumerate(last):
            here = pl.ds(n * k, n)
            pltpu.make_async_copy(src.at[here], dst.at[here], osem.at[base + i]).start()

    loop(half, rest)
    for c in outs:
        c.wait()
    for i, (src, dst, n) in enumerate(last):
        pltpu.make_async_copy(src, dst, osem.at[base + i]).wait()


def second_kernel(
    len_ref, hand, asum, bsum, og, og_got, wp, wf, ws, beta, beta1,
    block_out, hg, packed0, packed1, packed2, packed3, packed4, sums5, sums6, sums7,
    gown, grad, out, lsem, psem, qsem,
    hbuf, zin, zp, zf, stf, yp, tx, catf, cat, scat, pbuf, sbuf, dbuf, dzc, dzs, dz1, din,
    acc, st3, st4, acc7, accm, accs, accp, coef, coef_in,
    loc3, buf3, ss3, rs3, loc4, buf4, ss4, rs4, loc5, buf5, ss5, rs5,
    loc6, buf6, ss6, rs6, loc7, buf7, ss7, rs7,
):
    greet(partner=True)
    sec = lax.axis_index("section")
    own = pltpu.make_async_copy(og.at[sec], gown, lsem.at[0])
    own.start()
    side = hand.shape[0]
    rows = side * 8
    total = side * rows
    clips = Clips(len_ref, 8, 2)
    for ref in (acc, acc7, loc3, loc4, loc5, loc6, loc7):
        ref[...] = jnp.zeros_like(ref)

    hbuf[...] = hand[...].reshape(total, DP).astype(BF16)
    y = dot(hbuf[:, 0:D], wp[...])
    zf[:, :, 0:C0] = y[:, 0:C0].reshape(side, rows, C0)
    yp[...] = y[:, 256:384].reshape(side, rows, 128)
    zin[...] = y[:, 384:640].reshape(side, rows, 256)

    def first_sums(y):
        add_stats(clips, acc, pl.ds(0, 256), zf[y, :, 0:256])
        add_stats(clips, acc, pl.ds(384, 256), zin[y])

    loop(side, first_sums)
    pool_forward(clips, side, lambda y: yp[y], tx, zp, acc)
    pack_stats(clips, loc3, acc, FIRST, side * side)
    greeted(partner=True)
    exchange_start(loc3, buf3, ss3, rs3)
    own.wait()
    mine, theirs = gown[...].astype(F32), og_got[...].astype(F32)
    low = jnp.where(sec == 0, mine, theirs)
    high = jnp.where(sec == 0, theirs, mine)
    grad[...] = jnp.concatenate([low, high], 2)
    exchange_finish(loc3, buf3, ss3, rs3, st3, FIRST)

    fill_inner(coef_in, st3, beta)
    catf[0] = jnp.zeros(catf.shape[1:], F32)
    catf[side + 1] = jnp.zeros(catf.shape[1:], F32)

    def build(y):
        a, b = inner_tiles(clips, zin[y], coef_in)
        parts, small = tap_tiles(clips, a, b)
        for t, v in enumerate(parts + [small]):
            catf[y + 1, :, 128 * t : 128 * t + 128] = v

    loop(side, build)
    for dy in range(3):
        v = catf[dy : dy + side].reshape(total, 640).astype(BF16)
        cat[:, 512 * dy : 512 * dy + 512] = v[:, 0:512]
        scat[:, 128 * dy : 128 * dy + 128] = v[:, 512:640]
    pbuf[...] = dot(cat[...], wf[...]).reshape(side, rows, 1024)
    sbuf[...] = dot(scat[...], ws[...]).reshape(side, rows, 384)
    acc[...] = jnp.zeros_like(acc)

    def put_row(y, lane, v):
        zf[y, :, lane : lane + v.shape[-1]] = v

    loop(side, lambda y: store_conv(clips, y, pbuf[y], sbuf[y], zp, put_row, acc))
    pack_stats(clips, loc4, acc, CONV)
    exchange(loc4, buf4, ss4, rs4, st4, CONV)
    final_stats(st3, st4, stf)
    for t in range(7):
        lanes = pl.ds(128 * t, 128)
        fill_norm(coef, lanes, stf, lanes, beta[0:1, lanes])

    def emit(y):
        for t in range(7):
            lanes = pl.ds(128 * t, 128)
            t_in = zf[y, :, lanes] * coef[0:1, lanes] + coef[2:3, lanes]
            u = t_in - coef[3:4, lanes]
            sp, sg = soft(t_in)
            width = 128 if t < 6 else 64
            gr = grad[y, :, :, 128 * t : 128 * t + width].reshape(rows, width)
            if t == 6:
                gr = jnp.concatenate([gr, jnp.zeros((rows, 64), F32)], 1)
            d = gr * clips.times(sg, clips.valid)
            dbuf[y, :, lanes] = d
            add_stats(clips, acc7, lanes, d, u)
            sp = clips.times(sp, clips.valid).reshape(side, 8, 128)[:, :, 0:width]
            for h in range(2):
                out[h, y, :, :, 128 * t : 128 * t + width] = sp[:, 4 * h : 4 * h + 4].astype(BF16)

    loop(side, emit)
    mine = pltpu.make_async_copy(out.at[sec], block_out.at[sec], lsem.at[1])
    mine.start()
    theirs = swap_copy(out.at[1 - sec], block_out.at[sec], psem, qsem)
    theirs.start()
    pack_stats(clips, loc5, acc7, FINAL)
    exchange(loc5, buf5, ss5, rs5, sums5, FINAL)
    count = st3[2:3, 0:128]
    for t in range(7):
        lanes = pl.ds(128 * t, 128)
        fill_back(coef, lanes, sums5, lanes, count)

    def dz_of(y, t):
        lanes = pl.ds(128 * t, 128)
        v = dbuf[y, :, lanes] * coef[0:1, lanes] + zf[y, :, lanes] * coef[4:5, lanes]
        return clips.times(v + coef[5:6, lanes], clips.valid)

    def dz_final(y):
        for t in range(2):
            dz1[y, :, 128 * t : 128 * t + 128] = dz_of(y, t)
        main = jnp.concatenate([dz_of(y, 2), dz_of(y, 3)], 1)
        small, tail, pool = split_final(*(dz_of(y, t) for t in (4, 5, 6)))
        yp[y] = clips.times(pool * inv_edges(side, 8, y), clips.inv)

        def put(ref):
            def go(lane, v):
                ref[y, :, lane : lane + v.shape[-1]] = v

            return go

        put_spread(8, main, small, tail, put(dzc), put(dzs))

    loop(side, dz_final)

    def boxed(y, v):
        dz1[y, :, 256:384] = clips.times(v, clips.valid)

    box(clips, side, lambda y: yp[y], tx, boxed)
    dzc_b = dzc[...].reshape(total, 1024).astype(BF16)
    dzs_b = dzs[...].reshape(total, 384).astype(BF16)
    for dy in (-1, 0, 1):
        k = dy + 1
        q = dot_nt(dzc_b, wf[512 * k : 512 * k + 512]).reshape(side, rows, 512)
        r = dot_nt(dzs_b, ws[128 * k : 128 * k + 128]).reshape(side, rows, 128)
        if k == 0:
            catf[1 : side + 1] = jnp.zeros((side, rows, 640), F32)
        catf[1 + dy : 1 + dy + side, :, 0:512] += q
        catf[1 + dy : 1 + dy + side, :, 512:640] += r
    acc[...] = jnp.zeros_like(acc)

    def inner_back(y):
        parts = [catf[y + 1, :, 128 * t : 128 * t + 128] for t in range(5)]
        inner_up(clips, zin[y], untap(clips, parts[:4], parts[4]), coef_in, acc, din, y)

    loop(side, inner_back)
    pack_stats(clips, loc6, acc, INNER)
    exchange_start(loc6, buf6, ss6, rs6)
    accm[...] = dot_tn(cat[...], dzc_b)
    exchange_finish(loc6, buf6, ss6, rs6, sums6, INNER)
    fill_inner_back(coef_in, sums6, count)

    def dz_inner(y):
        for t in range(2):
            dz1[y, :, 384 + 128 * t : 512 + 128 * t] = inner_dz(
                clips, t, zin[y], din[y], coef_in
            )

    loop(side, dz_inner)
    dz1_b = dz1[...].reshape(total, 640).astype(BF16)
    hgv = dot_nt(dz1_b, wp[...]).astype(BF16).astype(F32)
    hg[:, :, :, 0:D] = hgv.reshape(side, side, 8, D)
    hg[:, :, :, D:DP] = jnp.zeros((side, side, 8, DP - D), F32)
    acc7[...] = jnp.zeros_like(acc7)

    def upstream(y):
        for t in range(7):
            lanes = pl.ds(128 * t, 128)
            gr = hg[y, :, :, lanes]
            acc7[0, :, lanes] += jnp.sum(gr * asum[y, :, :, lanes], axis=0)
            acc7[1, :, lanes] += jnp.sum(gr * bsum[y, :, :, lanes], axis=0)

    loop(side, upstream)
    pack_stats(clips, loc7, acc7, FINAL)
    exchange_start(loc7, buf7, ss7, rs7)
    accs[...] = dot_tn(scat[...], dzs_b)
    accp[...] = dot_tn(hbuf[...], dz1_b)
    pool = dz1[:, :, 256:384].reshape(total, 128)
    rest = (pool - dz1_b[:, 256:384].astype(F32)).astype(BF16)
    accp[:, 256:384] += dot_tn(hbuf[...], rest)
    c = jnp.concatenate([typical(beta1[0:1, 0:D]), jnp.zeros((8, DP - D), F32)], 1)
    full = accp[...] - outer(c, accp[DP - 1 : DP, :])
    mid = centre_mid(accm[992:993, :], beta)
    small = centre_small(accs, beta)
    for k, packed in enumerate((packed0, packed1, packed2)):
        pack_mid(packed, accm.at[512 * k : 512 * k + 512], mid, accs, small, k)

    def column(t, r, rows):
        return full[r : r + rows, 128 * t : 128 * t + 128]

    pack_one(packed3, column)
    pack_inner(packed4, column, accs, small)
    exchange_finish(loc7, buf7, ss7, rs7, sums7, FINAL)
    mine.wait()
    theirs.wait()


def pack_mid(packed, acc, mid, accs, small, k):
    for t in range(8):
        lanes = slice(128 * t, 128 * t + 128)
        packed[t, 0:480] = (acc[0:480, lanes] - mid[0:480, lanes]).astype(BF16)
        packed[t, 480:512] = small_piece(accs, small, 8 * k + t)
        if packed.shape[1] > 512:
            packed[t, 512:] = jnp.zeros((packed.shape[1] - 512, 128), BF16)


def small_piece(accs, small, b):
    dy, dt, dx = b // 9, b // 3 % 3, b % 3
    lanes = slice(128 * dx, 128 * dx + 128)
    r = 128 * dy + 32 * dt
    return (accs[r : r + 32, lanes] - small[32 * dt : 32 * dt + 32, lanes]).astype(BF16)


def pack_one(packed, column):
    end = packed.shape[1]
    for j in range(8):
        packed[j, 0:208] = column(j // 4, 208 * (j % 4), 208).astype(BF16)
        rows = min(112, D - 112 * j)
        packed[j, 208 : 208 + rows] = column(2, 112 * j, rows).astype(BF16)
        if 208 + rows < end:
            packed[j, 208 + rows : end] = jnp.zeros((end - 208 - rows, 128), BF16)


def pack_inner(packed, column, accs, small):
    end = packed.shape[1]
    for j in range(8):
        packed[j, 0:208] = column(3 + j // 4, 208 * (j % 4), 208).astype(BF16)
        packed[j, 208:end] = jnp.zeros((end - 208, 128), BF16)
        if j < 3:
            packed[j, 208:240] = small_piece(accs, small, 24 + j)


def inner_up(clips, z, backs, coef, acc, din, y):
    for t in range(2):
        lanes = slice(128 * t, 128 * t + 128)
        zs = z[:, lanes] * coef[0:1, lanes]
        d = backs[t] * clips.times(sigm(zs + coef[2:3, lanes]), clips.valid)
        din[y, :, lanes] = d
        add_stats(clips, acc, pl.ds(384 + 128 * t, 128), d, zs - coef[1:2, lanes])


def fill_inner_back(coef, sums, count):
    for t in range(2):
        fill_back(coef, pl.ds(128 * t, 128), sums, pl.ds(384 + 128 * t, 128), count)


def inner_dz(clips, t, z, d, coef):
    lanes = slice(128 * t, 128 * t + 128)
    v = d[:, lanes] * coef[0:1, lanes] + z[:, lanes] * coef[4:5, lanes] + coef[5:6, lanes]
    dz = clips.times(v, clips.valid)
    return lane_below(dz, 64) if t == 1 else dz


def put_halves(ref, y, lane, v):
    side, lanes = v.shape[0] // 16, v.shape[1]
    v = v.reshape(side, 2, 8, lanes)
    for h in range(2):
        ref[h, y, :, lane : lane + lanes] = v[:, h].reshape(side * 8, lanes).astype(BF16)


Z_FIRST = (3,)
SCHEDULE = {
    "start": ((1, 0), (4, 0),),
    "dz2": ((3, 0),),
    "dz3": ((1, 1), (2, 0),),
    "dz4": ((4, 1), (0, 0), (3, 1),),
    "dzend": ((1, 2), (2, 1),),
    "scat": ((0, 1), (1, 3),),
    "d1": ((4, 2), (6, 0), (3, 2), (2, 2), (1, 4),),
    "m0": ((6, 1),),
    "d0": ((5, 0), (2, 3), (0, 2), (1, 5), (4, 3),),
    "m2": ((5, 1),),
    "d2": ((0, 3), (2, 4), (6, 2), (7, 0), (3, 3),),
    "e": ((7, 1), (4, 4), (8, 0), (0, 4),),
    "cb0": ((5, 2),),
    "cb1": ((8, 1),),
    "cb2": ((2, 5), (5, 3), (4, 5), (7, 2),),
    "cb3": ((3, 4), (6, 3), (8, 2),),
    "cb4": ((0, 5), (2, 6),),
    "cb5": ((5, 4), (3, 5), (1, 6),),
    "cb6": ((6, 4), (8, 3),),
    "s8a": ((0, 6),),
    "s8b": ((5, 5), (6, 5), (7, 3),),
    "l": ((5, 6), (9, 0), (8, 4), (7, 4),),
    "in0": ((9, 1),),
    "in2": ((4, 6),),
    "in4": ((9, 2),),
    "in5": ((7, 5), (5, 7), (6, 6),),
    "in8": ((8, 5), (9, 3), (9, 4), (7, 6),),
    "in9": ((2, 7), (9, 5), (4, 7), (3, 6), (1, 7), (6, 7), (8, 6),),
    "in11": ((9, 6),),
    "end": ((3, 7), (8, 7), (0, 7), (7, 7), (9, 7),),
}


def backward_kernel(
    bits, len_ref, hg, stf, sums7, st1, beta, sums5, sums6,
    zf, sig, zin_in, wf_in, ws_in, wp_in, cat_in, scat_in, x, x_got, two0, two1, two2, two3, two4,
    gin, full0, full1, full2, full3, full4, offs,
    zin, wf, ws, wp, cat, scat, x0, x1, dzc, dzs, dz1, dzi, sums8, snd, got,
    coef, coef_in, acc, loc, buf, ss8, rs8, lsem, csend, crecv, ssem, rsem, gsend, grecv, *arrays,
):
    greet(partner=True)
    sec = lax.axis_index("section")
    side = dz1.shape[1]
    half = side // 2
    rows = side * 16
    clips = Clips(len_ref, 16, 1)
    count = stf[2:3, 0:128]
    loads = [
        pltpu.make_async_copy(a, b, lsem.at[i])
        for i, (a, b) in enumerate(
            (
                (zin_in, zin),
                (wf_in, wf),
                (ws_in, ws),
                (wp_in, wp),
                (cat_in, cat),
                (scat_in, scat),
                (x.at[sec], x0),
                (x_got, x1),
            )
        )
    ]
    two = (two0, two1, two2, two3, two4)
    full = (full0, full1, full2, full3, full4)
    own_two, ones = arrays[0:5], arrays[5:10]
    core_land = arrays[10:20]
    pieces = 2 ** len(groups(bits)[-1]) - 1 + len(groups(bits)) - 1
    lands = arrays[20:]

    def part(ref, which):
        h = ref.shape[1] // 2
        return ref.at[:, pl.ds(pl.multiple_of(which * h, 16), h)]

    def reducer(i, q, base, rows, swap_src, flip, load):
        return Reducer(
            bits, i, q, base, rows, swap_src, core_land[i], lands[pieces * i : pieces * i + pieces],
            csend, crecv, ssem, rsem, flip, load,
        )

    g, h = [], []
    for i, (a, b) in enumerate(zip(two, own_two)):
        load = pltpu.make_async_copy(part(a, sec), b, lsem.at[8 + i])
        load.start()
        g.append(reducer(i, b, 0, b.shape[1], part(a, 1 - sec), 1 - sec, load))
    for i, a in enumerate(ones):
        rows_half = a.shape[1] // 2
        h.append(
            reducer(5 + i, a, sec * rows_half, rows_half, part(a, 1 - sec), sec, None)
        )
    def at(name):
        for r, e in SCHEDULE.get(name, ()):
            (g + h)[r].event(e)

    acc[...] = jnp.zeros_like(acc)
    loc[...] = jnp.zeros_like(loc)
    for t in range(7):
        lanes = pl.ds(128 * t, 128)
        fill_norm(coef, lanes, stf, lanes, beta[0:1, lanes])
        fill_back(coef, lanes, sums7, lanes, count)
    fill_inner(coef_in, st1, beta)
    for y in (0, side + 1):
        dzc[y] = jnp.zeros(dzc.shape[1:], BF16)
        dzs[y] = jnp.zeros(dzs.shape[1:], BF16)

    def dz_phase(zb, sb, scr, yp, tx, zsem):
        def fetch(k, slot):
            here = pl.ds(2 * k, 2)
            return (
                pltpu.make_async_copy(zf.at[here], zb.at[slot], zsem.at[0, slot]),
                pltpu.make_async_copy(sig.at[here], sb.at[slot], zsem.at[1, slot]),
            )

        for c in fetch(0, 0):
            c.start()
        for c in loads[4:] + loads[:4]:
            c.start()

        def body(k):
            slot = lax.rem(k, 2)

            @pl.when(k < half - 1)
            def _():
                for c in fetch(k + 1, 1 - slot):
                    c.start()

            @pl.when(k == 1)
            def _():
                greeted(partner=True)
                at("start")

            for j in range(2, half):
                pl.when(k == j)(lambda j=j: at(f"dz{j}"))
            for c in fetch(k, slot):
                c.wait()
            tiles = ([], [])
            for t in range(7):
                lanes = pl.ds(128 * t, 128)
                by_z, rest = coef[4:5, lanes], coef[5:6, lanes]
                gr = hg[k, :, :, lanes] * (coef[0:1, lanes] * 0.125)
                scr[:, pl.ds(0, 8, stride=2), :] = gr
                scr[:, pl.ds(1, 8, stride=2), :] = gr
                gr = scr[...]
                gr = jnp.broadcast_to(gr[:, None], (half, 2, 16, 128)).reshape(rows, 128)
                for q in range(2):
                    v = gr * sb[slot, q, :, lanes].astype(F32) + zb[slot, q, :, lanes] * by_z
                    dz = clips.times(v + rest, clips.valid)
                    if t < 2:
                        put_halves(dz1, 2 * k + q, 128 * t, dz)
                    else:
                        tiles[q].append(dz)
            for q in range(2):
                y = 2 * k + q
                small, tail, pool = split_final(*tiles[q][2:])
                yp[y] = clips.times(pool * inv_edges(side, 16, y), clips.inv)

                def put(ref, y=y):
                    def go(lane, v):
                        ref[y + 1, :, lane : lane + v.shape[-1]] = v.astype(BF16)

                    return go

                main = jnp.concatenate(tiles[q][:2], 1).astype(BF16)
                put_spread(16, main, small.astype(BF16), tail, put(dzc), put(dzs))

        loop(half, body)
        at("dzend")

        def boxed(y, v):
            put_halves(dz1, y, 256, clips.times(v, clips.valid))

        box(clips, side, lambda y: yp[y], tx, boxed)
        at("box")

    pl.run_scoped(
        dz_phase,
        vmem(2, 2, rows, DP),
        vmem(2, 2, rows, DP, dtype=BF16),
        vmem(half, 16, 128),
        vmem(side, rows, 128),
        vmem(side + 2, rows, 128),
        pltpu.SemaphoreType.DMA((2, 2)),
    )

    def grad_phase(accm, mid, accs, accp):
        for c in loads[4:6]:
            c.wait()
        ny = side // 2

        def take(ref, y):
            return ref[pl.ds(y, ny)].reshape(ny * rows, ref.shape[-1])

        def sums(k, between):
            accm[...] = dot_tn(take(cat, 1), take(dzc, 2 - k))
            between()
            accm[...] += dot_tn(take(cat, 1 + ny), take(dzc, 2 - k + ny))

        for k in range(3):
            here = slice(128 * k, 128 * k + 128)
            accs[here] = dot_tn(take(scat, 1), take(dzs, 2 - k))
            accs[here] += dot_tn(take(scat, 1 + ny), take(dzs, 2 - k + ny))
        small = centre_small(accs, beta)
        at("scat")
        for k in (1, 0, 2):
            sums(k, lambda: at(f"m{k}"))
            if k == 1:
                mid[...] = centre_mid(accm[480:481, :], beta)
            pack_mid(ones[k], accm, mid, accs, small, k)
            at(f"d{k}")
        for c in loads[6:]:
            c.wait()
        accp[...] = jnp.zeros_like(accp)
        add_outer(accp, dz1, ((x1, 1 - sec), (x0, sec)))
        pack_one(ones[3], lambda t, r, n: accp[r : r + n, 128 * t : 128 * t + 128])
        pack_inner(ones[4], lambda t, r, n: jnp.zeros((n, 128), F32), accs, small)
        at("e")

    def add_outer(accp, d_ref, sides):
        step = side // 2
        size = step * side * 8
        for src, which in sides:

            def body(i, src=src, which=which):
                at = pl.ds(pl.multiple_of(i * size, 16), size)
                d = d_ref[which, pl.ds(i * step, step)].reshape(size, d_ref.shape[-1])
                accp[...] += dot_tn(src[at], d)

            loop(side // step, body)

    pl.run_scoped(
        grad_phase,
        vmem(512, 1024),
        vmem(512, 1024),
        vmem(384, 384),
        vmem(D, 384),
    )

    def last_phase(din, ring, accp, sems):
        for c in loads[:4]:
            c.wait()
        ny = 2

        def body(i):
            y0 = i * ny + 1
            for j in range(side // ny):
                pl.when(i == j)(lambda j=j: at(f"cb{j}"))
            q = s = None
            for dy in (-1, 0, 1):
                k = dy + 1
                here = pl.ds(y0 - dy, ny)
                t = dot_nt(dzc[here].reshape(ny * rows, 1024), wf[512 * k : 512 * k + 512])
                q = t if q is None else q + t
                t = dot_nt(dzs[here].reshape(ny * rows, 384), ws[128 * k : 128 * k + 128])
                s = t if s is None else s + t
            for j in range(ny):
                y = i * ny + j
                here = slice(j * rows, (j + 1) * rows)
                parts = [q[here, 128 * t : 128 * t + 128] for t in range(4)]
                inner_up(clips, zin[y], untap(clips, parts, s[here]), coef_in, acc, din, y)

        loop(side // ny, body)
        pack_stats(clips, loc, acc, INNER)
        exchange_start(loc, buf, ss8, rs8)
        at("s8a")
        sides = ((x1, 1 - sec), (x0, sec))
        step = side // 2
        size = step * side * 8
        exchange_finish(loc, buf, ss8, rs8, sums8, INNER)
        fill_inner_back(coef_in, sums8, count)
        at("s8b")

        def dz(y):
            for t in range(2):
                put_halves(dzi, y, 128 * t, inner_dz(clips, t, zin[y], din[y], coef_in))

        loop(side, dz)
        at("dzi")
        accp[...] = jnp.zeros_like(accp)
        add_outer(accp, dzi, sides)
        for j in range(8):
            ones[4][j, 0:208] = accp[
                208 * (j % 4) : 208 * (j % 4) + 208, 128 * (j // 4) : 128 * (j // 4) + 128
            ].astype(BF16)
        at("l")
        sent = []
        step = 2
        size = step * side * 8
        chunks = side // step
        slots = ring.shape[0]
        for p in range(2 * chunks):
            which = sides[p // chunks][1]
            i = p % chunks
            slot = p % slots
            if p >= slots:
                sent[p - slots].wait()
            here = pl.ds(i * step, step)
            d = jnp.concatenate([dz1[which, here], dzi[which, here]], -1).reshape(size, 640)
            ring[slot] = dot_nt(d, wp[...]).astype(BF16)
            to = gin.at[sec, i * size : (i + 1) * size]
            if p < chunks:
                c = swap_copy(ring.at[slot], to, gsend.at[i], grecv.at[i])
            else:
                c = pltpu.make_async_copy(ring.at[slot], to, sems.at[slot])
            c.start()
            sent.append(c)
            at(f"in{p}")
        for c in sent[-slots:]:
            c.wait()

    dma = pltpu.SemaphoreType.DMA
    pl.run_scoped(
        last_phase,
        vmem(side, rows, 256),
        vmem(4, 2 * side * 8, D, dtype=BF16),
        vmem(D, 256),
        dma((4,)),
    )
    snd[:, 0:DP] = jnp.where(sec == 0, sums5[...], sums7[...])
    snd[:, DP : DP + 640] = jnp.where(sec == 0, sums6[...], sums8[...])
    small = swap_copy(snd, got, csend.at[15], crecv.at[15])
    small.start()
    at("end")

    def finish(mine, theirs):
        copies = []
        for i, (dst, m, t) in enumerate(zip(full, mine, theirs)):
            copies.append(pltpu.make_async_copy(m, dst.at[sec], lsem.at[13 + i]))
            copies.append(swap_copy(t, dst.at[sec], csend.at[10 + i], crecv.at[10 + i]))
        for c in copies:
            c.start()
        for c in copies:
            c.wait()

    pl.when(sec == 0)(lambda: finish(core_land[5:10], core_land[0:5]))
    pl.when(sec == 1)(lambda: finish(core_land[0:5], core_land[5:10]))
    small.wait()
    for lanes, a, b in ((slice(0, DP), sums7, sums5), (slice(DP, DP + 640), sums8, sums6)):
        offs[:, lanes] = jnp.where(sec == 0, a[...], b[...]) + got[:, lanes]


def put_halves(ref, y, lane, v):
    side, lanes = v.shape[0] // 16, v.shape[1]
    v = v.reshape(side, 2, 8, lanes)
    for h in range(2):
        ref[h, y, :, lane : lane + lanes] = v[:, h].reshape(side * 8, lanes).astype(BF16)


def groups(bits, last_first=False):
    if bits < 3:
        return [(k,) for k in range(bits)]
    plan = [(k,) for k in range(bits - 2)] + [(bits - 2, bits - 1)]
    return plan[-1:] + plan[:-1] if last_first else plan


class Reducer:
    EVENTS = 8

    def __init__(
        self, bits, index, q, base, rows, swap_src, core_land, land, csend, crecv, ssem, rsem, flip, load
    ):
        self.index, self.q, self.base, self.rows = index, q, base, rows
        self.core_land, self.land, self.load = core_land, land, load
        self.ssem, self.rsem = ssem, rsem
        self.swap = swap_copy(swap_src, core_land, csend.at[index], crecv.at[index])
        me = lax.axis_index("dp")
        plan = groups(bits, index in Z_FIRST)
        self.count = len(plan)
        self.last = 2 * self.count
        self.steps = []
        tiles, t0, r0 = 8, 0, 0
        at = 0
        for step, ks in enumerate(plan):
            powers = []
            for k in ks:
                power = 1 << k
                if bits > 1 and k < 2:
                    power = power + flip * ((1 << (1 - k)) - power)
                powers.append((power, lax.rem(me // power, 2)))
            cuts = []
            for power, bit in powers:
                if tiles > 1:
                    tiles //= 2
                    cuts.append((bit, tiles, 0))
                else:
                    rows //= 2
                    cuts.append((bit, 0, rows))
            sends = []
            for c in range(1, 1 << len(ks)):
                partner, t, r = me, t0, r0
                for i, ((power, bit), (_, dt, dr)) in enumerate(zip(powers, cuts)):
                    turned = (c >> i) & 1
                    partner = partner + turned * (1 - 2 * bit) * power
                    here = bit + turned * (1 - 2 * bit)
                    t, r = t + here * dt, r + here * dr
                sends.append((partner, (t, r), at))
                at += 1
            for bit, dt, dr in cuts:
                t0, r0 = t0 + bit * dt, r0 + bit * dr
            self.steps.append((sends, (t0, r0), tiles, rows))
        self.pieces = at

    def region(self, ref, base, at, tiles, rows):
        t, r = at
        r = base + r
        if not isinstance(r, int):
            r = pl.multiple_of(r, 16)
        return ref.at[pl.ds(t, tiles), pl.ds(r, rows)]

    def mine(self, at, tiles, rows):
        return self.region(self.q, self.base, at, tiles, rows)

    def total(self, at, tiles, rows):
        return self.region(self.core_land, 0, at, tiles, rows)

    def copies(self, i):
        if i == 0:
            return [self.swap]
        halving = i <= self.count
        sends, keep, tiles, rows = self.steps[i - 1 if halving else self.last - i]
        out = []
        for partner, send, piece in sends:
            src = self.mine(send, tiles, rows) if halving else self.total(keep, tiles, rows)
            sem = 2 * (self.index * self.pieces + piece) + int(halving)
            out.append(
                pltpu.make_async_remote_copy(
                    src_ref=src,
                    dst_ref=self.land[piece] if halving else src,
                    send_sem=self.ssem.at[sem],
                    recv_sem=self.rsem.at[sem],
                    device_id={"dp": partner},
                    device_id_type=MESH,
                )
            )
        return out

    def received(self, i):
        sends, keep, tiles, rows = self.steps[self.last - i]
        out = []
        for partner, send, piece in sends:
            sem = 2 * (self.index * self.pieces + piece)
            dst = self.total(send, tiles, rows)
            out.append(
                pltpu.make_async_remote_copy(
                    src_ref=dst,
                    dst_ref=dst,
                    send_sem=self.ssem.at[sem],
                    recv_sem=self.rsem.at[sem],
                    device_id={"dp": partner},
                    device_id_type=MESH,
                )
            )
        return out

    def add(self, dst, q, lands, tiles, rows):
        chunk = next(c for c in range(min(rows, 256), 0, -16) if rows % c == 0 and c % 16 == 0)
        parts = rows // chunk

        def body(j):
            t, r = j // parts, pl.multiple_of(lax.rem(j, parts) * chunk, 16)
            at = pl.ds(r, chunk)
            total = q[t, at].astype(F32)
            for land in lands:
                total = total + land[t, at].astype(F32)
            dst[t, at] = total.astype(BF16)

        loop(tiles * parts, body)

    def finish(self, i):
        if i > self.count:
            for c in self.copies(i):
                c.wait_send()
            for c in self.received(i):
                c.wait_recv()
            return
        for c in self.copies(i):
            c.wait()
        if i == 0:
            if self.load is not None:
                self.load.wait()
            q = self.mine((0, 0), 8, self.rows)
            self.add(q, q, [self.core_land], 8, self.rows)
        else:
            sends, keep, tiles, rows = self.steps[i - 1]
            lands = [self.land[piece] for _, _, piece in sends]
            q = self.mine(keep, tiles, rows)
            dst = self.total(keep, tiles, rows) if i == self.count else q
            self.add(dst, q, lands, tiles, rows)

    def event(self, e):
        count = self.last + 2
        for i in range(e * count // self.EVENTS, (e + 1) * count // self.EVENTS):
            if i > 0:
                self.finish(i - 1)
            if i <= self.last:
                for c in self.copies(i):
                    c.start()


def land_shapes(tiles, rows, bits, last_first):
    out = []
    for ks in groups(bits, last_first):
        for _ in ks:
            if tiles > 1:
                tiles //= 2
            else:
                rows //= 2
        out += [(tiles, rows, 128)] * (2 ** len(ks) - 1)
    return out


def unpack_kernel(
    full0, full1, full2, full3, full4, gin_in, out_in, offs,
    one, mid_in, mid, small_in, small, pool, offset, gin, out,
    buf0, buf1, buf2, buf3, buf4, nat, inner, gin_buf, out_buf, sem,
):
    copies = []
    bufs = (buf0, buf1, buf2, buf3, buf4)
    for i, (full, buf) in enumerate(zip((full0, full1, full2, full3, full4), bufs)):
        half = full.shape[2]
        for h in range(2):
            copies.append(
                pltpu.make_async_copy(full.at[h], buf.at[:, h * half : (h + 1) * half], sem.at[2 * i + h])
            )
    for c in copies:
        c.start()
    through = ((gin_in, gin_buf, gin), (out_in, out_buf, out))
    for i, (src, buf, dst) in enumerate(through):
        pltpu.make_async_copy(src, buf, sem.at[10 + i]).start()
    v = offs[...]
    lane = lax.broadcasted_iota(jnp.int32, v.shape, 1)
    out = jnp.where(lane < 256, v, 0.0)
    for lo, hi, by in ((256, 416, -1024), (416, 736, 160), (736, 768, -704), (768, 1024, 192)):
        out = jnp.where((lane >= lo) & (lane < hi), roll_lanes(v, by), out)
    offset[...] = out[0:1, 0:1024]
    for c in copies:
        c.wait()

    def take(b, t, r, rows):
        return bufs[b][t, r : r + rows].astype(F32)

    for dt in range(3):
        for dy in range(3):
            for dx in range(3):
                to = 160 * (9 * dt + 3 * dy + dx)
                for rows, r in ((128, 128 * dt), (32, 384 + 32 * dt)):
                    nat[to : to + rows, 0:128] = take(dy, 2 * dx, r, rows)
                    nat[to : to + rows, 128:256] = take(dy, 2 * dx + 1, r, rows)
                    tail = take(dy, 6 + dx // 2, r, rows)
                    nat[to : to + rows, 256:384] = roll_lanes(tail, 64) if dx == 1 else tail
                    to = to + rows
                b = 9 * dy + 3 * dt + dx
                to = 32 * (9 * dt + 3 * dy + dx)
                small[to : to + 32, :] = (
                    take(b // 8, b % 8, 480, 32) if b < 24 else take(4, b - 24, 208, 32)
                )

    def turn(i):
        at = pl.ds(pl.multiple_of(i * 128, 128), 128)
        mid[0:256, at] = nat[at, 0:256].T
        mid[256:320, at] = nat[at, 256:384].T[0:64]

    total = mid.shape[1]
    passed = []
    for i, (src, buf, dst) in enumerate(through):
        pltpu.make_async_copy(src, buf, sem.at[10 + i]).wait()
        passed.append(pltpu.make_async_copy(buf, dst, sem.at[10 + i]))
        passed[i].start()
    loop(total // 128, turn)
    at = slice(total - total % 128, total)
    mid[0:256, at] = nat[at, 0:256].T
    mid[256:320, at] = nat[at, 256:384].T[0:64]
    for j in range(8):
        at = slice(208 * (j % 4), 208 * (j % 4) + 208)
        one[at, 128 * (j // 4) : 128 * (j // 4) + 128] = take(3, j, 0, 208)
        inner[j // 4, at] = take(4, j, 0, 208)
        rows = min(112, D - 112 * j)
        pool[112 * j : 112 * j + rows, :] = take(3, j, 208, rows)
    for r in range(0, D, 128):
        at = slice(r, min(r + 128, D))
        mid_in[0:128, at] = inner[0, at].T
        last = inner[1, at].T
        mid_in[128:160, at] = last[0:32]
        small_in[:, at] = last[32:64]
    for c in passed:
        c.wait()


def vmem(*shape, dtype=F32):
    return pltpu.VMEM(shape, dtype)


def call(kernel, outs, args, scratch, collective=None, smem_first=True, any_in=(), any_out=()):
    def specs(count, anywhere):
        return [
            pl.BlockSpec(memory_space=pl.ANY if i in anywhere else pltpu.VMEM)
            for i in range(count)
        ]

    in_specs = specs(len(args), any_in)
    if smem_first:
        in_specs[0] = pl.BlockSpec(memory_space=pltpu.SMEM)
    params = {"vmem_limit_bytes": VMEM_LIMIT}
    if collective is not None:
        params.update(collective_id=collective, has_side_effects=True)
    return pl.pallas_call(
        kernel,
        out_shape=[jax.ShapeDtypeStruct(shape, dtype) for shape, dtype in outs],
        in_specs=in_specs,
        out_specs=specs(len(outs), any_out),
        scratch_shapes=scratch,
        compiler_params=pltpu.CompilerParams(**params),
    )(*args)


def on_device(
    clip_input, out_grad, clip_lengths, w_one, w_mid_in, w_mid, w_small_in, w_small, w_pool, bn_offset
):
    n = lax.axis_size("dp")
    bits = n.bit_length() - 1
    half, side = clip_input.shape[1], clip_input.shape[2]
    rows = side * 16
    side2 = side // 2
    rows2 = side2 * 8
    total2 = side2 * rows2
    unit = 32 << max(bits - 3, 0)
    packed_rows = [-(-r // unit) * unit for r in (512, 512, 512, 320, 256)]
    x = clip_input.transpose(0, 2, 3, 1, 4).reshape(2, side * side * half, D)
    og = out_grad.transpose(0, 2, 3, 1, 4)

    def like(a, dtype=BF16):
        return pltpu.VMEM(a.shape[1:], dtype)

    def turned(w):
        return w.transpose(0, 2, 1)

    weights = (w_one, turned(w_mid_in), turned(w_small_in), w_pool, turned(w_mid), w_small)
    dma = pltpu.SemaphoreType.DMA
    grid = (side, side, 2, 8)

    def bf(*shape):
        return vmem(*shape, dtype=BF16)

    pooled = (side2, side2, 8, DP)
    st1, stf, beta1, beta2, xgot, zin, zf, sig, hand, asum, bsum, cat, scat, *arranged, og_got = call(
        forward_kernel,
        [
            ((8, 640), F32),
            ((8, DP), F32),
            ((1, 1152), F32),
            ((1, 1152), F32),
            (x.shape[1:], BF16),
            (grid + (256,), F32),
            (grid + (DP,), F32),
            ((side, rows, DP), BF16),
            (pooled, F32),
            (pooled, F32),
            (pooled, F32),
            ((side + 2, rows, 512), BF16),
            ((side + 2, rows, 128), BF16),
            ((D, 640), BF16),
            ((D, 640), BF16),
            ((1536, 1024), BF16),
            ((1536, 1024), BF16),
            ((384, 384), BF16),
            ((384, 384), BF16),
            (og.shape[1:], BF16),
        ],
        (clip_lengths, bn_offset, x, og) + weights,
        [
            like(x),
            vmem(*grid, DP),
            vmem(*grid, 256),
            vmem(side, rows, 128),
            bf(side + 2, rows, 512),
            bf(side + 2, rows, 128),
            bf(side, rows, DP),
            vmem(*pooled),
            vmem(*pooled),
            vmem(*pooled),
            vmem(side2, 16, 128),
            vmem(1, 1152),
            vmem(1, 1152),
            bf(2, D, 640),
            bf(2, 1536, 1024),
            bf(2, 384, 384),
            vmem(8, 512),
            vmem(8, DP),
            vmem(8, 256),
            vmem(2, 2, 8, 640),
            vmem(2, 16, 640),
            vmem(2, 16, 512),
        ]
        + exchange_scratch(n, 16)
        + exchange_scratch(n, 8)
        + [dma((15,)), dma((6,)), dma((6,))],
        collective=1,
        any_in=range(2, 10),
        any_out=range(4, 20),
    )
    wp1, wp2, wf1, wf2, ws1, ws2 = arranged
    zin = zin.reshape(side, rows, 256)
    zf = zf.reshape(side, rows, DP)
    block_output, hg, *two, sums5, sums6, sums7 = call(
        second_kernel,
        [
            (og.shape, BF16),
            ((side2, side2, 8, DP), F32),
        ]
        + [((8, r, 128), BF16) for r in packed_rows]
        + [
            ((8, DP), F32),
            ((8, 640), F32),
            ((8, DP), F32),
        ],
        (clip_lengths, hand, asum, bsum, og, og_got, wp2, wf2, ws2, beta2, beta1),
        [
            like(og),
            vmem(side2, side2, 8, D),
            vmem(2, *og.shape[1:], dtype=BF16),
            dma((2,)),
            dma(()),
            dma(()),
            vmem(total2, DP, dtype=BF16),
            vmem(side2, rows2, 256),
            vmem(side2, rows2, 128),
            vmem(side2, rows2, DP),
            vmem(8, DP),
            vmem(side2, rows2, 128),
            vmem(side2 + 2, rows2, 128),
            vmem(side2 + 2, rows2, 640),
            vmem(total2, 1536, dtype=BF16),
            vmem(total2, 384, dtype=BF16),
            vmem(side2, rows2, 1024),
            vmem(side2, rows2, 384),
            vmem(side2, rows2, DP),
            vmem(side2, rows2, 1024),
            vmem(side2, rows2, 384),
            vmem(side2, rows2, 640),
            vmem(side2, rows2, 256),
            vmem(2, 8, 640),
            vmem(8, 640),
            vmem(8, 512),
            vmem(2, 8, DP),
            vmem(1536, 1024),
            vmem(384, 384),
            vmem(DP, 640),
            vmem(8, DP),
            vmem(8, 256),
        ]
        + exchange_scratch(n, 16)
        + exchange_scratch(n, 8)
        + exchange_scratch(n, 16)
        + exchange_scratch(n, 8)
        + exchange_scratch(n, 16),
        collective=2,
        any_in=(4,),
        any_out=(0,),
    )
    halves = [r // 2 for r in packed_rows]
    lands = []
    for i, h in enumerate(halves * 2):
        lands += [bf(*shape) for shape in land_shapes(8, h, bits, i in Z_FIRST)]
    gin, *full, offs = call(
        functools.partial(backward_kernel, bits),
        [(x.shape, BF16)]
        + [((2, 8, h, 128), BF16) for h in halves]
        + [((8, DP + 640), F32)],
        (clip_lengths, hg, stf, sums7, st1, beta1, sums5, sums6)
        + (zf, sig, zin, wf1, ws1, wp1, cat, scat, x, xgot, *two),
        [
            vmem(side, rows, 256),
            bf(1536, 1024),
            bf(384, 384),
            bf(D, 640),
            bf(side + 2, rows, 512),
            bf(side + 2, rows, 128),
            like(x),
            like(x),
            bf(side + 2, rows, 1024),
            bf(side + 2, rows, 384),
            bf(2, side, rows // 2, 384),
            bf(2, side, rows // 2, 256),
            vmem(8, 640),
            vmem(8, DP + 640),
            vmem(8, DP + 640),
            vmem(8, DP),
            vmem(8, 256),
            vmem(2, 16, 640),
        ]
        + exchange_scratch(n, 8)
        + [dma((18,)), dma((16,)), dma((16,)), dma((2 * len(lands),)), dma((2 * len(lands),))]
        + [dma((side,)), dma((side,))]
        + [bf(8, h, 128) for h in halves]
        + [bf(8, r, 128) for r in packed_rows]
        + [bf(8, h, 128) for h in halves * 2]
        + lands,
        collective=3,
        any_in=range(8, 23),
        any_out=range(6),
    )
    one, mid_in, mid, small_in, small, pool, offset, gin, block_output = call(
        unpack_kernel,
        [
            ((D, C0), F32),
            ((C1A, D), F32),
            ((C1B, 27 * C1A), F32),
            ((C2A, D), F32),
            ((27 * C2A, C2B), F32),
            ((D, C3), F32),
            ((1, 1024), F32),
            (x.shape, BF16),
            (og.shape, BF16),
        ],
        (*full, gin, block_output, offs),
        [bf(8, r, 128) for r in packed_rows]
        + [vmem(27 * C1A, 384), vmem(2, D, 128), bf(*x.shape), bf(*og.shape), dma((12,))],
        smem_first=False,
        any_in=range(7),
        any_out=(7, 8),
    )
    input_grad = gin.reshape(2, side, side, half, D).transpose(0, 3, 1, 2, 4)
    return (
        block_output.transpose(0, 3, 1, 2, 4),
        input_grad,
        one[None],
        mid_in.T[None],
        mid.T[None],
        small_in.T[None],
        small[None],
        pool[None],
        offset,
    )


def solution(mesh):
    placed = (
        P("dp", "section", None, None, None),
        P("dp", "section", None, None, None),
        P("dp", None),
        P("section", None, None),
        P("section", None, None),
        P("section", None, None),
        P("section", None, None),
        P("section", None, None),
        P("section", None, None),
        P("section", None),
    )
    return jax.shard_map(
        on_device,
        mesh=mesh,
        in_specs=placed,
        out_specs=(
            P("dp", "section", None, None, None),
            P("dp", "section", None, None, None),
            P("section", None, None),
            P("section", None, None),
            P("section", None, None),
            P("section", None, None),
            P("section", None, None),
            P("section", None, None),
            P("section", None),
        ),
        check_vma=False,
    )
```

```python
import functools

import jax
import jax.numpy as jnp
from jax import lax
from jax.experimental import pallas as pl
from jax.experimental.pallas import tpu as pltpu
from jax.sharding import PartitionSpec as P

D = 832
DP = 896
C0 = 256
C1A = 160
C1B = 320
C2A = 32
C2B = 128
C3 = 128
EPS = 0.001
MESH = pl.DeviceIdType.MESH
F32 = jnp.float32
BF16 = jnp.bfloat16
VMEM_LIMIT = 60 * 2**20


def dot(a, b):
    return jnp.dot(a, b, preferred_element_type=F32)


def dot_nt(a, b):
    return lax.dot_general(a, b, (((1,), (1,)), ((), ())), preferred_element_type=F32)


def dot_tn(a, b):
    return lax.dot_general(a, b, (((0,), (0,)), ((), ())), preferred_element_type=F32)


def roll_rows(x, by):
    return pltpu.roll(x, by % x.shape[0], 0)


def roll_lanes(x, by):
    return pltpu.roll(x, by % x.shape[1], 1)


def lane_below(x, count):
    lanes = lax.broadcasted_iota(jnp.int32, x.shape, 1)
    return jnp.where(lanes < count, x, 0.0)


class Clips:
    def __init__(self, len_ref, frames, stride):
        sec = lax.axis_index("section")
        f = lax.broadcasted_iota(jnp.int32, (frames, 128), 0)

        def label(v):
            place = v * stride
            out = jnp.zeros_like(v)
            start = jnp.int32(0)
            for c in range(len_ref.shape[1]):
                end = start + len_ref[sec, c]
                out = jnp.where((place >= start) & (place < end), c + 1, out)
                start = end
            return out

        here = label(f)
        inside = here > 0

        def mask(m):
            return jnp.where(m, 1.0, 0.0).astype(F32)

        self.frames = frames
        self.valid = mask(inside)
        self.before = mask(inside & (f > 0) & (label(f - 1) == here))
        self.after = mask(inside & (f < frames - 1) & (label(f + 1) == here))
        self.inv = 1.0 / jnp.maximum(self.valid + self.before + self.after, 1.0)

    def times(self, v, pattern):
        return (v.reshape(-1, self.frames, 128) * pattern).reshape(v.shape)

    def fold(self, v):
        return jnp.sum(v.reshape(-1, self.frames, v.shape[-1]), axis=0)


def shift_places(v, frames, by):
    lanes = v.shape[-1]
    v3 = v.reshape(-1, frames, lanes)
    zero = jnp.zeros((1, frames, lanes), v.dtype)
    if by > 0:
        v3 = jnp.concatenate([v3[1:], zero], 0)
    else:
        v3 = jnp.concatenate([zero, v3[:-1]], 0)
    return v3.reshape(v.shape)


def add_stats(clips, acc, lanes, v, w=None):
    acc[0, :, lanes] += clips.fold(v)
    acc[1, :, lanes] += clips.fold(v * (v if w is None else w))


def affine(st, lanes):
    total, square, count = st[0:1, lanes], st[1:2, lanes], st[2:3, lanes]
    mean = total / count
    scale = lax.rsqrt(square / count - mean * mean + EPS)
    return scale, mean


def fill_norm(coef, to, st, lanes, beta):
    scale, mean = affine(st, lanes)
    coef[0:1, to] = scale
    coef[1:2, to] = mean * scale
    coef[2:3, to] = beta - mean * scale
    coef[3:4, to] = beta


def fill_back(coef, to, sums, lanes, count):
    m1, m2 = sums[0:1, lanes] / count, sums[1:2, lanes] / count
    scale = coef[0:1, to]
    coef[4:5, to] = -scale * scale * m2
    coef[5:6, to] = scale * (coef[1:2, to] * m2 - m1)


def soft(t):
    s = 0.5 + 0.5 * jnp.tanh(0.5 * jnp.abs(t))
    return jnp.maximum(t, 0.0) - jnp.log(s), jnp.where(t >= 0, s, 1.0 - s)


def sigm(t):
    return 0.5 + 0.5 * jnp.tanh(0.5 * t)


def greet(partner=False):
    n = lax.axis_size("dp")
    me = lax.axis_index("dp")
    barrier = pltpu.get_barrier_semaphore()

    def go(k, _):
        pl.semaphore_signal(
            barrier, inc=1, device_id={"dp": lax.rem(me + k, n)}, device_id_type=MESH
        )
        return 0

    if partner:
        other = 1 - lax.axis_index("section")
        pl.semaphore_signal(barrier, inc=1, device_id={"section": other}, device_id_type=MESH)
    lax.fori_loop(1, n, go, 0)


def greeted(partner=False):
    pl.semaphore_wait(pltpu.get_barrier_semaphore(), lax.axis_size("dp") - 1 + int(partner))


def exchange_start(loc, buf, ssem, rsem):
    n = lax.axis_size("dp")
    me = lax.axis_index("dp")

    def start(k, _):
        pltpu.make_async_remote_copy(
            src_ref=loc,
            dst_ref=buf.at[me],
            send_sem=ssem.at[k],
            recv_sem=rsem.at[me],
            device_id={"dp": lax.rem(me + k, n)},
            device_id_type=MESH,
        ).start()
        return 0

    lax.fori_loop(1, n, start, 0)
    buf[me] = loc[...]


def exchange_finish(loc, buf, ssem, rsem, out, tiles):
    n = lax.axis_size("dp")
    me = lax.axis_index("dp")

    def wait(k, _):
        j = lax.rem(me + k, n)
        copy = pltpu.make_async_remote_copy(
            src_ref=loc,
            dst_ref=buf.at[j],
            send_sem=ssem.at[k],
            recv_sem=rsem.at[j],
            device_id={"dp": j},
            device_id_type=MESH,
        )
        copy.wait_send()
        copy.wait_recv()
        return 0

    lax.fori_loop(1, n, wait, 0)
    total = jnp.sum(buf[...], axis=0)
    at = 2 * len(tiles)
    for i, t in enumerate(tiles):
        lanes = slice(128 * t, 128 * t + 128)
        out[0:1, lanes] = total[2 * i : 2 * i + 1]
        out[1:2, lanes] = total[2 * i + 1 : 2 * i + 2]
        if at < loc.shape[0]:
            out[2:3, lanes] = total[at : at + 1]


def exchange(loc, buf, ssem, rsem, out, tiles):
    exchange_start(loc, buf, ssem, rsem)
    exchange_finish(loc, buf, ssem, rsem, out, tiles)


def swap_copy(src, dst, ssem, rsem):
    return pltpu.make_async_remote_copy(
        src_ref=src,
        dst_ref=dst,
        send_sem=ssem,
        recv_sem=rsem,
        device_id={"section": 1 - lax.axis_index("section")},
        device_id_type=MESH,
    )


def exchange_scratch(n, rows):
    return [
        pltpu.VMEM((rows, 128), F32),
        pltpu.VMEM((n, rows, 128), F32),
        pltpu.SemaphoreType.DMA((n,)),
        pltpu.SemaphoreType.DMA((n,)),
    ]


FIRST, CONV, FINAL, INNER = range(5), range(4), range(7), (3, 4)


def pack_stats(clips, loc, acc, tiles, count=None):
    for i, t in enumerate(tiles):
        lanes = pl.ds(128 * t, 128)
        for k in range(2):
            loc[2 * i + k : 2 * i + k + 1, :] = jnp.sum(
                acc[k, :, lanes] * clips.valid, axis=0, keepdims=True
            )
    if count is not None:
        at = 2 * len(tiles)
        loc[at : at + 1, :] = jnp.sum(clips.valid, axis=0, keepdims=True) * float(count)


def loop(n, body):
    def step(i, _):
        body(i)
        return 0

    lax.fori_loop(0, n, step, 0)


def inv_edges(side, frames, y):
    x = lax.broadcasted_iota(jnp.int32, (side, frames, 128), 0)
    ex = jnp.where((x == 0) | (x == side - 1), 0.5, 1.0 / 3.0).astype(F32)
    ey = jnp.where((y == 0) | (y == side - 1), 0.5, 1.0 / 3.0).astype(F32)
    return (ex * ey).reshape(side * frames, 128)


def box(clips, side, load, tx, store):
    frames = clips.frames
    tx[0] = jnp.zeros(tx.shape[1:], F32)
    tx[side + 1] = jnp.zeros(tx.shape[1:], F32)

    def across(y):
        v = load(y)
        t = clips.times(v, clips.valid)
        t = t + clips.times(roll_rows(v, 1), clips.before)
        t = t + clips.times(roll_rows(v, -1), clips.after)
        tx[y + 1] = t + shift_places(t, frames, 1) + shift_places(t, frames, -1)

    def down(y):
        store(y, tx[y] + tx[y + 1] + tx[y + 2])

    loop(side, across)
    loop(side, down)


def pool_forward(clips, side, load, tx, zp, acc):
    def store(y, v):
        z = clips.times(v * inv_edges(side, clips.frames, y), clips.inv)
        zp[y] = z
        add_stats(clips, acc, pl.ds(256, 128), z)

    box(clips, side, load, tx, store)


def upright(src, dst):
    rows = src.shape[1]
    width = src.shape[0]

    def body(i):
        at = pl.ds(pl.multiple_of(i * 128, 128), 128)
        dst[at, 0:width] = src[:, at].astype(F32).T.astype(BF16)

    loop(rows // 128, body)
    if rows % 128:
        at = slice(rows - rows % 128, rows)
        dst[at, 0:width] = src[:, at].astype(F32).T.astype(BF16)


def arrange_first(src, wp, b, flip):
    one, mid_in, small_in, pool = src
    wp[b, :, 0:256] = one[...]
    wp[b, :, 256:384] = pool[...]
    upright(mid_in, flip)
    wp[b, :, 384:544] = flip[0:D, 0:C1A]
    upright(small_in, flip)
    wp[b, :, 544:576] = flip[0:D, 0:C2A]
    wp[b, :, 576:640] = jnp.zeros((D, 64), BF16)


def arrange_beta(src, dst):
    v = jnp.concatenate([jnp.broadcast_to(src[...], (8, 1024)), jnp.zeros((8, 128), F32)], 1)
    lane = lax.broadcasted_iota(jnp.int32, v.shape, 1)
    out = jnp.zeros_like(v)
    for lo, hi, by in (
        (0, 256, 0),
        (256, 576, -160),
        (576, 832, -192),
        (896, 1056, 640),
        (1056, 1088, 320),
    ):
        out = jnp.where((lane >= lo) & (lane < hi), roll_lanes(v, by), out)
    dst[...] = out[0:1]


def arrange_conv(mid_flat, small, wf, ws, b, mid):
    upright(mid_flat, mid)
    for dy in range(3):
        wf[b, 512 * dy + 480 : 512 * dy + 512, :] = jnp.zeros((32, 1024), BF16)
        ws[b, 128 * dy + 96 : 128 * dy + 128, :] = jnp.zeros((32, 384), BF16)
        wf[b, 512 * dy : 512 * dy + 512, 960:1024] = jnp.zeros((512, 64), BF16)
        for dt in range(3):
            for dx in range(3):
                r = 96 * (3 * dt + dy) + 32 * dx
                to = 128 * dy + 32 * dt
                ws[b, to : to + 32, 128 * dx : 128 * dx + 128] = small[r : r + 32, :]
            for dx in range(3):
                r = 480 * (3 * dt + dy) + 160 * dx
                for rows, to in ((128, 128 * dt), (32, 384 + 32 * dt)):
                    to = to + 512 * dy
                    wf[b, to : to + rows, 256 * dx : 256 * dx + 256] = mid[r : r + rows, 0:256]
                    wf[b, to : to + rows, 768 + 64 * dx : 832 + 64 * dx] = mid[
                        r : r + rows, 256:320
                    ]
                    r = r + rows


def inner_tiles(clips, z, coef):
    tiles = []
    for t in range(2):
        lanes = slice(128 * t, 128 * t + 128)
        act, _ = soft(z[:, lanes] * coef[0:1, lanes] + coef[2:3, lanes])
        tiles.append(clips.times(act, clips.valid))
    return tiles


def fill_inner(coef, st, beta):
    for t in range(2):
        lanes = pl.ds(128 * t, 128)
        fill_norm(coef, lanes, st, pl.ds(384 + 128 * t, 128), beta[0:1, 896 + 128 * t : 1024 + 128 * t])


def tap_tiles(clips, a, b):
    def before(v):
        return clips.times(roll_rows(v, 1), clips.before)

    def after(v):
        return clips.times(roll_rows(v, -1), clips.after)

    lane = lax.broadcasted_iota(jnp.int32, b.shape, 1)
    ones = clips.times(jnp.where(lane == 96, 1.0, 0.0).astype(F32), clips.valid)

    def three32(v):
        return before(v) + roll_lanes(v, 32) + roll_lanes(after(v), 64) + ones

    tail = lane_below(b, 32)
    small = lane_below(roll_lanes(b, -32), 32)
    return [before(a), a, after(a), three32(tail)], three32(small)


def untap(clips, parts, small):
    def before(v):
        return roll_rows(clips.times(v, clips.before), -1)

    def after(v):
        return roll_rows(clips.times(v, clips.after), 1)

    def back32(v):
        return (
            lane_below(before(v), 32)
            + lane_below(roll_lanes(v, -32), 32)
            + lane_below(roll_lanes(after(v), -64), 32)
        )

    a = before(parts[0]) + parts[1] + after(parts[2])
    return a, back32(parts[3]) + roll_lanes(back32(small), 32)


def typical(beta):
    sp, sg = soft(jnp.broadcast_to(beta, (8, beta.shape[-1])))
    return sp + 0.5 * sg * (1.0 - sg)


def outer(c, s):
    k = lax.broadcasted_iota(jnp.int32, c.shape, 0)
    c = jnp.where(k < 2, c, 0.0).astype(BF16)
    s = jnp.broadcast_to(s, (8, s.shape[-1]))
    high = s.astype(BF16).astype(F32)
    k = lax.broadcasted_iota(jnp.int32, s.shape, 0)
    s = jnp.where(k == 0, high, jnp.where(k == 1, s - high, 0.0)).astype(BF16)
    return dot_tn(c, s)


def tap_points(beta):
    a = typical(beta[0:1, 896:1024])
    b = typical(beta[0:1, 1024:1152])

    def three(v):
        return v + roll_lanes(v, 32) + roll_lanes(v, 64)

    tail = three(lane_below(b, 32))
    small = three(lane_below(roll_lanes(b, -32), 32))
    return jnp.concatenate([a, a, a, tail], 1), small


def centre_mid(row, beta):
    c, _ = tap_points(beta)
    row = jnp.broadcast_to(row, (8, 1024))
    main = row[:, 256:512]
    tail = lane_below(roll_lanes(row[:, 768:896], 64), 64)
    s = jnp.concatenate([main, main, main, tail + roll_lanes(tail, 64), tail], 1)
    return outer(c, s)


def centre_small(grad, beta):
    _, c = tap_points(beta)
    row = jnp.broadcast_to(grad[224:225, 128:256], (8, 128))
    return outer(c, jnp.concatenate([row, row, row], 1))


def conv_gather(frames, p, s):
    def three(at):
        return (
            shift_places(at(0), frames, -1) + at(1) + shift_places(at(2), frames, 1)
        )

    main = three(lambda k: p[:, 256 * k : 256 * k + 256])
    small = three(lambda k: s[:, 128 * k : 128 * k + 128])
    ends = p[:, 768:896]
    tail = three(lambda k: (ends, roll_lanes(ends, 64), p[:, 896:1024])[k])
    return main, small, lane_below(tail, 64)


def spread_x(frames, v, by):
    return v if by == 0 else shift_places(v, frames, -by)


def put_spread(frames, main, small, tail, put_mid, put_small):
    for k in range(3):
        put_mid(256 * k, spread_x(frames, main, k - 1))
        put_small(128 * k, spread_x(frames, small, k - 1))
    put_mid(768, spread_x(frames, tail, -1) + roll_lanes(tail, 64))
    put_mid(896, spread_x(frames, tail, 1))


def join_final(small, tail, pool):
    s, p = roll_lanes(small, 64), roll_lanes(pool, 64)
    low = lax.broadcasted_iota(jnp.int32, small.shape, 1) < 64
    return jnp.where(low, tail, s), jnp.where(low, s, p), jnp.where(low, p, 0.0)


def split_final(t4, t5, t6):
    a, b, c = roll_lanes(t4, 64), roll_lanes(t5, 64), roll_lanes(t6, 64)
    low = lax.broadcasted_iota(jnp.int32, t4.shape, 1) < 64
    return jnp.where(low, a, b), jnp.where(low, t4, 0.0), jnp.where(low, b, c)


def final_stats(st1, st2, stf):
    stf[:, 0:256] = st1[:, 0:256]
    stf[:, 256:512] = st2[:, 0:256]
    for t, v in enumerate(join_final(st2[:, 256:384], st2[:, 384:512], st1[:, 256:384])):
        stf[:, 512 + 128 * t : 640 + 128 * t] = v
    stf[2:3, :] = jnp.broadcast_to(st1[2:3, 0:1], (1, DP))


def store_conv(clips, y, p, s, zp, put, acc):
    main, small, tail = conv_gather(clips.frames, p, s)
    put(y, 256, main)
    for t, v in enumerate(join_final(small, tail, zp[y])):
        put(y, 512 + 128 * t, v)
    add_stats(clips, acc, pl.ds(0, 256), main)
    add_stats(clips, acc, pl.ds(256, 128), small)
    add_stats(clips, acc, pl.ds(384, 128), tail)


def forward_part(
    len_ref, bn, x, og, w_one, w_mid_in, w_small_in, w_pool, w_mid, w_small,
    st1, stf, beta1, xgot_out, zin_out, zf_out, sig_out, cat_out, scat_out, wp1, wf1, ws1, og_got,
    x_got, hand, asum, bsum, beta2, beta, got_beta, wp, wf, ws,
    loc, buf, ssem, rsem, loc2, buf2, ssem2, rsem2, osem, psem, qsem,
    zf, zin, zp, cat, scat, sig, scr, st2, coef, coef_in, hacc, acc, acc2,
):
    greet(partner=True)
    sec = lax.axis_index("section")
    side = zp.shape[0]
    rows = side * 16
    clips = Clips(len_ref, 16, 1)
    hacc[...] = jnp.zeros_like(hacc)
    acc[...] = jnp.zeros_like(acc)
    acc2[...] = jnp.zeros_like(acc2)
    loc[...] = jnp.zeros_like(loc)
    loc2[...] = jnp.zeros_like(loc2)
    outs = []

    def put(src, dst):
        c = pltpu.make_async_copy(src, dst, osem.at[len(outs)])
        c.start()
        outs.append(c)

    pairs = ((wp.at[sec], wp.at[sec]), (beta, got_beta), (x.at[1 - sec], x_got))
    pairs += ((og.at[1 - sec], og_got), (wf.at[sec], wf.at[sec]), (ws.at[sec], ws.at[sec]))
    remote = [swap_copy(a, b, psem.at[i], qsem.at[i]) for i, (a, b) in enumerate(pairs)]

    def first_phase(x_own, yp, tx, one, mid_in, small_in, pool, mid, small, flip, lsem):
        local = [
            pltpu.make_async_copy(a, b, lsem.at[i])
            for i, (a, b) in enumerate(
                (
                    (x.at[sec], x_own),
                    (w_one.at[0], one),
                    (w_mid_in.at[0], mid_in),
                    (w_small_in.at[0], small_in),
                    (w_pool.at[0], pool),
                    (w_mid.at[0], mid),
                    (w_small.at[0], small),
                )
            )
        ]
        for c in local[1:] + local[:1]:
            c.start()
        arrange_beta(bn, beta)
        for c in local[1:5]:
            c.wait()
        arrange_first((one, mid_in, small_in, pool), wp, sec, flip)
        greeted(partner=True)
        for c in remote[:4]:
            c.start()
        for c in local[5:]:
            c.wait()
        arrange_conv(mid, small, wf, ws, sec, flip)
        for c in remote[4:]:
            c.start()
        for c in remote[:2]:
            c.wait()
        beta1[...] = jnp.where(sec == 0, beta[...], got_beta[...])
        beta2[...] = jnp.where(sec == 0, got_beta[...], beta[...])
        ny = side // 2
        size = ny * side * 8
        for k, src in enumerate((x_own, x_got)):
            (local[0] if k == 0 else remote[2]).wait()
            half = sec if k == 0 else 1 - sec

            def body(i, src=src, half=half):
                here = pl.ds(i * ny, ny)
                y = dot(src[pl.ds(pl.multiple_of(i * size, 16), size)], wp[0])

                def place(lo, hi):
                    return y[:, lo:hi].reshape(ny, side, 8, hi - lo)

                zf[here, :, half, :, 0:256] = place(0, 256)
                yp[here, :, half] = place(256, 384)
                zin[here, :, half] = place(384, 640)
                for lo, hi in ((0, 256), (384, 640)):
                    v = y[:, lo:hi].reshape(-1, 8, 256)
                    hacc[0, half, :, lo:hi] += jnp.sum(v, axis=0)
                    hacc[1, half, :, lo:hi] += jnp.sum(v * v, axis=0)

            loop(2, body)
        acc[...] = hacc[...].reshape(acc.shape)
        pool_forward(clips, side, lambda y: yp[y].reshape(rows, 128), tx, zp, acc)

    like = [pltpu.VMEM(a.shape[1:], BF16) for a in (w_one, w_mid_in, w_small_in, w_pool, w_mid, w_small)]
    pl.run_scoped(
        first_phase,
        pltpu.VMEM(x.shape[1:], BF16),
        vmem(side, side, 2, 8, 128),
        vmem(side + 2, rows, 128),
        *like,
        vmem(27 * C1A, 384, dtype=BF16),
        pltpu.SemaphoreType.DMA((7,)),
    )
    pack_stats(clips, loc, acc, FIRST, side * side)
    exchange_start(loc, buf, ssem, rsem)
    put(x_got, xgot_out)
    put(zin, zin_out)
    for y in (0, side + 1):
        cat[y] = jnp.zeros(cat.shape[1:], BF16)
        scat[y] = jnp.zeros(scat.shape[1:], BF16)
    exchange_finish(loc, buf, ssem, rsem, st1, FIRST)
    fill_inner(coef_in, st1, beta1)

    def build(y):
        a, b = inner_tiles(clips, zin[y].reshape(rows, 256), coef_in)
        parts, small = tap_tiles(clips, a, b)
        for i, part in enumerate(parts):
            cat[y + 1, :, 128 * i : 128 * i + 128] = part.astype(BF16)
        scat[y + 1] = small.astype(BF16)

    loop(side, build)
    for c in remote[3:]:
        c.wait()
    put(cat, cat_out)
    put(scat, scat_out)
    for a, b in ((wf, wf1), (ws, ws1), (wp, wp1)):
        put(a.at[0], b)
    ny = 2

    def put_row(y, lane, v):
        zf[y, :, :, :, lane : lane + v.shape[-1]] = v.reshape(side, 2, 8, v.shape[-1])

    def products(i):
        y0 = i * ny

        def taps(ref):
            return jnp.concatenate(
                [ref[pl.ds(y0 + dy, ny)].reshape(ny * rows, ref.shape[-1]) for dy in range(3)], axis=1
            )

        p = dot(taps(cat), wf[0])
        s = dot(taps(scat), ws[0])
        for q in range(ny):
            here = slice(q * rows, (q + 1) * rows)
            store_conv(clips, y0 + q, p[here], s[here], zp, put_row, acc2)

    loop(side // ny, products)
    pack_stats(clips, loc2, acc2, CONV)
    exchange_start(loc2, buf2, ssem2, rsem2)
    put(zf, zf_out)
    half = side // 2

    pair_valid = clips.valid.reshape(8, 2, 128)[:, 0] * 0.125

    def emit(k, tiles):
        for t in tiles:
            lanes = pl.ds(128 * t, 128)
            scale, shift, b = coef[0:1, lanes], coef[2:3, lanes], coef[3:4, lanes]
            pooled = None
            for q in range(2):
                t_in = zf[2 * k + q, :, :, :, lanes].reshape(rows, 128) * scale + shift
                sp, sg = soft(t_in)
                if t == 6:
                    lane = lax.broadcasted_iota(jnp.int32, sp.shape, 1)
                    sp = jnp.where(lane == 127, 1.0, lane_below(sp, 64))
                    sg = lane_below(sg, 64)
                sig[2 * k + q, :, lanes] = sg.astype(BF16)
                three = [
                    jnp.sum(v.reshape(half, 2, 16, 128), axis=1) for v in (sp, sg, sg * (t_in - b))
                ]
                pooled = three if pooled is None else [x + y for x, y in zip(pooled, three)]
            for v, dst in zip(pooled, (hand, asum, bsum)):
                scr[...] = v
                dst[k, :, :, lanes] = (
                    scr[:, pl.ds(0, 8, stride=2), :] + scr[:, pl.ds(1, 8, stride=2), :]
                ) * pair_valid

    for t in range(2):
        lanes = pl.ds(128 * t, 128)
        fill_norm(coef, lanes, st1, lanes, beta1[0:1, lanes])
    loop(half, lambda k: emit(k, (0, 1)))
    exchange_finish(loc2, buf2, ssem2, rsem2, st2, CONV)
    final_stats(st1, st2, stf)
    for t in range(2, 7):
        lanes = pl.ds(128 * t, 128)
        fill_norm(coef, lanes, stf, lanes, beta1[0:1, lanes])
    base = len(outs)

    def rest(k):
        emit(k, range(2, 7))
        here = pl.ds(2 * k, 2)
        pltpu.make_async_copy(sig.at[here], sig_out.at[here], osem.at[base]).start()

    loop(half, rest)
    for c in outs:
        c.wait()
    pltpu.make_async_copy(sig, sig_out, osem.at[base]).wait()


def second_part(
    len_ref, og, beta1, block_out, hg_out, packed_out, sums5, sums6, sums7, og_got,
    hand, asum, bsum, beta, wp, wf, ws, psem, qsem, sums_scratch,
    gown, ggot, grad, out, lsem, hg, packed,
    hbuf, zin, zp, zf, stf, yp, tx, catf, cat, scat, pbuf, sbuf, dbuf, dzc, dzs, dz1, din,
    acc, st3, st4, acc7, accm, accs, accp, coef, coef_in,
):
    (
        loc3, buf3, ss3, rs3, loc4, buf4, ss4, rs4, loc5, buf5, ss5, rs5,
        loc6, buf6, ss6, rs6, loc7, buf7, ss7, rs7,
    ) = sums_scratch
    sec = lax.axis_index("section")
    own = pltpu.make_async_copy(og.at[sec], gown, lsem.at[0])
    other = pltpu.make_async_copy(og_got, ggot, lsem.at[2])
    own.start()
    other.start()
    side = hand.shape[0]
    rows = side * 8
    total = side * rows
    clips = Clips(len_ref, 8, 2)
    for ref in (acc, acc7, loc3, loc4, loc5, loc6, loc7):
        ref[...] = jnp.zeros_like(ref)

    hbuf[...] = hand[...].reshape(total, DP).astype(BF16)
    y = dot(hbuf[:, 0:D], wp[...])
    zf[:, :, 0:C0] = y[:, 0:C0].reshape(side, rows, C0)
    yp[...] = y[:, 256:384].reshape(side, rows, 128)
    zin[...] = y[:, 384:640].reshape(side, rows, 256)

    def first_sums(y):
        add_stats(clips, acc, pl.ds(0, 256), zf[y, :, 0:256])
        add_stats(clips, acc, pl.ds(384, 256), zin[y])

    loop(side, first_sums)
    pool_forward(clips, side, lambda y: yp[y], tx, zp, acc)
    pack_stats(clips, loc3, acc, FIRST, side * side)
    exchange_start(loc3, buf3, ss3, rs3)
    own.wait()
    other.wait()
    mine, theirs = gown[...].astype(F32), ggot[...].astype(F32)
    low = jnp.where(sec == 0, mine, theirs)
    high = jnp.where(sec == 0, theirs, mine)
    grad[...] = jnp.concatenate([low, high], 2)
    exchange_finish(loc3, buf3, ss3, rs3, st3, FIRST)

    fill_inner(coef_in, st3, beta)
    catf[0] = jnp.zeros(catf.shape[1:], F32)
    catf[side + 1] = jnp.zeros(catf.shape[1:], F32)

    def build(y):
        a, b = inner_tiles(clips, zin[y], coef_in)
        parts, small = tap_tiles(clips, a, b)
        for t, v in enumerate(parts + [small]):
            catf[y + 1, :, 128 * t : 128 * t + 128] = v

    loop(side, build)
    for dy in range(3):
        v = catf[dy : dy + side].reshape(total, 640).astype(BF16)
        cat[:, 512 * dy : 512 * dy + 512] = v[:, 0:512]
        scat[:, 128 * dy : 128 * dy + 128] = v[:, 512:640]
    pbuf[...] = dot(cat[...], wf[...]).reshape(side, rows, 1024)
    sbuf[...] = dot(scat[...], ws[...]).reshape(side, rows, 384)
    acc[...] = jnp.zeros_like(acc)

    def put_row(y, lane, v):
        zf[y, :, lane : lane + v.shape[-1]] = v

    loop(side, lambda y: store_conv(clips, y, pbuf[y], sbuf[y], zp, put_row, acc))
    pack_stats(clips, loc4, acc, CONV)
    exchange(loc4, buf4, ss4, rs4, st4, CONV)
    final_stats(st3, st4, stf)
    for t in range(7):
        lanes = pl.ds(128 * t, 128)
        fill_norm(coef, lanes, stf, lanes, beta[0:1, lanes])

    def emit(y):
        for t in range(7):
            lanes = pl.ds(128 * t, 128)
            t_in = zf[y, :, lanes] * coef[0:1, lanes] + coef[2:3, lanes]
            u = t_in - coef[3:4, lanes]
            sp, sg = soft(t_in)
            width = 128 if t < 6 else 64
            gr = grad[y, :, :, 128 * t : 128 * t + width].reshape(rows, width)
            if t == 6:
                gr = jnp.concatenate([gr, jnp.zeros((rows, 64), F32)], 1)
            d = gr * clips.times(sg, clips.valid)
            dbuf[y, :, lanes] = d
            add_stats(clips, acc7, lanes, d, u)
            sp = clips.times(sp, clips.valid).reshape(side, 8, 128)[:, :, 0:width]
            for h in range(2):
                out[h, y, :, :, 128 * t : 128 * t + width] = sp[:, 4 * h : 4 * h + 4].astype(BF16)

    loop(side, emit)
    mine = pltpu.make_async_copy(out.at[sec], block_out.at[sec], lsem.at[1])
    mine.start()
    theirs = swap_copy(out.at[1 - sec], block_out.at[sec], psem, qsem)
    theirs.start()
    pack_stats(clips, loc5, acc7, FINAL)
    exchange(loc5, buf5, ss5, rs5, sums5, FINAL)
    count = st3[2:3, 0:128]
    for t in range(7):
        lanes = pl.ds(128 * t, 128)
        fill_back(coef, lanes, sums5, lanes, count)

    def dz_of(y, t):
        lanes = pl.ds(128 * t, 128)
        v = dbuf[y, :, lanes] * coef[0:1, lanes] + zf[y, :, lanes] * coef[4:5, lanes]
        return clips.times(v + coef[5:6, lanes], clips.valid)

    def dz_final(y):
        for t in range(2):
            dz1[y, :, 128 * t : 128 * t + 128] = dz_of(y, t)
        main = jnp.concatenate([dz_of(y, 2), dz_of(y, 3)], 1)
        small, tail, pool = split_final(*(dz_of(y, t) for t in (4, 5, 6)))
        yp[y] = clips.times(pool * inv_edges(side, 8, y), clips.inv)

        def put(ref):
            def go(lane, v):
                ref[y, :, lane : lane + v.shape[-1]] = v

            return go

        put_spread(8, main, small, tail, put(dzc), put(dzs))

    loop(side, dz_final)

    def boxed(y, v):
        dz1[y, :, 256:384] = clips.times(v, clips.valid)

    box(clips, side, lambda y: yp[y], tx, boxed)
    dzc_b = dzc[...].reshape(total, 1024).astype(BF16)
    dzs_b = dzs[...].reshape(total, 384).astype(BF16)
    for dy in (-1, 0, 1):
        k = dy + 1
        q = dot_nt(dzc_b, wf[512 * k : 512 * k + 512]).reshape(side, rows, 512)
        r = dot_nt(dzs_b, ws[128 * k : 128 * k + 128]).reshape(side, rows, 128)
        if k == 0:
            catf[1 : side + 1] = jnp.zeros((side, rows, 640), F32)
        catf[1 + dy : 1 + dy + side, :, 0:512] += q
        catf[1 + dy : 1 + dy + side, :, 512:640] += r
    acc[...] = jnp.zeros_like(acc)

    def inner_back(y):
        parts = [catf[y + 1, :, 128 * t : 128 * t + 128] for t in range(5)]
        inner_up(clips, zin[y], untap(clips, parts[:4], parts[4]), coef_in, acc, din, y)

    loop(side, inner_back)
    pack_stats(clips, loc6, acc, INNER)
    exchange_start(loc6, buf6, ss6, rs6)
    accm[...] = dot_tn(cat[...], dzc_b)
    exchange_finish(loc6, buf6, ss6, rs6, sums6, INNER)
    fill_inner_back(coef_in, sums6, count)

    def dz_inner(y):
        for t in range(2):
            dz1[y, :, 384 + 128 * t : 512 + 128 * t] = inner_dz(
                clips, t, zin[y], din[y], coef_in
            )

    loop(side, dz_inner)
    dz1_b = dz1[...].reshape(total, 640).astype(BF16)
    hgv = dot_nt(dz1_b, wp[...]).astype(BF16).astype(F32)
    hg[:, :, :, 0:D] = hgv.reshape(side, side, 8, D)
    hg[:, :, :, D:DP] = jnp.zeros((side, side, 8, DP - D), F32)
    acc7[...] = jnp.zeros_like(acc7)

    def upstream(y):
        for t in range(7):
            lanes = pl.ds(128 * t, 128)
            gr = hg[y, :, :, lanes]
            acc7[0, :, lanes] += jnp.sum(gr * asum[y, :, :, lanes], axis=0)
            acc7[1, :, lanes] += jnp.sum(gr * bsum[y, :, :, lanes], axis=0)

    loop(side, upstream)
    pack_stats(clips, loc7, acc7, FINAL)
    exchange_start(loc7, buf7, ss7, rs7)
    accs[...] = dot_tn(scat[...], dzs_b)
    accp[...] = dot_tn(hbuf[...], dz1_b)
    pool = dz1[:, :, 256:384].reshape(total, 128)
    rest = (pool - dz1_b[:, 256:384].astype(F32)).astype(BF16)
    accp[:, 256:384] += dot_tn(hbuf[...], rest)
    c = jnp.concatenate([typical(beta1[0:1, 0:D]), jnp.zeros((8, DP - D), F32)], 1)
    full = accp[...] - outer(c, accp[DP - 1 : DP, :])
    mid = centre_mid(accm[992:993, :], beta)
    small = centre_small(accs, beta)
    for k in range(3):
        pack_mid(packed[k], accm.at[512 * k : 512 * k + 512], mid, accs, small, k)

    def column(t, r, rows):
        return full[r : r + rows, 128 * t : 128 * t + 128]

    pack_one(packed[3], column)
    pack_inner(packed[4], column, accs, small)
    puts = [
        pltpu.make_async_copy(a, b, lsem.at[3 + i])
        for i, (a, b) in enumerate(zip((hg,) + packed, (hg_out,) + packed_out))
    ]
    for c in puts:
        c.start()
    exchange_finish(loc7, buf7, ss7, rs7, sums7, FINAL)
    mine.wait()
    theirs.wait()
    for c in puts:
        c.wait()


def blocks_kernel(first_scope, second_scope, *refs):
    ins, outs, refs = refs[:10], refs[10:33], refs[33:]
    len_ref, og = ins[0], ins[3]
    st1, stf, beta1, sums5, sums6, sums7 = outs[:6]
    kept, og_got, block_out, hg_out, packed_out = outs[6:15], outs[15], outs[16], outs[17], outs[18:]
    x_got, hand, asum, bsum, beta2, beta, got_beta, wp, wf, ws = refs[:10]
    sums1, sums2, (osem, psem, qsem, psem2, qsem2) = refs[10:18], refs[18:38], refs[38:]

    def one(*own):
        forward_part(
            *ins, st1, stf, beta1, *kept, og_got,
            x_got, hand, asum, bsum, beta2, beta, got_beta, wp, wf, ws,
            *sums1, osem, psem, qsem, *own,
        )

    def two(gown, ggot, grad, out, lsem, hg, p0, p1, p2, p3, p4, *own):
        second_part(
            len_ref, og, beta1, block_out, hg_out, tuple(packed_out), sums5, sums6, sums7, og_got,
            hand, asum, bsum, beta2, wp.at[1], wf.at[1], ws.at[1], psem2, qsem2, sums2,
            gown, ggot, grad, out, lsem, hg, (p0, p1, p2, p3, p4), *own,
        )

    pl.run_scoped(one, *first_scope)
    pl.run_scoped(two, *second_scope)


def pack_mid(packed, acc, mid, accs, small, k):
    for t in range(8):
        lanes = slice(128 * t, 128 * t + 128)
        packed[t, 0:480] = (acc[0:480, lanes] - mid[0:480, lanes]).astype(BF16)
        packed[t, 480:512] = small_piece(accs, small, 8 * k + t)
        if packed.shape[1] > 512:
            packed[t, 512:] = jnp.zeros((packed.shape[1] - 512, 128), BF16)


def small_piece(accs, small, b):
    dy, dt, dx = b // 9, b // 3 % 3, b % 3
    lanes = slice(128 * dx, 128 * dx + 128)
    r = 128 * dy + 32 * dt
    return (accs[r : r + 32, lanes] - small[32 * dt : 32 * dt + 32, lanes]).astype(BF16)


def pack_one(packed, column):
    end = packed.shape[1]
    for j in range(8):
        packed[j, 0:208] = column(j // 4, 208 * (j % 4), 208).astype(BF16)
        rows = min(112, D - 112 * j)
        packed[j, 208 : 208 + rows] = column(2, 112 * j, rows).astype(BF16)
        if 208 + rows < end:
            packed[j, 208 + rows : end] = jnp.zeros((end - 208 - rows, 128), BF16)


def pack_inner(packed, column, accs, small):
    end = packed.shape[1]
    for j in range(8):
        packed[j, 0:208] = column(3 + j // 4, 208 * (j % 4), 208).astype(BF16)
        packed[j, 208:end] = jnp.zeros((end - 208, 128), BF16)
        if j < 3:
            packed[j, 208:240] = small_piece(accs, small, 24 + j)


def inner_up(clips, z, backs, coef, acc, din, y):
    for t in range(2):
        lanes = slice(128 * t, 128 * t + 128)
        zs = z[:, lanes] * coef[0:1, lanes]
        d = backs[t] * clips.times(sigm(zs + coef[2:3, lanes]), clips.valid)
        din[y, :, lanes] = d
        add_stats(clips, acc, pl.ds(384 + 128 * t, 128), d, zs - coef[1:2, lanes])


def fill_inner_back(coef, sums, count):
    for t in range(2):
        fill_back(coef, pl.ds(128 * t, 128), sums, pl.ds(384 + 128 * t, 128), count)


def inner_dz(clips, t, z, d, coef):
    lanes = slice(128 * t, 128 * t + 128)
    v = d[:, lanes] * coef[0:1, lanes] + z[:, lanes] * coef[4:5, lanes] + coef[5:6, lanes]
    dz = clips.times(v, clips.valid)
    return lane_below(dz, 64) if t == 1 else dz


def put_halves(ref, y, lane, v):
    side, lanes = v.shape[0] // 16, v.shape[1]
    v = v.reshape(side, 2, 8, lanes)
    for h in range(2):
        ref[h, y, :, lane : lane + lanes] = v[:, h].reshape(side * 8, lanes).astype(BF16)


Z_FIRST = (3,)
SCHEDULE = {
    "start": ((1, 0), (4, 0),),
    "dz2": ((3, 0),),
    "dz3": ((1, 1), (2, 0),),
    "dz4": ((4, 1), (0, 0), (3, 1),),
    "dzend": ((1, 2), (2, 1),),
    "scat": ((0, 1), (1, 3),),
    "d1": ((4, 2), (6, 0), (3, 2), (2, 2), (1, 4),),
    "m0": ((6, 1),),
    "d0": ((5, 0), (2, 3), (0, 2), (1, 5), (4, 3),),
    "m2": ((5, 1),),
    "d2": ((0, 3), (2, 4), (6, 2), (7, 0), (3, 3),),
    "e": ((7, 1), (4, 4), (8, 0), (0, 4),),
    "cb0": ((5, 2),),
    "cb1": ((8, 1),),
    "cb2": ((2, 5), (5, 3), (4, 5), (7, 2),),
    "cb3": ((3, 4), (6, 3), (8, 2),),
    "cb4": ((0, 5), (2, 6),),
    "cb5": ((5, 4), (3, 5), (1, 6),),
    "cb6": ((6, 4), (8, 3),),
    "s8a": ((0, 6),),
    "s8b": ((5, 5), (6, 5), (7, 3),),
    "l": ((5, 6), (9, 0), (8, 4), (7, 4),),
    "in0": ((9, 1),),
    "in2": ((4, 6),),
    "in4": ((9, 2),),
    "in5": ((7, 5), (5, 7), (6, 6),),
    "in8": ((8, 5), (9, 3), (9, 4), (7, 6),),
    "in9": ((2, 7), (9, 5), (4, 7), (3, 6), (1, 7), (6, 7), (8, 6),),
    "in11": ((9, 6),),
    "end": ((3, 7), (8, 7), (0, 7), (7, 7), (9, 7),),
}


def backward_kernel(
    bits, len_ref, hg, stf, sums7, st1, beta, sums5, sums6,
    zf, sig, zin_in, wf_in, ws_in, wp_in, cat_in, scat_in, x, x_got, two0, two1, two2, two3, two4,
    gin, full0, full1, full2, full3, full4, offs,
    zin, wf, ws, wp, cat, scat, x0, x1, dzc, dzs, dz1, dzi, sums8, snd, got,
    coef, coef_in, acc, loc, buf, ss8, rs8, lsem, csend, crecv, ssem, rsem, gsend, grecv, *arrays,
):
    greet(partner=True)
    sec = lax.axis_index("section")
    side = dz1.shape[1]
    half = side // 2
    rows = side * 16
    clips = Clips(len_ref, 16, 1)
    count = stf[2:3, 0:128]
    loads = [
        pltpu.make_async_copy(a, b, lsem.at[i])
        for i, (a, b) in enumerate(
            (
                (zin_in, zin),
                (wf_in, wf),
                (ws_in, ws),
                (wp_in, wp),
                (cat_in, cat),
                (scat_in, scat),
                (x.at[sec], x0),
                (x_got, x1),
            )
        )
    ]
    two = (two0, two1, two2, two3, two4)
    full = (full0, full1, full2, full3, full4)
    own_two, ones = arrays[0:5], arrays[5:10]
    core_land = arrays[10:20]
    pieces = 2 ** len(groups(bits)[-1]) - 1 + len(groups(bits)) - 1
    lands = arrays[20:]

    def part(ref, which):
        h = ref.shape[1] // 2
        return ref.at[:, pl.ds(pl.multiple_of(which * h, 16), h)]

    def reducer(i, q, base, rows, swap_src, flip, load):
        return Reducer(
            bits, i, q, base, rows, swap_src, core_land[i], lands[pieces * i : pieces * i + pieces],
            csend, crecv, ssem, rsem, flip, load,
        )

    g, h = [], []
    for i, (a, b) in enumerate(zip(two, own_two)):
        load = pltpu.make_async_copy(part(a, sec), b, lsem.at[8 + i])
        load.start()
        g.append(reducer(i, b, 0, b.shape[1], part(a, 1 - sec), 1 - sec, load))
    for i, a in enumerate(ones):
        rows_half = a.shape[1] // 2
        h.append(
            reducer(5 + i, a, sec * rows_half, rows_half, part(a, 1 - sec), sec, None)
        )
    def at(name):
        for r, e in SCHEDULE.get(name, ()):
            (g + h)[r].event(e)

    acc[...] = jnp.zeros_like(acc)
    loc[...] = jnp.zeros_like(loc)
    for t in range(7):
        lanes = pl.ds(128 * t, 128)
        fill_norm(coef, lanes, stf, lanes, beta[0:1, lanes])
        fill_back(coef, lanes, sums7, lanes, count)
    fill_inner(coef_in, st1, beta)
    for y in (0, side + 1):
        dzc[y] = jnp.zeros(dzc.shape[1:], BF16)
        dzs[y] = jnp.zeros(dzs.shape[1:], BF16)

    def dz_phase(zb, sb, scr, yp, tx, zsem):
        def fetch(k, slot):
            here = pl.ds(2 * k, 2)
            return (
                pltpu.make_async_copy(zf.at[here], zb.at[slot], zsem.at[0, slot]),
                pltpu.make_async_copy(sig.at[here], sb.at[slot], zsem.at[1, slot]),
            )

        for c in fetch(0, 0):
            c.start()
        for c in loads[4:] + loads[:4]:
            c.start()

        def body(k):
            slot = lax.rem(k, 2)

            @pl.when(k < half - 1)
            def _():
                for c in fetch(k + 1, 1 - slot):
                    c.start()

            @pl.when(k == 1)
            def _():
                greeted(partner=True)
                at("start")

            for j in range(2, half):
                pl.when(k == j)(lambda j=j: at(f"dz{j}"))
            for c in fetch(k, slot):
                c.wait()
            tiles = ([], [])
            for t in range(7):
                lanes = pl.ds(128 * t, 128)
                by_z, rest = coef[4:5, lanes], coef[5:6, lanes]
                gr = hg[k, :, :, lanes] * (coef[0:1, lanes] * 0.125)
                scr[:, pl.ds(0, 8, stride=2), :] = gr
                scr[:, pl.ds(1, 8, stride=2), :] = gr
                gr = scr[...]
                gr = jnp.broadcast_to(gr[:, None], (half, 2, 16, 128)).reshape(rows, 128)
                for q in range(2):
                    v = gr * sb[slot, q, :, lanes].astype(F32) + zb[slot, q, :, lanes] * by_z
                    dz = clips.times(v + rest, clips.valid)
                    if t < 2:
                        put_halves(dz1, 2 * k + q, 128 * t, dz)
                    else:
                        tiles[q].append(dz)
            for q in range(2):
                y = 2 * k + q
                small, tail, pool = split_final(*tiles[q][2:])
                yp[y] = clips.times(pool * inv_edges(side, 16, y), clips.inv)

                def put(ref, y=y):
                    def go(lane, v):
                        ref[y + 1, :, lane : lane + v.shape[-1]] = v.astype(BF16)

                    return go

                main = jnp.concatenate(tiles[q][:2], 1).astype(BF16)
                put_spread(16, main, small.astype(BF16), tail, put(dzc), put(dzs))

        loop(half, body)
        at("dzend")

        def boxed(y, v):
            put_halves(dz1, y, 256, clips.times(v, clips.valid))

        box(clips, side, lambda y: yp[y], tx, boxed)
        at("box")

    pl.run_scoped(
        dz_phase,
        vmem(2, 2, rows, DP),
        vmem(2, 2, rows, DP, dtype=BF16),
        vmem(half, 16, 128),
        vmem(side, rows, 128),
        vmem(side + 2, rows, 128),
        pltpu.SemaphoreType.DMA((2, 2)),
    )

    def grad_phase(accm, mid, accs, accp):
        for c in loads[4:6]:
            c.wait()
        ny = side // 2

        def take(ref, y):
            return ref[pl.ds(y, ny)].reshape(ny * rows, ref.shape[-1])

        def sums(k, between):
            accm[...] = dot_tn(take(cat, 1), take(dzc, 2 - k))
            between()
            accm[...] += dot_tn(take(cat, 1 + ny), take(dzc, 2 - k + ny))

        for k in range(3):
            here = slice(128 * k, 128 * k + 128)
            accs[here] = dot_tn(take(scat, 1), take(dzs, 2 - k))
            accs[here] += dot_tn(take(scat, 1 + ny), take(dzs, 2 - k + ny))
        small = centre_small(accs, beta)
        at("scat")
        for k in (1, 0, 2):
            sums(k, lambda: at(f"m{k}"))
            if k == 1:
                mid[...] = centre_mid(accm[480:481, :], beta)
            pack_mid(ones[k], accm, mid, accs, small, k)
            at(f"d{k}")
        for c in loads[6:]:
            c.wait()
        accp[...] = jnp.zeros_like(accp)
        add_outer(accp, dz1, ((x1, 1 - sec), (x0, sec)))
        pack_one(ones[3], lambda t, r, n: accp[r : r + n, 128 * t : 128 * t + 128])
        pack_inner(ones[4], lambda t, r, n: jnp.zeros((n, 128), F32), accs, small)
        at("e")

    def add_outer(accp, d_ref, sides):
        step = side // 2
        size = step * side * 8
        for src, which in sides:

            def body(i, src=src, which=which):
                at = pl.ds(pl.multiple_of(i * size, 16), size)
                d = d_ref[which, pl.ds(i * step, step)].reshape(size, d_ref.shape[-1])
                accp[...] += dot_tn(src[at], d)

            loop(side // step, body)

    pl.run_scoped(
        grad_phase,
        vmem(512, 1024),
        vmem(512, 1024),
        vmem(384, 384),
        vmem(D, 384),
    )

    def last_phase(din, ring, accp, sems):
        for c in loads[:4]:
            c.wait()
        ny = 2

        def body(i):
            y0 = i * ny + 1
            for j in range(side // ny):
                pl.when(i == j)(lambda j=j: at(f"cb{j}"))
            q = s = None
            for dy in (-1, 0, 1):
                k = dy + 1
                here = pl.ds(y0 - dy, ny)
                t = dot_nt(dzc[here].reshape(ny * rows, 1024), wf[512 * k : 512 * k + 512])
                q = t if q is None else q + t
                t = dot_nt(dzs[here].reshape(ny * rows, 384), ws[128 * k : 128 * k + 128])
                s = t if s is None else s + t
            for j in range(ny):
                y = i * ny + j
                here = slice(j * rows, (j + 1) * rows)
                parts = [q[here, 128 * t : 128 * t + 128] for t in range(4)]
                inner_up(clips, zin[y], untap(clips, parts, s[here]), coef_in, acc, din, y)

        loop(side // ny, body)
        pack_stats(clips, loc, acc, INNER)
        exchange_start(loc, buf, ss8, rs8)
        at("s8a")
        sides = ((x1, 1 - sec), (x0, sec))
        step = side // 2
        size = step * side * 8
        exchange_finish(loc, buf, ss8, rs8, sums8, INNER)
        fill_inner_back(coef_in, sums8, count)
        at("s8b")

        def dz(y):
            for t in range(2):
                put_halves(dzi, y, 128 * t, inner_dz(clips, t, zin[y], din[y], coef_in))

        loop(side, dz)
        at("dzi")
        accp[...] = jnp.zeros_like(accp)
        add_outer(accp, dzi, sides)
        for j in range(8):
            ones[4][j, 0:208] = accp[
                208 * (j % 4) : 208 * (j % 4) + 208, 128 * (j // 4) : 128 * (j // 4) + 128
            ].astype(BF16)
        at("l")
        sent = []
        step = 2
        size = step * side * 8
        chunks = side // step
        slots = ring.shape[0]
        for p in range(2 * chunks):
            which = sides[p // chunks][1]
            i = p % chunks
            slot = p % slots
            if p >= slots:
                sent[p - slots].wait()
            here = pl.ds(i * step, step)
            d = jnp.concatenate([dz1[which, here], dzi[which, here]], -1).reshape(size, 640)
            ring[slot] = dot_nt(d, wp[...]).astype(BF16)
            to = gin.at[sec, i * size : (i + 1) * size]
            if p < chunks:
                c = swap_copy(ring.at[slot], to, gsend.at[i], grecv.at[i])
            else:
                c = pltpu.make_async_copy(ring.at[slot], to, sems.at[slot])
            c.start()
            sent.append(c)
            at(f"in{p}")
        for c in sent[-slots:]:
            c.wait()

    dma = pltpu.SemaphoreType.DMA
    pl.run_scoped(
        last_phase,
        vmem(side, rows, 256),
        vmem(4, 2 * side * 8, D, dtype=BF16),
        vmem(D, 256),
        dma((4,)),
    )
    snd[:, 0:DP] = jnp.where(sec == 0, sums5[...], sums7[...])
    snd[:, DP : DP + 640] = jnp.where(sec == 0, sums6[...], sums8[...])
    small = swap_copy(snd, got, csend.at[15], crecv.at[15])
    small.start()
    at("end")

    def finish(mine, theirs):
        copies = []
        for i, (dst, m, t) in enumerate(zip(full, mine, theirs)):
            copies.append(pltpu.make_async_copy(m, dst.at[sec], lsem.at[13 + i]))
            copies.append(swap_copy(t, dst.at[sec], csend.at[10 + i], crecv.at[10 + i]))
        for c in copies:
            c.start()
        for c in copies:
            c.wait()

    pl.when(sec == 0)(lambda: finish(core_land[5:10], core_land[0:5]))
    pl.when(sec == 1)(lambda: finish(core_land[0:5], core_land[5:10]))
    small.wait()
    for lanes, a, b in ((slice(0, DP), sums7, sums5), (slice(DP, DP + 640), sums8, sums6)):
        offs[:, lanes] = jnp.where(sec == 0, a[...], b[...]) + got[:, lanes]


def put_halves(ref, y, lane, v):
    side, lanes = v.shape[0] // 16, v.shape[1]
    v = v.reshape(side, 2, 8, lanes)
    for h in range(2):
        ref[h, y, :, lane : lane + lanes] = v[:, h].reshape(side * 8, lanes).astype(BF16)


def groups(bits, last_first=False):
    if bits < 3:
        return [(k,) for k in range(bits)]
    plan = [(k,) for k in range(bits - 2)] + [(bits - 2, bits - 1)]
    return plan[-1:] + plan[:-1] if last_first else plan


class Reducer:
    EVENTS = 8

    def __init__(
        self, bits, index, q, base, rows, swap_src, core_land, land, csend, crecv, ssem, rsem, flip, load
    ):
        self.index, self.q, self.base, self.rows = index, q, base, rows
        self.core_land, self.land, self.load = core_land, land, load
        self.ssem, self.rsem = ssem, rsem
        self.swap = swap_copy(swap_src, core_land, csend.at[index], crecv.at[index])
        me = lax.axis_index("dp")
        plan = groups(bits, index in Z_FIRST)
        self.count = len(plan)
        self.last = 2 * self.count
        self.steps = []
        tiles, t0, r0 = 8, 0, 0
        at = 0
        for step, ks in enumerate(plan):
            powers = []
            for k in ks:
                power = 1 << k
                if bits > 1 and k < 2:
                    power = power + flip * ((1 << (1 - k)) - power)
                powers.append((power, lax.rem(me // power, 2)))
            cuts = []
            for power, bit in powers:
                if tiles > 1:
                    tiles //= 2
                    cuts.append((bit, tiles, 0))
                else:
                    rows //= 2
                    cuts.append((bit, 0, rows))
            sends = []
            for c in range(1, 1 << len(ks)):
                partner, t, r = me, t0, r0
                for i, ((power, bit), (_, dt, dr)) in enumerate(zip(powers, cuts)):
                    turned = (c >> i) & 1
                    partner = partner + turned * (1 - 2 * bit) * power
                    here = bit + turned * (1 - 2 * bit)
                    t, r = t + here * dt, r + here * dr
                sends.append((partner, (t, r), at))
                at += 1
            for bit, dt, dr in cuts:
                t0, r0 = t0 + bit * dt, r0 + bit * dr
            self.steps.append((sends, (t0, r0), tiles, rows))
        self.pieces = at

    def region(self, ref, base, at, tiles, rows):
        t, r = at
        r = base + r
        if not isinstance(r, int):
            r = pl.multiple_of(r, 16)
        return ref.at[pl.ds(t, tiles), pl.ds(r, rows)]

    def mine(self, at, tiles, rows):
        return self.region(self.q, self.base, at, tiles, rows)

    def total(self, at, tiles, rows):
        return self.region(self.core_land, 0, at, tiles, rows)

    def copies(self, i):
        if i == 0:
            return [self.swap]
        halving = i <= self.count
        sends, keep, tiles, rows = self.steps[i - 1 if halving else self.last - i]
        out = []
        for partner, send, piece in sends:
            src = self.mine(send, tiles, rows) if halving else self.total(keep, tiles, rows)
            sem = 2 * (self.index * self.pieces + piece) + int(halving)
            out.append(
                pltpu.make_async_remote_copy(
                    src_ref=src,
                    dst_ref=self.land[piece] if halving else src,
                    send_sem=self.ssem.at[sem],
                    recv_sem=self.rsem.at[sem],
                    device_id={"dp": partner},
                    device_id_type=MESH,
                )
            )
        return out

    def received(self, i):
        sends, keep, tiles, rows = self.steps[self.last - i]
        out = []
        for partner, send, piece in sends:
            sem = 2 * (self.index * self.pieces + piece)
            dst = self.total(send, tiles, rows)
            out.append(
                pltpu.make_async_remote_copy(
                    src_ref=dst,
                    dst_ref=dst,
                    send_sem=self.ssem.at[sem],
                    recv_sem=self.rsem.at[sem],
                    device_id={"dp": partner},
                    device_id_type=MESH,
                )
            )
        return out

    def add(self, dst, q, lands, tiles, rows):
        chunk = next(c for c in range(min(rows, 256), 0, -16) if rows % c == 0 and c % 16 == 0)
        parts = rows // chunk

        def body(j):
            t, r = j // parts, pl.multiple_of(lax.rem(j, parts) * chunk, 16)
            at = pl.ds(r, chunk)
            total = q[t, at].astype(F32)
            for land in lands:
                total = total + land[t, at].astype(F32)
            dst[t, at] = total.astype(BF16)

        loop(tiles * parts, body)

    def finish(self, i):
        if i > self.count:
            for c in self.copies(i):
                c.wait_send()
            for c in self.received(i):
                c.wait_recv()
            return
        for c in self.copies(i):
            c.wait()
        if i == 0:
            if self.load is not None:
                self.load.wait()
            q = self.mine((0, 0), 8, self.rows)
            self.add(q, q, [self.core_land], 8, self.rows)
        else:
            sends, keep, tiles, rows = self.steps[i - 1]
            lands = [self.land[piece] for _, _, piece in sends]
            q = self.mine(keep, tiles, rows)
            dst = self.total(keep, tiles, rows) if i == self.count else q
            self.add(dst, q, lands, tiles, rows)

    def event(self, e):
        count = self.last + 2
        for i in range(e * count // self.EVENTS, (e + 1) * count // self.EVENTS):
            if i > 0:
                self.finish(i - 1)
            if i <= self.last:
                for c in self.copies(i):
                    c.start()


def land_shapes(tiles, rows, bits, last_first):
    out = []
    for ks in groups(bits, last_first):
        for _ in ks:
            if tiles > 1:
                tiles //= 2
            else:
                rows //= 2
        out += [(tiles, rows, 128)] * (2 ** len(ks) - 1)
    return out


def unpack_kernel(
    full0, full1, full2, full3, full4, gin_in, out_in, offs,
    one, mid_in, mid, small_in, small, pool, offset, gin, out,
    buf0, buf1, buf2, buf3, buf4, nat, inner, gin_buf, out_buf, sem,
):
    copies = []
    bufs = (buf0, buf1, buf2, buf3, buf4)
    for i, (full, buf) in enumerate(zip((full0, full1, full2, full3, full4), bufs)):
        half = full.shape[2]
        for h in range(2):
            copies.append(
                pltpu.make_async_copy(full.at[h], buf.at[:, h * half : (h + 1) * half], sem.at[2 * i + h])
            )
    for c in copies:
        c.start()
    through = ((gin_in, gin_buf, gin), (out_in, out_buf, out))
    for i, (src, buf, dst) in enumerate(through):
        pltpu.make_async_copy(src, buf, sem.at[10 + i]).start()
    v = offs[...]
    lane = lax.broadcasted_iota(jnp.int32, v.shape, 1)
    out = jnp.where(lane < 256, v, 0.0)
    for lo, hi, by in ((256, 416, -1024), (416, 736, 160), (736, 768, -704), (768, 1024, 192)):
        out = jnp.where((lane >= lo) & (lane < hi), roll_lanes(v, by), out)
    offset[...] = out[0:1, 0:1024]
    for c in copies:
        c.wait()

    def take(b, t, r, rows):
        return bufs[b][t, r : r + rows].astype(F32)

    for dt in range(3):
        for dy in range(3):
            for dx in range(3):
                to = 160 * (9 * dt + 3 * dy + dx)
                for rows, r in ((128, 128 * dt), (32, 384 + 32 * dt)):
                    nat[to : to + rows, 0:128] = take(dy, 2 * dx, r, rows)
                    nat[to : to + rows, 128:256] = take(dy, 2 * dx + 1, r, rows)
                    tail = take(dy, 6 + dx // 2, r, rows)
                    nat[to : to + rows, 256:384] = roll_lanes(tail, 64) if dx == 1 else tail
                    to = to + rows
                b = 9 * dy + 3 * dt + dx
                to = 32 * (9 * dt + 3 * dy + dx)
                small[to : to + 32, :] = (
                    take(b // 8, b % 8, 480, 32) if b < 24 else take(4, b - 24, 208, 32)
                )

    def turn(i):
        at = pl.ds(pl.multiple_of(i * 128, 128), 128)
        mid[0:256, at] = nat[at, 0:256].T
        mid[256:320, at] = nat[at, 256:384].T[0:64]

    total = mid.shape[1]
    passed = []
    for i, (src, buf, dst) in enumerate(through):
        pltpu.make_async_copy(src, buf, sem.at[10 + i]).wait()
        passed.append(pltpu.make_async_copy(buf, dst, sem.at[10 + i]))
        passed[i].start()
    loop(total // 128, turn)
    at = slice(total - total % 128, total)
    mid[0:256, at] = nat[at, 0:256].T
    mid[256:320, at] = nat[at, 256:384].T[0:64]
    for j in range(8):
        at = slice(208 * (j % 4), 208 * (j % 4) + 208)
        one[at, 128 * (j // 4) : 128 * (j // 4) + 128] = take(3, j, 0, 208)
        inner[j // 4, at] = take(4, j, 0, 208)
        rows = min(112, D - 112 * j)
        pool[112 * j : 112 * j + rows, :] = take(3, j, 208, rows)
    for r in range(0, D, 128):
        at = slice(r, min(r + 128, D))
        mid_in[0:128, at] = inner[0, at].T
        last = inner[1, at].T
        mid_in[128:160, at] = last[0:32]
        small_in[:, at] = last[32:64]
    for c in passed:
        c.wait()


def vmem(*shape, dtype=F32):
    return pltpu.VMEM(shape, dtype)


def call(kernel, outs, args, scratch, collective=None, smem_first=True, any_in=(), any_out=()):
    def specs(count, anywhere):
        return [
            pl.BlockSpec(memory_space=pl.ANY if i in anywhere else pltpu.VMEM)
            for i in range(count)
        ]

    in_specs = specs(len(args), any_in)
    if smem_first:
        in_specs[0] = pl.BlockSpec(memory_space=pltpu.SMEM)
    params = {"vmem_limit_bytes": VMEM_LIMIT}
    if collective is not None:
        params.update(collective_id=collective, has_side_effects=True)
    return pl.pallas_call(
        kernel,
        out_shape=[jax.ShapeDtypeStruct(shape, dtype) for shape, dtype in outs],
        in_specs=in_specs,
        out_specs=specs(len(outs), any_out),
        scratch_shapes=scratch,
        compiler_params=pltpu.CompilerParams(**params),
    )(*args)


def on_device(
    clip_input, out_grad, clip_lengths, w_one, w_mid_in, w_mid, w_small_in, w_small, w_pool, bn_offset
):
    n = lax.axis_size("dp")
    bits = n.bit_length() - 1
    half, side = clip_input.shape[1], clip_input.shape[2]
    rows = side * 16
    side2 = side // 2
    rows2 = side2 * 8
    total2 = side2 * rows2
    unit = 32 << max(bits - 3, 0)
    packed_rows = [-(-r // unit) * unit for r in (512, 512, 512, 320, 256)]
    x = clip_input.transpose(0, 2, 3, 1, 4).reshape(2, side * side * half, D)
    og = out_grad.transpose(0, 2, 3, 1, 4)

    def like(a, dtype=BF16):
        return pltpu.VMEM(a.shape[1:], dtype)

    def turned(w):
        return w.transpose(0, 2, 1)

    weights = (w_one, turned(w_mid_in), turned(w_small_in), w_pool, turned(w_mid), w_small)
    dma = pltpu.SemaphoreType.DMA
    grid = (side, side, 2, 8)

    def bf(*shape):
        return vmem(*shape, dtype=BF16)

    pooled = (side2, side2, 8, DP)
    first_scope = [
        vmem(*grid, DP),
        vmem(*grid, 256),
        vmem(side, rows, 128),
        bf(side + 2, rows, 512),
        bf(side + 2, rows, 128),
        bf(side, rows, DP),
        vmem(side2, 16, 128),
        vmem(8, 512),
        vmem(8, DP),
        vmem(8, 256),
        vmem(2, 2, 8, 640),
        vmem(2, 16, 640),
        vmem(2, 16, 512),
    ]
    second_scope = (
        [
            like(og),
            like(og),
            vmem(side2, side2, 8, D),
            bf(2, *og.shape[1:]),
            dma((9,)),
            vmem(*pooled),
        ]
        + [bf(8, r, 128) for r in packed_rows]
        + [
            bf(total2, DP),
            vmem(side2, rows2, 256),
            vmem(side2, rows2, 128),
            vmem(side2, rows2, DP),
            vmem(8, DP),
            vmem(side2, rows2, 128),
            vmem(side2 + 2, rows2, 128),
            vmem(side2 + 2, rows2, 640),
            bf(total2, 1536),
            bf(total2, 384),
            vmem(side2, rows2, 1024),
            vmem(side2, rows2, 384),
            vmem(side2, rows2, DP),
            vmem(side2, rows2, 1024),
            vmem(side2, rows2, 384),
            vmem(side2, rows2, 640),
            vmem(side2, rows2, 256),
            vmem(2, 8, 640),
            vmem(8, 640),
            vmem(8, 512),
            vmem(2, 8, DP),
            vmem(1536, 1024),
            vmem(384, 384),
            vmem(DP, 640),
            vmem(8, DP),
            vmem(8, 256),
        ]
    )
    st1, stf, beta1, sums5, sums6, sums7, *rest = call(
        functools.partial(blocks_kernel, first_scope, second_scope),
        [
            ((8, 640), F32),
            ((8, DP), F32),
            ((1, 1152), F32),
            ((8, DP), F32),
            ((8, 640), F32),
            ((8, DP), F32),
            (x.shape[1:], BF16),
            (grid + (256,), F32),
            (grid + (DP,), F32),
            ((side, rows, DP), BF16),
            ((side + 2, rows, 512), BF16),
            ((side + 2, rows, 128), BF16),
            ((D, 640), BF16),
            ((1536, 1024), BF16),
            ((384, 384), BF16),
            (og.shape[1:], BF16),
            (og.shape, BF16),
            (pooled, F32),
        ]
        + [((8, r, 128), BF16) for r in packed_rows],
        (clip_lengths, bn_offset, x, og) + weights,
        [
            like(x),
            vmem(*pooled),
            vmem(*pooled),
            vmem(*pooled),
            vmem(1, 1152),
            vmem(1, 1152),
            vmem(1, 1152),
            bf(2, D, 640),
            bf(2, 1536, 1024),
            bf(2, 384, 384),
        ]
        + exchange_scratch(n, 16)
        + exchange_scratch(n, 8)
        + exchange_scratch(n, 16)
        + exchange_scratch(n, 8)
        + exchange_scratch(n, 16)
        + exchange_scratch(n, 8)
        + exchange_scratch(n, 16)
        + [dma((9,)), dma((6,)), dma((6,)), dma(()), dma(())],
        collective=1,
        any_in=range(2, 10),
        any_out=range(6, 23),
    )
    xgot, zin, zf, sig, cat, scat, wp1, wf1, ws1, og_got, block_output, hg, *two = rest
    zin = zin.reshape(side, rows, 256)
    zf = zf.reshape(side, rows, DP)
    halves = [r // 2 for r in packed_rows]
    lands = []
    for i, h in enumerate(halves * 2):
        lands += [bf(*shape) for shape in land_shapes(8, h, bits, i in Z_FIRST)]
    gin, *full, offs = call(
        functools.partial(backward_kernel, bits),
        [(x.shape, BF16)]
        + [((2, 8, h, 128), BF16) for h in halves]
        + [((8, DP + 640), F32)],
        (clip_lengths, hg, stf, sums7, st1, beta1, sums5, sums6)
        + (zf, sig, zin, wf1, ws1, wp1, cat, scat, x, xgot, *two),
        [
            vmem(side, rows, 256),
            bf(1536, 1024),
            bf(384, 384),
            bf(D, 640),
            bf(side + 2, rows, 512),
            bf(side + 2, rows, 128),
            like(x),
            like(x),
            bf(side + 2, rows, 1024),
            bf(side + 2, rows, 384),
            bf(2, side, rows // 2, 384),
            bf(2, side, rows // 2, 256),
            vmem(8, 640),
            vmem(8, DP + 640),
            vmem(8, DP + 640),
            vmem(8, DP),
            vmem(8, 256),
            vmem(2, 16, 640),
        ]
        + exchange_scratch(n, 8)
        + [dma((18,)), dma((16,)), dma((16,)), dma((2 * len(lands),)), dma((2 * len(lands),))]
        + [dma((side,)), dma((side,))]
        + [bf(8, h, 128) for h in halves]
        + [bf(8, r, 128) for r in packed_rows]
        + [bf(8, h, 128) for h in halves * 2]
        + lands,
        collective=3,
        any_in=range(8, 23),
        any_out=range(6),
    )
    one, mid_in, mid, small_in, small, pool, offset, gin, block_output = call(
        unpack_kernel,
        [
            ((D, C0), F32),
            ((C1A, D), F32),
            ((C1B, 27 * C1A), F32),
            ((C2A, D), F32),
            ((27 * C2A, C2B), F32),
            ((D, C3), F32),
            ((1, 1024), F32),
            (x.shape, BF16),
            (og.shape, BF16),
        ],
        (*full, gin, block_output, offs),
        [bf(8, r, 128) for r in packed_rows]
        + [vmem(27 * C1A, 384), vmem(2, D, 128), bf(*x.shape), bf(*og.shape), dma((12,))],
        smem_first=False,
        any_in=range(7),
        any_out=(7, 8),
    )
    input_grad = gin.reshape(2, side, side, half, D).transpose(0, 3, 1, 2, 4)
    return (
        block_output.transpose(0, 3, 1, 2, 4),
        input_grad,
        one[None],
        mid_in.T[None],
        mid.T[None],
        small_in.T[None],
        small[None],
        pool[None],
        offset,
    )


def solution(mesh):
    placed = (
        P("dp", "section", None, None, None),
        P("dp", "section", None, None, None),
        P("dp", None),
        P("section", None, None),
        P("section", None, None),
        P("section", None, None),
        P("section", None, None),
        P("section", None, None),
        P("section", None, None),
        P("section", None),
    )
    return jax.shard_map(
        on_device,
        mesh=mesh,
        in_specs=placed,
        out_specs=(
            P("dp", "section", None, None, None),
            P("dp", "section", None, None, None),
            P("section", None, None),
            P("section", None, None),
            P("section", None, None),
            P("section", None, None),
            P("section", None, None),
            P("section", None, None),
            P("section", None),
        ),
        check_vma=False,
    )
```

```python
import functools

import jax
import jax.numpy as jnp
from jax import lax
from jax.experimental import pallas as pl
from jax.experimental.pallas import tpu as pltpu
from jax.sharding import PartitionSpec as P

D = 832
DP = 896
C0 = 256
C1A = 160
C1B = 320
C2A = 32
C2B = 128
C3 = 128
EPS = 0.001
MESH = pl.DeviceIdType.MESH
F32 = jnp.float32
BF16 = jnp.bfloat16
VMEM_LIMIT = 60 * 2**20


def dot(a, b):
    return jnp.dot(a, b, preferred_element_type=F32)


def dot_nt(a, b):
    return lax.dot_general(a, b, (((1,), (1,)), ((), ())), preferred_element_type=F32)


def dot_tn(a, b):
    return lax.dot_general(a, b, (((0,), (0,)), ((), ())), preferred_element_type=F32)


def roll_rows(x, by):
    return pltpu.roll(x, by % x.shape[0], 0)


def roll_lanes(x, by):
    return pltpu.roll(x, by % x.shape[1], 1)


def lane_below(x, count):
    lanes = lax.broadcasted_iota(jnp.int32, x.shape, 1)
    return jnp.where(lanes < count, x, 0.0)


class Clips:
    def __init__(self, len_ref, frames, stride):
        sec = lax.axis_index("section")
        f = lax.broadcasted_iota(jnp.int32, (frames, 128), 0)

        def label(v):
            place = v * stride
            out = jnp.zeros_like(v)
            start = jnp.int32(0)
            for c in range(len_ref.shape[1]):
                end = start + len_ref[sec, c]
                out = jnp.where((place >= start) & (place < end), c + 1, out)
                start = end
            return out

        here = label(f)
        inside = here > 0

        def mask(m):
            return jnp.where(m, 1.0, 0.0).astype(F32)

        self.frames = frames
        self.valid = mask(inside)
        self.before = mask(inside & (f > 0) & (label(f - 1) == here))
        self.after = mask(inside & (f < frames - 1) & (label(f + 1) == here))
        self.inv = 1.0 / jnp.maximum(self.valid + self.before + self.after, 1.0)

    def times(self, v, pattern):
        return (v.reshape(-1, self.frames, 128) * pattern).reshape(v.shape)

    def fold(self, v):
        return jnp.sum(v.reshape(-1, self.frames, v.shape[-1]), axis=0)


def shift_places(v, frames, by):
    lanes = v.shape[-1]
    v3 = v.reshape(-1, frames, lanes)
    zero = jnp.zeros((1, frames, lanes), v.dtype)
    if by > 0:
        v3 = jnp.concatenate([v3[1:], zero], 0)
    else:
        v3 = jnp.concatenate([zero, v3[:-1]], 0)
    return v3.reshape(v.shape)


def add_stats(clips, acc, lanes, v, w=None):
    acc[0, :, lanes] += clips.fold(v)
    acc[1, :, lanes] += clips.fold(v * (v if w is None else w))


def affine(st, lanes):
    total, square, count = st[0:1, lanes], st[1:2, lanes], st[2:3, lanes]
    mean = total / count
    scale = lax.rsqrt(square / count - mean * mean + EPS)
    return scale, mean


def fill_norm(coef, to, st, lanes, beta):
    scale, mean = affine(st, lanes)
    coef[0:1, to] = scale
    coef[1:2, to] = mean * scale
    coef[2:3, to] = beta - mean * scale
    coef[3:4, to] = beta


def fill_back(coef, to, sums, lanes, count):
    m1, m2 = sums[0:1, lanes] / count, sums[1:2, lanes] / count
    scale = coef[0:1, to]
    coef[4:5, to] = -scale * scale * m2
    coef[5:6, to] = scale * (coef[1:2, to] * m2 - m1)


def soft(t):
    s = 0.5 + 0.5 * jnp.tanh(0.5 * jnp.abs(t))
    return jnp.maximum(t, 0.0) - jnp.log(s), jnp.where(t >= 0, s, 1.0 - s)


def sigm(t):
    return 0.5 + 0.5 * jnp.tanh(0.5 * t)


def greet(partner=False):
    n = lax.axis_size("dp")
    me = lax.axis_index("dp")
    barrier = pltpu.get_barrier_semaphore()

    def go(k, _):
        pl.semaphore_signal(
            barrier, inc=1, device_id={"dp": lax.rem(me + k, n)}, device_id_type=MESH
        )
        return 0

    if partner:
        other = 1 - lax.axis_index("section")
        pl.semaphore_signal(barrier, inc=1, device_id={"section": other}, device_id_type=MESH)
    lax.fori_loop(1, n, go, 0)


def greeted(partner=False):
    pl.semaphore_wait(pltpu.get_barrier_semaphore(), lax.axis_size("dp") - 1 + int(partner))


def exchange_start(loc, buf, ssem, rsem):
    n = lax.axis_size("dp")
    me = lax.axis_index("dp")

    def start(k, _):
        pltpu.make_async_remote_copy(
            src_ref=loc,
            dst_ref=buf.at[me],
            send_sem=ssem.at[k],
            recv_sem=rsem.at[me],
            device_id={"dp": lax.rem(me + k, n)},
            device_id_type=MESH,
        ).start()
        return 0

    lax.fori_loop(1, n, start, 0)
    buf[me] = loc[...]


def exchange_finish(loc, buf, ssem, rsem, out, tiles):
    n = lax.axis_size("dp")
    me = lax.axis_index("dp")

    def wait(k, _):
        j = lax.rem(me + k, n)
        copy = pltpu.make_async_remote_copy(
            src_ref=loc,
            dst_ref=buf.at[j],
            send_sem=ssem.at[k],
            recv_sem=rsem.at[j],
            device_id={"dp": j},
            device_id_type=MESH,
        )
        copy.wait_send()
        copy.wait_recv()
        return 0

    lax.fori_loop(1, n, wait, 0)
    total = jnp.sum(buf[...], axis=0)
    at = 2 * len(tiles)
    for i, t in enumerate(tiles):
        lanes = slice(128 * t, 128 * t + 128)
        out[0:1, lanes] = total[2 * i : 2 * i + 1]
        out[1:2, lanes] = total[2 * i + 1 : 2 * i + 2]
        if at < loc.shape[0]:
            out[2:3, lanes] = total[at : at + 1]


def exchange(loc, buf, ssem, rsem, out, tiles):
    exchange_start(loc, buf, ssem, rsem)
    exchange_finish(loc, buf, ssem, rsem, out, tiles)


def swap_copy(src, dst, ssem, rsem):
    return pltpu.make_async_remote_copy(
        src_ref=src,
        dst_ref=dst,
        send_sem=ssem,
        recv_sem=rsem,
        device_id={"section": 1 - lax.axis_index("section")},
        device_id_type=MESH,
    )


def exchange_scratch(n, rows):
    return [
        pltpu.VMEM((rows, 128), F32),
        pltpu.VMEM((n, rows, 128), F32),
        pltpu.SemaphoreType.DMA((n,)),
        pltpu.SemaphoreType.DMA((n,)),
    ]


FIRST, CONV, FINAL, INNER = range(5), range(4), range(7), (3, 4)


def pack_stats(clips, loc, acc, tiles, count=None):
    for i, t in enumerate(tiles):
        lanes = pl.ds(128 * t, 128)
        for k in range(2):
            loc[2 * i + k : 2 * i + k + 1, :] = jnp.sum(
                acc[k, :, lanes] * clips.valid, axis=0, keepdims=True
            )
    if count is not None:
        at = 2 * len(tiles)
        loc[at : at + 1, :] = jnp.sum(clips.valid, axis=0, keepdims=True) * float(count)


def loop(n, body):
    def step(i, _):
        body(i)
        return 0

    lax.fori_loop(0, n, step, 0)


def inv_edges(side, frames, y):
    x = lax.broadcasted_iota(jnp.int32, (side, frames, 128), 0)
    ex = jnp.where((x == 0) | (x == side - 1), 0.5, 1.0 / 3.0).astype(F32)
    ey = jnp.where((y == 0) | (y == side - 1), 0.5, 1.0 / 3.0).astype(F32)
    return (ex * ey).reshape(side * frames, 128)


def box(clips, side, load, tx, store):
    frames = clips.frames
    tx[0] = jnp.zeros(tx.shape[1:], F32)
    tx[side + 1] = jnp.zeros(tx.shape[1:], F32)

    def across(y):
        v = load(y)
        t = clips.times(v, clips.valid)
        t = t + clips.times(roll_rows(v, 1), clips.before)
        t = t + clips.times(roll_rows(v, -1), clips.after)
        tx[y + 1] = t + shift_places(t, frames, 1) + shift_places(t, frames, -1)

    def down(y):
        store(y, tx[y] + tx[y + 1] + tx[y + 2])

    loop(side, across)
    loop(side, down)


def pool_forward(clips, side, load, tx, zp, acc):
    def store(y, v):
        z = clips.times(v * inv_edges(side, clips.frames, y), clips.inv)
        zp[y] = z
        add_stats(clips, acc, pl.ds(256, 128), z)

    box(clips, side, load, tx, store)


def upright(src, dst):
    rows = src.shape[1]
    width = src.shape[0]

    def body(i):
        at = pl.ds(pl.multiple_of(i * 128, 128), 128)
        dst[at, 0:width] = src[:, at].astype(F32).T.astype(BF16)

    loop(rows // 128, body)
    if rows % 128:
        at = slice(rows - rows % 128, rows)
        dst[at, 0:width] = src[:, at].astype(F32).T.astype(BF16)


def arrange_first(src, wp, b, flip):
    one, mid_in, small_in, pool = src
    wp[b, :, 0:256] = one[...]
    wp[b, :, 256:384] = pool[...]
    upright(mid_in, flip)
    wp[b, :, 384:544] = flip[0:D, 0:C1A]
    upright(small_in, flip)
    wp[b, :, 544:576] = flip[0:D, 0:C2A]
    wp[b, :, 576:640] = jnp.zeros((D, 64), BF16)


def arrange_beta(src, dst):
    v = jnp.concatenate([jnp.broadcast_to(src[...], (8, 1024)), jnp.zeros((8, 128), F32)], 1)
    lane = lax.broadcasted_iota(jnp.int32, v.shape, 1)
    out = jnp.zeros_like(v)
    for lo, hi, by in (
        (0, 256, 0),
        (256, 576, -160),
        (576, 832, -192),
        (896, 1056, 640),
        (1056, 1088, 320),
    ):
        out = jnp.where((lane >= lo) & (lane < hi), roll_lanes(v, by), out)
    dst[...] = out[0:1]


def arrange_conv(mid_flat, small, wf, ws, b, mid):
    upright(mid_flat, mid)
    for dy in range(3):
        wf[b, 512 * dy + 480 : 512 * dy + 512, :] = jnp.zeros((32, 1024), BF16)
        ws[b, 128 * dy + 96 : 128 * dy + 128, :] = jnp.zeros((32, 384), BF16)
        wf[b, 512 * dy : 512 * dy + 512, 960:1024] = jnp.zeros((512, 64), BF16)
        for dt in range(3):
            for dx in range(3):
                r = 96 * (3 * dt + dy) + 32 * dx
                to = 128 * dy + 32 * dt
                ws[b, to : to + 32, 128 * dx : 128 * dx + 128] = small[r : r + 32, :]
            for dx in range(3):
                r = 480 * (3 * dt + dy) + 160 * dx
                for rows, to in ((128, 128 * dt), (32, 384 + 32 * dt)):
                    to = to + 512 * dy
                    wf[b, to : to + rows, 256 * dx : 256 * dx + 256] = mid[r : r + rows, 0:256]
                    wf[b, to : to + rows, 768 + 64 * dx : 832 + 64 * dx] = mid[
                        r : r + rows, 256:320
                    ]
                    r = r + rows


def inner_tiles(clips, z, coef):
    tiles = []
    for t in range(2):
        lanes = slice(128 * t, 128 * t + 128)
        act, _ = soft(z[:, lanes] * coef[0:1, lanes] + coef[2:3, lanes])
        tiles.append(clips.times(act, clips.valid))
    return tiles


def fill_inner(coef, st, beta):
    for t in range(2):
        lanes = pl.ds(128 * t, 128)
        fill_norm(coef, lanes, st, pl.ds(384 + 128 * t, 128), beta[0:1, 896 + 128 * t : 1024 + 128 * t])


def tap_tiles(clips, a, b):
    def before(v):
        return clips.times(roll_rows(v, 1), clips.before)

    def after(v):
        return clips.times(roll_rows(v, -1), clips.after)

    lane = lax.broadcasted_iota(jnp.int32, b.shape, 1)
    ones = clips.times(jnp.where(lane == 96, 1.0, 0.0).astype(F32), clips.valid)

    def three32(v):
        return before(v) + roll_lanes(v, 32) + roll_lanes(after(v), 64) + ones

    tail = lane_below(b, 32)
    small = lane_below(roll_lanes(b, -32), 32)
    return [before(a), a, after(a), three32(tail)], three32(small)


def untap(clips, parts, small):
    def before(v):
        return roll_rows(clips.times(v, clips.before), -1)

    def after(v):
        return roll_rows(clips.times(v, clips.after), 1)

    def back32(v):
        return (
            lane_below(before(v), 32)
            + lane_below(roll_lanes(v, -32), 32)
            + lane_below(roll_lanes(after(v), -64), 32)
        )

    a = before(parts[0]) + parts[1] + after(parts[2])
    return a, back32(parts[3]) + roll_lanes(back32(small), 32)


def typical(beta):
    sp, sg = soft(jnp.broadcast_to(beta, (8, beta.shape[-1])))
    return sp + 0.5 * sg * (1.0 - sg)


def outer(c, s):
    k = lax.broadcasted_iota(jnp.int32, c.shape, 0)
    c = jnp.where(k < 2, c, 0.0).astype(BF16)
    s = jnp.broadcast_to(s, (8, s.shape[-1]))
    high = s.astype(BF16).astype(F32)
    k = lax.broadcasted_iota(jnp.int32, s.shape, 0)
    s = jnp.where(k == 0, high, jnp.where(k == 1, s - high, 0.0)).astype(BF16)
    return dot_tn(c, s)


def tap_points(beta):
    a = typical(beta[0:1, 896:1024])
    b = typical(beta[0:1, 1024:1152])

    def three(v):
        return v + roll_lanes(v, 32) + roll_lanes(v, 64)

    tail = three(lane_below(b, 32))
    small = three(lane_below(roll_lanes(b, -32), 32))
    return jnp.concatenate([a, a, a, tail], 1), small


def centre_mid(row, beta):
    c, _ = tap_points(beta)
    row = jnp.broadcast_to(row, (8, 1024))
    main = row[:, 256:512]
    tail = lane_below(roll_lanes(row[:, 768:896], 64), 64)
    s = jnp.concatenate([main, main, main, tail + roll_lanes(tail, 64), tail], 1)
    return outer(c, s)


def centre_small(grad, beta):
    _, c = tap_points(beta)
    row = jnp.broadcast_to(grad[224:225, 128:256], (8, 128))
    return outer(c, jnp.concatenate([row, row, row], 1))


def conv_gather(frames, p, s):
    def three(at):
        return (
            shift_places(at(0), frames, -1) + at(1) + shift_places(at(2), frames, 1)
        )

    main = three(lambda k: p[:, 256 * k : 256 * k + 256])
    small = three(lambda k: s[:, 128 * k : 128 * k + 128])
    ends = p[:, 768:896]
    tail = three(lambda k: (ends, roll_lanes(ends, 64), p[:, 896:1024])[k])
    return main, small, lane_below(tail, 64)


def spread_x(frames, v, by):
    return v if by == 0 else shift_places(v, frames, -by)


def put_spread(frames, main, small, tail, put_mid, put_small):
    for k in range(3):
        put_mid(256 * k, spread_x(frames, main, k - 1))
        put_small(128 * k, spread_x(frames, small, k - 1))
    put_mid(768, spread_x(frames, tail, -1) + roll_lanes(tail, 64))
    put_mid(896, spread_x(frames, tail, 1))


def join_final(small, tail, pool):
    s, p = roll_lanes(small, 64), roll_lanes(pool, 64)
    low = lax.broadcasted_iota(jnp.int32, small.shape, 1) < 64
    return jnp.where(low, tail, s), jnp.where(low, s, p), jnp.where(low, p, 0.0)


def split_final(t4, t5, t6):
    a, b, c = roll_lanes(t4, 64), roll_lanes(t5, 64), roll_lanes(t6, 64)
    low = lax.broadcasted_iota(jnp.int32, t4.shape, 1) < 64
    return jnp.where(low, a, b), jnp.where(low, t4, 0.0), jnp.where(low, b, c)


def final_stats(st1, st2, stf):
    stf[:, 0:256] = st1[:, 0:256]
    stf[:, 256:512] = st2[:, 0:256]
    for t, v in enumerate(join_final(st2[:, 256:384], st2[:, 384:512], st1[:, 256:384])):
        stf[:, 512 + 128 * t : 640 + 128 * t] = v
    stf[2:3, :] = jnp.broadcast_to(st1[2:3, 0:1], (1, DP))


def store_conv(clips, y, p, s, zp, put, acc):
    main, small, tail = conv_gather(clips.frames, p, s)
    put(y, 256, main)
    for t, v in enumerate(join_final(small, tail, zp[y])):
        put(y, 512 + 128 * t, v)
    add_stats(clips, acc, pl.ds(0, 256), main)
    add_stats(clips, acc, pl.ds(256, 128), small)
    add_stats(clips, acc, pl.ds(384, 128), tail)


def forward_part(
    len_ref, bn, x, og, w_one, w_mid_in, w_small_in, w_pool, w_mid, w_small,
    st1, stf, beta1, xgot_out, zin_out, zf_out, sig_out, cat_out, scat_out, wp1, wf1, ws1, og_got,
    x_got, hand, asum, bsum, beta2, beta, got_beta, wp, wf, ws,
    loc, buf, ssem, rsem, loc2, buf2, ssem2, rsem2, osem, psem, qsem,
    zf, zin, zp, cat, scat, sig, scr, st2, coef, coef_in, hacc, acc, acc2,
):
    greet(partner=True)
    sec = lax.axis_index("section")
    side = zp.shape[0]
    rows = side * 16
    clips = Clips(len_ref, 16, 1)
    hacc[...] = jnp.zeros_like(hacc)
    acc[...] = jnp.zeros_like(acc)
    acc2[...] = jnp.zeros_like(acc2)
    loc[...] = jnp.zeros_like(loc)
    loc2[...] = jnp.zeros_like(loc2)
    outs = []

    def put(src, dst):
        c = pltpu.make_async_copy(src, dst, osem.at[len(outs)])
        c.start()
        outs.append(c)

    pairs = ((wp.at[sec], wp.at[sec]), (beta, got_beta), (x.at[1 - sec], x_got))
    pairs += ((og.at[1 - sec], og_got), (wf.at[sec], wf.at[sec]), (ws.at[sec], ws.at[sec]))
    remote = [swap_copy(a, b, psem.at[i], qsem.at[i]) for i, (a, b) in enumerate(pairs)]

    def first_phase(x_own, yp, tx, one, mid_in, small_in, pool, mid, small, flip, lsem):
        local = [
            pltpu.make_async_copy(a, b, lsem.at[i])
            for i, (a, b) in enumerate(
                (
                    (x.at[sec], x_own),
                    (w_one.at[0], one),
                    (w_mid_in.at[0], mid_in),
                    (w_small_in.at[0], small_in),
                    (w_pool.at[0], pool),
                    (w_mid.at[0], mid),
                    (w_small.at[0], small),
                )
            )
        ]
        for c in local[1:] + local[:1]:
            c.start()
        arrange_beta(bn, beta)
        for c in local[1:5]:
            c.wait()
        arrange_first((one, mid_in, small_in, pool), wp, sec, flip)
        greeted(partner=True)
        for c in remote[:4]:
            c.start()
        for c in local[5:]:
            c.wait()
        arrange_conv(mid, small, wf, ws, sec, flip)
        for c in remote[4:]:
            c.start()
        for c in remote[:2]:
            c.wait()
        beta1[...] = jnp.where(sec == 0, beta[...], got_beta[...])
        beta2[...] = jnp.where(sec == 0, got_beta[...], beta[...])
        ny = side // 2
        size = ny * side * 8
        for k, src in enumerate((x_own, x_got)):
            (local[0] if k == 0 else remote[2]).wait()
            half = sec if k == 0 else 1 - sec

            def body(i, src=src, half=half):
                here = pl.ds(i * ny, ny)
                y = dot(src[pl.ds(pl.multiple_of(i * size, 16), size)], wp[0])

                def place(lo, hi):
                    return y[:, lo:hi].reshape(ny, side, 8, hi - lo)

                zf[here, :, half, :, 0:256] = place(0, 256)
                yp[here, :, half] = place(256, 384)
                zin[here, :, half] = place(384, 640)
                for lo, hi in ((0, 256), (384, 640)):
                    v = y[:, lo:hi].reshape(-1, 8, 256)
                    hacc[0, half, :, lo:hi] += jnp.sum(v, axis=0)
                    hacc[1, half, :, lo:hi] += jnp.sum(v * v, axis=0)

            loop(2, body)
        acc[...] = hacc[...].reshape(acc.shape)
        pool_forward(clips, side, lambda y: yp[y].reshape(rows, 128), tx, zp, acc)

    like = [pltpu.VMEM(a.shape[1:], BF16) for a in (w_one, w_mid_in, w_small_in, w_pool, w_mid, w_small)]
    pl.run_scoped(
        first_phase,
        pltpu.VMEM(x.shape[1:], BF16),
        vmem(side, side, 2, 8, 128),
        vmem(side + 2, rows, 128),
        *like,
        vmem(27 * C1A, 384, dtype=BF16),
        pltpu.SemaphoreType.DMA((7,)),
    )
    pack_stats(clips, loc, acc, FIRST, side * side)
    exchange_start(loc, buf, ssem, rsem)
    put(x_got, xgot_out)
    put(zin, zin_out)
    for y in (0, side + 1):
        cat[y] = jnp.zeros(cat.shape[1:], BF16)
        scat[y] = jnp.zeros(scat.shape[1:], BF16)
    exchange_finish(loc, buf, ssem, rsem, st1, FIRST)
    fill_inner(coef_in, st1, beta1)

    def build(y):
        a, b = inner_tiles(clips, zin[y].reshape(rows, 256), coef_in)
        parts, small = tap_tiles(clips, a, b)
        for i, part in enumerate(parts):
            cat[y + 1, :, 128 * i : 128 * i + 128] = part.astype(BF16)
        scat[y + 1] = small.astype(BF16)

    loop(side, build)
    for c in remote[3:]:
        c.wait()
    put(cat, cat_out)
    put(scat, scat_out)
    for a, b in ((wf, wf1), (ws, ws1), (wp, wp1)):
        put(a.at[0], b)
    ny = 2

    def put_row(y, lane, v):
        zf[y, :, :, :, lane : lane + v.shape[-1]] = v.reshape(side, 2, 8, v.shape[-1])

    def products(i):
        y0 = i * ny

        def taps(ref):
            return jnp.concatenate(
                [ref[pl.ds(y0 + dy, ny)].reshape(ny * rows, ref.shape[-1]) for dy in range(3)], axis=1
            )

        p = dot(taps(cat), wf[0])
        s = dot(taps(scat), ws[0])
        for q in range(ny):
            here = slice(q * rows, (q + 1) * rows)
            store_conv(clips, y0 + q, p[here], s[here], zp, put_row, acc2)

    loop(side // ny, products)
    pack_stats(clips, loc2, acc2, CONV)
    exchange_start(loc2, buf2, ssem2, rsem2)
    put(zf, zf_out)
    half = side // 2

    pair_valid = clips.valid.reshape(8, 2, 128)[:, 0] * 0.125

    def emit(k, tiles):
        for t in tiles:
            lanes = pl.ds(128 * t, 128)
            scale, shift, b = coef[0:1, lanes], coef[2:3, lanes], coef[3:4, lanes]
            pooled = None
            for q in range(2):
                t_in = zf[2 * k + q, :, :, :, lanes].reshape(rows, 128) * scale + shift
                sp, sg = soft(t_in)
                if t == 6:
                    lane = lax.broadcasted_iota(jnp.int32, sp.shape, 1)
                    sp = jnp.where(lane == 127, 1.0, lane_below(sp, 64))
                    sg = lane_below(sg, 64)
                sig[2 * k + q, :, lanes] = sg.astype(BF16)
                three = [
                    jnp.sum(v.reshape(half, 2, 16, 128), axis=1) for v in (sp, sg, sg * (t_in - b))
                ]
                pooled = three if pooled is None else [x + y for x, y in zip(pooled, three)]
            for v, dst in zip(pooled, (hand, asum, bsum)):
                scr[...] = v
                dst[k, :, :, lanes] = (
                    scr[:, pl.ds(0, 8, stride=2), :] + scr[:, pl.ds(1, 8, stride=2), :]
                ) * pair_valid

    for t in range(2):
        lanes = pl.ds(128 * t, 128)
        fill_norm(coef, lanes, st1, lanes, beta1[0:1, lanes])
    loop(half, lambda k: emit(k, (0, 1)))
    exchange_finish(loc2, buf2, ssem2, rsem2, st2, CONV)
    final_stats(st1, st2, stf)
    for t in range(2, 7):
        lanes = pl.ds(128 * t, 128)
        fill_norm(coef, lanes, stf, lanes, beta1[0:1, lanes])
    base = len(outs)

    def rest(k):
        emit(k, range(2, 7))
        here = pl.ds(2 * k, 2)
        pltpu.make_async_copy(sig.at[here], sig_out.at[here], osem.at[base]).start()

    loop(half, rest)
    for c in outs:
        c.wait()
    pltpu.make_async_copy(sig, sig_out, osem.at[base]).wait()


def second_part(
    len_ref, og, beta1, block_out, hg_out, packed_out, sums5, sums6, sums7, og_got,
    hand, asum, bsum, beta, wp, wf, ws, psem, qsem, sums_scratch,
    gown, ggot, grad, out, lsem, hg, packed,
    hbuf, zin, zp, zf, stf, yp, tx, catf, cat, scat, pbuf, sbuf, dbuf, dzc, dzs, dz1, din,
    acc, st3, st4, acc7, accm, accs, accp, coef, coef_in,
):
    (
        loc3, buf3, ss3, rs3, loc4, buf4, ss4, rs4, loc5, buf5, ss5, rs5,
        loc6, buf6, ss6, rs6, loc7, buf7, ss7, rs7,
    ) = sums_scratch
    sec = lax.axis_index("section")
    own = pltpu.make_async_copy(og.at[sec], gown, lsem.at[0])
    other = pltpu.make_async_copy(og_got, ggot, lsem.at[2])
    own.start()
    other.start()
    side = hand.shape[0]
    rows = side * 8
    total = side * rows
    clips = Clips(len_ref, 8, 2)
    for ref in (acc, acc7, loc3, loc4, loc5, loc6, loc7):
        ref[...] = jnp.zeros_like(ref)

    hbuf[...] = hand[...].reshape(total, DP).astype(BF16)
    y = dot(hbuf[:, 0:D], wp[...])
    zf[:, :, 0:C0] = y[:, 0:C0].reshape(side, rows, C0)
    yp[...] = y[:, 256:384].reshape(side, rows, 128)
    zin[...] = y[:, 384:640].reshape(side, rows, 256)

    def first_sums(y):
        add_stats(clips, acc, pl.ds(0, 256), zf[y, :, 0:256])
        add_stats(clips, acc, pl.ds(384, 256), zin[y])

    loop(side, first_sums)
    pool_forward(clips, side, lambda y: yp[y], tx, zp, acc)
    pack_stats(clips, loc3, acc, FIRST, side * side)
    exchange_start(loc3, buf3, ss3, rs3)
    own.wait()
    other.wait()
    mine, theirs = gown[...].astype(F32), ggot[...].astype(F32)
    low = jnp.where(sec == 0, mine, theirs)
    high = jnp.where(sec == 0, theirs, mine)
    grad[...] = jnp.concatenate([low, high], 2)
    exchange_finish(loc3, buf3, ss3, rs3, st3, FIRST)

    fill_inner(coef_in, st3, beta)
    catf[0] = jnp.zeros(catf.shape[1:], F32)
    catf[side + 1] = jnp.zeros(catf.shape[1:], F32)

    def build(y):
        a, b = inner_tiles(clips, zin[y], coef_in)
        parts, small = tap_tiles(clips, a, b)
        for t, v in enumerate(parts + [small]):
            catf[y + 1, :, 128 * t : 128 * t + 128] = v

    loop(side, build)
    for dy in range(3):
        v = catf[dy : dy + side].reshape(total, 640).astype(BF16)
        cat[:, 512 * dy : 512 * dy + 512] = v[:, 0:512]
        scat[:, 128 * dy : 128 * dy + 128] = v[:, 512:640]
    pbuf[...] = dot(cat[...], wf[...]).reshape(side, rows, 1024)
    sbuf[...] = dot(scat[...], ws[...]).reshape(side, rows, 384)
    acc[...] = jnp.zeros_like(acc)

    def put_row(y, lane, v):
        zf[y, :, lane : lane + v.shape[-1]] = v

    loop(side, lambda y: store_conv(clips, y, pbuf[y], sbuf[y], zp, put_row, acc))
    pack_stats(clips, loc4, acc, CONV)
    exchange(loc4, buf4, ss4, rs4, st4, CONV)
    final_stats(st3, st4, stf)
    for t in range(7):
        lanes = pl.ds(128 * t, 128)
        fill_norm(coef, lanes, stf, lanes, beta[0:1, lanes])

    def emit(y):
        for t in range(7):
            lanes = pl.ds(128 * t, 128)
            t_in = zf[y, :, lanes] * coef[0:1, lanes] + coef[2:3, lanes]
            u = t_in - coef[3:4, lanes]
            sp, sg = soft(t_in)
            width = 128 if t < 6 else 64
            gr = grad[y, :, :, 128 * t : 128 * t + width].reshape(rows, width)
            if t == 6:
                gr = jnp.concatenate([gr, jnp.zeros((rows, 64), F32)], 1)
            d = gr * clips.times(sg, clips.valid)
            dbuf[y, :, lanes] = d
            add_stats(clips, acc7, lanes, d, u)
            sp = clips.times(sp, clips.valid).reshape(side, 8, 128)[:, :, 0:width]
            for h in range(2):
                out[h, y, :, :, 128 * t : 128 * t + width] = sp[:, 4 * h : 4 * h + 4].astype(BF16)

    loop(side, emit)
    mine = pltpu.make_async_copy(out.at[sec], block_out.at[sec], lsem.at[1])
    mine.start()
    theirs = swap_copy(out.at[1 - sec], block_out.at[sec], psem, qsem)
    theirs.start()
    pack_stats(clips, loc5, acc7, FINAL)
    exchange(loc5, buf5, ss5, rs5, sums5, FINAL)
    count = st3[2:3, 0:128]
    for t in range(7):
        lanes = pl.ds(128 * t, 128)
        fill_back(coef, lanes, sums5, lanes, count)

    def dz_of(y, t):
        lanes = pl.ds(128 * t, 128)
        v = dbuf[y, :, lanes] * coef[0:1, lanes] + zf[y, :, lanes] * coef[4:5, lanes]
        return clips.times(v + coef[5:6, lanes], clips.valid)

    def dz_final(y):
        for t in range(2):
            dz1[y, :, 128 * t : 128 * t + 128] = dz_of(y, t)
        main = jnp.concatenate([dz_of(y, 2), dz_of(y, 3)], 1)
        small, tail, pool = split_final(*(dz_of(y, t) for t in (4, 5, 6)))
        yp[y] = clips.times(pool * inv_edges(side, 8, y), clips.inv)

        def put(ref):
            def go(lane, v):
                ref[y, :, lane : lane + v.shape[-1]] = v

            return go

        put_spread(8, main, small, tail, put(dzc), put(dzs))

    loop(side, dz_final)

    def boxed(y, v):
        dz1[y, :, 256:384] = clips.times(v, clips.valid)

    box(clips, side, lambda y: yp[y], tx, boxed)
    dzc_b = dzc[...].reshape(total, 1024).astype(BF16)
    dzs_b = dzs[...].reshape(total, 384).astype(BF16)
    for dy in (-1, 0, 1):
        k = dy + 1
        q = dot_nt(dzc_b, wf[512 * k : 512 * k + 512]).reshape(side, rows, 512)
        r = dot_nt(dzs_b, ws[128 * k : 128 * k + 128]).reshape(side, rows, 128)
        if k == 0:
            catf[1 : side + 1] = jnp.zeros((side, rows, 640), F32)
        catf[1 + dy : 1 + dy + side, :, 0:512] += q
        catf[1 + dy : 1 + dy + side, :, 512:640] += r
    acc[...] = jnp.zeros_like(acc)

    def inner_back(y):
        parts = [catf[y + 1, :, 128 * t : 128 * t + 128] for t in range(5)]
        inner_up(clips, zin[y], untap(clips, parts[:4], parts[4]), coef_in, acc, din, y)

    loop(side, inner_back)
    pack_stats(clips, loc6, acc, INNER)
    exchange_start(loc6, buf6, ss6, rs6)
    accm[...] = dot_tn(cat[...], dzc_b)
    exchange_finish(loc6, buf6, ss6, rs6, sums6, INNER)
    fill_inner_back(coef_in, sums6, count)

    def dz_inner(y):
        for t in range(2):
            dz1[y, :, 384 + 128 * t : 512 + 128 * t] = inner_dz(
                clips, t, zin[y], din[y], coef_in
            )

    loop(side, dz_inner)
    dz1_b = dz1[...].reshape(total, 640).astype(BF16)
    hgv = dot_nt(dz1_b, wp[...]).astype(BF16).astype(F32)
    hg[:, :, :, 0:D] = hgv.reshape(side, side, 8, D)
    hg[:, :, :, D:DP] = jnp.zeros((side, side, 8, DP - D), F32)
    acc7[...] = jnp.zeros_like(acc7)

    def upstream(y):
        for t in range(7):
            lanes = pl.ds(128 * t, 128)
            gr = hg[y, :, :, lanes]
            acc7[0, :, lanes] += jnp.sum(gr * asum[y, :, :, lanes], axis=0)
            acc7[1, :, lanes] += jnp.sum(gr * bsum[y, :, :, lanes], axis=0)

    loop(side, upstream)
    pack_stats(clips, loc7, acc7, FINAL)
    exchange_start(loc7, buf7, ss7, rs7)
    accs[...] = dot_tn(scat[...], dzs_b)
    accp[...] = dot_tn(hbuf[...], dz1_b)
    pool = dz1[:, :, 256:384].reshape(total, 128)
    rest = (pool - dz1_b[:, 256:384].astype(F32)).astype(BF16)
    accp[:, 256:384] += dot_tn(hbuf[...], rest)
    c = jnp.concatenate([typical(beta1[0:1, 0:D]), jnp.zeros((8, DP - D), F32)], 1)
    full = accp[...] - outer(c, accp[DP - 1 : DP, :])
    mid = centre_mid(accm[992:993, :], beta)
    small = centre_small(accs, beta)
    for k in range(3):
        pack_mid(packed[k], accm.at[512 * k : 512 * k + 512], mid, accs, small, k)

    def column(t, r, rows):
        return full[r : r + rows, 128 * t : 128 * t + 128]

    pack_one(packed[3], column)
    pack_inner(packed[4], column, accs, small)
    puts = [
        pltpu.make_async_copy(a, b, lsem.at[3 + i])
        for i, (a, b) in enumerate(zip((hg,) + packed, (hg_out,) + packed_out))
    ]
    for c in puts:
        c.start()
    exchange_finish(loc7, buf7, ss7, rs7, sums7, FINAL)
    mine.wait()
    theirs.wait()
    for c in puts:
        c.wait()


def blocks_kernel(first_scope, second_scope, *refs):
    ins, outs, refs = refs[:10], refs[10:33], refs[33:]
    len_ref, og = ins[0], ins[3]
    st1, stf, beta1, sums5, sums6, sums7 = outs[:6]
    kept, og_got, block_out, hg_out, packed_out = outs[6:15], outs[15], outs[16], outs[17], outs[18:]
    x_got, hand, asum, bsum, beta2, beta, got_beta, wp, wf, ws = refs[:10]
    sums1, sums2, (osem, psem, qsem, psem2, qsem2) = refs[10:18], refs[18:38], refs[38:]

    def one(*own):
        forward_part(
            *ins, st1, stf, beta1, *kept, og_got,
            x_got, hand, asum, bsum, beta2, beta, got_beta, wp, wf, ws,
            *sums1, osem, psem, qsem, *own,
        )

    def two(gown, ggot, grad, out, lsem, hg, p0, p1, p2, p3, p4, *own):
        second_part(
            len_ref, og, beta1, block_out, hg_out, tuple(packed_out), sums5, sums6, sums7, og_got,
            hand, asum, bsum, beta2, wp.at[1], wf.at[1], ws.at[1], psem2, qsem2, sums2,
            gown, ggot, grad, out, lsem, hg, (p0, p1, p2, p3, p4), *own,
        )

    pl.run_scoped(one, *first_scope)
    pl.run_scoped(two, *second_scope)


def pack_mid(packed, acc, mid, accs, small, k):
    for t in range(8):
        lanes = slice(128 * t, 128 * t + 128)
        packed[t, 0:480] = (acc[0:480, lanes] - mid[0:480, lanes]).astype(BF16)
        packed[t, 480:512] = small_piece(accs, small, 8 * k + t)
        if packed.shape[1] > 512:
            packed[t, 512:] = jnp.zeros((packed.shape[1] - 512, 128), BF16)


def small_piece(accs, small, b):
    dy, dt, dx = b // 9, b // 3 % 3, b % 3
    lanes = slice(128 * dx, 128 * dx + 128)
    r = 128 * dy + 32 * dt
    return (accs[r : r + 32, lanes] - small[32 * dt : 32 * dt + 32, lanes]).astype(BF16)


def pack_one(packed, column):
    end = packed.shape[1]
    for j in range(8):
        packed[j, 0:208] = column(j // 4, 208 * (j % 4), 208).astype(BF16)
        rows = min(112, D - 112 * j)
        packed[j, 208 : 208 + rows] = column(2, 112 * j, rows).astype(BF16)
        if 208 + rows < end:
            packed[j, 208 + rows : end] = jnp.zeros((end - 208 - rows, 128), BF16)


def pack_inner(packed, column, accs, small):
    end = packed.shape[1]
    for j in range(8):
        packed[j, 0:208] = column(3 + j // 4, 208 * (j % 4), 208).astype(BF16)
        packed[j, 208:end] = jnp.zeros((end - 208, 128), BF16)
        if j < 3:
            packed[j, 208:240] = small_piece(accs, small, 24 + j)


def inner_up(clips, z, backs, coef, acc, din, y):
    for t in range(2):
        lanes = slice(128 * t, 128 * t + 128)
        zs = z[:, lanes] * coef[0:1, lanes]
        d = backs[t] * clips.times(sigm(zs + coef[2:3, lanes]), clips.valid)
        din[y, :, lanes] = d
        add_stats(clips, acc, pl.ds(384 + 128 * t, 128), d, zs - coef[1:2, lanes])


def fill_inner_back(coef, sums, count):
    for t in range(2):
        fill_back(coef, pl.ds(128 * t, 128), sums, pl.ds(384 + 128 * t, 128), count)


def inner_dz(clips, t, z, d, coef):
    lanes = slice(128 * t, 128 * t + 128)
    v = d[:, lanes] * coef[0:1, lanes] + z[:, lanes] * coef[4:5, lanes] + coef[5:6, lanes]
    dz = clips.times(v, clips.valid)
    return lane_below(dz, 64) if t == 1 else dz


def put_halves(ref, y, lane, v):
    side, lanes = v.shape[0] // 16, v.shape[1]
    v = v.reshape(side, 2, 8, lanes)
    for h in range(2):
        ref[h, y, :, lane : lane + lanes] = v[:, h].reshape(side * 8, lanes).astype(BF16)


Z_FIRST = (3,)
SCHEDULE = {
    "start": ((2, 0), (0, 0),),
    "dz3": ((4, 0), (2, 1),),
    "dz4": ((3, 0), (0, 1),),
    "dz5": ((1, 0),),
    "dzend": ((3, 1), (4, 1), (2, 2),),
    "scat": ((1, 1),),
    "m1": ((0, 2),),
    "d1": ((6, 0), (2, 3), (4, 2), (3, 2),),
    "m0": ((6, 1), (0, 3), (1, 2),),
    "d0": ((5, 0), (3, 3), (2, 4),),
    "m2": ((6, 2), (4, 3), (5, 1),),
    "d2": ((3, 4), (1, 3), (0, 4), (7, 0), (2, 5),),
    "e": ((5, 2),),
    "cb0": ((7, 1), (8, 0), (1, 4),),
    "cb1": ((8, 1), (5, 3), (4, 4), (6, 3), (2, 6),),
    "cb3": ((0, 5), (7, 2), (1, 5), (8, 2),),
    "cb5": ((5, 4),),
    "cb6": ((4, 5), (6, 4), (1, 6),),
    "s8a": ((0, 6), (5, 5), (7, 3), (4, 6),),
    "l": ((9, 0), (6, 5), (8, 3), (3, 5), (7, 4),),
    "in0": ((9, 1), (5, 6),),
    "in1": ((8, 4), (9, 2),),
    "in2": ((7, 5),),
    "in5": ((6, 6), (1, 7), (9, 3), (8, 5),),
    "in6": ((7, 6), (9, 4),),
    "in7": ((0, 7),),
    "in8": ((4, 7),),
    "in10": ((5, 7), (9, 5), (3, 6), (8, 6), (6, 7), (2, 7),),
    "in12": ((9, 6),),
    "in13": ((8, 7), (7, 7), (3, 7),),
    "end": ((9, 7),),
}


def backward_kernel(
    bits, len_ref, hg, stf, sums7, st1, beta, sums5, sums6,
    zf, sig, zin_in, wf_in, ws_in, wp_in, cat_in, scat_in, x, x_got, two0, two1, two2, two3, two4,
    gin, full0, full1, full2, full3, full4, offs,
    zin, wf, ws, wp, cat, scat, x0, x1, dzc, dzs, dz1, dzi, sums8, snd, got,
    coef, coef_in, acc, loc, buf, ss8, rs8, lsem, csend, crecv, ssem, rsem, gsend, grecv, *arrays,
):
    greet(partner=True)
    sec = lax.axis_index("section")
    side = dz1.shape[1]
    half = side // 2
    rows = side * 16
    clips = Clips(len_ref, 16, 1)
    count = stf[2:3, 0:128]
    loads = [
        pltpu.make_async_copy(a, b, lsem.at[i])
        for i, (a, b) in enumerate(
            (
                (zin_in, zin),
                (wf_in, wf),
                (ws_in, ws),
                (wp_in, wp),
                (cat_in, cat),
                (scat_in, scat),
                (x.at[sec], x0),
                (x_got, x1),
            )
        )
    ]
    two = (two0, two1, two2, two3, two4)
    full = (full0, full1, full2, full3, full4)
    own_two, ones = arrays[0:5], arrays[5:10]
    core_land = arrays[10:20]
    pieces = 2 ** len(groups(bits)[-1]) - 1 + len(groups(bits)) - 1
    lands = arrays[20:]

    def part(ref, which):
        h = ref.shape[1] // 2
        return ref.at[:, pl.ds(pl.multiple_of(which * h, 16), h)]

    def reducer(i, q, base, rows, swap_src, flip, load):
        return Reducer(
            bits, i, q, base, rows, swap_src, core_land[i], lands[pieces * i : pieces * i + pieces],
            csend, crecv, ssem, rsem, flip, load,
        )

    g, h = [], []
    for i, (a, b) in enumerate(zip(two, own_two)):
        load = pltpu.make_async_copy(part(a, sec), b, lsem.at[8 + i])
        load.start()
        g.append(reducer(i, b, 0, b.shape[1], part(a, 1 - sec), 1 - sec, load))
    for i, a in enumerate(ones):
        rows_half = a.shape[1] // 2
        h.append(
            reducer(5 + i, a, sec * rows_half, rows_half, part(a, 1 - sec), sec, None)
        )
    def at(name):
        for r, e in SCHEDULE.get(name, ()):
            (g + h)[r].event(e)

    acc[...] = jnp.zeros_like(acc)
    loc[...] = jnp.zeros_like(loc)
    for t in range(7):
        lanes = pl.ds(128 * t, 128)
        fill_norm(coef, lanes, stf, lanes, beta[0:1, lanes])
        fill_back(coef, lanes, sums7, lanes, count)
    fill_inner(coef_in, st1, beta)
    for y in (0, side + 1):
        dzc[y] = jnp.zeros(dzc.shape[1:], BF16)
        dzs[y] = jnp.zeros(dzs.shape[1:], BF16)

    def dz_phase(zb, sb, scr, yp, tx, zsem):
        def fetch(k, slot):
            here = pl.ds(2 * k, 2)
            return (
                pltpu.make_async_copy(zf.at[here], zb.at[slot], zsem.at[0, slot]),
                pltpu.make_async_copy(sig.at[here], sb.at[slot], zsem.at[1, slot]),
            )

        for c in fetch(0, 0):
            c.start()
        for c in loads[4:] + loads[:4]:
            c.start()

        def body(k):
            slot = lax.rem(k, 2)

            @pl.when(k < half - 1)
            def _():
                for c in fetch(k + 1, 1 - slot):
                    c.start()

            @pl.when(k == 1)
            def _():
                greeted(partner=True)
                at("start")

            for j in range(2, half):
                pl.when(k == j)(lambda j=j: at(f"dz{j}"))
            for c in fetch(k, slot):
                c.wait()
            tiles = ([], [])
            for t in range(7):
                lanes = pl.ds(128 * t, 128)
                by_z, rest = coef[4:5, lanes], coef[5:6, lanes]
                gr = hg[k, :, :, lanes] * (coef[0:1, lanes] * 0.125)
                scr[:, pl.ds(0, 8, stride=2), :] = gr
                scr[:, pl.ds(1, 8, stride=2), :] = gr
                gr = scr[...]
                gr = jnp.broadcast_to(gr[:, None], (half, 2, 16, 128)).reshape(rows, 128)
                for q in range(2):
                    v = gr * sb[slot, q, :, lanes].astype(F32) + zb[slot, q, :, lanes] * by_z
                    dz = clips.times(v + rest, clips.valid)
                    if t < 2:
                        put_halves(dz1, 2 * k + q, 128 * t, dz)
                    else:
                        tiles[q].append(dz)
            for q in range(2):
                y = 2 * k + q
                small, tail, pool = split_final(*tiles[q][2:])
                yp[y] = clips.times(pool * inv_edges(side, 16, y), clips.inv)

                def put(ref, y=y):
                    def go(lane, v):
                        ref[y + 1, :, lane : lane + v.shape[-1]] = v.astype(BF16)

                    return go

                main = jnp.concatenate(tiles[q][:2], 1).astype(BF16)
                put_spread(16, main, small.astype(BF16), tail, put(dzc), put(dzs))

        loop(half, body)
        at("dzend")

        def boxed(y, v):
            put_halves(dz1, y, 256, clips.times(v, clips.valid))

        box(clips, side, lambda y: yp[y], tx, boxed)
        at("box")

    pl.run_scoped(
        dz_phase,
        vmem(2, 2, rows, DP),
        vmem(2, 2, rows, DP, dtype=BF16),
        vmem(half, 16, 128),
        vmem(side, rows, 128),
        vmem(side + 2, rows, 128),
        pltpu.SemaphoreType.DMA((2, 2)),
    )

    def grad_phase(accm, mid, accs, accp):
        for c in loads[4:6]:
            c.wait()
        ny = side // 2

        def take(ref, y):
            return ref[pl.ds(y, ny)].reshape(ny * rows, ref.shape[-1])

        def sums(k, between):
            accm[...] = dot_tn(take(cat, 1), take(dzc, 2 - k))
            between()
            accm[...] += dot_tn(take(cat, 1 + ny), take(dzc, 2 - k + ny))

        for k in range(3):
            here = slice(128 * k, 128 * k + 128)
            accs[here] = dot_tn(take(scat, 1), take(dzs, 2 - k))
            accs[here] += dot_tn(take(scat, 1 + ny), take(dzs, 2 - k + ny))
        small = centre_small(accs, beta)
        at("scat")
        for k in (1, 0, 2):
            sums(k, lambda: at(f"m{k}"))
            if k == 1:
                mid[...] = centre_mid(accm[480:481, :], beta)
            pack_mid(ones[k], accm, mid, accs, small, k)
            at(f"d{k}")
        for c in loads[6:]:
            c.wait()
        accp[...] = jnp.zeros_like(accp)
        add_outer(accp, dz1, ((x1, 1 - sec), (x0, sec)))
        pack_one(ones[3], lambda t, r, n: accp[r : r + n, 128 * t : 128 * t + 128])
        pack_inner(ones[4], lambda t, r, n: jnp.zeros((n, 128), F32), accs, small)
        at("e")

    def add_outer(accp, d_ref, sides):
        step = side // 2
        size = step * side * 8
        for src, which in sides:

            def body(i, src=src, which=which):
                at = pl.ds(pl.multiple_of(i * size, 16), size)
                d = d_ref[which, pl.ds(i * step, step)].reshape(size, d_ref.shape[-1])
                accp[...] += dot_tn(src[at], d)

            loop(side // step, body)

    pl.run_scoped(
        grad_phase,
        vmem(512, 1024),
        vmem(512, 1024),
        vmem(384, 384),
        vmem(D, 384),
    )

    def last_phase(din, ring, accp, sems):
        for c in loads[:4]:
            c.wait()
        ny = 2

        def body(i):
            y0 = i * ny + 1
            for j in range(side // ny):
                pl.when(i == j)(lambda j=j: at(f"cb{j}"))
            q = s = None
            for dy in (-1, 0, 1):
                k = dy + 1
                here = pl.ds(y0 - dy, ny)
                t = dot_nt(dzc[here].reshape(ny * rows, 1024), wf[512 * k : 512 * k + 512])
                q = t if q is None else q + t
                t = dot_nt(dzs[here].reshape(ny * rows, 384), ws[128 * k : 128 * k + 128])
                s = t if s is None else s + t
            for j in range(ny):
                y = i * ny + j
                here = slice(j * rows, (j + 1) * rows)
                parts = [q[here, 128 * t : 128 * t + 128] for t in range(4)]
                inner_up(clips, zin[y], untap(clips, parts, s[here]), coef_in, acc, din, y)

        loop(side // ny, body)
        pack_stats(clips, loc, acc, INNER)
        exchange_start(loc, buf, ss8, rs8)
        at("s8a")
        sides = ((x1, 1 - sec), (x0, sec))
        step = side // 2
        size = step * side * 8
        exchange_finish(loc, buf, ss8, rs8, sums8, INNER)
        fill_inner_back(coef_in, sums8, count)
        at("s8b")

        def dz(y):
            for t in range(2):
                put_halves(dzi, y, 128 * t, inner_dz(clips, t, zin[y], din[y], coef_in))

        loop(side, dz)
        at("dzi")
        accp[...] = jnp.zeros_like(accp)
        add_outer(accp, dzi, sides)
        for j in range(8):
            ones[4][j, 0:208] = accp[
                208 * (j % 4) : 208 * (j % 4) + 208, 128 * (j // 4) : 128 * (j // 4) + 128
            ].astype(BF16)
        at("l")
        sent = []
        step = 2
        size = step * side * 8
        chunks = side // step
        slots = ring.shape[0]
        for p in range(2 * chunks):
            which = sides[p // chunks][1]
            i = p % chunks
            slot = p % slots
            if p >= slots:
                sent[p - slots].wait()
            here = pl.ds(i * step, step)
            d = jnp.concatenate([dz1[which, here], dzi[which, here]], -1).reshape(size, 640)
            ring[slot] = dot_nt(d, wp[...]).astype(BF16)
            to = gin.at[sec, i * size : (i + 1) * size]
            if p < chunks:
                c = swap_copy(ring.at[slot], to, gsend.at[i], grecv.at[i])
            else:
                c = pltpu.make_async_copy(ring.at[slot], to, sems.at[slot])
            c.start()
            sent.append(c)
            at(f"in{p}")
        for c in sent[-slots:]:
            c.wait()

    dma = pltpu.SemaphoreType.DMA
    pl.run_scoped(
        last_phase,
        vmem(side, rows, 256),
        vmem(4, 2 * side * 8, D, dtype=BF16),
        vmem(D, 256),
        dma((4,)),
    )
    snd[:, 0:DP] = jnp.where(sec == 0, sums5[...], sums7[...])
    snd[:, DP : DP + 640] = jnp.where(sec == 0, sums6[...], sums8[...])
    small = swap_copy(snd, got, csend.at[15], crecv.at[15])
    small.start()
    at("end")

    def finish(mine, theirs):
        copies = []
        for i, (dst, m, t) in enumerate(zip(full, mine, theirs)):
            copies.append(pltpu.make_async_copy(m, dst.at[sec], lsem.at[13 + i]))
            copies.append(swap_copy(t, dst.at[sec], csend.at[10 + i], crecv.at[10 + i]))
        for c in copies:
            c.start()
        for c in copies:
            c.wait()

    pl.when(sec == 0)(lambda: finish(core_land[5:10], core_land[0:5]))
    pl.when(sec == 1)(lambda: finish(core_land[0:5], core_land[5:10]))
    small.wait()
    for lanes, a, b in ((slice(0, DP), sums7, sums5), (slice(DP, DP + 640), sums8, sums6)):
        offs[:, lanes] = jnp.where(sec == 0, a[...], b[...]) + got[:, lanes]


def put_halves(ref, y, lane, v):
    side, lanes = v.shape[0] // 16, v.shape[1]
    v = v.reshape(side, 2, 8, lanes)
    for h in range(2):
        ref[h, y, :, lane : lane + lanes] = v[:, h].reshape(side * 8, lanes).astype(BF16)


def groups(bits, last_first=False):
    if bits < 3:
        return [(k,) for k in range(bits)]
    plan = [(k,) for k in range(bits - 2)] + [(bits - 2, bits - 1)]
    return plan[-1:] + plan[:-1] if last_first else plan


class Reducer:
    EVENTS = 8

    def __init__(
        self, bits, index, q, base, rows, swap_src, core_land, land, csend, crecv, ssem, rsem, flip, load
    ):
        self.index, self.q, self.base, self.rows = index, q, base, rows
        self.core_land, self.land, self.load = core_land, land, load
        self.ssem, self.rsem = ssem, rsem
        self.swap = swap_copy(swap_src, core_land, csend.at[index], crecv.at[index])
        me = lax.axis_index("dp")
        plan = groups(bits, index in Z_FIRST)
        self.count = len(plan)
        self.last = 2 * self.count
        self.steps = []
        tiles, t0, r0 = 8, 0, 0
        at = 0
        for step, ks in enumerate(plan):
            powers = []
            for k in ks:
                power = 1 << k
                if bits > 1 and k < 2:
                    power = power + flip * ((1 << (1 - k)) - power)
                powers.append((power, lax.rem(me // power, 2)))
            cuts = []
            for power, bit in powers:
                if tiles > 1:
                    tiles //= 2
                    cuts.append((bit, tiles, 0))
                else:
                    rows //= 2
                    cuts.append((bit, 0, rows))
            sends = []
            for c in range(1, 1 << len(ks)):
                partner, t, r = me, t0, r0
                for i, ((power, bit), (_, dt, dr)) in enumerate(zip(powers, cuts)):
                    turned = (c >> i) & 1
                    partner = partner + turned * (1 - 2 * bit) * power
                    here = bit + turned * (1 - 2 * bit)
                    t, r = t + here * dt, r + here * dr
                sends.append((partner, (t, r), at))
                at += 1
            for bit, dt, dr in cuts:
                t0, r0 = t0 + bit * dt, r0 + bit * dr
            self.steps.append((sends, (t0, r0), tiles, rows))
        self.pieces = at

    def region(self, ref, base, at, tiles, rows):
        t, r = at
        r = base + r
        if not isinstance(r, int):
            r = pl.multiple_of(r, 16)
        return ref.at[pl.ds(t, tiles), pl.ds(r, rows)]

    def mine(self, at, tiles, rows):
        return self.region(self.q, self.base, at, tiles, rows)

    def total(self, at, tiles, rows):
        return self.region(self.core_land, 0, at, tiles, rows)

    def copies(self, i):
        if i == 0:
            return [self.swap]
        halving = i <= self.count
        sends, keep, tiles, rows = self.steps[i - 1 if halving else self.last - i]
        out = []
        for partner, send, piece in sends:
            src = self.mine(send, tiles, rows) if halving else self.total(keep, tiles, rows)
            sem = 2 * (self.index * self.pieces + piece) + int(halving)
            out.append(
                pltpu.make_async_remote_copy(
                    src_ref=src,
                    dst_ref=self.land[piece] if halving else src,
                    send_sem=self.ssem.at[sem],
                    recv_sem=self.rsem.at[sem],
                    device_id={"dp": partner},
                    device_id_type=MESH,
                )
            )
        return out

    def received(self, i):
        sends, keep, tiles, rows = self.steps[self.last - i]
        out = []
        for partner, send, piece in sends:
            sem = 2 * (self.index * self.pieces + piece)
            dst = self.total(send, tiles, rows)
            out.append(
                pltpu.make_async_remote_copy(
                    src_ref=dst,
                    dst_ref=dst,
                    send_sem=self.ssem.at[sem],
                    recv_sem=self.rsem.at[sem],
                    device_id={"dp": partner},
                    device_id_type=MESH,
                )
            )
        return out

    def add(self, dst, q, lands, tiles, rows):
        chunk = next(c for c in range(min(rows, 256), 0, -16) if rows % c == 0 and c % 16 == 0)
        parts = rows // chunk

        def body(j):
            t, r = j // parts, pl.multiple_of(lax.rem(j, parts) * chunk, 16)
            at = pl.ds(r, chunk)
            total = q[t, at].astype(F32)
            for land in lands:
                total = total + land[t, at].astype(F32)
            dst[t, at] = total.astype(BF16)

        loop(tiles * parts, body)

    def finish(self, i):
        if i > self.count:
            for c in self.copies(i):
                c.wait_send()
            for c in self.received(i):
                c.wait_recv()
            return
        for c in self.copies(i):
            c.wait()
        if i == 0:
            if self.load is not None:
                self.load.wait()
            q = self.mine((0, 0), 8, self.rows)
            self.add(q, q, [self.core_land], 8, self.rows)
        else:
            sends, keep, tiles, rows = self.steps[i - 1]
            lands = [self.land[piece] for _, _, piece in sends]
            q = self.mine(keep, tiles, rows)
            dst = self.total(keep, tiles, rows) if i == self.count else q
            self.add(dst, q, lands, tiles, rows)

    def event(self, e):
        count = self.last + 2
        for i in range(e * count // self.EVENTS, (e + 1) * count // self.EVENTS):
            if i > 0:
                self.finish(i - 1)
            if i <= self.last:
                for c in self.copies(i):
                    c.start()


def land_shapes(tiles, rows, bits, last_first):
    out = []
    for ks in groups(bits, last_first):
        for _ in ks:
            if tiles > 1:
                tiles //= 2
            else:
                rows //= 2
        out += [(tiles, rows, 128)] * (2 ** len(ks) - 1)
    return out


def unpack_kernel(
    full0, full1, full2, full3, full4, gin_in, out_in, offs,
    one, mid_in, mid_out, small_in, small, pool, offset, gin, out,
    buf0, buf1, buf2, buf3, buf4, nat, inner, gin_buf, out_buf, mid, sem,
):
    copies = []
    bufs = (buf0, buf1, buf2, buf3, buf4)
    for i, (full, buf) in enumerate(zip((full0, full1, full2, full3, full4), bufs)):
        half = full.shape[2]
        for h in range(2):
            copies.append(
                pltpu.make_async_copy(full.at[h], buf.at[:, h * half : (h + 1) * half], sem.at[2 * i + h])
            )
    for c in copies:
        c.start()
    through = ((gin_in, gin_buf, gin), (out_in, out_buf, out))
    for i, (src, buf, dst) in enumerate(through):
        pltpu.make_async_copy(src, buf, sem.at[10 + i]).start()
    v = offs[...]
    lane = lax.broadcasted_iota(jnp.int32, v.shape, 1)
    out = jnp.where(lane < 256, v, 0.0)
    for lo, hi, by in ((256, 416, -1024), (416, 736, 160), (736, 768, -704), (768, 1024, 192)):
        out = jnp.where((lane >= lo) & (lane < hi), roll_lanes(v, by), out)
    offset[...] = out[0:1, 0:1024]
    for c in copies:
        c.wait()

    def take(b, t, r, rows):
        return bufs[b][t, r : r + rows].astype(F32)

    for dt in range(3):
        for dy in range(3):
            for dx in range(3):
                to = 160 * (9 * dt + 3 * dy + dx)
                for rows, r in ((128, 128 * dt), (32, 384 + 32 * dt)):
                    nat[to : to + rows, 0:128] = take(dy, 2 * dx, r, rows)
                    nat[to : to + rows, 128:256] = take(dy, 2 * dx + 1, r, rows)
                    tail = take(dy, 6 + dx // 2, r, rows)
                    nat[to : to + rows, 256:384] = roll_lanes(tail, 64) if dx == 1 else tail
                    to = to + rows
                b = 9 * dy + 3 * dt + dx
                to = 32 * (9 * dt + 3 * dy + dx)
                small[to : to + 32, :] = (
                    take(b // 8, b % 8, 480, 32) if b < 24 else take(4, b - 24, 208, 32)
                )

    def turn(i):
        at = pl.ds(pl.multiple_of(i * 128, 128), 128)
        mid[0:256, at] = nat[at, 0:256].T
        mid[256:320, at] = nat[at, 256:384].T[0:64]

    total = mid.shape[1]
    passed = []
    for i, (src, buf, dst) in enumerate(through):
        pltpu.make_async_copy(src, buf, sem.at[10 + i]).wait()
        passed.append(pltpu.make_async_copy(buf, dst, sem.at[10 + i]))
        passed[i].start()
    blocks = total // 128
    for part in range(3):
        lo, hi = part * blocks // 3, (part + 1) * blocks // 3
        loop(hi - lo, lambda i, lo=lo: turn(i + lo))
        end = 128 * hi
        if part == 2:
            at = slice(end, total)
            mid[0:256, at] = nat[at, 0:256].T
            mid[256:320, at] = nat[at, 256:384].T[0:64]
            end = total
        at = slice(128 * lo, end)
        passed.append(pltpu.make_async_copy(mid.at[:, at], mid_out.at[:, at], sem.at[12 + part]))
        passed[-1].start()
    for j in range(8):
        at = slice(208 * (j % 4), 208 * (j % 4) + 208)
        one[at, 128 * (j // 4) : 128 * (j // 4) + 128] = take(3, j, 0, 208)
        inner[j // 4, at] = take(4, j, 0, 208)
        rows = min(112, D - 112 * j)
        pool[112 * j : 112 * j + rows, :] = take(3, j, 208, rows)
    for r in range(0, D, 128):
        at = slice(r, min(r + 128, D))
        mid_in[0:128, at] = inner[0, at].T
        last = inner[1, at].T
        mid_in[128:160, at] = last[0:32]
        small_in[:, at] = last[32:64]
    for c in passed:
        c.wait()


def vmem(*shape, dtype=F32):
    return pltpu.VMEM(shape, dtype)


def call(kernel, outs, args, scratch, collective=None, smem_first=True, any_in=(), any_out=()):
    def specs(count, anywhere):
        return [
            pl.BlockSpec(memory_space=pl.ANY if i in anywhere else pltpu.VMEM)
            for i in range(count)
        ]

    in_specs = specs(len(args), any_in)
    if smem_first:
        in_specs[0] = pl.BlockSpec(memory_space=pltpu.SMEM)
    params = {"vmem_limit_bytes": VMEM_LIMIT}
    if collective is not None:
        params.update(collective_id=collective, has_side_effects=True)
    return pl.pallas_call(
        kernel,
        out_shape=[jax.ShapeDtypeStruct(shape, dtype) for shape, dtype in outs],
        in_specs=in_specs,
        out_specs=specs(len(outs), any_out),
        scratch_shapes=scratch,
        compiler_params=pltpu.CompilerParams(**params),
    )(*args)


def on_device(
    clip_input, out_grad, clip_lengths, w_one, w_mid_in, w_mid, w_small_in, w_small, w_pool, bn_offset
):
    n = lax.axis_size("dp")
    bits = n.bit_length() - 1
    half, side = clip_input.shape[1], clip_input.shape[2]
    rows = side * 16
    side2 = side // 2
    rows2 = side2 * 8
    total2 = side2 * rows2
    unit = 32 << max(bits - 3, 0)
    packed_rows = [-(-r // unit) * unit for r in (512, 512, 512, 320, 256)]
    x = clip_input.transpose(0, 2, 3, 1, 4).reshape(2, side * side * half, D)
    og = out_grad.transpose(0, 2, 3, 1, 4)

    def like(a, dtype=BF16):
        return pltpu.VMEM(a.shape[1:], dtype)

    def turned(w):
        return w.transpose(0, 2, 1)

    weights = (w_one, turned(w_mid_in), turned(w_small_in), w_pool, turned(w_mid), w_small)
    dma = pltpu.SemaphoreType.DMA
    grid = (side, side, 2, 8)

    def bf(*shape):
        return vmem(*shape, dtype=BF16)

    pooled = (side2, side2, 8, DP)
    first_scope = [
        vmem(*grid, DP),
        vmem(*grid, 256),
        vmem(side, rows, 128),
        bf(side + 2, rows, 512),
        bf(side + 2, rows, 128),
        bf(side, rows, DP),
        vmem(side2, 16, 128),
        vmem(8, 512),
        vmem(8, DP),
        vmem(8, 256),
        vmem(2, 2, 8, 640),
        vmem(2, 16, 640),
        vmem(2, 16, 512),
    ]
    second_scope = (
        [
            like(og),
            like(og),
            vmem(side2, side2, 8, D),
            bf(2, *og.shape[1:]),
            dma((9,)),
            vmem(*pooled),
        ]
        + [bf(8, r, 128) for r in packed_rows]
        + [
            bf(total2, DP),
            vmem(side2, rows2, 256),
            vmem(side2, rows2, 128),
            vmem(side2, rows2, DP),
            vmem(8, DP),
            vmem(side2, rows2, 128),
            vmem(side2 + 2, rows2, 128),
            vmem(side2 + 2, rows2, 640),
            bf(total2, 1536),
            bf(total2, 384),
            vmem(side2, rows2, 1024),
            vmem(side2, rows2, 384),
            vmem(side2, rows2, DP),
            vmem(side2, rows2, 1024),
            vmem(side2, rows2, 384),
            vmem(side2, rows2, 640),
            vmem(side2, rows2, 256),
            vmem(2, 8, 640),
            vmem(8, 640),
            vmem(8, 512),
            vmem(2, 8, DP),
            vmem(1536, 1024),
            vmem(384, 384),
            vmem(DP, 640),
            vmem(8, DP),
            vmem(8, 256),
        ]
    )
    st1, stf, beta1, sums5, sums6, sums7, *rest = call(
        functools.partial(blocks_kernel, first_scope, second_scope),
        [
            ((8, 640), F32),
            ((8, DP), F32),
            ((1, 1152), F32),
            ((8, DP), F32),
            ((8, 640), F32),
            ((8, DP), F32),
            (x.shape[1:], BF16),
            (grid + (256,), F32),
            (grid + (DP,), F32),
            ((side, rows, DP), BF16),
            ((side + 2, rows, 512), BF16),
            ((side + 2, rows, 128), BF16),
            ((D, 640), BF16),
            ((1536, 1024), BF16),
            ((384, 384), BF16),
            (og.shape[1:], BF16),
            (og.shape, BF16),
            (pooled, F32),
        ]
        + [((8, r, 128), BF16) for r in packed_rows],
        (clip_lengths, bn_offset, x, og) + weights,
        [
            like(x),
            vmem(*pooled),
            vmem(*pooled),
            vmem(*pooled),
            vmem(1, 1152),
            vmem(1, 1152),
            vmem(1, 1152),
            bf(2, D, 640),
            bf(2, 1536, 1024),
            bf(2, 384, 384),
        ]
        + exchange_scratch(n, 16)
        + exchange_scratch(n, 8)
        + exchange_scratch(n, 16)
        + exchange_scratch(n, 8)
        + exchange_scratch(n, 16)
        + exchange_scratch(n, 8)
        + exchange_scratch(n, 16)
        + [dma((9,)), dma((6,)), dma((6,)), dma(()), dma(())],
        collective=1,
        any_in=range(2, 10),
        any_out=range(6, 23),
    )
    xgot, zin, zf, sig, cat, scat, wp1, wf1, ws1, og_got, block_output, hg, *two = rest
    zin = zin.reshape(side, rows, 256)
    zf = zf.reshape(side, rows, DP)
    halves = [r // 2 for r in packed_rows]
    lands = []
    for i, h in enumerate(halves * 2):
        lands += [bf(*shape) for shape in land_shapes(8, h, bits, i in Z_FIRST)]
    gin, *full, offs = call(
        functools.partial(backward_kernel, bits),
        [(x.shape, BF16)]
        + [((2, 8, h, 128), BF16) for h in halves]
        + [((8, DP + 640), F32)],
        (clip_lengths, hg, stf, sums7, st1, beta1, sums5, sums6)
        + (zf, sig, zin, wf1, ws1, wp1, cat, scat, x, xgot, *two),
        [
            vmem(side, rows, 256),
            bf(1536, 1024),
            bf(384, 384),
            bf(D, 640),
            bf(side + 2, rows, 512),
            bf(side + 2, rows, 128),
            like(x),
            like(x),
            bf(side + 2, rows, 1024),
            bf(side + 2, rows, 384),
            bf(2, side, rows // 2, 384),
            bf(2, side, rows // 2, 256),
            vmem(8, 640),
            vmem(8, DP + 640),
            vmem(8, DP + 640),
            vmem(8, DP),
            vmem(8, 256),
            vmem(2, 16, 640),
        ]
        + exchange_scratch(n, 8)
        + [dma((18,)), dma((16,)), dma((16,)), dma((2 * len(lands),)), dma((2 * len(lands),))]
        + [dma((side,)), dma((side,))]
        + [bf(8, h, 128) for h in halves]
        + [bf(8, r, 128) for r in packed_rows]
        + [bf(8, h, 128) for h in halves * 2]
        + lands,
        collective=3,
        any_in=range(8, 23),
        any_out=range(6),
    )
    one, mid_in, mid, small_in, small, pool, offset, gin, block_output = call(
        unpack_kernel,
        [
            ((D, C0), F32),
            ((C1A, D), F32),
            ((C1B, 27 * C1A), F32),
            ((C2A, D), F32),
            ((27 * C2A, C2B), F32),
            ((D, C3), F32),
            ((1, 1024), F32),
            (x.shape, BF16),
            (og.shape, BF16),
        ],
        (*full, gin, block_output, offs),
        [bf(8, r, 128) for r in packed_rows]
        + [vmem(27 * C1A, 384), vmem(2, D, 128), bf(*x.shape), bf(*og.shape), vmem(C1B, 27 * C1A), dma((15,))],
        smem_first=False,
        any_in=range(7),
        any_out=(2, 7, 8),
    )
    input_grad = gin.reshape(2, side, side, half, D).transpose(0, 3, 1, 2, 4)
    return (
        block_output.transpose(0, 3, 1, 2, 4),
        input_grad,
        one[None],
        mid_in.T[None],
        mid.T[None],
        small_in.T[None],
        small[None],
        pool[None],
        offset,
    )


def solution(mesh):
    placed = (
        P("dp", "section", None, None, None),
        P("dp", "section", None, None, None),
        P("dp", None),
        P("section", None, None),
        P("section", None, None),
        P("section", None, None),
        P("section", None, None),
        P("section", None, None),
        P("section", None, None),
        P("section", None),
    )
    return jax.shard_map(
        on_device,
        mesh=mesh,
        in_specs=placed,
        out_specs=(
            P("dp", "section", None, None, None),
            P("dp", "section", None, None, None),
            P("section", None, None),
            P("section", None, None),
            P("section", None, None),
            P("section", None, None),
            P("section", None, None),
            P("section", None, None),
            P("section", None),
        ),
        check_vma=False,
    )
```

```python
import functools

import jax
import jax.numpy as jnp
from jax import lax
from jax.experimental import pallas as pl
from jax.experimental.pallas import tpu as pltpu
from jax.sharding import PartitionSpec as P

D = 832
DP = 896
C0 = 256
C1A = 160
C1B = 320
C2A = 32
C2B = 128
C3 = 128
EPS = 0.001
MESH = pl.DeviceIdType.MESH
F32 = jnp.float32
BF16 = jnp.bfloat16
VMEM_LIMIT = 60 * 2**20


def dot(a, b):
    return jnp.dot(a, b, preferred_element_type=F32)


def dot_nt(a, b):
    return lax.dot_general(a, b, (((1,), (1,)), ((), ())), preferred_element_type=F32)


def dot_tn(a, b):
    return lax.dot_general(a, b, (((0,), (0,)), ((), ())), preferred_element_type=F32)


def roll_rows(x, by):
    return pltpu.roll(x, by % x.shape[0], 0)


def roll_lanes(x, by):
    return pltpu.roll(x, by % x.shape[1], 1)


def lane_below(x, count):
    lanes = lax.broadcasted_iota(jnp.int32, x.shape, 1)
    return jnp.where(lanes < count, x, 0.0)


class Clips:
    def __init__(self, len_ref, frames, stride):
        sec = lax.axis_index("section")
        f = lax.broadcasted_iota(jnp.int32, (frames, 128), 0)

        def label(v):
            place = v * stride
            out = jnp.zeros_like(v)
            start = jnp.int32(0)
            for c in range(len_ref.shape[1]):
                end = start + len_ref[sec, c]
                out = jnp.where((place >= start) & (place < end), c + 1, out)
                start = end
            return out

        here = label(f)
        inside = here > 0

        def mask(m):
            return jnp.where(m, 1.0, 0.0).astype(F32)

        self.frames = frames
        self.valid = mask(inside)
        self.before = mask(inside & (f > 0) & (label(f - 1) == here))
        self.after = mask(inside & (f < frames - 1) & (label(f + 1) == here))
        self.inv = 1.0 / jnp.maximum(self.valid + self.before + self.after, 1.0)

    def times(self, v, pattern):
        return (v.reshape(-1, self.frames, 128) * pattern).reshape(v.shape)

    def fold(self, v):
        return jnp.sum(v.reshape(-1, self.frames, v.shape[-1]), axis=0)


def shift_places(v, frames, by):
    lanes = v.shape[-1]
    v3 = v.reshape(-1, frames, lanes)
    zero = jnp.zeros((1, frames, lanes), v.dtype)
    if by > 0:
        v3 = jnp.concatenate([v3[1:], zero], 0)
    else:
        v3 = jnp.concatenate([zero, v3[:-1]], 0)
    return v3.reshape(v.shape)


def add_stats(clips, acc, lanes, v, w=None):
    acc[0, :, lanes] += clips.fold(v)
    acc[1, :, lanes] += clips.fold(v * (v if w is None else w))


def affine(st, lanes):
    total, square, count = st[0:1, lanes], st[1:2, lanes], st[2:3, lanes]
    mean = total / count
    scale = lax.rsqrt(square / count - mean * mean + EPS)
    return scale, mean


def fill_norm(coef, to, st, lanes, beta):
    scale, mean = affine(st, lanes)
    coef[0:1, to] = scale
    coef[1:2, to] = mean * scale
    coef[2:3, to] = beta - mean * scale
    coef[3:4, to] = beta


def fill_back(coef, to, sums, lanes, count):
    m1, m2 = sums[0:1, lanes] / count, sums[1:2, lanes] / count
    scale = coef[0:1, to]
    coef[4:5, to] = -scale * scale * m2
    coef[5:6, to] = scale * (coef[1:2, to] * m2 - m1)


def soft(t):
    s = 0.5 + 0.5 * jnp.tanh(0.5 * jnp.abs(t))
    return jnp.maximum(t, 0.0) - jnp.log(s), jnp.where(t >= 0, s, 1.0 - s)


def sigm(t):
    return 0.5 + 0.5 * jnp.tanh(0.5 * t)


def greet(partner=False):
    n = lax.axis_size("dp")
    me = lax.axis_index("dp")
    barrier = pltpu.get_barrier_semaphore()

    def go(k, _):
        pl.semaphore_signal(
            barrier, inc=1, device_id={"dp": lax.rem(me + k, n)}, device_id_type=MESH
        )
        return 0

    if partner:
        other = 1 - lax.axis_index("section")
        pl.semaphore_signal(barrier, inc=1, device_id={"section": other}, device_id_type=MESH)
    lax.fori_loop(1, n, go, 0)


def greeted(partner=False):
    pl.semaphore_wait(pltpu.get_barrier_semaphore(), lax.axis_size("dp") - 1 + int(partner))


def exchange_start(loc, buf, ssem, rsem):
    n = lax.axis_size("dp")
    me = lax.axis_index("dp")

    def start(k, _):
        pltpu.make_async_remote_copy(
            src_ref=loc,
            dst_ref=buf.at[me],
            send_sem=ssem.at[k],
            recv_sem=rsem.at[me],
            device_id={"dp": lax.rem(me + k, n)},
            device_id_type=MESH,
        ).start()
        return 0

    lax.fori_loop(1, n, start, 0)
    buf[me] = loc[...]


def exchange_finish(loc, buf, ssem, rsem, out, tiles):
    n = lax.axis_size("dp")
    me = lax.axis_index("dp")

    def wait(k, _):
        j = lax.rem(me + k, n)
        copy = pltpu.make_async_remote_copy(
            src_ref=loc,
            dst_ref=buf.at[j],
            send_sem=ssem.at[k],
            recv_sem=rsem.at[j],
            device_id={"dp": j},
            device_id_type=MESH,
        )
        copy.wait_send()
        copy.wait_recv()
        return 0

    lax.fori_loop(1, n, wait, 0)
    total = jnp.sum(buf[...], axis=0)
    at = 2 * len(tiles)
    for i, t in enumerate(tiles):
        lanes = slice(128 * t, 128 * t + 128)
        out[0:1, lanes] = total[2 * i : 2 * i + 1]
        out[1:2, lanes] = total[2 * i + 1 : 2 * i + 2]
        if at < loc.shape[0]:
            out[2:3, lanes] = total[at : at + 1]


def exchange(loc, buf, ssem, rsem, out, tiles):
    exchange_start(loc, buf, ssem, rsem)
    exchange_finish(loc, buf, ssem, rsem, out, tiles)


def swap_copy(src, dst, ssem, rsem):
    return pltpu.make_async_remote_copy(
        src_ref=src,
        dst_ref=dst,
        send_sem=ssem,
        recv_sem=rsem,
        device_id={"section": 1 - lax.axis_index("section")},
        device_id_type=MESH,
    )


def exchange_scratch(n, rows):
    return [
        pltpu.VMEM((rows, 128), F32),
        pltpu.VMEM((n, rows, 128), F32),
        pltpu.SemaphoreType.DMA((n,)),
        pltpu.SemaphoreType.DMA((n,)),
    ]


FIRST, CONV, FINAL, INNER = range(5), range(4), range(7), (3, 4)


def pack_stats(clips, loc, acc, tiles, count=None):
    for i, t in enumerate(tiles):
        lanes = pl.ds(128 * t, 128)
        for k in range(2):
            loc[2 * i + k : 2 * i + k + 1, :] = jnp.sum(
                acc[k, :, lanes] * clips.valid, axis=0, keepdims=True
            )
    if count is not None:
        at = 2 * len(tiles)
        loc[at : at + 1, :] = jnp.sum(clips.valid, axis=0, keepdims=True) * float(count)


def loop(n, body):
    def step(i, _):
        body(i)
        return 0

    lax.fori_loop(0, n, step, 0)


def inv_edges(side, frames, y):
    x = lax.broadcasted_iota(jnp.int32, (side, frames, 128), 0)
    ex = jnp.where((x == 0) | (x == side - 1), 0.5, 1.0 / 3.0).astype(F32)
    ey = jnp.where((y == 0) | (y == side - 1), 0.5, 1.0 / 3.0).astype(F32)
    return (ex * ey).reshape(side * frames, 128)


def box(clips, side, load, tx, store):
    frames = clips.frames
    tx[0] = jnp.zeros(tx.shape[1:], F32)
    tx[side + 1] = jnp.zeros(tx.shape[1:], F32)

    def across(y):
        v = load(y)
        t = clips.times(v, clips.valid)
        t = t + clips.times(roll_rows(v, 1), clips.before)
        t = t + clips.times(roll_rows(v, -1), clips.after)
        tx[y + 1] = t + shift_places(t, frames, 1) + shift_places(t, frames, -1)

    def down(y):
        store(y, tx[y] + tx[y + 1] + tx[y + 2])

    loop(side, across)
    loop(side, down)


def pool_forward(clips, side, load, tx, zp, acc):
    def store(y, v):
        z = clips.times(v * inv_edges(side, clips.frames, y), clips.inv)
        zp[y] = z
        add_stats(clips, acc, pl.ds(256, 128), z)

    box(clips, side, load, tx, store)


def upright(src, dst):
    rows = src.shape[1]
    width = src.shape[0]

    def body(i):
        at = pl.ds(pl.multiple_of(i * 128, 128), 128)
        dst[at, 0:width] = src[:, at].astype(F32).T.astype(BF16)

    loop(rows // 128, body)
    if rows % 128:
        at = slice(rows - rows % 128, rows)
        dst[at, 0:width] = src[:, at].astype(F32).T.astype(BF16)


def arrange_first(src, wp, b, flip):
    one, mid_in, small_in, pool = src
    wp[b, :, 0:256] = one[...]
    wp[b, :, 256:384] = pool[...]
    upright(mid_in, flip)
    wp[b, :, 384:544] = flip[0:D, 0:C1A]
    upright(small_in, flip)
    wp[b, :, 544:576] = flip[0:D, 0:C2A]
    wp[b, :, 576:640] = jnp.zeros((D, 64), BF16)


def arrange_beta(src, dst):
    v = jnp.concatenate([jnp.broadcast_to(src[...], (8, 1024)), jnp.zeros((8, 128), F32)], 1)
    lane = lax.broadcasted_iota(jnp.int32, v.shape, 1)
    out = jnp.zeros_like(v)
    for lo, hi, by in (
        (0, 256, 0),
        (256, 576, -160),
        (576, 832, -192),
        (896, 1056, 640),
        (1056, 1088, 320),
    ):
        out = jnp.where((lane >= lo) & (lane < hi), roll_lanes(v, by), out)
    dst[...] = out[0:1]


def arrange_conv(mid_flat, small, wf, ws, b, mid):
    upright(mid_flat, mid)
    for dy in range(3):
        wf[b, 512 * dy + 480 : 512 * dy + 512, :] = jnp.zeros((32, 1024), BF16)
        ws[b, 128 * dy + 96 : 128 * dy + 128, :] = jnp.zeros((32, 384), BF16)
        wf[b, 512 * dy : 512 * dy + 512, 960:1024] = jnp.zeros((512, 64), BF16)
        for dt in range(3):
            for dx in range(3):
                r = 96 * (3 * dt + dy) + 32 * dx
                to = 128 * dy + 32 * dt
                ws[b, to : to + 32, 128 * dx : 128 * dx + 128] = small[r : r + 32, :]
            for dx in range(3):
                r = 480 * (3 * dt + dy) + 160 * dx
                for rows, to in ((128, 128 * dt), (32, 384 + 32 * dt)):
                    to = to + 512 * dy
                    wf[b, to : to + rows, 256 * dx : 256 * dx + 256] = mid[r : r + rows, 0:256]
                    wf[b, to : to + rows, 768 + 64 * dx : 832 + 64 * dx] = mid[
                        r : r + rows, 256:320
                    ]
                    r = r + rows


def inner_tiles(clips, z, coef):
    tiles = []
    for t in range(2):
        lanes = slice(128 * t, 128 * t + 128)
        act, _ = soft(z[:, lanes] * coef[0:1, lanes] + coef[2:3, lanes])
        tiles.append(clips.times(act, clips.valid))
    return tiles


def fill_inner(coef, st, beta):
    for t in range(2):
        lanes = pl.ds(128 * t, 128)
        fill_norm(coef, lanes, st, pl.ds(384 + 128 * t, 128), beta[0:1, 896 + 128 * t : 1024 + 128 * t])


def tap_tiles(clips, a, b):
    def before(v):
        return clips.times(roll_rows(v, 1), clips.before)

    def after(v):
        return clips.times(roll_rows(v, -1), clips.after)

    lane = lax.broadcasted_iota(jnp.int32, b.shape, 1)
    ones = clips.times(jnp.where(lane == 96, 1.0, 0.0).astype(F32), clips.valid)

    def three32(v):
        return before(v) + roll_lanes(v, 32) + roll_lanes(after(v), 64) + ones

    tail = lane_below(b, 32)
    small = lane_below(roll_lanes(b, -32), 32)
    return [before(a), a, after(a), three32(tail)], three32(small)


def untap(clips, parts, small):
    def before(v):
        return roll_rows(clips.times(v, clips.before), -1)

    def after(v):
        return roll_rows(clips.times(v, clips.after), 1)

    def back32(v):
        return (
            lane_below(before(v), 32)
            + lane_below(roll_lanes(v, -32), 32)
            + lane_below(roll_lanes(after(v), -64), 32)
        )

    a = before(parts[0]) + parts[1] + after(parts[2])
    return a, back32(parts[3]) + roll_lanes(back32(small), 32)


def typical(beta):
    sp, sg = soft(jnp.broadcast_to(beta, (8, beta.shape[-1])))
    return sp + 0.5 * sg * (1.0 - sg)


def outer(c, s):
    k = lax.broadcasted_iota(jnp.int32, c.shape, 0)
    c = jnp.where(k < 2, c, 0.0).astype(BF16)
    s = jnp.broadcast_to(s, (8, s.shape[-1]))
    high = s.astype(BF16).astype(F32)
    k = lax.broadcasted_iota(jnp.int32, s.shape, 0)
    s = jnp.where(k == 0, high, jnp.where(k == 1, s - high, 0.0)).astype(BF16)
    return dot_tn(c, s)


def tap_points(beta):
    a = typical(beta[0:1, 896:1024])
    b = typical(beta[0:1, 1024:1152])

    def three(v):
        return v + roll_lanes(v, 32) + roll_lanes(v, 64)

    tail = three(lane_below(b, 32))
    small = three(lane_below(roll_lanes(b, -32), 32))
    return jnp.concatenate([a, a, a, tail], 1), small


def centre_mid(row, beta):
    c, _ = tap_points(beta)
    row = jnp.broadcast_to(row, (8, 1024))
    main = row[:, 256:512]
    tail = lane_below(roll_lanes(row[:, 768:896], 64), 64)
    s = jnp.concatenate([main, main, main, tail + roll_lanes(tail, 64), tail], 1)
    return outer(c, s)


def centre_small(grad, beta):
    _, c = tap_points(beta)
    row = jnp.broadcast_to(grad[224:225, 128:256], (8, 128))
    return outer(c, jnp.concatenate([row, row, row], 1))


def conv_gather(frames, p, s):
    def three(at):
        return (
            shift_places(at(0), frames, -1) + at(1) + shift_places(at(2), frames, 1)
        )

    main = three(lambda k: p[:, 256 * k : 256 * k + 256])
    small = three(lambda k: s[:, 128 * k : 128 * k + 128])
    ends = p[:, 768:896]
    tail = three(lambda k: (ends, roll_lanes(ends, 64), p[:, 896:1024])[k])
    return main, small, lane_below(tail, 64)


def spread_x(frames, v, by):
    return v if by == 0 else shift_places(v, frames, -by)


def put_spread(frames, main, small, tail, put_mid, put_small):
    for k in range(3):
        put_mid(256 * k, spread_x(frames, main, k - 1))
        put_small(128 * k, spread_x(frames, small, k - 1))
    put_mid(768, spread_x(frames, tail, -1) + roll_lanes(tail, 64))
    put_mid(896, spread_x(frames, tail, 1))


def join_final(small, tail, pool):
    s, p = roll_lanes(small, 64), roll_lanes(pool, 64)
    low = lax.broadcasted_iota(jnp.int32, small.shape, 1) < 64
    return jnp.where(low, tail, s), jnp.where(low, s, p), jnp.where(low, p, 0.0)


def split_final(t4, t5, t6):
    a, b, c = roll_lanes(t4, 64), roll_lanes(t5, 64), roll_lanes(t6, 64)
    low = lax.broadcasted_iota(jnp.int32, t4.shape, 1) < 64
    return jnp.where(low, a, b), jnp.where(low, t4, 0.0), jnp.where(low, b, c)


def final_stats(st1, st2, stf):
    stf[:, 0:256] = st1[:, 0:256]
    stf[:, 256:512] = st2[:, 0:256]
    for t, v in enumerate(join_final(st2[:, 256:384], st2[:, 384:512], st1[:, 256:384])):
        stf[:, 512 + 128 * t : 640 + 128 * t] = v
    stf[2:3, :] = jnp.broadcast_to(st1[2:3, 0:1], (1, DP))


def store_conv(clips, y, p, s, zp, put, acc):
    main, small, tail = conv_gather(clips.frames, p, s)
    put(y, 256, main)
    for t, v in enumerate(join_final(small, tail, zp[y])):
        put(y, 512 + 128 * t, v)
    add_stats(clips, acc, pl.ds(0, 256), main)
    add_stats(clips, acc, pl.ds(256, 128), small)
    add_stats(clips, acc, pl.ds(384, 128), tail)


def forward_part(
    len_ref, bn, x, og, w_one, w_mid_in, w_small_in, w_pool, w_mid, w_small,
    st1, stf, beta1, xgot_out, zin_out, zf_out, sig_out, cat_out, scat_out, wp1, wf1, ws1, og_got,
    x_got, hand, asum, bsum, beta2, beta, got_beta, wp, wf, ws,
    loc, buf, ssem, rsem, loc2, buf2, ssem2, rsem2, osem, psem, qsem,
    zf, zin, zp, cat, scat, sig, scr, st2, coef, coef_in, hacc, acc, acc2,
):
    greet(partner=True)
    sec = lax.axis_index("section")
    side = zp.shape[0]
    rows = side * 16
    clips = Clips(len_ref, 16, 1)
    hacc[...] = jnp.zeros_like(hacc)
    acc[...] = jnp.zeros_like(acc)
    acc2[...] = jnp.zeros_like(acc2)
    loc[...] = jnp.zeros_like(loc)
    loc2[...] = jnp.zeros_like(loc2)
    outs = []

    def put(src, dst):
        c = pltpu.make_async_copy(src, dst, osem.at[len(outs)])
        c.start()
        outs.append(c)

    pairs = ((wp.at[sec], wp.at[sec]), (beta, got_beta), (x.at[1 - sec], x_got))
    pairs += ((og.at[1 - sec], og_got), (wf.at[sec], wf.at[sec]), (ws.at[sec], ws.at[sec]))
    remote = [swap_copy(a, b, psem.at[i], qsem.at[i]) for i, (a, b) in enumerate(pairs)]

    def first_phase(x_own, yp, tx, one, mid_in, small_in, pool, mid, small, flip, lsem):
        local = [
            pltpu.make_async_copy(a, b, lsem.at[i])
            for i, (a, b) in enumerate(
                (
                    (x.at[sec], x_own),
                    (w_one.at[0], one),
                    (w_mid_in.at[0], mid_in),
                    (w_small_in.at[0], small_in),
                    (w_pool.at[0], pool),
                    (w_mid.at[0], mid),
                    (w_small.at[0], small),
                )
            )
        ]
        for c in local[1:] + local[:1]:
            c.start()
        arrange_beta(bn, beta)
        for c in local[1:5]:
            c.wait()
        arrange_first((one, mid_in, small_in, pool), wp, sec, flip)
        greeted(partner=True)
        for c in remote[:4]:
            c.start()
        for c in local[5:]:
            c.wait()
        arrange_conv(mid, small, wf, ws, sec, flip)
        for c in remote[4:]:
            c.start()
        for c in remote[:2]:
            c.wait()
        beta1[...] = jnp.where(sec == 0, beta[...], got_beta[...])
        beta2[...] = jnp.where(sec == 0, got_beta[...], beta[...])
        ny = side // 2
        size = ny * side * 8
        for k, src in enumerate((x_own, x_got)):
            (local[0] if k == 0 else remote[2]).wait()
            half = sec if k == 0 else 1 - sec

            def body(i, src=src, half=half):
                here = pl.ds(i * ny, ny)
                y = dot(src[pl.ds(pl.multiple_of(i * size, 16), size)], wp[0])

                def place(lo, hi):
                    return y[:, lo:hi].reshape(ny, side, 8, hi - lo)

                zf[here, :, half, :, 0:256] = place(0, 256)
                yp[here, :, half] = place(256, 384)
                zin[here, :, half] = place(384, 640)
                for lo, hi in ((0, 256), (384, 640)):
                    v = y[:, lo:hi].reshape(-1, 8, 256)
                    hacc[0, half, :, lo:hi] += jnp.sum(v, axis=0)
                    hacc[1, half, :, lo:hi] += jnp.sum(v * v, axis=0)

            loop(2, body)
        acc[...] = hacc[...].reshape(acc.shape)
        pool_forward(clips, side, lambda y: yp[y].reshape(rows, 128), tx, zp, acc)

    like = [pltpu.VMEM(a.shape[1:], BF16) for a in (w_one, w_mid_in, w_small_in, w_pool, w_mid, w_small)]
    pl.run_scoped(
        first_phase,
        pltpu.VMEM(x.shape[1:], BF16),
        vmem(side, side, 2, 8, 128),
        vmem(side + 2, rows, 128),
        *like,
        vmem(27 * C1A, 384, dtype=BF16),
        pltpu.SemaphoreType.DMA((7,)),
    )
    pack_stats(clips, loc, acc, FIRST, side * side)
    exchange_start(loc, buf, ssem, rsem)
    put(x_got, xgot_out)
    put(zin, zin_out)
    for y in (0, side + 1):
        cat[y] = jnp.zeros(cat.shape[1:], BF16)
        scat[y] = jnp.zeros(scat.shape[1:], BF16)
    exchange_finish(loc, buf, ssem, rsem, st1, FIRST)
    fill_inner(coef_in, st1, beta1)

    def build(y):
        a, b = inner_tiles(clips, zin[y].reshape(rows, 256), coef_in)
        parts, small = tap_tiles(clips, a, b)
        for i, part in enumerate(parts):
            cat[y + 1, :, 128 * i : 128 * i + 128] = part.astype(BF16)
        scat[y + 1] = small.astype(BF16)

    loop(side, build)
    for c in remote[3:]:
        c.wait()
    put(cat, cat_out)
    put(scat, scat_out)
    for a, b in ((wf, wf1), (ws, ws1), (wp, wp1)):
        put(a.at[0], b)
    ny = 2

    def put_row(y, lane, v):
        zf[y, :, :, :, lane : lane + v.shape[-1]] = v.reshape(side, 2, 8, v.shape[-1])

    def products(i):
        y0 = i * ny

        def taps(ref):
            return jnp.concatenate(
                [ref[pl.ds(y0 + dy, ny)].reshape(ny * rows, ref.shape[-1]) for dy in range(3)], axis=1
            )

        p = dot(taps(cat), wf[0])
        s = dot(taps(scat), ws[0])
        for q in range(ny):
            here = slice(q * rows, (q + 1) * rows)
            store_conv(clips, y0 + q, p[here], s[here], zp, put_row, acc2)

    loop(side // ny, products)
    pack_stats(clips, loc2, acc2, CONV)
    exchange_start(loc2, buf2, ssem2, rsem2)
    put(zf, zf_out)
    half = side // 2

    pair_valid = clips.valid.reshape(8, 2, 128)[:, 0] * 0.125

    def emit(k, tiles):
        for t in tiles:
            lanes = pl.ds(128 * t, 128)
            scale, shift, b = coef[0:1, lanes], coef[2:3, lanes], coef[3:4, lanes]
            pooled = None
            for q in range(2):
                t_in = zf[2 * k + q, :, :, :, lanes].reshape(rows, 128) * scale + shift
                sp, sg = soft(t_in)
                if t == 6:
                    lane = lax.broadcasted_iota(jnp.int32, sp.shape, 1)
                    sp = jnp.where(lane == 127, 1.0, lane_below(sp, 64))
                    sg = lane_below(sg, 64)
                sig[2 * k + q, :, lanes] = sg.astype(BF16)
                three = [
                    jnp.sum(v.reshape(half, 2, 16, 128), axis=1) for v in (sp, sg, sg * (t_in - b))
                ]
                pooled = three if pooled is None else [x + y for x, y in zip(pooled, three)]
            for v, dst in zip(pooled, (hand, asum, bsum)):
                scr[...] = v
                dst[k, :, :, lanes] = (
                    scr[:, pl.ds(0, 8, stride=2), :] + scr[:, pl.ds(1, 8, stride=2), :]
                ) * pair_valid

    for t in range(2):
        lanes = pl.ds(128 * t, 128)
        fill_norm(coef, lanes, st1, lanes, beta1[0:1, lanes])
    loop(half, lambda k: emit(k, (0, 1)))
    exchange_finish(loc2, buf2, ssem2, rsem2, st2, CONV)
    final_stats(st1, st2, stf)
    for t in range(2, 7):
        lanes = pl.ds(128 * t, 128)
        fill_norm(coef, lanes, stf, lanes, beta1[0:1, lanes])
    base = len(outs)

    def rest(k):
        emit(k, range(2, 7))
        here = pl.ds(2 * k, 2)
        pltpu.make_async_copy(sig.at[here], sig_out.at[here], osem.at[base]).start()

    loop(half, rest)
    for c in outs:
        c.wait()
    pltpu.make_async_copy(sig, sig_out, osem.at[base]).wait()


def second_part(
    len_ref, og, beta1, block_out, hg_out, packed_out, sums5, sums6, sums7, og_got,
    hand, asum, bsum, beta, wp, wf, ws, psem, qsem, sums_scratch,
    gown, ggot, grad, out, lsem, hg, packed,
    hbuf, zin, zp, zf, stf, yp, tx, catf, cat, scat, pbuf, sbuf, dbuf, dzc, dzs, dz1, din,
    acc, st3, st4, acc7, accm, accs, accp, coef, coef_in,
):
    (
        loc3, buf3, ss3, rs3, loc4, buf4, ss4, rs4, loc5, buf5, ss5, rs5,
        loc6, buf6, ss6, rs6, loc7, buf7, ss7, rs7,
    ) = sums_scratch
    sec = lax.axis_index("section")
    own = pltpu.make_async_copy(og.at[sec], gown, lsem.at[0])
    other = pltpu.make_async_copy(og_got, ggot, lsem.at[2])
    own.start()
    other.start()
    side = hand.shape[0]
    rows = side * 8
    total = side * rows
    clips = Clips(len_ref, 8, 2)
    for ref in (acc, acc7, loc3, loc4, loc5, loc6, loc7):
        ref[...] = jnp.zeros_like(ref)

    hbuf[...] = hand[...].reshape(total, DP).astype(BF16)
    y = dot(hbuf[:, 0:D], wp[...])
    zf[:, :, 0:C0] = y[:, 0:C0].reshape(side, rows, C0)
    yp[...] = y[:, 256:384].reshape(side, rows, 128)
    zin[...] = y[:, 384:640].reshape(side, rows, 256)

    def first_sums(y):
        add_stats(clips, acc, pl.ds(0, 256), zf[y, :, 0:256])
        add_stats(clips, acc, pl.ds(384, 256), zin[y])

    loop(side, first_sums)
    pool_forward(clips, side, lambda y: yp[y], tx, zp, acc)
    pack_stats(clips, loc3, acc, FIRST, side * side)
    exchange_start(loc3, buf3, ss3, rs3)
    own.wait()
    other.wait()
    mine, theirs = gown[...].astype(F32), ggot[...].astype(F32)
    low = jnp.where(sec == 0, mine, theirs)
    high = jnp.where(sec == 0, theirs, mine)
    grad[...] = jnp.concatenate([low, high], 2)
    exchange_finish(loc3, buf3, ss3, rs3, st3, FIRST)

    fill_inner(coef_in, st3, beta)
    catf[0] = jnp.zeros(catf.shape[1:], F32)
    catf[side + 1] = jnp.zeros(catf.shape[1:], F32)

    def build(y):
        a, b = inner_tiles(clips, zin[y], coef_in)
        parts, small = tap_tiles(clips, a, b)
        for t, v in enumerate(parts + [small]):
            catf[y + 1, :, 128 * t : 128 * t + 128] = v

    loop(side, build)
    for dy in range(3):
        v = catf[dy : dy + side].reshape(total, 640).astype(BF16)
        cat[:, 512 * dy : 512 * dy + 512] = v[:, 0:512]
        scat[:, 128 * dy : 128 * dy + 128] = v[:, 512:640]
    pbuf[...] = dot(cat[...], wf[...]).reshape(side, rows, 1024)
    sbuf[...] = dot(scat[...], ws[...]).reshape(side, rows, 384)
    acc[...] = jnp.zeros_like(acc)

    def put_row(y, lane, v):
        zf[y, :, lane : lane + v.shape[-1]] = v

    loop(side, lambda y: store_conv(clips, y, pbuf[y], sbuf[y], zp, put_row, acc))
    pack_stats(clips, loc4, acc, CONV)
    exchange(loc4, buf4, ss4, rs4, st4, CONV)
    final_stats(st3, st4, stf)
    for t in range(7):
        lanes = pl.ds(128 * t, 128)
        fill_norm(coef, lanes, stf, lanes, beta[0:1, lanes])

    def emit(y):
        for t in range(7):
            lanes = pl.ds(128 * t, 128)
            t_in = zf[y, :, lanes] * coef[0:1, lanes] + coef[2:3, lanes]
            u = t_in - coef[3:4, lanes]
            sp, sg = soft(t_in)
            width = 128 if t < 6 else 64
            gr = grad[y, :, :, 128 * t : 128 * t + width].reshape(rows, width)
            if t == 6:
                gr = jnp.concatenate([gr, jnp.zeros((rows, 64), F32)], 1)
            d = gr * clips.times(sg, clips.valid)
            dbuf[y, :, lanes] = d
            add_stats(clips, acc7, lanes, d, u)
            sp = clips.times(sp, clips.valid).reshape(side, 8, 128)[:, :, 0:width]
            for h in range(2):
                out[h, y, :, :, 128 * t : 128 * t + width] = sp[:, 4 * h : 4 * h + 4].astype(BF16)

    loop(side, emit)
    mine = pltpu.make_async_copy(out.at[sec], block_out.at[sec], lsem.at[1])
    mine.start()
    theirs = swap_copy(out.at[1 - sec], block_out.at[sec], psem, qsem)
    theirs.start()
    pack_stats(clips, loc5, acc7, FINAL)
    exchange(loc5, buf5, ss5, rs5, sums5, FINAL)
    count = st3[2:3, 0:128]
    for t in range(7):
        lanes = pl.ds(128 * t, 128)
        fill_back(coef, lanes, sums5, lanes, count)

    def dz_of(y, t):
        lanes = pl.ds(128 * t, 128)
        v = dbuf[y, :, lanes] * coef[0:1, lanes] + zf[y, :, lanes] * coef[4:5, lanes]
        return clips.times(v + coef[5:6, lanes], clips.valid)

    def dz_final(y):
        for t in range(2):
            dz1[y, :, 128 * t : 128 * t + 128] = dz_of(y, t)
        main = jnp.concatenate([dz_of(y, 2), dz_of(y, 3)], 1)
        small, tail, pool = split_final(*(dz_of(y, t) for t in (4, 5, 6)))
        yp[y] = clips.times(pool * inv_edges(side, 8, y), clips.inv)

        def put(ref):
            def go(lane, v):
                ref[y, :, lane : lane + v.shape[-1]] = v

            return go

        put_spread(8, main, small, tail, put(dzc), put(dzs))

    loop(side, dz_final)

    def boxed(y, v):
        dz1[y, :, 256:384] = clips.times(v, clips.valid)

    box(clips, side, lambda y: yp[y], tx, boxed)
    dzc_b = dzc[...].reshape(total, 1024).astype(BF16)
    dzs_b = dzs[...].reshape(total, 384).astype(BF16)
    for dy in (-1, 0, 1):
        k = dy + 1
        q = dot_nt(dzc_b, wf[512 * k : 512 * k + 512]).reshape(side, rows, 512)
        r = dot_nt(dzs_b, ws[128 * k : 128 * k + 128]).reshape(side, rows, 128)
        if k == 0:
            catf[1 : side + 1] = jnp.zeros((side, rows, 640), F32)
        catf[1 + dy : 1 + dy + side, :, 0:512] += q
        catf[1 + dy : 1 + dy + side, :, 512:640] += r
    acc[...] = jnp.zeros_like(acc)

    def inner_back(y):
        parts = [catf[y + 1, :, 128 * t : 128 * t + 128] for t in range(5)]
        inner_up(clips, zin[y], untap(clips, parts[:4], parts[4]), coef_in, acc, din, y)

    loop(side, inner_back)
    pack_stats(clips, loc6, acc, INNER)
    exchange_start(loc6, buf6, ss6, rs6)
    accm[...] = dot_tn(cat[...], dzc_b)
    exchange_finish(loc6, buf6, ss6, rs6, sums6, INNER)
    fill_inner_back(coef_in, sums6, count)

    def dz_inner(y):
        for t in range(2):
            dz1[y, :, 384 + 128 * t : 512 + 128 * t] = inner_dz(
                clips, t, zin[y], din[y], coef_in
            )

    loop(side, dz_inner)
    dz1_b = dz1[...].reshape(total, 640).astype(BF16)
    hgv = dot_nt(dz1_b, wp[...]).astype(BF16).astype(F32)
    hg[:, :, :, 0:D] = hgv.reshape(side, side, 8, D)
    hg[:, :, :, D:DP] = jnp.zeros((side, side, 8, DP - D), F32)
    acc7[...] = jnp.zeros_like(acc7)

    def upstream(y):
        for t in range(7):
            lanes = pl.ds(128 * t, 128)
            gr = hg[y, :, :, lanes]
            acc7[0, :, lanes] += jnp.sum(gr * asum[y, :, :, lanes], axis=0)
            acc7[1, :, lanes] += jnp.sum(gr * bsum[y, :, :, lanes], axis=0)

    loop(side, upstream)
    pack_stats(clips, loc7, acc7, FINAL)
    exchange_start(loc7, buf7, ss7, rs7)
    accs[...] = dot_tn(scat[...], dzs_b)
    accp[...] = dot_tn(hbuf[...], dz1_b)
    pool = dz1[:, :, 256:384].reshape(total, 128)
    rest = (pool - dz1_b[:, 256:384].astype(F32)).astype(BF16)
    accp[:, 256:384] += dot_tn(hbuf[...], rest)
    c = jnp.concatenate([typical(beta1[0:1, 0:D]), jnp.zeros((8, DP - D), F32)], 1)
    full = accp[...] - outer(c, accp[DP - 1 : DP, :])
    mid = centre_mid(accm[992:993, :], beta)
    small = centre_small(accs, beta)
    for k in range(3):
        pack_mid(packed[k], accm.at[512 * k : 512 * k + 512], mid, accs, small, k)

    def column(t, r, rows):
        return full[r : r + rows, 128 * t : 128 * t + 128]

    pack_one(packed[3], column)
    pack_inner(packed[4], column, accs, small)
    puts = [
        pltpu.make_async_copy(a, b, lsem.at[3 + i])
        for i, (a, b) in enumerate(zip((hg,) + packed, (hg_out,) + packed_out))
    ]
    for c in puts:
        c.start()
    exchange_finish(loc7, buf7, ss7, rs7, sums7, FINAL)
    mine.wait()
    theirs.wait()
    for c in puts:
        c.wait()


def blocks_kernel(first_scope, second_scope, *refs):
    ins, outs, refs = refs[:10], refs[10:33], refs[33:]
    len_ref, og = ins[0], ins[3]
    st1, stf, beta1, sums5, sums6, sums7 = outs[:6]
    kept, og_got, block_out, hg_out, packed_out = outs[6:15], outs[15], outs[16], outs[17], outs[18:]
    x_got, hand, asum, bsum, beta2, beta, got_beta, wp, wf, ws = refs[:10]
    sums1, sums2, (osem, psem, qsem, psem2, qsem2) = refs[10:18], refs[18:38], refs[38:]

    def one(*own):
        forward_part(
            *ins, st1, stf, beta1, *kept, og_got,
            x_got, hand, asum, bsum, beta2, beta, got_beta, wp, wf, ws,
            *sums1, osem, psem, qsem, *own,
        )

    def two(gown, ggot, grad, out, lsem, hg, p0, p1, p2, p3, p4, *own):
        second_part(
            len_ref, og, beta1, block_out, hg_out, tuple(packed_out), sums5, sums6, sums7, og_got,
            hand, asum, bsum, beta2, wp.at[1], wf.at[1], ws.at[1], psem2, qsem2, sums2,
            gown, ggot, grad, out, lsem, hg, (p0, p1, p2, p3, p4), *own,
        )

    pl.run_scoped(one, *first_scope)
    pl.run_scoped(two, *second_scope)


def pack_mid(packed, acc, mid, accs, small, k):
    for t in range(8):
        lanes = slice(128 * t, 128 * t + 128)
        packed[t, 0:480] = (acc[0:480, lanes] - mid[0:480, lanes]).astype(BF16)
        packed[t, 480:512] = small_piece(accs, small, 8 * k + t)
        if packed.shape[1] > 512:
            packed[t, 512:] = jnp.zeros((packed.shape[1] - 512, 128), BF16)


def small_piece(accs, small, b):
    dy, dt, dx = b // 9, b // 3 % 3, b % 3
    lanes = slice(128 * dx, 128 * dx + 128)
    r = 128 * dy + 32 * dt
    return (accs[r : r + 32, lanes] - small[32 * dt : 32 * dt + 32, lanes]).astype(BF16)


def pack_one(packed, column):
    end = packed.shape[1]
    for j in range(8):
        packed[j, 0:208] = column(j // 4, 208 * (j % 4), 208).astype(BF16)
        rows = min(112, D - 112 * j)
        packed[j, 208 : 208 + rows] = column(2, 112 * j, rows).astype(BF16)
        if 208 + rows < end:
            packed[j, 208 + rows : end] = jnp.zeros((end - 208 - rows, 128), BF16)


def pack_inner(packed, column, accs, small):
    end = packed.shape[1]
    for j in range(8):
        packed[j, 0:208] = column(3 + j // 4, 208 * (j % 4), 208).astype(BF16)
        packed[j, 208:end] = jnp.zeros((end - 208, 128), BF16)
        if j < 3:
            packed[j, 208:240] = small_piece(accs, small, 24 + j)


def inner_up(clips, z, backs, coef, acc, din, y):
    for t in range(2):
        lanes = slice(128 * t, 128 * t + 128)
        zs = z[:, lanes] * coef[0:1, lanes]
        d = backs[t] * clips.times(sigm(zs + coef[2:3, lanes]), clips.valid)
        din[y, :, lanes] = d
        add_stats(clips, acc, pl.ds(384 + 128 * t, 128), d, zs - coef[1:2, lanes])


def fill_inner_back(coef, sums, count):
    for t in range(2):
        fill_back(coef, pl.ds(128 * t, 128), sums, pl.ds(384 + 128 * t, 128), count)


def inner_dz(clips, t, z, d, coef):
    lanes = slice(128 * t, 128 * t + 128)
    v = d[:, lanes] * coef[0:1, lanes] + z[:, lanes] * coef[4:5, lanes] + coef[5:6, lanes]
    dz = clips.times(v, clips.valid)
    return lane_below(dz, 64) if t == 1 else dz


def put_halves(ref, y, lane, v):
    side, lanes = v.shape[0] // 16, v.shape[1]
    v = v.reshape(side, 2, 8, lanes)
    for h in range(2):
        ref[h, y, :, lane : lane + lanes] = v[:, h].reshape(side * 8, lanes).astype(BF16)


Z_FIRST = (3,)
SCHEDULE = {
    "start": ((2, 0), (3, 0),),
    "dz3": ((2, 1), (0, 0),),
    "dz5": ((4, 0), (0, 1),),
    "dz6": ((3, 1), (1, 0), (2, 2),),
    "box": ((4, 1),),
    "scat": ((1, 1), (2, 3), (0, 2),),
    "d1": ((6, 0), (3, 2), (4, 2), (1, 2), (2, 4),),
    "m0": ((6, 1), (0, 3),),
    "d0": ((5, 0), (4, 3), (2, 5),),
    "m2": ((1, 3), (3, 3), (5, 1),),
    "d2": ((6, 2), (0, 4), (2, 6), (7, 0),),
    "e": ((8, 0), (7, 1), (4, 4), (5, 2), (1, 4),),
    "cb2": ((8, 1), (6, 3), (4, 5), (0, 5),),
    "cb4": ((1, 5), (5, 3), (3, 4),),
    "cb5": ((6, 4), (7, 2), (8, 2), (0, 6), (4, 6),),
    "cb6": ((1, 6),),
    "s8a": ((5, 4), (7, 3),),
    "dzi": ((6, 5),),
    "l": ((9, 0), (3, 5), (8, 3), (5, 5),),
    "in1": ((9, 1), (7, 4),),
    "in2": ((6, 6),),
    "in3": ((9, 2), (7, 5), (8, 4), (2, 7), (5, 6), (9, 3),),
    "in5": ((1, 7), (8, 5), (6, 7), (9, 4),),
    "in6": ((3, 6), (7, 6),),
    "in9": ((9, 5), (4, 7), (8, 6),),
    "in13": ((7, 7), (9, 6), (0, 7), (5, 7), (3, 7), (8, 7), (9, 7),),
}


def backward_kernel(
    bits, len_ref, hg, stf, sums7, st1, beta, sums5, sums6,
    zf, sig, zin_in, wf_in, ws_in, wp_in, cat_in, scat_in, x, x_got, two0, two1, two2, two3, two4,
    gin, full0, full1, full2, full3, full4, offs,
    zin, wf, ws, wp, cat, scat, x0, x1, dzc, dzs, dz1, dzi, sums8, snd, got,
    coef, coef_in, acc, loc, buf, ss8, rs8, lsem, csend, crecv, ssem, rsem, gsend, grecv, *arrays,
):
    greet(partner=True)
    sec = lax.axis_index("section")
    side = dz1.shape[1]
    half = side // 2
    rows = side * 16
    clips = Clips(len_ref, 16, 1)
    count = stf[2:3, 0:128]
    loads = [
        pltpu.make_async_copy(a, b, lsem.at[i])
        for i, (a, b) in enumerate(
            (
                (zin_in, zin),
                (wf_in, wf),
                (ws_in, ws),
                (wp_in, wp),
                (cat_in, cat),
                (scat_in, scat),
                (x.at[sec], x0),
                (x_got, x1),
            )
        )
    ]
    two = (two0, two1, two2, two3, two4)
    full = (full0, full1, full2, full3, full4)
    own_two, ones = arrays[0:5], arrays[5:10]
    core_land = arrays[10:20]
    pieces = 2 ** len(groups(bits)[-1]) - 1 + len(groups(bits)) - 1
    lands = arrays[20:]

    def part(ref, which):
        h = ref.shape[1] // 2
        return ref.at[:, pl.ds(pl.multiple_of(which * h, 16), h)]

    def reducer(i, q, base, rows, swap_src, flip, load):
        return Reducer(
            bits, i, q, base, rows, swap_src, core_land[i], lands[pieces * i : pieces * i + pieces],
            csend, crecv, ssem, rsem, flip, load,
        )

    g, h = [], []
    for i, (a, b) in enumerate(zip(two, own_two)):
        load = pltpu.make_async_copy(part(a, sec), b, lsem.at[8 + i])
        load.start()
        g.append(reducer(i, b, 0, b.shape[1], part(a, 1 - sec), 1 - sec, load))
    for i, a in enumerate(ones):
        rows_half = a.shape[1] // 2
        h.append(
            reducer(5 + i, a, sec * rows_half, rows_half, part(a, 1 - sec), sec, None)
        )
    def at(name):
        for r, e in SCHEDULE.get(name, ()):
            (g + h)[r].event(e)

    acc[...] = jnp.zeros_like(acc)
    loc[...] = jnp.zeros_like(loc)
    for t in range(7):
        lanes = pl.ds(128 * t, 128)
        fill_norm(coef, lanes, stf, lanes, beta[0:1, lanes])
        fill_back(coef, lanes, sums7, lanes, count)
    fill_inner(coef_in, st1, beta)
    for y in (0, side + 1):
        dzc[y] = jnp.zeros(dzc.shape[1:], BF16)
        dzs[y] = jnp.zeros(dzs.shape[1:], BF16)

    def dz_phase(zb, sb, scr, yp, tx, zsem):
        def fetch(k, slot):
            here = pl.ds(2 * k, 2)
            return (
                pltpu.make_async_copy(zf.at[here], zb.at[slot], zsem.at[0, slot]),
                pltpu.make_async_copy(sig.at[here], sb.at[slot], zsem.at[1, slot]),
            )

        for c in fetch(0, 0):
            c.start()
        for c in loads[4:] + loads[:4]:
            c.start()

        def body(k):
            slot = lax.rem(k, 2)

            @pl.when(k < half - 1)
            def _():
                for c in fetch(k + 1, 1 - slot):
                    c.start()

            @pl.when(k == 1)
            def _():
                greeted(partner=True)
                at("start")

            for j in range(2, half):
                pl.when(k == j)(lambda j=j: at(f"dz{j}"))
            for c in fetch(k, slot):
                c.wait()
            tiles = ([], [])
            for t in range(7):
                lanes = pl.ds(128 * t, 128)
                by_z, rest = coef[4:5, lanes], coef[5:6, lanes]
                gr = hg[k, :, :, lanes] * (coef[0:1, lanes] * 0.125)
                scr[:, pl.ds(0, 8, stride=2), :] = gr
                scr[:, pl.ds(1, 8, stride=2), :] = gr
                gr = scr[...]
                gr = jnp.broadcast_to(gr[:, None], (half, 2, 16, 128)).reshape(rows, 128)
                for q in range(2):
                    v = gr * sb[slot, q, :, lanes].astype(F32) + zb[slot, q, :, lanes] * by_z
                    dz = clips.times(v + rest, clips.valid)
                    if t < 2:
                        put_halves(dz1, 2 * k + q, 128 * t, dz)
                    else:
                        tiles[q].append(dz)
            for q in range(2):
                y = 2 * k + q
                small, tail, pool = split_final(*tiles[q][2:])
                yp[y] = clips.times(pool * inv_edges(side, 16, y), clips.inv)

                def put(ref, y=y):
                    def go(lane, v):
                        ref[y + 1, :, lane : lane + v.shape[-1]] = v.astype(BF16)

                    return go

                main = jnp.concatenate(tiles[q][:2], 1).astype(BF16)
                put_spread(16, main, small.astype(BF16), tail, put(dzc), put(dzs))

        loop(half, body)
        at("dzend")

        def boxed(y, v):
            put_halves(dz1, y, 256, clips.times(v, clips.valid))

        box(clips, side, lambda y: yp[y], tx, boxed)
        at("box")

    pl.run_scoped(
        dz_phase,
        vmem(2, 2, rows, DP),
        vmem(2, 2, rows, DP, dtype=BF16),
        vmem(half, 16, 128),
        vmem(side, rows, 128),
        vmem(side + 2, rows, 128),
        pltpu.SemaphoreType.DMA((2, 2)),
    )

    def grad_phase(accm, mid, accs, accp):
        for c in loads[4:6]:
            c.wait()
        ny = side // 2

        def take(ref, y):
            return ref[pl.ds(y, ny)].reshape(ny * rows, ref.shape[-1])

        def sums(k, between):
            accm[...] = dot_tn(take(cat, 1), take(dzc, 2 - k))
            between()
            accm[...] += dot_tn(take(cat, 1 + ny), take(dzc, 2 - k + ny))

        for k in range(3):
            here = slice(128 * k, 128 * k + 128)
            accs[here] = dot_tn(take(scat, 1), take(dzs, 2 - k))
            accs[here] += dot_tn(take(scat, 1 + ny), take(dzs, 2 - k + ny))
        small = centre_small(accs, beta)
        at("scat")
        for k in (1, 0, 2):
            sums(k, lambda: at(f"m{k}"))
            if k == 1:
                mid[...] = centre_mid(accm[480:481, :], beta)
            pack_mid(ones[k], accm, mid, accs, small, k)
            at(f"d{k}")
        for c in loads[6:]:
            c.wait()
        accp[...] = jnp.zeros_like(accp)
        add_outer(accp, dz1, ((x1, 1 - sec), (x0, sec)))
        pack_one(ones[3], lambda t, r, n: accp[r : r + n, 128 * t : 128 * t + 128])
        pack_inner(ones[4], lambda t, r, n: jnp.zeros((n, 128), F32), accs, small)
        at("e")

    def add_outer(accp, d_ref, sides):
        step = side // 2
        size = step * side * 8
        for src, which in sides:

            def body(i, src=src, which=which):
                at = pl.ds(pl.multiple_of(i * size, 16), size)
                d = d_ref[which, pl.ds(i * step, step)].reshape(size, d_ref.shape[-1])
                accp[...] += dot_tn(src[at], d)

            loop(side // step, body)

    pl.run_scoped(
        grad_phase,
        vmem(512, 1024),
        vmem(512, 1024),
        vmem(384, 384),
        vmem(D, 384),
    )

    def last_phase(din, ring, accp, sems):
        for c in loads[:4]:
            c.wait()
        ny = 2

        def body(i):
            y0 = i * ny + 1
            for j in range(side // ny):
                pl.when(i == j)(lambda j=j: at(f"cb{j}"))
            q = s = None
            for dy in (-1, 0, 1):
                k = dy + 1
                here = pl.ds(y0 - dy, ny)
                t = dot_nt(dzc[here].reshape(ny * rows, 1024), wf[512 * k : 512 * k + 512])
                q = t if q is None else q + t
                t = dot_nt(dzs[here].reshape(ny * rows, 384), ws[128 * k : 128 * k + 128])
                s = t if s is None else s + t
            for j in range(ny):
                y = i * ny + j
                here = slice(j * rows, (j + 1) * rows)
                parts = [q[here, 128 * t : 128 * t + 128] for t in range(4)]
                inner_up(clips, zin[y], untap(clips, parts, s[here]), coef_in, acc, din, y)

        loop(side // ny, body)
        pack_stats(clips, loc, acc, INNER)
        exchange_start(loc, buf, ss8, rs8)
        at("s8a")
        sides = ((x1, 1 - sec), (x0, sec))
        step = side // 2
        size = step * side * 8
        exchange_finish(loc, buf, ss8, rs8, sums8, INNER)
        fill_inner_back(coef_in, sums8, count)
        at("s8b")

        def dz(y):
            for t in range(2):
                put_halves(dzi, y, 128 * t, inner_dz(clips, t, zin[y], din[y], coef_in))

        loop(side, dz)
        at("dzi")
        accp[...] = jnp.zeros_like(accp)
        add_outer(accp, dzi, sides)
        for j in range(8):
            ones[4][j, 0:208] = accp[
                208 * (j % 4) : 208 * (j % 4) + 208, 128 * (j // 4) : 128 * (j // 4) + 128
            ].astype(BF16)
        at("l")
        sent = []
        step = 2
        size = step * side * 8
        chunks = side // step
        slots = ring.shape[0]
        for p in range(2 * chunks):
            which = sides[p // chunks][1]
            i = p % chunks
            slot = p % slots
            if p >= slots:
                sent[p - slots].wait()
            here = pl.ds(i * step, step)
            d = jnp.concatenate([dz1[which, here], dzi[which, here]], -1).reshape(size, 640)
            ring[slot] = dot_nt(d, wp[...]).astype(BF16)
            to = gin.at[sec, i * size : (i + 1) * size]
            if p < chunks:
                c = swap_copy(ring.at[slot], to, gsend.at[i], grecv.at[i])
            else:
                c = pltpu.make_async_copy(ring.at[slot], to, sems.at[slot])
            c.start()
            sent.append(c)
            at(f"in{p}")
        for c in sent[-slots:]:
            c.wait()

    dma = pltpu.SemaphoreType.DMA
    pl.run_scoped(
        last_phase,
        vmem(side, rows, 256),
        vmem(4, 2 * side * 8, D, dtype=BF16),
        vmem(D, 256),
        dma((4,)),
    )
    snd[:, 0:DP] = jnp.where(sec == 0, sums5[...], sums7[...])
    snd[:, DP : DP + 640] = jnp.where(sec == 0, sums6[...], sums8[...])
    small = swap_copy(snd, got, csend.at[15], crecv.at[15])
    small.start()
    at("end")

    def finish(mine, theirs):
        copies = []
        for i, (dst, m, t) in enumerate(zip(full, mine, theirs)):
            copies.append(pltpu.make_async_copy(m, dst.at[sec], lsem.at[13 + i]))
            copies.append(swap_copy(t, dst.at[sec], csend.at[10 + i], crecv.at[10 + i]))
        for c in copies:
            c.start()
        for c in copies:
            c.wait()

    pl.when(sec == 0)(lambda: finish(core_land[5:10], core_land[0:5]))
    pl.when(sec == 1)(lambda: finish(core_land[0:5], core_land[5:10]))
    small.wait()
    for lanes, a, b in ((slice(0, DP), sums7, sums5), (slice(DP, DP + 640), sums8, sums6)):
        offs[:, lanes] = jnp.where(sec == 0, a[...], b[...]) + got[:, lanes]


def put_halves(ref, y, lane, v):
    side, lanes = v.shape[0] // 16, v.shape[1]
    v = v.reshape(side, 2, 8, lanes)
    for h in range(2):
        ref[h, y, :, lane : lane + lanes] = v[:, h].reshape(side * 8, lanes).astype(BF16)


def groups(bits, last_first=False):
    if bits < 3:
        return [(k,) for k in range(bits)]
    plan = [(k,) for k in range(bits - 2)] + [(bits - 2, bits - 1)]
    return plan[-1:] + plan[:-1] if last_first else plan


class Reducer:
    EVENTS = 8

    def __init__(
        self, bits, index, q, base, rows, swap_src, core_land, land, csend, crecv, ssem, rsem, flip, load
    ):
        self.index, self.q, self.base, self.rows = index, q, base, rows
        self.core_land, self.land, self.load = core_land, land, load
        self.ssem, self.rsem = ssem, rsem
        self.swap = swap_copy(swap_src, core_land, csend.at[index], crecv.at[index])
        me = lax.axis_index("dp")
        plan = groups(bits, index in Z_FIRST)
        self.count = len(plan)
        self.last = 2 * self.count
        self.steps = []
        tiles, t0, r0 = 8, 0, 0
        at = 0
        for step, ks in enumerate(plan):
            powers = []
            for k in ks:
                power = 1 << k
                if bits > 1 and k < 2:
                    power = power + flip * ((1 << (1 - k)) - power)
                powers.append((power, lax.rem(me // power, 2)))
            cuts = []
            for power, bit in powers:
                if tiles > 1:
                    tiles //= 2
                    cuts.append((bit, tiles, 0))
                else:
                    rows //= 2
                    cuts.append((bit, 0, rows))
            sends = []
            for c in range(1, 1 << len(ks)):
                partner, t, r = me, t0, r0
                for i, ((power, bit), (_, dt, dr)) in enumerate(zip(powers, cuts)):
                    turned = (c >> i) & 1
                    partner = partner + turned * (1 - 2 * bit) * power
                    here = bit + turned * (1 - 2 * bit)
                    t, r = t + here * dt, r + here * dr
                sends.append((partner, (t, r), at))
                at += 1
            for bit, dt, dr in cuts:
                t0, r0 = t0 + bit * dt, r0 + bit * dr
            self.steps.append((sends, (t0, r0), tiles, rows))
        self.pieces = at

    def region(self, ref, base, at, tiles, rows):
        t, r = at
        r = base + r
        if not isinstance(r, int):
            r = pl.multiple_of(r, 16)
        return ref.at[pl.ds(t, tiles), pl.ds(r, rows)]

    def mine(self, at, tiles, rows):
        return self.region(self.q, self.base, at, tiles, rows)

    def total(self, at, tiles, rows):
        return self.region(self.core_land, 0, at, tiles, rows)

    def copies(self, i):
        if i == 0:
            return [self.swap]
        halving = i <= self.count
        sends, keep, tiles, rows = self.steps[i - 1 if halving else self.last - i]
        out = []
        for partner, send, piece in sends:
            src = self.mine(send, tiles, rows) if halving else self.total(keep, tiles, rows)
            sem = 2 * (self.index * self.pieces + piece) + int(halving)
            out.append(
                pltpu.make_async_remote_copy(
                    src_ref=src,
                    dst_ref=self.land[piece] if halving else src,
                    send_sem=self.ssem.at[sem],
                    recv_sem=self.rsem.at[sem],
                    device_id={"dp": partner},
                    device_id_type=MESH,
                )
            )
        return out

    def received(self, i):
        sends, keep, tiles, rows = self.steps[self.last - i]
        out = []
        for partner, send, piece in sends:
            sem = 2 * (self.index * self.pieces + piece)
            dst = self.total(send, tiles, rows)
            out.append(
                pltpu.make_async_remote_copy(
                    src_ref=dst,
                    dst_ref=dst,
                    send_sem=self.ssem.at[sem],
                    recv_sem=self.rsem.at[sem],
                    device_id={"dp": partner},
                    device_id_type=MESH,
                )
            )
        return out

    def add(self, dst, q, lands, tiles, rows):
        chunk = next(c for c in range(min(rows, 256), 0, -16) if rows % c == 0 and c % 16 == 0)
        parts = rows // chunk

        def body(j):
            t, r = j // parts, pl.multiple_of(lax.rem(j, parts) * chunk, 16)
            at = pl.ds(r, chunk)
            total = q[t, at].astype(F32)
            for land in lands:
                total = total + land[t, at].astype(F32)
            dst[t, at] = total.astype(BF16)

        loop(tiles * parts, body)

    def finish(self, i):
        if i > self.count:
            for c in self.copies(i):
                c.wait_send()
            for c in self.received(i):
                c.wait_recv()
            return
        for c in self.copies(i):
            c.wait()
        if i == 0:
            if self.load is not None:
                self.load.wait()
            q = self.mine((0, 0), 8, self.rows)
            self.add(q, q, [self.core_land], 8, self.rows)
        else:
            sends, keep, tiles, rows = self.steps[i - 1]
            lands = [self.land[piece] for _, _, piece in sends]
            q = self.mine(keep, tiles, rows)
            dst = self.total(keep, tiles, rows) if i == self.count else q
            self.add(dst, q, lands, tiles, rows)

    def event(self, e):
        count = self.last + 2
        for i in range(e * count // self.EVENTS, (e + 1) * count // self.EVENTS):
            if i > 0:
                self.finish(i - 1)
            if i <= self.last:
                for c in self.copies(i):
                    c.start()


def land_shapes(tiles, rows, bits, last_first):
    out = []
    for ks in groups(bits, last_first):
        for _ in ks:
            if tiles > 1:
                tiles //= 2
            else:
                rows //= 2
        out += [(tiles, rows, 128)] * (2 ** len(ks) - 1)
    return out


def unpack_kernel(
    full0, full1, full2, full3, full4, gin_in, out_in, offs,
    one, mid_in, mid_out, small_in, small, pool, offset, gin, out,
    buf0, buf1, buf2, buf3, buf4, nat, inner, gin_buf, out_buf, mid, sem,
):
    copies = []
    bufs = (buf0, buf1, buf2, buf3, buf4)
    for i, (full, buf) in enumerate(zip((full0, full1, full2, full3, full4), bufs)):
        half = full.shape[2]
        for h in range(2):
            copies.append(
                pltpu.make_async_copy(full.at[h], buf.at[:, h * half : (h + 1) * half], sem.at[2 * i + h])
            )
    for c in copies:
        c.start()
    through = ((gin_in, gin_buf, gin), (out_in, out_buf, out))
    for i, (src, buf, dst) in enumerate(through):
        pltpu.make_async_copy(src, buf, sem.at[10 + i]).start()
    v = offs[...]
    lane = lax.broadcasted_iota(jnp.int32, v.shape, 1)
    out = jnp.where(lane < 256, v, 0.0)
    for lo, hi, by in ((256, 416, -1024), (416, 736, 160), (736, 768, -704), (768, 1024, 192)):
        out = jnp.where((lane >= lo) & (lane < hi), roll_lanes(v, by), out)
    offset[...] = out[0:1, 0:1024]
    for c in copies:
        c.wait()

    def take(b, t, r, rows):
        return bufs[b][t, r : r + rows].astype(F32)

    for dt in range(3):
        for dy in range(3):
            for dx in range(3):
                to = 160 * (9 * dt + 3 * dy + dx)
                for rows, r in ((128, 128 * dt), (32, 384 + 32 * dt)):
                    nat[to : to + rows, 0:128] = take(dy, 2 * dx, r, rows)
                    nat[to : to + rows, 128:256] = take(dy, 2 * dx + 1, r, rows)
                    tail = take(dy, 6 + dx // 2, r, rows)
                    nat[to : to + rows, 256:384] = roll_lanes(tail, 64) if dx == 1 else tail
                    to = to + rows
                b = 9 * dy + 3 * dt + dx
                to = 32 * (9 * dt + 3 * dy + dx)
                small[to : to + 32, :] = (
                    take(b // 8, b % 8, 480, 32) if b < 24 else take(4, b - 24, 208, 32)
                )

    def turn(i):
        at = pl.ds(pl.multiple_of(i * 128, 128), 128)
        mid[0:256, at] = nat[at, 0:256].T
        mid[256:320, at] = nat[at, 256:384].T[0:64]

    total = mid.shape[1]
    passed = []
    for i, (src, buf, dst) in enumerate(through):
        pltpu.make_async_copy(src, buf, sem.at[10 + i]).wait()
        passed.append(pltpu.make_async_copy(buf, dst, sem.at[10 + i]))
        passed[i].start()
    blocks = total // 128
    for part in range(3):
        lo, hi = part * blocks // 3, (part + 1) * blocks // 3
        loop(hi - lo, lambda i, lo=lo: turn(i + lo))
        end = 128 * hi
        if part == 2:
            at = slice(end, total)
            mid[0:256, at] = nat[at, 0:256].T
            mid[256:320, at] = nat[at, 256:384].T[0:64]
            end = total
        at = slice(128 * lo, end)
        passed.append(pltpu.make_async_copy(mid.at[:, at], mid_out.at[:, at], sem.at[12 + part]))
        passed[-1].start()
    for j in range(8):
        at = slice(208 * (j % 4), 208 * (j % 4) + 208)
        one[at, 128 * (j // 4) : 128 * (j // 4) + 128] = take(3, j, 0, 208)
        inner[j // 4, at] = take(4, j, 0, 208)
        rows = min(112, D - 112 * j)
        pool[112 * j : 112 * j + rows, :] = take(3, j, 208, rows)
    for r in range(0, D, 128):
        at = slice(r, min(r + 128, D))
        mid_in[0:128, at] = inner[0, at].T
        last = inner[1, at].T
        mid_in[128:160, at] = last[0:32]
        small_in[:, at] = last[32:64]
    for c in passed:
        c.wait()


def vmem(*shape, dtype=F32):
    return pltpu.VMEM(shape, dtype)


def call(kernel, outs, args, scratch, collective=None, smem_first=True, any_in=(), any_out=()):
    def specs(count, anywhere):
        return [
            pl.BlockSpec(memory_space=pl.ANY if i in anywhere else pltpu.VMEM)
            for i in range(count)
        ]

    in_specs = specs(len(args), any_in)
    if smem_first:
        in_specs[0] = pl.BlockSpec(memory_space=pltpu.SMEM)
    params = {"vmem_limit_bytes": VMEM_LIMIT}
    if collective is not None:
        params.update(collective_id=collective, has_side_effects=True)
    return pl.pallas_call(
        kernel,
        out_shape=[jax.ShapeDtypeStruct(shape, dtype) for shape, dtype in outs],
        in_specs=in_specs,
        out_specs=specs(len(outs), any_out),
        scratch_shapes=scratch,
        compiler_params=pltpu.CompilerParams(**params),
    )(*args)


def on_device(
    clip_input, out_grad, clip_lengths, w_one, w_mid_in, w_mid, w_small_in, w_small, w_pool, bn_offset
):
    n = lax.axis_size("dp")
    bits = n.bit_length() - 1
    half, side = clip_input.shape[1], clip_input.shape[2]
    rows = side * 16
    side2 = side // 2
    rows2 = side2 * 8
    total2 = side2 * rows2
    unit = 32 << max(bits - 3, 0)
    packed_rows = [-(-r // unit) * unit for r in (512, 512, 512, 320, 256)]
    x = clip_input.transpose(0, 2, 3, 1, 4).reshape(2, side * side * half, D)
    og = out_grad.transpose(0, 2, 3, 1, 4)

    def like(a, dtype=BF16):
        return pltpu.VMEM(a.shape[1:], dtype)

    def turned(w):
        return w.transpose(0, 2, 1)

    weights = (w_one, turned(w_mid_in), turned(w_small_in), w_pool, turned(w_mid), w_small)
    dma = pltpu.SemaphoreType.DMA
    grid = (side, side, 2, 8)

    def bf(*shape):
        return vmem(*shape, dtype=BF16)

    pooled = (side2, side2, 8, DP)
    first_scope = [
        vmem(*grid, DP),
        vmem(*grid, 256),
        vmem(side, rows, 128),
        bf(side + 2, rows, 512),
        bf(side + 2, rows, 128),
        bf(side, rows, DP),
        vmem(side2, 16, 128),
        vmem(8, 512),
        vmem(8, DP),
        vmem(8, 256),
        vmem(2, 2, 8, 640),
        vmem(2, 16, 640),
        vmem(2, 16, 512),
    ]
    second_scope = (
        [
            like(og),
            like(og),
            vmem(side2, side2, 8, D),
            bf(2, *og.shape[1:]),
            dma((9,)),
            vmem(*pooled),
        ]
        + [bf(8, r, 128) for r in packed_rows]
        + [
            bf(total2, DP),
            vmem(side2, rows2, 256),
            vmem(side2, rows2, 128),
            vmem(side2, rows2, DP),
            vmem(8, DP),
            vmem(side2, rows2, 128),
            vmem(side2 + 2, rows2, 128),
            vmem(side2 + 2, rows2, 640),
            bf(total2, 1536),
            bf(total2, 384),
            vmem(side2, rows2, 1024),
            vmem(side2, rows2, 384),
            vmem(side2, rows2, DP),
            vmem(side2, rows2, 1024),
            vmem(side2, rows2, 384),
            vmem(side2, rows2, 640),
            vmem(side2, rows2, 256),
            vmem(2, 8, 640),
            vmem(8, 640),
            vmem(8, 512),
            vmem(2, 8, DP),
            vmem(1536, 1024),
            vmem(384, 384),
            vmem(DP, 640),
            vmem(8, DP),
            vmem(8, 256),
        ]
    )
    st1, stf, beta1, sums5, sums6, sums7, *rest = call(
        functools.partial(blocks_kernel, first_scope, second_scope),
        [
            ((8, 640), F32),
            ((8, DP), F32),
            ((1, 1152), F32),
            ((8, DP), F32),
            ((8, 640), F32),
            ((8, DP), F32),
            (x.shape[1:], BF16),
            (grid + (256,), F32),
            (grid + (DP,), F32),
            ((side, rows, DP), BF16),
            ((side + 2, rows, 512), BF16),
            ((side + 2, rows, 128), BF16),
            ((D, 640), BF16),
            ((1536, 1024), BF16),
            ((384, 384), BF16),
            (og.shape[1:], BF16),
            (og.shape, BF16),
            (pooled, F32),
        ]
        + [((8, r, 128), BF16) for r in packed_rows],
        (clip_lengths, bn_offset, x, og) + weights,
        [
            like(x),
            vmem(*pooled),
            vmem(*pooled),
            vmem(*pooled),
            vmem(1, 1152),
            vmem(1, 1152),
            vmem(1, 1152),
            bf(2, D, 640),
            bf(2, 1536, 1024),
            bf(2, 384, 384),
        ]
        + exchange_scratch(n, 16)
        + exchange_scratch(n, 8)
        + exchange_scratch(n, 16)
        + exchange_scratch(n, 8)
        + exchange_scratch(n, 16)
        + exchange_scratch(n, 8)
        + exchange_scratch(n, 16)
        + [dma((9,)), dma((6,)), dma((6,)), dma(()), dma(())],
        collective=1,
        any_in=range(2, 10),
        any_out=range(6, 23),
    )
    xgot, zin, zf, sig, cat, scat, wp1, wf1, ws1, og_got, block_output, hg, *two = rest
    zin = zin.reshape(side, rows, 256)
    zf = zf.reshape(side, rows, DP)
    halves = [r // 2 for r in packed_rows]
    lands = []
    for i, h in enumerate(halves * 2):
        lands += [bf(*shape) for shape in land_shapes(8, h, bits, i in Z_FIRST)]
    gin, *full, offs = call(
        functools.partial(backward_kernel, bits),
        [(x.shape, BF16)]
        + [((2, 8, h, 128), BF16) for h in halves]
        + [((8, DP + 640), F32)],
        (clip_lengths, hg, stf, sums7, st1, beta1, sums5, sums6)
        + (zf, sig, zin, wf1, ws1, wp1, cat, scat, x, xgot, *two),
        [
            vmem(side, rows, 256),
            bf(1536, 1024),
            bf(384, 384),
            bf(D, 640),
            bf(side + 2, rows, 512),
            bf(side + 2, rows, 128),
            like(x),
            like(x),
            bf(side + 2, rows, 1024),
            bf(side + 2, rows, 384),
            bf(2, side, rows // 2, 384),
            bf(2, side, rows // 2, 256),
            vmem(8, 640),
            vmem(8, DP + 640),
            vmem(8, DP + 640),
            vmem(8, DP),
            vmem(8, 256),
            vmem(2, 16, 640),
        ]
        + exchange_scratch(n, 8)
        + [dma((18,)), dma((16,)), dma((16,)), dma((2 * len(lands),)), dma((2 * len(lands),))]
        + [dma((side,)), dma((side,))]
        + [bf(8, h, 128) for h in halves]
        + [bf(8, r, 128) for r in packed_rows]
        + [bf(8, h, 128) for h in halves * 2]
        + lands,
        collective=3,
        any_in=range(8, 23),
        any_out=range(6),
    )
    one, mid_in, mid, small_in, small, pool, offset, gin, block_output = call(
        unpack_kernel,
        [
            ((D, C0), F32),
            ((C1A, D), F32),
            ((C1B, 27 * C1A), F32),
            ((C2A, D), F32),
            ((27 * C2A, C2B), F32),
            ((D, C3), F32),
            ((1, 1024), F32),
            (x.shape, BF16),
            (og.shape, BF16),
        ],
        (*full, gin, block_output, offs),
        [bf(8, r, 128) for r in packed_rows]
        + [vmem(27 * C1A, 384), vmem(2, D, 128), bf(*x.shape), bf(*og.shape), vmem(C1B, 27 * C1A), dma((15,))],
        smem_first=False,
        any_in=range(7),
        any_out=(2, 7, 8),
    )
    input_grad = gin.reshape(2, side, side, half, D).transpose(0, 3, 1, 2, 4)
    return (
        block_output.transpose(0, 3, 1, 2, 4),
        input_grad,
        one[None],
        mid_in.T[None],
        mid.T[None],
        small_in.T[None],
        small[None],
        pool[None],
        offset,
    )


def solution(mesh):
    placed = (
        P("dp", "section", None, None, None),
        P("dp", "section", None, None, None),
        P("dp", None),
        P("section", None, None),
        P("section", None, None),
        P("section", None, None),
        P("section", None, None),
        P("section", None, None),
        P("section", None, None),
        P("section", None),
    )
    return jax.shard_map(
        on_device,
        mesh=mesh,
        in_specs=placed,
        out_specs=(
            P("dp", "section", None, None, None),
            P("dp", "section", None, None, None),
            P("section", None, None),
            P("section", None, None),
            P("section", None, None),
            P("section", None, None),
            P("section", None, None),
            P("section", None, None),
            P("section", None),
        ),
        check_vma=False,
    )
```
